32 devices in a mesh: dp: 4 (over x, core), fsdp: 8 (over z, y).
Axes of the slice: x: 2, y: 2, z: 4, core: 2. Of those that a mesh axis runs over, the one named last changes fastest.
Arguments:
- token_ids: int32 [2, 128, 128], P(None, ('dp', 'fsdp')), may hold values from 0 to 30719
- valid_mask: int32 [2, 128, 128], P(None, ('dp', 'fsdp')), may hold values from 0 to 1, as said below
- seq_ids: int32 [2, 128, 128], P(None, ('dp', 'fsdp')), may hold values from 0 to 3, never falling along the last dimension, each value on 1 to 64 neighbouring positions
- mask_pos: int32 [2, 128, 20], P(None, ('dp', 'fsdp')), may hold values from 0 to 127, as said below
- mask_labels: int32 [2, 128, 20], P(None, ('dp', 'fsdp')), may hold values from 0 to 30719
- teacher_in: bfloat16 [2, 128, 128, 768], P(None, ('dp', 'fsdp')), may hold values from -6 to 6
- teacher_flat: bfloat16 [7077888], P(('dp', 'fsdp'))
- teacher_vec: bfloat16 [9984], replicated
- teacher_head: bfloat16 [30720, 768], P('fsdp')
- emb_table: float32 [30720, 312], P(('dp', 'fsdp'))
- emb_first: float32 [30720, 312], P(('dp', 'fsdp')), may hold values from -9.536743e-06 to 9.536743e-06
- emb_second: float32 [30720, 312], P(('dp', 'fsdp')), may hold values from 2.057727e-13 to 8.230908e-13
- pos_table: float32 [128, 312], P(('dp', 'fsdp')), may hold values from -6 to 6
- pos_first: float32 [128, 312], P(('dp', 'fsdp')), may hold values from -9.536743e-06 to 9.536743e-06
- pos_second: float32 [128, 312], P(('dp', 'fsdp')), may hold values from 2.057727e-13 to 8.230908e-13
- layer_flat: float32 [2, 1138176], P(None, ('dp', 'fsdp'))
- layer_first: float32 [2, 1138176], P(None, ('dp', 'fsdp')), may hold values from -9.536743e-06 to 9.536743e-06
- layer_second: float32 [2, 1138176], P(None, ('dp', 'fsdp')), may hold values from 2.057727e-13 to 8.230908e-13
- proj_weight: float32 [312, 768], P(None, ('dp', 'fsdp')), may hold values from -0.3125 to 0.3125
- proj_first: float32 [312, 768], P(None, ('dp', 'fsdp')), may hold values from -9.536743e-06 to 9.536743e-06
- proj_second: float32 [312, 768], P(None, ('dp', 'fsdp')), may hold values from 2.057727e-13 to 8.230908e-13
- layer_vec: float32 [2, 3696], replicated
- vec_first: float32 [2, 3696], replicated, may hold values from -3.8146973e-05 to 3.8146973e-05
- vec_second: float32 [2, 3696], replicated, may hold values from 3.2923631e-12 to 1.31694525e-11
- misc_vec: float32 [1392], replicated
- misc_first: float32 [1392], replicated, may hold values from -3.8146973e-05 to 3.8146973e-05
- misc_second: float32 [1392], replicated, may hold values from 3.2923631e-12 to 1.31694525e-11
Outputs:
- loss: float32 [], replicated
- pair_count: float32 [], replicated
- grad_norm: float32 [], replicated
- emb_first_new: float32 [30720, 312], P(('dp', 'fsdp'))
- emb_second_new: float32 [30720, 312], P(('dp', 'fsdp'))
- emb_new: float32 [30720, 312], P(('dp', 'fsdp'))
- pos_first_new: float32 [128, 312], P(('dp', 'fsdp'))
- pos_second_new: float32 [128, 312], P(('dp', 'fsdp'))
- pos_new: float32 [128, 312], P(('dp', 'fsdp'))
- layer_first_new: float32 [2, 1138176], P(None, ('dp', 'fsdp'))
- layer_second_new: float32 [2, 1138176], P(None, ('dp', 'fsdp'))
- layer_new: float32 [2, 1138176], P(None, ('dp', 'fsdp'))
- proj_first_new: float32 [312, 768], P(None, ('dp', 'fsdp'))
- proj_second_new: float32 [312, 768], P(None, ('dp', 'fsdp'))
- proj_new: float32 [312, 768], P(None, ('dp', 'fsdp'))
- vec_first_new: float32 [2, 3696], replicated
- vec_second_new: float32 [2, 3696], replicated
- vec_new: float32 [2, 3696], replicated
- misc_first_new: float32 [1392], replicated
- misc_second_new: float32 [1392], replicated
- misc_new: float32 [1392], replicated
The draws below stay inside these ranges and needn't reach their ends.
Inputs may be any that keep to these rules, and one draw needn't show every extreme that they name: `valid_mask`: the ones of each row form a prefix of one position or more. `mask_pos`: each masked position lies among its row's valid positions.
All inputs are finite; a program needn't handle non-finite values.
Results may differ from the reference program's by a relative error of at most 0.00075.
The reference program's roundings to bfloat16 on the way count: a program that leaves them out, or rounds other values in their place, can miss the bound.
Values may be sent and summed in bfloat16 or wider, within the bound.
A program may use at most 320 MiB of HBM per device.

```python
import math
from functools import partial
import jax
import jax.numpy as jnp
import numpy as np
from jax import lax

DS = 312
HS = 12
FS = 1200
DT = 768
HT = 12
FT = 3072
V = 30720
L = 128
R = 4
MICRO = 2
NL = 2
P_SIZE = 20
STEP = 5
ROWS = 128
FLAT_S = 1138176
FLAT_T = 7077888
NVEC = 3696
NMISC = 1392
NPARAMS = 12149328
N_DP = 4
N_FSDP = 8


def row_lengths(key):
    key = jax.random.fold_in(key, 101)
    row_index = jnp.arange(MICRO * ROWS, dtype=jnp.int32).reshape(MICRO, ROWS) % ROWS
    device = row_index // R
    outer_rank = device // N_FSDP
    inner_rank = device % N_FSDP
    highest = L * (N_DP - 1 + 2 * outer_rank) * (N_FSDP - 1 + 2 * inner_rank) // (9 * (N_DP - 1) * (N_FSDP - 1))
    highest = jnp.maximum(highest, 2)
    lowest = jnp.maximum(highest * 3 // 4, 1)
    return jax.random.randint(key, (MICRO, ROWS), lowest, highest + 1)


def draw_valid_mask(key, part):
    lengths = row_lengths(key)
    return (jnp.arange(L, dtype=jnp.int32)[None, None, :] < lengths[:, :, None]).astype(jnp.int32)


def draw_mask_pos(key, part):
    lengths = row_lengths(key)
    key = jax.random.fold_in(key, 2)
    return jax.random.randint(key, (MICRO, ROWS, P_SIZE), 0, lengths[:, :, None])


def vocab_scale(width, rise):
    return (1.0 + rise * jnp.arange(V, dtype=jnp.float32)[:, None] / V) * width ** (-0.5)


def draw_emb_table(key, part):
    key = jax.random.fold_in(key, 3)
    noise = jax.random.normal(key, (V, DS), jnp.float32)
    rise = 2.0
    return noise * vocab_scale(DS, rise)


def draw_teacher_head(key, part):
    key = jax.random.fold_in(key, 4)
    common = jax.random.normal(jax.random.fold_in(key, 11), (1, DT), jnp.float32) * (50.0 * DT ** (-0.5))
    noise = jax.random.normal(key, (V, DT), jnp.float32)
    rise = 2.0
    return (noise * vocab_scale(DT, rise) + common).astype(jnp.bfloat16)


def flat_scale(width, hidden, out_gain):
    return jnp.concatenate([jnp.full((3 * width * width,), width ** (-0.5), jnp.float32), jnp.full((width * width,), out_gain * width ** (-0.5), jnp.float32), jnp.full((width * hidden,), width ** (-0.5), jnp.float32), jnp.full((hidden * width,), hidden ** (-0.5), jnp.float32)])


def draw_layer_flat(key, part):
    key = jax.random.fold_in(key, 5)
    noise = jax.random.normal(key, (NL, FLAT_S), jnp.float32)
    return noise * flat_scale(DS, FS, 3.0)[None]


def draw_teacher_flat(key, part):
    key = jax.random.fold_in(key, 6)
    noise = jax.random.normal(key, (FLAT_T,), jnp.float32)
    return (noise * flat_scale(DT, FT, 3.0)).astype(jnp.bfloat16)


def vector_draw(key, sizes, gain_flags, leading):
    pieces = []
    for position, (amount, is_gain) in enumerate(zip(sizes, gain_flags)):
        piece_key = jax.random.fold_in(key, position)
        if is_gain:
            pieces.append(jax.random.uniform(piece_key, leading + (amount,), jnp.float32, 0.6, 1.4))
        else:
            pieces.append(0.3 * jax.random.normal(piece_key, leading + (amount,), jnp.float32))
    return jnp.concatenate(pieces, -1)


def draw_layer_vec(key, part):
    key = jax.random.fold_in(key, 7)
    return vector_draw(key, [DS] * 5 + [FS] + [DS] * 3, [0, 0, 0, 1, 0, 0, 0, 1, 0], (NL,))


def draw_teacher_vec(key, part):
    key = jax.random.fold_in(key, 8)
    return vector_draw(key, [DT] * 6 + [FT] + [DT] * 3, [0, 0, 0, 0, 1, 0, 0, 0, 1, 0], ()).astype(jnp.bfloat16)


def draw_misc_vec(key, part):
    key = jax.random.fold_in(key, 9)
    return vector_draw(key, [DS, DS, DT], [1, 0, 0], ())


def touch_ends(drawn, own_key, least, high):
    longest = drawn.shape.index(max(drawn.shape))
    spots = []
    for shift in (0, 1):
        where = [jax.random.randint(jax.random.fold_in(own_key, axis), (), 0, length) for axis, length in enumerate(drawn.shape)]
        where[longest] = (where[longest] + shift) % drawn.shape[longest]
        spots.append(tuple(where))
    return drawn.at[spots[0]].set(least).at[spots[1]].set(high)


def level_of(key, extent, shards, least, high):
    factor_of = 1.0
    for axis_at, blocks in shards:
        steps = jax.random.uniform(jax.random.fold_in(jax.random.fold_in(key, 6), axis_at), (blocks,), jnp.float32, least / len(shards), high / len(shards))
        factor_of = factor_of * jnp.repeat(jnp.exp(steps), extent[axis_at] // blocks).reshape((-1,) + (1,) * (len(extent) - 1 - axis_at))
    return factor_of


def rank_table(count, slope):
    loads = [(1 << 20) // math.isqrt(standing ** slope) + 1 for standing in range(1, count + 1)]
    scale = 1 + sum(loads) // (1 << 30)
    return np.cumsum(np.array([max(1, weight // scale) for weight in loads]))


def skewed_ids(stream_key, shape, count, lean):
    grid = rank_table(count, lean)
    lot = jax.random.randint(jax.random.fold_in(stream_key, 1), shape, 0, int(grid[count - 1]))
    rank = jnp.searchsorted(jnp.asarray(grid, jnp.int32), lot, side="right")
    return jax.random.permutation(jax.random.fold_in(stream_key, 2), count)[rank].astype(jnp.int32)


def split_up(count, total, reach, skew):
    portions = [(1 << 20) // math.isqrt(grade ** skew) + 1 for grade in range(2, count + 1)]
    surplus, given = total - reach - (count - 1), [1] * (count - 1)
    while surplus > 0:
        movable = [i for i in range(count - 1) if given[i] < reach]
        mass, budget = sum([portions[i] for i in movable]), surplus
        for i in movable:
            more = min(reach - given[i], max(1, budget * portions[i] // mass), surplus)
            given[i] = given[i] + more
            surplus = surplus - more
    return np.array([reach] + given)


def ragged(key, count, total, limit, lean):
    if count == 2:
        one = jax.random.randint(key, (), max(1, total - limit), min(limit, total - 1) + 1)
        return jnp.stack([one, total - one])
    sizes = jnp.asarray(split_up(count, total, limit, lean), jnp.int32)
    pairs = (count - 1) // 2
    donor, sink = sizes[1:1 + 2 * pairs:2], sizes[2:2 + 2 * pairs:2]
    slack = jnp.minimum(donor - 1, limit - sink)
    moved = jax.random.randint(jax.random.fold_in(key, 1), (pairs,), 0, 1 << 20) % (slack + 1)
    sizes = sizes.at[1:1 + 2 * pairs:2].set(donor - moved).at[2:2 + 2 * pairs:2].set(sink + moved)
    return sizes[jax.random.permutation(jax.random.fold_in(key, 2), count)]


def normal_values(key, shape, scale, limit, cuts=(), held_as=jnp.bfloat16):
    values = scale * jax.random.normal(key, shape, jnp.float32)
    if cuts:
        values = values * level_of(key, shape, cuts, -0.22, 0.18)
    return jnp.clip(values, -limit, limit).astype(held_as)


def setup_inputs(seed: int = 0) -> dict:
    splits = jax.random.split(jax.random.key(seed), 28)
    return {
        "token_ids": touch_ends(skewed_ids(splits[0], (MICRO, ROWS, L), V, 2), jax.random.fold_in(splits[0], 3), 0, V - 1).astype(jnp.int32),
        "valid_mask": draw_valid_mask(jax.random.fold_in(splits[27], 71), 0),
        "seq_ids": jax.vmap(lambda own: jnp.searchsorted(jnp.cumsum(ragged(own, 4, L, L // 2, 0)), jnp.arange(L), side="right"))(jax.random.split(splits[2], MICRO * ROWS)).reshape((MICRO, ROWS, L)).astype(jnp.int32),
        "mask_pos": draw_mask_pos(jax.random.fold_in(splits[27], 71), 0),
        "mask_labels": touch_ends(jax.random.randint(splits[4], (MICRO, ROWS, P_SIZE), 0, V), jax.random.fold_in(splits[4], 1), 0, V - 1).astype(jnp.int32),
        "teacher_in": normal_values(splits[5], (MICRO, ROWS, L, DT), 1.0, 6.0, ((1, 32),)),
        "teacher_flat": draw_teacher_flat(jax.random.fold_in(splits[27], 71), 0),
        "teacher_vec": draw_teacher_vec(jax.random.fold_in(splits[27], 71), 0),
        "teacher_head": draw_teacher_head(jax.random.fold_in(splits[27], 71), 0),
        "emb_table": draw_emb_table(jax.random.fold_in(splits[27], 71), 0),
        "emb_first": normal_values(splits[10], (V, DS), (0.0055 / NPARAMS ** 0.5), 9.5367431640625e-06, ((0, 32),), jnp.float32),
        "emb_second": jnp.clip(jnp.exp(math.log(8.230907817298461e-13) - 1.3862944 * jax.random.uniform(splits[11], (V, DS), jnp.float32) ** level_of(splits[11], (V, DS), ((0, 32),), -0.2, 0.2)), 2.0577269543246152e-13, 8.230907817298461e-13),
        "pos_table": normal_values(splits[12], (L, DS), 1.0, 6.0, ((0, 32),), jnp.float32),
        "pos_first": normal_values(splits[13], (L, DS), (0.0055 / NPARAMS ** 0.5), 9.5367431640625e-06, ((0, 32),), jnp.float32),
        "pos_second": jnp.clip(jnp.exp(math.log(8.230907817298461e-13) - 1.3862944 * jax.random.uniform(splits[14], (L, DS), jnp.float32) ** level_of(splits[14], (L, DS), ((0, 32),), -0.2, 0.2)), 2.0577269543246152e-13, 8.230907817298461e-13),
        "layer_flat": draw_layer_flat(jax.random.fold_in(splits[27], 71), 0),
        "layer_first": normal_values(splits[16], (NL, FLAT_S), (0.0055 / NPARAMS ** 0.5), 9.5367431640625e-06, ((1, 32),), jnp.float32),
        "layer_second": jnp.clip(jnp.exp(math.log(8.230907817298461e-13) - 1.3862944 * jax.random.uniform(splits[17], (NL, FLAT_S), jnp.float32) ** level_of(splits[17], (NL, FLAT_S), ((1, 32),), -0.2, 0.2)), 2.0577269543246152e-13, 8.230907817298461e-13),
        "proj_weight": normal_values(splits[18], (DS, DT), DS ** -0.5, 0.3125, ((1, 32),), jnp.float32),
        "proj_first": normal_values(splits[19], (DS, DT), (0.0055 / NPARAMS ** 0.5), 9.5367431640625e-06, ((1, 32),), jnp.float32),
        "proj_second": jnp.clip(jnp.exp(math.log(8.230907817298461e-13) - 1.3862944 * jax.random.uniform(splits[20], (DS, DT), jnp.float32) ** level_of(splits[20], (DS, DT), ((1, 32),), -0.2, 0.2)), 2.0577269543246152e-13, 8.230907817298461e-13),
        "layer_vec": draw_layer_vec(jax.random.fold_in(splits[27], 71), 0),
        "vec_first": normal_values(splits[22], (NL, NVEC), (0.022 / NPARAMS ** 0.5), 3.814697265625e-05, (), jnp.float32),
        "vec_second": jnp.clip(jnp.exp(jax.random.uniform(splits[23], (NL, NVEC), jnp.float32, math.log(3.2923631269193843e-12), math.log(1.3169452507677537e-11))), 3.2923631269193843e-12, 1.3169452507677537e-11),
        "misc_vec": draw_misc_vec(jax.random.fold_in(splits[27], 71), 0),
        "misc_first": normal_values(splits[25], (NMISC,), (0.022 / NPARAMS ** 0.5), 3.814697265625e-05, (), jnp.float32),
        "misc_second": jnp.clip(jnp.exp(jax.random.uniform(splits[26], (NMISC,), jnp.float32, math.log(3.2923631269193843e-12), math.log(1.3169452507677537e-11))), 3.2923631269193843e-12, 1.3169452507677537e-11),
    }


NORM_EPS = 1e-06
CLIP_NORM = 0.05
LEARN_RATE = 0.05
BETA_ONE = 0.9
BETA_TWO = 0.999
ADAM_EPS = 1e-06
WEIGHT_DECAY = 0.01
NEG_LARGE = -1e+30
HIGHEST = lax.Precision.HIGHEST

@jax.custom_vjp
def low(v):
    return lax.optimization_barrier(v.astype(jnp.bfloat16)).astype(jnp.float32)

@jax.custom_vjp
def low_back(v):
    return v

def low_keep(v):
    return (low(v), None)

def low_pass(kept, grad):
    return (grad,)

def back_keep(v):
    return (v, None)

def back_low(kept, grad):
    return (low(grad),)
low.defvjp(low_keep, low_pass)
low_back.defvjp(back_keep, back_low)

def matmul(left, right):
    return jnp.dot(left, right, precision=HIGHEST, preferred_element_type=jnp.float32)

def layer_norm(value, gain, bias):
    average = lax.optimization_barrier(jnp.mean(value, -1, keepdims=True))
    centered = value - average
    return centered * lax.rsqrt(lax.optimization_barrier(jnp.mean(centered * centered, -1, keepdims=True)) + NORM_EPS) * gain + bias

def cut_pieces(vector, sizes):
    pieces = []
    start = 0
    for amount in sizes:
        pieces.append(vector[..., start:start + amount])
        start += amount
    return pieces

def split_flat(flat, width, hidden):
    pieces = cut_pieces(flat, [3 * width * width, width * width, width * hidden, hidden * width])
    return (pieces[0].reshape(width, 3 * width), pieces[1].reshape(width, width), pieces[2].reshape(width, hidden), pieces[3].reshape(hidden, width))

def student_vectors(vector):
    bias_q, bias_v, bias_o, gain_one, shift_one, bias_up, bias_down, gain_two, shift_two = cut_pieces(vector, [DS] * 5 + [FS] + [DS] * 3)
    return (bias_q, jnp.zeros_like(bias_q), bias_v, bias_o, gain_one, shift_one, bias_up, bias_down, gain_two, shift_two)

def teacher_vectors(vector):
    return tuple(cut_pieces(vector, [DT] * 6 + [FT] + [DT] * 3))

def encoder_layer(hidden, matrices, vectors, allowed, heads):
    w_qkv, w_out, w_up, w_down = matrices
    bias_q, bias_k, bias_v, bias_o, gain_one, shift_one, bias_up, bias_down, gain_two, shift_two = vectors
    rows, length, width = hidden.shape
    size = width // heads
    flat = hidden.reshape(rows * length, width)
    qkv = low(low_back(matmul(low(flat), w_qkv) + jnp.concatenate([bias_q, bias_k, bias_v])))
    parts = qkv.reshape(rows, length, 3, heads, size)
    scores = low_back(jnp.einsum('rqhd,rkhd->rhqk', parts[:, :, 0], parts[:, :, 1], precision=HIGHEST) * size ** (-0.5))
    masked = jnp.where(allowed[:, None], scores, NEG_LARGE)
    topmost = lax.optimization_barrier(jnp.max(masked, -1, keepdims=True))
    expo = jnp.exp(masked - topmost)
    weights = expo / lax.optimization_barrier(jnp.sum(expo, -1, keepdims=True))
    context = jnp.einsum('rhqk,rkhd->rqhd', low(weights), parts[:, :, 2], precision=HIGHEST)
    context = low(low_back(context.reshape(rows * length, width)))
    attended = low_back(matmul(context, w_out) + bias_o)
    middle = layer_norm(flat + attended, gain_one, shift_one)
    inner = low_back(matmul(low(middle), w_up) + bias_up)
    outer = low_back(matmul(low(jax.nn.gelu(inner, approximate=True)), w_down) + bias_down)
    result = layer_norm(middle + outer, gain_two, shift_two)
    return (result.reshape(rows, length, width), scores)

def group_loss(weights, teacher, count, total, batch):
    table_low, places_low, proj_low, student, extra = weights
    t_matrices, t_vectors, t_head = teacher
    token_ids, valid_mask, seq_ids, mask_pos, mask_labels, t_input = batch
    length = token_ids.shape[1]
    usable = valid_mask > 0
    same_doc = seq_ids[:, :, None] == seq_ids[:, None, :]
    pair_mask = same_doc & usable[:, :, None] & usable[:, None, :]
    allowed = pair_mask | jnp.eye(length, dtype=bool)[None]
    hidden = layer_norm(table_low[token_ids] + places_low[None], extra[:DS], extra[DS:2 * DS])
    embedded = hidden
    for matrices, vectors in student:
        hidden, scores = encoder_layer(hidden, matrices, vectors, allowed, HS)
    t_out, t_scores = encoder_layer(t_input, t_matrices, t_vectors, allowed, HT)
    differ = scores - t_scores
    attention = jnp.sum(jnp.where(pair_mask[:, None], differ * differ, 0.0)) / count
    weight = valid_mask.astype(jnp.float32)[:, :, None]
    hidden_sum = jnp.float32(0.0)
    for source, target in ((embedded, t_input), (hidden, t_out)):
        mapped = low_back(jnp.einsum('rld,de->rle', low(source), proj_low, precision=HIGHEST) + extra[2 * DS:])
        spread = mapped - target
        hidden_sum = hidden_sum + jnp.sum(weight * spread * spread)
    position = mask_pos[:, :, None]
    picked = low(jnp.take_along_axis(hidden, position, axis=1))
    t_picked = low(jnp.take_along_axis(t_out, position, axis=1))
    student_logits = low_back(jnp.einsum('rpd,vd->rpv', picked, table_low, precision=HIGHEST))
    teacher_logits = jnp.einsum('rpd,vd->rpv', t_picked, t_head, precision=HIGHEST)
    topmost = lax.optimization_barrier(jnp.max(student_logits, -1, keepdims=True))
    log_total = topmost[..., 0] + jnp.log(lax.optimization_barrier(jnp.sum(jnp.exp(student_logits - topmost), -1)))
    teacher_top = lax.optimization_barrier(jnp.max(teacher_logits, -1, keepdims=True))
    teacher_exp = jnp.exp(teacher_logits - teacher_top)
    teacher_prob = teacher_exp / lax.optimization_barrier(jnp.sum(teacher_exp, -1, keepdims=True))
    soft_term = log_total - lax.optimization_barrier(jnp.sum(teacher_prob * student_logits, -1))
    target_logit = lax.optimization_barrier(jnp.sum(picked * table_low[mask_labels], -1))
    predict = jnp.sum(soft_term + log_total - target_logit) / (MICRO * ROWS * P_SIZE)
    return (total + attention + hidden_sum / (MICRO * ROWS * L * DT) + predict, None)

def adam_update(value, first, second, grad):
    first = BETA_ONE * first + (1.0 - BETA_ONE) * grad
    second = BETA_TWO * second + (1.0 - BETA_TWO) * grad * grad
    ratio = first / (1.0 - BETA_ONE ** STEP) / (jnp.sqrt(second / (1.0 - BETA_TWO ** STEP)) + ADAM_EPS)
    return (first, second, value - LEARN_RATE * (ratio + WEIGHT_DECAY * value))

def reference(token_ids, valid_mask, seq_ids, mask_pos, mask_labels, teacher_in, teacher_flat, teacher_vec, teacher_head, emb_table, emb_first, emb_second, pos_table, pos_first, pos_second, layer_flat, layer_first, layer_second, proj_weight, proj_first, proj_second, layer_vec, vec_first, vec_second, misc_vec, misc_first, misc_second):
    usable = valid_mask > 0
    same_doc = seq_ids[..., :, None] == seq_ids[..., None, :]
    pair_mask = same_doc & usable[..., :, None] & usable[..., None, :]
    count = jnp.sum(pair_mask.astype(jnp.int32)).astype(jnp.float32)
    teacher = (split_flat(teacher_flat.astype(jnp.float32), DT, FT), teacher_vectors(teacher_vec.astype(jnp.float32)), teacher_head.astype(jnp.float32))
    block = 8 * R
    batch = tuple((array.reshape((-1, block) + array.shape[2:]) for array in (token_ids, valid_mask, seq_ids, mask_pos, mask_labels, teacher_in.astype(jnp.float32))))

    def loss_of(params):
        table, places, flats, projection, vectors, extra = params
        student = [(split_flat(low(flats[layer_index]), DS, FS), student_vectors(vectors[layer_index])) for layer_index in range(NL)]
        weights = (low(table), low(places), low(projection), student, extra)
        total, unused = lax.scan(jax.checkpoint(partial(group_loss, weights, teacher, count)), jnp.float32(0.0), batch)
        return total
    params = (emb_table, pos_table, layer_flat, proj_weight, layer_vec, misc_vec)
    total, pull = jax.vjp(loss_of, params)
    grads = pull(jnp.float32(1.0))[0]
    squares = jnp.float32(0.0)
    for grad in grads:
        squares = squares + jnp.sum(grad * grad)
    norm = jnp.sqrt(squares)
    factor = CLIP_NORM / jnp.maximum(norm, CLIP_NORM)
    emb_a, emb_b, emb_c = adam_update(emb_table, emb_first, emb_second, grads[0] * factor)
    pos_a, pos_b, pos_c = adam_update(pos_table, pos_first, pos_second, grads[1] * factor)
    lay_a, lay_b, lay_c = adam_update(layer_flat, layer_first, layer_second, grads[2] * factor)
    pro_a, pro_b, pro_c = adam_update(proj_weight, proj_first, proj_second, grads[3] * factor)
    vec_a, vec_b, vec_c = adam_update(layer_vec, vec_first, vec_second, grads[4] * factor)
    mis_a, mis_b, mis_c = adam_update(misc_vec, misc_first, misc_second, grads[5] * factor)
    return (total, count, norm, emb_a, emb_b, emb_c, pos_a, pos_b, pos_c, lay_a, lay_b, lay_c, pro_a, pro_b, pro_c, vec_a, vec_b, vec_c, mis_a, mis_b, mis_c)
```

```python
import math
from functools import partial

import jax
import jax.numpy as jnp
from jax import lax
from jax.experimental import pallas as pl
from jax.experimental.pallas import tpu as pltpu
from jax.sharding import PartitionSpec as P

DS = 312
HS = 12
FS = 1200
DT = 768
HT = 12
FT = 3072
STEP = 5


NORM_EPS = 1e-06
CLIP_NORM = 0.05
LEARN_RATE = 0.05
BETA_ONE = 0.9
BETA_TWO = 0.999
ADAM_EPS = 1e-06
WEIGHT_DECAY = 0.01
NEG_LARGE = -1e30

BOTH = ("dp", "fsdp")
MESH = pl.DeviceIdType.MESH
SLOTS = 48
WIDE = 3 * DS + DS + 2 * FS


def place_of():
    fsdp = lax.axis_size("fsdp")
    return lax.axis_index("dp") * fsdp + lax.axis_index("fsdp")


def member(index, whole):
    fsdp = lax.axis_size("fsdp")
    if whole:
        return (index // fsdp, index % fsdp)
    return (lax.axis_index("dp"), index)


def greet(count, me, whole):
    barrier = pltpu.get_barrier_semaphore()

    def signal(step, carry):
        pl.semaphore_signal(
            barrier, inc=1, device_id=member((me + step) % count, whole), device_id_type=MESH
        )
        return carry

    lax.fori_loop(1, count, signal, 0)
    pl.semaphore_wait(barrier, count - 1)


def exchange_kernel(count, whole, spread, x_ref, o_ref, send, recv, local_sem):
    me = place_of() if whole else lax.axis_index("fsdp")
    own = pltpu.make_async_copy(x_ref if spread else x_ref.at[me], o_ref.at[me], local_sem)
    own.start()
    greet(count, me, whole)

    def copy(step):
        peer = (me + step) % count
        return pltpu.make_async_remote_copy(
            x_ref if spread else x_ref.at[peer],
            o_ref.at[me],
            send.at[step],
            recv.at[step],
            device_id=member(peer, whole),
            device_id_type=MESH,
        )

    def start(step, carry):
        copy(step).start()
        return carry

    def finish(step, carry):
        copy(step).wait()
        return carry

    lax.fori_loop(1, count, start, 0)
    own.wait()
    lax.fori_loop(1, count, finish, 0)


def exchange(x, number, whole=True, spread=False):
    count = lax.axis_size("fsdp") * (lax.axis_size("dp") if whole else 1)
    return pl.pallas_call(
        partial(exchange_kernel, count, whole, spread),
        out_shape=jax.ShapeDtypeStruct(((count,) if spread else ()) + x.shape, x.dtype),
        in_specs=[pl.BlockSpec(memory_space=pl.ANY)],
        out_specs=pl.BlockSpec(memory_space=pl.ANY),
        scratch_shapes=[
            pltpu.SemaphoreType.DMA((count,)),
            pltpu.SemaphoreType.DMA((count,)),
            pltpu.SemaphoreType.DMA,
        ],
        compiler_params=pltpu.CompilerParams(collective_id=number, has_side_effects=True),
    )(x)


class Grid:
    def __init__(self):
        self.fsdp = lax.axis_size("fsdp")
        self.z_size = 4 if self.fsdp % 4 == 0 else 1
        self.side = self.fsdp // self.z_size
        assert lax.axis_size("dp") == 2 * self.side
        dp, fsdp = lax.axis_index("dp"), lax.axis_index("fsdp")
        self.x, self.core = dp // 2, dp % 2
        self.z, self.y = fsdp // self.side, fsdp % self.side
        side, z_size = self.side, self.z_size
        self.keys = [(g, b, a) for g in range(side) for b in range(side) for a in range(z_size)]
        self.rank = {key: index for index, key in enumerate(self.keys)}
        self.count = len(self.keys)

    def at(self, third, second, z, other=0):
        core = (self.core + other) % 2
        x = (self.x + third * (1 - core) + second * core) % self.side
        y = (self.y + second * (1 - core) + third * core) % self.side
        return (x * 2 + core, ((self.z + z) % self.z_size) * self.side + y)

    def index(self, third, second, z, other=0):
        dp, fsdp = self.at(third, second, z, other)
        return dp * self.fsdp + fsdp

    def neighbours(self):
        return (
            [(0, 0, a, 0) for a in range(1, self.z_size)]
            + [(0, b, 0, 0) for b in range(1, self.side)]
            + [(g, 0, 0, 0) for g in range(1, self.side)]
            + [(0, 0, 0, 1)]
        )

    def greet(self):
        barrier = pltpu.get_barrier_semaphore()
        around = self.neighbours()
        for where in around:
            pl.semaphore_signal(barrier, inc=1, device_id=self.at(*where), device_id_type=MESH)
        pl.semaphore_wait(barrier, len(around))


class Spread:
    def __init__(self, grid, x_ref, o_ref, send, recv, local_sem):
        self.grid, self.x_ref, self.o_ref = grid, x_ref, o_ref
        self.send, self.recv = send, recv
        self.started = []
        self.own = pltpu.make_async_copy(x_ref, o_ref.at[self.slot((0, 0, 0))], local_sem)
        self.own.start()

    def slot(self, key, other=0):
        grid = self.grid
        third, second, z = key
        return grid.index(grid.side - third, grid.side - second, grid.z_size - z, other)

    def push(self, key, name, where):
        grid = self.grid
        index = grid.rank[name] + (grid.count if where[3] else 0)
        copy = pltpu.make_async_remote_copy(
            self.x_ref if key == (0, 0, 0) else self.o_ref.at[self.slot(key)],
            self.o_ref.at[self.slot(key)],
            self.send.at[index],
            self.recv.at[index],
            device_id=grid.at(*where),
            device_id_type=MESH,
        )
        copy.start()
        self.started.append(copy)

    def forward(self, key):
        grid = self.grid
        third, second, z = key
        if key == (0, 0, 0):
            for step in range(1, grid.z_size):
                self.push(key, (0, 0, step), (0, 0, step, 0))
        if third == 0 and second == 0:
            for step in range(1, grid.side):
                self.push(key, (0, step, z), (0, step, 0, 0))
        if third == 0:
            for step in range(1, grid.side):
                self.push(key, (step, second, z), (step, 0, 0, 0))
        self.push(key, key, (0, 0, 0, 1))

    def arrived(self, key, other=0):
        grid = self.grid
        index = grid.rank[key] + (grid.count if other else 0)
        pltpu.make_async_remote_copy(
            self.o_ref.at[self.slot(key, other)],
            self.o_ref.at[self.slot(key, other)],
            self.send.at[index],
            self.recv.at[index],
            device_id=grid.at(0, 0, 0, 1),
            device_id_type=MESH,
        ).wait_recv()

    def start(self):
        self.forward((0, 0, 0))

    def middle(self):
        for key in self.grid.keys[1:]:
            self.arrived(key)
            self.forward(key)

    def finish(self):
        for key in self.grid.keys:
            self.arrived(key, 1)
        self.own.wait()
        for copy in self.started:
            copy.wait_send()


def entry_kernel(
    ask_ref, w_ref, table_ref, got_ref, all_ref, rows_ref, sent, asks, *sems
):
    ask_send, ask_recv, ask_local, w_send, w_recv, w_local, row_send, row_recv, row_local, out_sem = sems
    grid = Grid()
    count = 2 * grid.count
    me = place_of()
    own = pltpu.make_async_copy(ask_ref.at[me], asks.at[me], ask_local)
    own.start()
    greet(count, me, True)

    def ask_copy(step):
        peer = (me + step) % count
        return pltpu.make_async_remote_copy(
            ask_ref.at[peer],
            asks.at[me],
            ask_send.at[step],
            ask_recv.at[step],
            device_id=member(peer, True),
            device_id_type=MESH,
        )

    def row_copy(step):
        peer = (me + step) % count
        return pltpu.make_async_remote_copy(
            sent.at[peer],
            rows_ref.at[me],
            row_send.at[step],
            row_recv.at[step],
            device_id=member(peer, True),
            device_id_type=MESH,
        )

    def each(first, action):
        def body(step, carry):
            action(step)
            return carry

        lax.fori_loop(first, count, body, 0)

    each(1, lambda step: ask_copy(step).start())
    spread = Spread(grid, w_ref, all_ref, w_send, w_recv, w_local)
    spread.start()
    own.wait()
    table = table_ref[...]
    line = lax.broadcasted_iota(jnp.int32, (table.shape[0], 128), 0)

    def answer(source):
        marks = jnp.where(line == asks[source], 1.0, 0.0).astype(jnp.bfloat16)
        sent[source] = outer_product(marks, table)[:SLOTS].astype(jnp.bfloat16)

    answer(me)
    mine = pltpu.make_async_copy(sent.at[me], rows_ref.at[me], row_local)
    mine.start()

    def serve(step):
        ask_copy(step).wait_recv()
        answer((me + count - step) % count)

    each(1, serve)
    each(1, lambda step: row_copy(step).start())
    keep = pltpu.make_async_copy(asks, got_ref, out_sem)
    keep.start()
    spread.middle()
    spread.finish()
    mine.wait()
    keep.wait()
    each(1, lambda step: row_copy(step).wait())
    each(1, lambda step: ask_copy(step).wait_send())


def entry(asked, weights, table_low, number):
    count = asked.shape[0]
    width = table_low.shape[1]
    anywhere = pl.BlockSpec(memory_space=pl.ANY)
    dma = pltpu.SemaphoreType.DMA
    return pl.pallas_call(
        entry_kernel,
        out_shape=(
            jax.ShapeDtypeStruct(asked.shape, asked.dtype),
            jax.ShapeDtypeStruct((count,) + weights.shape, weights.dtype),
            jax.ShapeDtypeStruct((count, SLOTS, width), table_low.dtype),
        ),
        in_specs=[anywhere, anywhere, pl.BlockSpec(memory_space=pltpu.VMEM)],
        out_specs=(anywhere, anywhere, anywhere),
        scratch_shapes=[
            pltpu.VMEM((count, SLOTS, width), table_low.dtype),
            pltpu.VMEM(asked.shape, asked.dtype),
            *[dma((count,)), dma((count,)), dma] * 3,
            dma,
        ],
        compiler_params=pltpu.CompilerParams(
            collective_id=number, has_side_effects=True, vmem_limit_bytes=32 * 1024 * 1024
        ),
    )(asked, weights, table_low)


def reduce_kernel(plan, sources, *refs):
    ins, rest = refs[:sources], refs[sources:]
    row_ref, o_ref, got_ref = rest[:3]
    if plan:
        x_ref, rest = rest[3], rest[1:]
    else:
        x_ref = ins[0]
    held, third_in, second_in, z_in, send, recv, row_send, row_recv, row_local = rest[3:]
    grid = Grid()
    side, z_size, count, rank = grid.side, grid.z_size, grid.count, grid.rank
    order = sorted(grid.keys, key=lambda key: (key[0] == 0, key[1] == 0, key[2] == 0))
    devices = 2 * count
    me = place_of()
    own = pltpu.make_async_copy(row_ref.at[me], got_ref.at[me], row_local)
    own.start()
    greet(devices, me, True)

    def row_copy(step):
        peer = (me + step) % devices
        return pltpu.make_async_remote_copy(
            row_ref.at[peer],
            got_ref.at[me],
            row_send.at[step],
            row_recv.at[step],
            device_id=member(peer, True),
            device_id_type=MESH,
        )

    def row_start(step, carry):
        row_copy(step).start()
        return carry

    def row_finish(step, carry):
        row_copy(step).wait()
        return carry

    started = []

    def push(source, target, index, where):
        copy = pltpu.make_async_remote_copy(
            source,
            target,
            send.at[index],
            recv.at[index],
            device_id=grid.at(*where),
            device_id_type=MESH,
        )
        copy.start()
        started.append(copy)

    def arrived(target, index):
        pltpu.make_async_remote_copy(
            target,
            target,
            send.at[index],
            recv.at[index],
            device_id=grid.at(0, 0, 0, 1),
            device_id_type=MESH,
        ).wait_recv()

    for source, at, rows, block, line in plan:
        value = jnp.zeros((rows, x_ref.shape[2]), x_ref.dtype)
        if source >= 0:
            value = ins[source][at : at + rows, :]
        x_ref[block, line : line + rows, :] = value
    for key in order:
        push(x_ref.at[grid.index(*key, 1)], held.at[rank[key]], rank[key], (0, 0, 0, 1))
    from_third = {}
    from_second = {}
    from_z = {}
    index = count
    for step in range(1, side):
        for second in range(side):
            for z in range(z_size):
                from_third[step, second, z] = (
                    third_in.at[((step - 1) * side + second) * z_size + z],
                    index,
                )
                index += 1
    for step in range(1, side):
        for z in range(z_size):
            from_second[step, z] = (second_in.at[(step - 1) * z_size + z], index)
            index += 1
    for z in range(1, z_size):
        from_z[z] = (z_in.at[z - 1], index)
        index += 1
    for number, key in enumerate(order):
        third, second, z = key
        arrived(held.at[rank[key]], rank[key])
        total = held[rank[key]] + x_ref[grid.index(*key)]
        if third == 0:
            for step in range(1, side):
                arrived(*from_third[step, second, z])
                total = total + from_third[step, second, z][0][...]
        if third == 0 and second == 0:
            for step in range(1, side):
                arrived(*from_second[step, z])
                total = total + from_second[step, z][0][...]
        if key == (0, 0, 0):
            for step in range(1, z_size):
                arrived(*from_z[step])
                total = total + from_z[step][0][...]
            o_ref[...] = total
            continue
        held[rank[key]] = total
        if third:
            target, where = from_third[third, second, z], (third, 0, 0, 0)
        elif second:
            target, where = from_second[second, z], (0, second, 0, 0)
        else:
            target, where = from_z[z], (0, 0, z, 0)
        push(held.at[rank[key]], target[0], target[1], where)
        if number == 0:
            lax.fori_loop(1, devices, row_start, 0)
    for copy in started:
        copy.wait_send()
    own.wait()
    lax.fori_loop(1, devices, row_finish, 0)


def reduce(parts, plan, block, rows, number):
    count = lax.axis_size("dp") * lax.axis_size("fsdp")
    side = lax.axis_size("dp") // 2
    z_size = count // 2 // side // side
    kind = parts[0].dtype
    vmem, anywhere = pl.BlockSpec(memory_space=pltpu.VMEM), pl.BlockSpec(memory_space=pl.ANY)
    dma = pltpu.SemaphoreType.DMA
    return pl.pallas_call(
        partial(reduce_kernel, plan, len(parts)),
        out_shape=(
            jax.ShapeDtypeStruct(block, kind),
            jax.ShapeDtypeStruct(rows.shape, rows.dtype),
        ),
        in_specs=[vmem] * len(parts) + [anywhere],
        out_specs=(vmem, anywhere),
        scratch_shapes=[
            *([pltpu.VMEM((count,) + block, kind)] if plan else []),
            pltpu.VMEM((count // 2,) + block, kind),
            pltpu.VMEM(((side - 1) * side * z_size,) + block, kind),
            pltpu.VMEM(((side - 1) * z_size,) + block, kind),
            pltpu.VMEM((z_size - 1,) + block, kind),
            *[dma((count,))] * 4,
            dma,
        ],
        compiler_params=pltpu.CompilerParams(
            collective_id=number, has_side_effects=True, vmem_limit_bytes=58 * 1024 * 1024
        ),
    )(*parts, rows)


def woven(block, weave):
    chunk = block.shape[0]
    me = place_of()
    made = block
    for index in range(-(-3 * DS // chunk)):
        amount = min(chunk, 3 * DS - index * chunk)
        head = block[:amount].reshape((3, amount // 3, DS) if weave else (amount // 3, 3, DS))
        head = head.transpose(1, 0, 2).reshape(amount, DS)
        if index == 0:
            made = jnp.where(me < 3 * DS // chunk, head, made)
        elif amount < chunk:
            made = jnp.where(me == index, jnp.concatenate([head, block[amount:]]), made)
    return made


def block_plan(devices, chunk, layers, others):
    plan = []
    for block in range(devices):
        for layer in range(layers):
            base = 6 * layer
            row, end, line = block * chunk, (block + 1) * chunk, layer * chunk
            first = row
            if row < 3 * DS:
                stop = min(end, 3 * DS)
                amount = (stop - row) // 3
                for part in range(3):
                    plan.append((base + part, row // 3, amount, block, line + part * amount))
                row = stop
            for part, start, size in ((3, 3 * DS, DS), (4, 4 * DS, FS), (5, 4 * DS + FS, FS)):
                stop = min(end, start + size)
                if row < stop:
                    where = line + row - first
                    plan.append((base + part, row - start, stop - row, block, where))
                    row = stop
        line = layers * chunk
        for index, amount in enumerate(others):
            plan.append((6 * layers + index, block * amount, amount, block, line))
            line += amount
        spare = -line % 8
        if spare:
            plan.append((-1, 0, spare, block, line))
    return tuple(plan)


def pack(parts, width, rows):
    count = parts[0].shape[0]
    if all(part.ndim == 3 for part in parts):
        joined = jnp.concatenate(parts, 1)
        return jnp.pad(joined, ((0, 0), (0, rows - joined.shape[1]), (0, 0)))
    joined = jnp.concatenate([part.reshape(count, -1) for part in parts], 1)
    joined = jnp.pad(joined, ((0, 0), (0, rows * width - joined.shape[1])))
    return joined.reshape(count, rows, width)


def outer_product(left, right):
    return lax.dot_general(
        left, right, (((0,), (0,)), ((), ())), preferred_element_type=jnp.float32
    )


def back_product(grad, weight):
    return lax.dot_general(
        grad, weight, (((1,), (1,)), ((), ())), preferred_element_type=jnp.float32
    )


def norm_forward(value, gain, bias):
    average = jnp.mean(value, -1, keepdims=True)
    centered = value - average
    inverse = lax.rsqrt(jnp.mean(centered * centered, -1, keepdims=True) + NORM_EPS)
    normed = centered * inverse
    return (normed * gain + bias, normed, inverse)


def norm_backward(grad, normed, inverse, gain):
    d_normed = grad * gain
    d_value = inverse * (
        d_normed
        - jnp.mean(d_normed, -1, keepdims=True)
        - normed * jnp.mean(d_normed * normed, -1, keepdims=True)
    )
    return (d_value, jnp.sum(grad * normed, 0), jnp.sum(grad, 0))


def cut_pieces(vector, sizes):
    pieces = []
    start = 0
    for amount in sizes:
        pieces.append(vector[..., start : start + amount])
        start += amount
    return pieces


def split_rows(wide, width, hidden):
    first, second, third = 3 * width, 4 * width, 4 * width + hidden
    return (
        wide[:first].reshape(width, 3 * width),
        wide[first:second],
        wide[second:third].reshape(width, hidden),
        wide[third:],
    )


def combine_stats(first_half, second_half):
    s_top = jnp.maximum(first_half[0], second_half[0])
    s_sum = first_half[1] * jnp.exp(first_half[0] - s_top) + second_half[1] * jnp.exp(
        second_half[0] - s_top
    )
    t_top = jnp.maximum(first_half[2], second_half[2])
    scale_one = jnp.exp(first_half[2] - t_top)
    scale_two = jnp.exp(second_half[2] - t_top)
    t_sum = first_half[3] * scale_one + second_half[3] * scale_two
    cross = first_half[4] * scale_one + second_half[4] * scale_two
    return (s_top, s_sum, t_top, t_sum, cross)


def hidden_term(source, target, proj_turned, proj_bias, weight, denom):
    source_low = source.astype(jnp.bfloat16)
    mapped = back_product(source_low, proj_turned) + proj_bias
    spread = mapped - target
    d_mapped = (2.0 * weight * spread / denom).astype(jnp.bfloat16)
    return (
        jnp.sum(weight * spread * spread) / denom,
        outer_product(d_mapped, source_low),
        jnp.sum(d_mapped.astype(jnp.float32), 0),
        jnp.dot(d_mapped, proj_turned, preferred_element_type=jnp.float32),
    )


def sum_cores(value):
    first = lax.axis_index("dp") % 2 == 0
    parts = value.reshape(2, 2, -1, value.shape[1])
    given = jnp.where(first, parts[:, 1], parts[:, 0])
    kept = jnp.where(first, parts[:, 0], parts[:, 1])
    return kept + lax.ppermute(given, "dp", [(0, 1), (1, 0), (2, 3), (3, 2)])


def sum_along_x(parts):
    first = lax.axis_index("dp") // 2 == 0
    given = jnp.where(first, parts[1], parts[0])
    kept = jnp.where(first, parts[0], parts[1])
    return kept + lax.ppermute(given, "dp", [(0, 2), (2, 0), (1, 3), (3, 1)])


def adam_update(value, first, second, grad):
    first = BETA_ONE * first + (1.0 - BETA_ONE) * grad
    second = BETA_TWO * second + (1.0 - BETA_TWO) * grad * grad
    ratio = first / (1.0 - BETA_ONE**STEP) / (jnp.sqrt(second / (1.0 - BETA_TWO**STEP)) + ADAM_EPS)
    return (first, second, value - LEARN_RATE * (ratio + WEIGHT_DECAY * value))


def gelu(value):
    return 0.5 * value * (1.0 + jnp.tanh(0.7978845608028654 * (value + 0.044715 * value * value * value)))


def regroup(weights, group):
    amount = weights.shape[0]
    made = lax.broadcasted_iota(jnp.int32, (amount, amount), 0)
    taken = lax.broadcasted_iota(jnp.int32, (amount, amount), 1)
    inner = amount // group
    marks = jnp.where((made % inner) * group + made // inner == taken, 1.0, 0.0)
    return jnp.dot(
        marks.astype(jnp.bfloat16), weights, preferred_element_type=jnp.float32
    ).astype(jnp.bfloat16)


def softmax_low(scores, mask):
    masked = jnp.where(mask > 0.0, scores, NEG_LARGE)
    expo = jnp.exp(masked - jnp.max(masked, -1, keepdims=True))
    return (expo * (1.0 / jnp.sum(expo, -1, keepdims=True))).astype(jnp.bfloat16)


TILE = 256
CHUNK = 96


def teacher_kernel(x_ref, w_ref, vec_ref, mask_ref, y_ref, s_ref, qkv_ref, up_ref, context_ref):
    size = DT // HT
    for index in range(3 * DT // CHUNK):
        made = regroup(w_ref[index], 3)
        for part in range(3):
            rows = CHUNK // 3
            qkv_ref[part, index * rows : (index + 1) * rows, :] = made[part * rows : (part + 1) * rows]
    first_up, first_down = 4 * DT // CHUNK, (4 * DT + FT) // CHUNK
    many = FT // DT
    for index in range(FT // CHUNK // 2):
        at = first_up + 2 * index
        made = regroup(w_ref[at : at + 2].reshape(2 * CHUNK, DT), many)
        rows = 2 * CHUNK // many
        for part in range(many):
            up_ref[part, index * rows : (index + 1) * rows, :] = made[part * rows : (part + 1) * rows]
    line = lax.broadcasted_iota(jnp.int32, (1, 2 * size), 1)
    low_half = line < size
    length = mask_ref.shape[1]

    def vector(index, amount=1):
        return vec_ref[:, index * DT : (index + amount) * DT]

    def tile(step, carry):
        at = pl.ds(pl.multiple_of(step * TILE, TILE), TILE)
        x_low = x_ref[at, :]
        q, k, v = (
            (
                jnp.dot(x_low, qkv_ref[part], preferred_element_type=jnp.float32) + vector(part)
            ).astype(jnp.bfloat16)
            for part in range(3)
        )
        nothing = jnp.zeros((length, 2 * size), jnp.bfloat16)
        for row in range(TILE // length):
            span = slice(row * length, (row + 1) * length)
            here = pl.ds(pl.multiple_of(step * TILE + row * length, length), length)
            mask = mask_ref[here, :]
            for pair in range(HT // 2):
                lanes = slice(pair * 2 * size, (pair + 1) * 2 * size)
                k_pair, v_pair = k[span, lanes], v[span, lanes]
                k_both = jnp.concatenate(
                    [jnp.where(low_half, k_pair, nothing), jnp.where(low_half, nothing, k_pair)]
                )
                v_both = jnp.concatenate(
                    [jnp.where(low_half, v_pair, nothing), jnp.where(low_half, nothing, v_pair)]
                )
                scores = back_product(q[span, lanes], k_both) * size ** (-0.5)
                s_ref[here, pair * 2 * length : (pair + 1) * 2 * length] = scores
                weights = jnp.concatenate(
                    [softmax_low(scores[:, :length], mask), softmax_low(scores[:, length:], mask)], 1
                )
                context_ref[span, lanes] = jnp.dot(
                    weights, v_both, preferred_element_type=jnp.float32
                ).astype(jnp.bfloat16)
        w_out = w_ref[3 * DT // CHUNK : first_up].reshape(DT, DT)
        attended = jnp.dot(context_ref[...], w_out, preferred_element_type=jnp.float32) + vector(3)
        middle = norm_forward(x_low.astype(jnp.float32) + attended, vector(4), vector(5))[0]
        middle_low = middle.astype(jnp.bfloat16)
        outer = jnp.zeros((TILE, DT), jnp.float32)
        for part in range(many):
            inner = jnp.dot(middle_low, up_ref[part], preferred_element_type=jnp.float32) + vector(
                6 + part
            )
            begin = first_down + part * (DT // CHUNK)
            w_down = w_ref[begin : begin + DT // CHUNK].reshape(DT, DT)
            outer = outer + jnp.dot(
                gelu(inner).astype(jnp.bfloat16), w_down, preferred_element_type=jnp.float32
            )
        y_ref[at, :] = norm_forward(
            middle + outer + vector(6 + many), vector(7 + many), vector(8 + many)
        )[0]
        return carry

    lax.fori_loop(0, x_ref.shape[0] // TILE, tile, 0)


def teacher_forward(x_low, blocks, vectors, mask):
    tokens, length = mask.shape
    vmem = pl.BlockSpec(memory_space=pltpu.VMEM)
    return pl.pallas_call(
        teacher_kernel,
        out_shape=(
            jax.ShapeDtypeStruct((tokens, DT), jnp.float32),
            jax.ShapeDtypeStruct((tokens, HT * length), jnp.float32),
        ),
        in_specs=[vmem] * 4,
        out_specs=(vmem, vmem),
        scratch_shapes=[
            pltpu.VMEM((3, DT, DT), jnp.bfloat16),
            pltpu.VMEM((FT // DT, DT, DT), jnp.bfloat16),
            pltpu.VMEM((TILE, DT), jnp.bfloat16),
        ],
        compiler_params=pltpu.CompilerParams(vmem_limit_bytes=58 * 1024 * 1024),
        cost_estimate=pl.CostEstimate(
            flops=20 * 10**9, bytes_accessed=25 * 10**6, transcendentals=5 * 10**6
        ),
    )(x_low, blocks, vectors, mask)


WIDER = -(-FS // 128) * 128
VMEM_SPEC = pl.BlockSpec(memory_space=pltpu.VMEM)


def refold(source, target, source_width, target_width):
    period = math.lcm(source_width, target_width)
    groups = source.shape[1] * source_width // period
    step_in, step_out = period // source_width, period // target_width
    lane = lax.broadcasted_iota(jnp.int32, (groups, 128), 1)
    for row in range(step_out):
        for tile in range(-(-target_width // 128)):
            begin = row * target_width + 128 * tile
            amount = min(128, target_width - 128 * tile)
            made, at = jnp.zeros((groups, 128), source.dtype), 0
            while at < amount:
                line, column = divmod(begin + at, source_width)
                where, lanes = divmod(column, 128)
                piece = source[where, pl.ds(line, groups, stride=step_in), :]
                if (at - lanes) % 128:
                    piece = pltpu.roll(piece, (at - lanes) % 128, 1)
                length = min(128 - lanes, source_width - column, amount - at)
                made = jnp.where((lane >= at) & (lane < at + length), piece, made)
                at += length
            target[tile, pl.ds(row, groups, stride=step_out), :] = made


def unpack_kernel(plan, layers, w_ref, qkv_ref, out_ref, up_ref, down_ref, place_ref, proj_ref, *scratch):
    square, wide, folded, unfolded, small = scratch
    for layer in range(layers):
        for matrix, at, rows, block, line in plan:
            part = matrix - 6 * layer
            if not 0 <= part < 6:
                continue
            value = w_ref[block].astype(jnp.float32)[line : line + rows]
            if part < 4:
                square[part, at : at + rows, :] = value
            elif part == 4:
                for tile in range(-(-DS // 128)):
                    lanes = min(128, DS - 128 * tile)
                    folded[tile, at : at + rows, :lanes] = value[:, 128 * tile : 128 * tile + lanes]
            else:
                wide[at : at + rows, :] = value
        for part in range(3):
            qkv_ref[layer, part] = square[part].astype(jnp.bfloat16)
        out_ref[layer] = square[3].astype(jnp.bfloat16)
        refold(folded, unfolded, DS, FS)
        for tile in range(WIDER // 128):
            up_ref[layer, :, 128 * tile : 128 * tile + 128] = unfolded[tile].astype(jnp.bfloat16)
        down_ref[layer, :FS, :] = wide[...].astype(jnp.bfloat16)
        down_ref[layer, FS:, :] = jnp.zeros((WIDER - FS, DS), jnp.bfloat16)
    for matrix, at, rows, block, line in plan:
        if matrix >= 6 * layers:
            value = w_ref[block].astype(jnp.float32)[line : line + rows]
            small[matrix - 6 * layers, at : at + rows, :] = value
    place_ref[...] = small[0, : place_ref.shape[0]].astype(jnp.bfloat16)
    proj_ref[...] = small[1].astype(jnp.bfloat16)


def unpack(blocks, plan, layers, length):
    low = partial(jax.ShapeDtypeStruct, dtype=jnp.bfloat16)
    full = jnp.float32
    return pl.pallas_call(
        partial(unpack_kernel, plan, layers),
        out_shape=(
            low((layers, 3, DS, DS)),
            low((layers, DS, DS)),
            low((layers, DS, WIDER)),
            low((layers, WIDER, DS)),
            low((length, DS)),
            low((DT, DS)),
        ),
        in_specs=[VMEM_SPEC],
        out_specs=(VMEM_SPEC,) * 6,
        scratch_shapes=[
            pltpu.VMEM((4, DS, DS), full),
            pltpu.VMEM((FS, DS), full),
            pltpu.VMEM((-(-DS // 128), FS, 128), full),
            pltpu.VMEM((WIDER // 128, DS, 128), full),
            pltpu.VMEM((2, DT, DS), full),
        ],
        compiler_params=pltpu.CompilerParams(vmem_limit_bytes=50 * 1024 * 1024),
        cost_estimate=pl.CostEstimate(flops=0, bytes_accessed=20 * 10**6, transcendentals=0),
    )(blocks)


def by_heads(value, heads):
    width = value.shape[1]
    size = width // heads
    lane = lax.broadcasted_iota(jnp.int32, (1, width), 1)
    nothing = jnp.zeros_like(value)
    return jnp.concatenate(
        [
            jnp.where((lane >= head * size) & (lane < (head + 1) * size), value, nothing)
            for head in range(heads)
        ]
    )


def student_kernel(
    layers, token_ref, place_ref, evec_ref, vec_ref, bias_ref, mask_ref,
    qkv_w, out_w, up_w, down_w,
    emb_ref, zero_ref, zero_inv, last_ref, low_ref, qkv_ref, context_ref, one_ref, one_inv, two_ref, two_inv,
):
    length = mask_ref.shape[1]
    size = DS // HS

    def tile(step, carry):
        at = pl.ds(pl.multiple_of(step * TILE, TILE), TILE)
        places = jnp.concatenate([place_ref[...].astype(jnp.float32)] * (TILE // length))
        hidden, normed, inverse = norm_forward(
            token_ref[at, :] + places, evec_ref[0:1, :], evec_ref[1:2, :]
        )
        emb_ref[at, :] = hidden
        zero_ref[at, :] = normed
        zero_inv[at, :] = inverse
        for layer in range(layers):
            def vector(index):
                return vec_ref[layer, index : index + 1, :]

            low = hidden.astype(jnp.bfloat16)
            low_ref[layer, at, :] = low
            parts = []
            for part in range(3):
                made = jnp.dot(low, qkv_w[layer, part], preferred_element_type=jnp.float32)
                if part != 1:
                    made = made + vector(part // 2)
                parts.append(made.astype(jnp.bfloat16))
                qkv_ref[layer, part, at, :] = parts[part]
            contexts = []
            for row in range(TILE // length):
                span = slice(row * length, (row + 1) * length)
                here = pl.ds(pl.multiple_of(step * TILE + row * length, length), length)
                mask = mask_ref[here, :]
                q, k, v = (part[span] for part in parts)
                scores = back_product(q, by_heads(k, HS)) * size ** (-0.5)
                weights = jnp.concatenate(
                    [
                        softmax_low(scores[:, head * length : (head + 1) * length], mask)
                        for head in range(HS)
                    ],
                    1,
                )
                contexts.append(
                    jnp.dot(weights, by_heads(v, HS), preferred_element_type=jnp.float32)
                )
            context = jnp.concatenate(contexts).astype(jnp.bfloat16)
            context_ref[layer, at, :] = context
            attended = jnp.dot(context, out_w[layer], preferred_element_type=jnp.float32) + vector(2)
            middle, normed, inverse = norm_forward(hidden + attended, vector(3), vector(4))
            one_ref[layer, at, :] = normed
            one_inv[layer, at, :] = inverse
            inner = jnp.dot(
                middle.astype(jnp.bfloat16), up_w[layer], preferred_element_type=jnp.float32
            ) + bias_ref[layer]
            outer = jnp.dot(
                gelu(inner).astype(jnp.bfloat16), down_w[layer], preferred_element_type=jnp.float32
            ) + vector(5)
            hidden, normed, inverse = norm_forward(middle + outer, vector(6), vector(7))
            two_ref[layer, at, :] = normed
            two_inv[layer, at, :] = inverse
        last_ref[at, :] = hidden
        return carry

    lax.fori_loop(0, token_ref.shape[0] // TILE, tile, 0)


def student_forward(token_rows, places, evec, vectors, biases, mask, matrices):
    tokens = token_rows.shape[0]
    layers = vectors.shape[0]
    full = partial(jax.ShapeDtypeStruct, dtype=jnp.float32)
    low = partial(jax.ShapeDtypeStruct, dtype=jnp.bfloat16)
    made = (
        full((tokens, DS)),
        full((tokens, DS)),
        full((tokens, 1)),
        full((tokens, DS)),
        low((layers, tokens, DS)),
        low((layers, 3, tokens, DS)),
        low((layers, tokens, DS)),
        full((layers, tokens, DS)),
        full((layers, tokens, 1)),
        full((layers, tokens, DS)),
        full((layers, tokens, 1)),
    )
    return pl.pallas_call(
        partial(student_kernel, layers),
        out_shape=made,
        in_specs=[VMEM_SPEC] * 10,
        out_specs=(VMEM_SPEC,) * len(made),
        compiler_params=pltpu.CompilerParams(vmem_limit_bytes=58 * 1024 * 1024),
        cost_estimate=pl.CostEstimate(
            flops=8 * 10**9, bytes_accessed=40 * 10**6, transcendentals=6 * 10**6
        ),
    )(token_rows, places, evec, vectors, biases, mask, *matrices)


def back_kernel(
    last, grad_ref, vec_ref, bias_ref, mask_ref, qkv_w, out_w, up_w, down_w,
    low_ref, qkv_ref, context_ref, one_ref, one_inv, two_ref, two_inv, *refs,
):
    if last:
        score_ref, count_ref, refs = refs[0], refs[1], refs[2:]
    hidden_ref, *weight_refs, vec_out, bias_out, refs = (*refs[:9], refs[9:])
    dq_ref, dk_ref, dv_ref, do_ref, du_ref, dd_ref = weight_refs
    if last:
        loss_ref, refs = refs[0], refs[1:]
        loss_ref[...] = jnp.zeros_like(loss_ref)
    outer_s, attended_s, q_s, k_s, v_s, middle_s, active_s, inner_s, unfolded, folded = refs
    length = mask_ref.shape[1]
    size = DS // HS
    vec_out[...] = jnp.zeros_like(vec_out)
    bias_out[...] = jnp.zeros_like(bias_out)
    many = 256

    def vector(index):
        return vec_ref[index : index + 1, :]

    def note(index, value):
        vec_out[index : index + 1, :] += jnp.sum(value.astype(jnp.float32), 0, keepdims=True)

    def norm_back(grad, normed, inverse, gain, index):
        d_normed = grad * gain
        note(index, grad * normed)
        note(index + 1, grad)
        return inverse * (
            d_normed
            - jnp.mean(d_normed, -1, keepdims=True)
            - normed * jnp.mean(d_normed * normed, -1, keepdims=True)
        )

    def tile(step, carry):
        at = pl.ds(pl.multiple_of(step * TILE, TILE), TILE)
        d_sum = norm_back(grad_ref[at, :], two_ref[at, :], two_inv[at, :], vector(6), 6)
        d_outer = d_sum.astype(jnp.bfloat16)
        outer_s[at, :] = d_outer
        note(5, d_outer)
        middle = (one_ref[at, :] * vector(3) + vector(4)).astype(jnp.bfloat16)
        middle_s[at, :] = middle
        d_middle = d_sum
        for first in range(0, WIDER, many):
            lanes = slice(first, first + many)
            inner = jnp.dot(
                middle, up_w[:, lanes], preferred_element_type=jnp.float32
            ) + bias_ref[:, lanes]
            squared = inner * inner
            bent = jnp.tanh(0.7978845608028654 * (inner + 0.044715 * squared * inner))
            active_s[at, lanes] = (0.5 * inner * (1.0 + bent)).astype(jnp.bfloat16)
            slope = 0.5 * (1.0 + bent) + 0.5 * inner * (1.0 - bent * bent) * (
                0.7978845608028654 * (1.0 + 3.0 * 0.044715 * squared)
            )
            d_inner = (back_product(d_outer, down_w[lanes, :]) * slope).astype(jnp.bfloat16)
            inner_s[at, lanes] = d_inner
            bias_out[:, lanes] += jnp.sum(d_inner.astype(jnp.float32), 0, keepdims=True)
            d_middle = d_middle + back_product(d_inner, up_w[:, lanes])
        d_one = norm_back(d_middle, one_ref[at, :], one_inv[at, :], vector(3), 3)
        d_attended = d_one.astype(jnp.bfloat16)
        attended_s[at, :] = d_attended
        note(2, d_attended)
        d_context = back_product(d_attended, out_w[...]).astype(jnp.bfloat16)
        for row in range(TILE // length):
            here = pl.ds(pl.multiple_of(step * TILE + row * length, length), length)
            mask = mask_ref[here, :]
            d_row = d_context[row * length : (row + 1) * length]
            q, k, v = (qkv_ref[part, here, :] for part in range(3))
            keys = by_heads(k, HS)
            scores = back_product(q, keys) * size ** (-0.5)
            d_weights = back_product(d_row, by_heads(v, HS))
            low_weights, d_scores = [], []
            for head in range(HS):
                lanes = slice(head * length, (head + 1) * length)
                masked = jnp.where(mask > 0.0, scores[:, lanes], NEG_LARGE)
                expo = jnp.exp(masked - jnp.max(masked, -1, keepdims=True))
                weights = expo * (1.0 / jnp.sum(expo, -1, keepdims=True))
                low_weights.append(weights.astype(jnp.bfloat16))
                turned = weights * d_weights[:, lanes]
                made = turned - weights * jnp.sum(turned, -1, keepdims=True)
                if last:
                    differ = jnp.where(mask > 1.0, scores[:, lanes] - score_ref[here, lanes], 0.0)
                    loss_ref[...] += jnp.sum(differ * differ, 0, keepdims=True)
                    made = made + differ * (2.0 / count_ref[...])
                d_scores.append(made.astype(jnp.bfloat16))
            scale = size ** (-0.5)
            q_s[here, :] = (
                jnp.dot(jnp.concatenate(d_scores, 1), keys, preferred_element_type=jnp.float32)
                * scale
            ).astype(jnp.bfloat16)
            k_s[here, :] = (
                outer_product(jnp.concatenate(d_scores), by_heads(q, HS)) * scale
            ).astype(jnp.bfloat16)
            v_s[here, :] = outer_product(
                jnp.concatenate(low_weights), by_heads(d_row, HS)
            ).astype(jnp.bfloat16)
        d_hidden = d_one
        for part, held in enumerate((q_s, k_s, v_s)):
            d_part = held[at, :]
            if part != 1:
                note(part // 2, d_part)
            d_hidden = d_hidden + back_product(d_part, qkv_w[part])
        hidden_ref[at, :] = d_hidden
        return carry

    lax.fori_loop(0, grad_ref.shape[0] // TILE, tile, 0)
    low = low_ref[...]
    dq_ref[...] = outer_product(low, q_s[...])
    dk_ref[...] = outer_product(low, k_s[...])
    dv_ref[...] = outer_product(low, v_s[...])
    do_ref[...] = outer_product(context_ref[...], attended_s[...])
    for first in range(0, WIDER, many):
        lanes = slice(first, first + many)
        stop = min(first + many, FS)
        dd_ref[first:stop, :] = outer_product(active_s[:, lanes], outer_s[...])[: stop - first]
        made = outer_product(middle_s[...], inner_s[:, lanes])
        for tile_at in range(many // 128):
            unfolded[first // 128 + tile_at] = made[:, 128 * tile_at : 128 * tile_at + 128]
    refold(unfolded, folded, FS, DS)
    for tile_at in range(-(-DS // 128)):
        lanes = min(128, DS - 128 * tile_at)
        du_ref[:, 128 * tile_at : 128 * tile_at + lanes] = folded[tile_at, :, :lanes]


def student_backward(grad, vectors, biases, mask, matrices, saved, last):
    tokens, length = mask.shape
    full = partial(jax.ShapeDtypeStruct, dtype=jnp.float32)
    made = [
        full((tokens, DS)),
        *[full((DS, DS))] * 4,
        full((FS, DS)),
        full((FS, DS)),
        full((8, DS)),
        full((1, WIDER)),
    ]
    given = [grad, vectors, biases, mask, *matrices, *saved]
    if last:
        given += last
        made.append(full((1, length)))
    low = partial(pltpu.VMEM, dtype=jnp.bfloat16)
    return pl.pallas_call(
        partial(back_kernel, bool(last)),
        out_shape=tuple(made),
        in_specs=[VMEM_SPEC] * len(given),
        out_specs=(VMEM_SPEC,) * len(made),
        scratch_shapes=[
            *[low((tokens, DS))] * 6,
            *[low((tokens, WIDER))] * 2,
            pltpu.VMEM((WIDER // 128, DS, 128), jnp.float32),
            pltpu.VMEM((-(-DS // 128), FS, 128), jnp.float32),
        ],
        compiler_params=pltpu.CompilerParams(vmem_limit_bytes=58 * 1024 * 1024),
        cost_estimate=pl.CostEstimate(
            flops=10**9, bytes_accessed=4 * 10**6, transcendentals=3 * 10**5
        ),
    )(*given)


def three_parts(value):
    high = lax.reduce_precision(value, 8, 7)
    rest = value - high
    middle = lax.reduce_precision(rest, 8, 7)
    low = rest - middle
    return jnp.concatenate([high, middle, low], -1).astype(jnp.bfloat16)


def pick_exact(marks, value, turned=False):
    width = value.shape[1]
    terms = three_parts(value)
    made = outer_product(marks, terms) if turned else jnp.dot(
        marks, terms, preferred_element_type=jnp.float32
    )
    return made[:, :width] + made[:, width : 2 * width] + made[:, 2 * width :]


def plan_requests(ids, local_rows):
    order = lax.broadcasted_iota(jnp.int32, (ids.shape[0],), 0)
    same = ids[:, None] == ids[None, :]
    leader = jnp.min(jnp.where(same, order[None, :], ids.shape[0]), 1)
    leads = leader == order
    owner = ids // local_rows
    before = (
        (owner[:, None] == owner[None, :]) & leads[None, :] & (order[None, :] < leader[:, None])
    )
    rank = jnp.sum(before.astype(jnp.int32), 1)
    return (leads, owner, ids - owner * local_rows, rank)


def round_marks(plan, turn, devices):
    leads, owner, local_id, rank = plan
    inside = (rank >= turn * SLOTS) & (rank < (turn + 1) * SLOTS)
    slot = jnp.where(inside, owner * SLOTS + rank - turn * SLOTS, -1)
    line = lax.broadcasted_iota(jnp.int32, (devices * SLOTS, 1), 0)
    hit = line == slot[None, :]
    asked = jnp.max(jnp.where(hit & leads[None, :], local_id[None, :], -1), 1)
    return (hit.astype(jnp.bfloat16), asked.reshape(devices, 1, SLOTS))


def question(plan, turn, devices, extra):
    marks, asked = round_marks(plan, turn, devices)
    fill = jnp.full((devices, 1, 128 - SLOTS - extra.shape[0]), -1, jnp.int32)
    note = jnp.broadcast_to(extra[None, None, :], (devices, 1, extra.shape[0]))
    return (marks, jnp.concatenate([asked, note, fill], 2))


def ask(plan, turn, devices, extra):
    marks, asked = question(plan, turn, devices, extra)
    return (marks, exchange(asked, 0)[:, 0, :SLOTS].reshape(-1))


def wanted_marks(wanted, local_rows):
    return (wanted[:, None] == lax.broadcasted_iota(jnp.int32, (1, local_rows), 1)).astype(
        jnp.bfloat16
    )


def fetch(marks, wanted, table_low, devices):
    rows = jnp.dot(
        wanted_marks(wanted, table_low.shape[0]), table_low, preferred_element_type=jnp.float32
    ).astype(jnp.bfloat16)
    got = exchange(rows.reshape(devices, SLOTS, -1), 1)
    return outer_product(marks, got.reshape(devices * SLOTS, -1))


def give_back(marks, wanted, grads, local_rows, devices):
    sent = pick_exact(marks, grads)
    got = exchange(sent.reshape(devices, SLOTS, -1), 2)
    return pick_exact(wanted_marks(wanted, local_rows), got.reshape(devices * SLOTS, -1), True)


def local(
    token_ids,
    valid_mask,
    seq_ids,
    mask_pos,
    mask_labels,
    teacher_in,
    teacher_flat,
    teacher_vec,
    teacher_head,
    emb_table,
    emb_first,
    emb_second,
    pos_table,
    pos_first,
    pos_second,
    layer_flat,
    layer_first,
    layer_second,
    proj_weight,
    proj_first,
    proj_second,
    layer_vec,
    vec_first,
    vec_second,
    misc_vec,
    misc_first,
    misc_second,
):
    micro, micro_rows, length = token_ids.shape
    rows = micro * micro_rows
    local_rows, width = emb_table.shape
    layers = layer_vec.shape[0]
    picks = mask_pos.shape[2]
    tokens = rows * length
    n_dp, groups = lax.axis_size("dp"), lax.axis_size("fsdp")
    place = lax.axis_index("fsdp")
    devices = n_dp * groups
    hidden_denom = float(rows * devices * length * DT)
    predict_denom = float(rows * devices * picks)
    flat_local = layer_flat.shape[1]
    by_rows = flat_local % DS == 0

    usable = valid_mask.reshape(rows, length) > 0
    docs = seq_ids.reshape(rows, length)
    same_doc = docs[:, :, None] == docs[:, None, :]
    pair_mask = same_doc & usable[:, :, None] & usable[:, None, :]
    allowed = pair_mask | jnp.eye(length, dtype=bool)
    table_low = emb_table.astype(jnp.bfloat16)
    ids = jnp.concatenate([token_ids.reshape(-1), mask_labels.reshape(-1)])
    plan = plan_requests(ids, local_rows)
    extra = jnp.stack([-1 - jnp.sum(pair_mask.astype(jnp.int32)), -1 - jnp.max(plan[3])])
    teacher_lines = teacher_flat.reshape(-1, DT)
    teacher_all = lax.all_gather(teacher_lines, BOTH, axis=0, tiled=True).reshape(-1, CHUNK, DT)
    own_parts = [
        layer_flat.astype(jnp.bfloat16),
        pos_table.astype(jnp.bfloat16),
        proj_weight.astype(jnp.bfloat16).T,
    ]
    if by_rows:
        chunk = flat_local // DS
        own_layers = [woven(part.reshape(-1, DS), False) for part in own_parts[0]]
        own_parts = [part.reshape(1, -1, DS) for part in own_layers + own_parts[1:]]
        line, lines = DS, sum(part.shape[1] for part in own_parts)
    else:
        own_parts = [part.reshape(1, -1) for part in own_parts]
        line, lines = 128, -(-sum(part.shape[1] for part in own_parts) // 128)
    block_rows = -(-lines // 16) * 16
    marks, asked = question(plan, 0, devices, extra)
    got, weights_all, token_blocks = entry(asked, pack(own_parts, line, block_rows)[0], table_low, 3)
    wanted = got[:, 0, :SLOTS].reshape(-1)
    notes = got[:, 0, SLOTS : SLOTS + 2]
    count = jnp.sum(-1 - notes[:, 0]).astype(jnp.float32)
    rounds = jnp.max(-1 - notes[:, 1]) // SLOTS + 1
    all_rows = outer_product(marks, token_blocks.reshape(devices * SLOTS, width))

    def more_rows(state):
        turn, so_far = state
        marks_now, wanted_now = ask(plan, turn, devices, extra)
        return (turn + 1, so_far + fetch(marks_now, wanted_now, table_low, devices))

    all_rows = lax.while_loop(lambda state: state[0] < rounds, more_rows, (1, all_rows))[1]
    token_rows, label_rows = (all_rows[:tokens], all_rows[tokens:])
    pos_local, proj_local = pos_table.shape[0], proj_weight.shape[1]
    if by_rows:
        where = block_plan(devices, chunk, layers, (pos_local, proj_local))
        *matrices, places_all, proj_all = unpack(weights_all, where, layers, length)
    else:
        flat_all = weights_all.reshape(devices, -1)
        split = []
        for index in range(layers):
            wide = flat_all[:, index * flat_local : (index + 1) * flat_local].reshape(WIDE, DS)
            qkv, out, up, down = split_rows(wide, DS, FS)
            split.append(
                (
                    qkv.reshape(DS, 3, DS).transpose(1, 0, 2),
                    out,
                    jnp.pad(up, ((0, 0), (0, WIDER - FS))),
                    jnp.pad(down, ((0, WIDER - FS), (0, 0))),
                )
            )
        matrices = [jnp.stack(group) for group in zip(*split)]
        start = layers * flat_local
        places_all = flat_all[:, start : start + pos_local * DS].reshape(length, DS)
        start += pos_local * DS
        proj_all = flat_all[:, start : start + proj_local * DS].reshape(DT, DS)

    to_owner = [
        (d * groups + f, f * n_dp + d) for d in range(n_dp) for f in range(groups)
    ]
    from_owner = [(owner, holder) for holder, owner in to_owner]
    table_then = lax.optimization_barrier((table_low, teacher_all))[0]
    slice_part = lax.ppermute(table_then, BOTH, from_owner)
    slice_table = lax.all_gather(slice_part, "dp", axis=0, tiled=True)

    proj_bias = misc_vec[2 * DS :]
    evec = misc_vec[: 2 * DS].reshape(2, DS)
    cut = 5 * DS
    vectors = jnp.concatenate([layer_vec[:, :cut], layer_vec[:, cut + FS :]], 1).reshape(
        layers, 8, DS
    )
    biases = jnp.pad(layer_vec[:, cut : cut + FS], ((0, 0), (0, WIDER - FS)))[:, None]

    mask = jnp.where(pair_mask, 2.0, jnp.where(allowed, 1.0, 0.0)).reshape(tokens, length)
    embedded, normed_zero, inverse_zero, hidden, *saved = student_forward(
        token_rows, places_all, evec, vectors, biases, mask, matrices
    )
    t_input = teacher_in.reshape(tokens, DT).astype(jnp.float32)
    t_out, t_scores = teacher_forward(
        teacher_in.reshape(tokens, DT), teacher_all, teacher_vec.astype(jnp.float32)[None], mask
    )
    weight = valid_mask.reshape(tokens, 1).astype(jnp.float32)
    loss_zero, proj_zero, bias_zero, back_zero = hidden_term(
        embedded, t_input, proj_all, proj_bias, weight, hidden_denom
    )
    loss_last, proj_last, bias_last, back_last = hidden_term(
        hidden, t_out, proj_all, proj_bias, weight, hidden_denom
    )
    hidden_sum = loss_zero + loss_last
    grad_proj = proj_zero + proj_last

    flat_pick = (
        jnp.arange(rows, dtype=jnp.int32)[:, None] * length + mask_pos.reshape(rows, picks)
    ).reshape(-1)
    pick_marks = (flat_pick[:, None] == lax.broadcasted_iota(jnp.int32, (1, tokens), 1)).astype(
        jnp.bfloat16
    )
    both_low = jnp.concatenate([hidden.astype(jnp.bfloat16), t_out.astype(jnp.bfloat16)], 1)
    both_picked = jnp.dot(pick_marks, both_low, preferred_element_type=jnp.float32).astype(
        jnp.bfloat16
    )
    picked = both_picked[:, :width]
    both_all = exchange(both_picked, 4, whole=False, spread=True).reshape(-1, width + DT)
    picked_all, t_picked_all = both_all[:, :width], both_all[:, width:]
    s_logits = jnp.einsum("gd,vd->gv", picked_all, slice_table, preferred_element_type=jnp.float32)
    t_logits = jnp.einsum(
        "gd,vd->gv", t_picked_all, teacher_head, preferred_element_type=jnp.float32
    )
    s_top = jnp.max(s_logits, -1)
    t_top = jnp.max(t_logits, -1)
    t_exp = jnp.exp(t_logits - t_top[:, None])
    local_stats = jnp.stack(
        [
            s_top,
            jnp.sum(jnp.exp(s_logits - s_top[:, None]), -1),
            t_top,
            jnp.sum(t_exp, -1),
            jnp.sum(t_exp * s_logits, -1),
        ]
    )
    stats_all = exchange(local_stats, 5, whole=False, spread=True)
    stats = tuple(stats_all[0])
    for other in range(1, groups):
        stats = combine_stats(stats, tuple(stats_all[other]))
    s_top, s_sum, t_top, t_sum, cross = stats
    log_total = s_top + jnp.log(s_sum)
    d_logits = (
        2.0 * jnp.exp(s_logits - log_total[:, None])
        - jnp.exp(t_logits - t_top[:, None]) / t_sum[:, None]
    ) / predict_denom
    d_logits = d_logits.astype(jnp.bfloat16)
    grad_slice = outer_product(d_logits, picked_all)
    d_logits, grad_slice = lax.optimization_barrier((d_logits, grad_slice))
    if n_dp == 4:
        to_send = [sum_cores, sum_along_x, lambda part: lax.ppermute(part, BOTH, to_owner)]
    else:
        to_send = [
            lambda value: lax.psum_scatter(value, "dp", scatter_dimension=0, tiled=True),
            lambda part: lax.ppermute(part, BOTH, to_owner),
        ]
    d_logits, head_grad = lax.optimization_barrier((d_logits, to_send.pop(0)(grad_slice)))
    if len(to_send) > 1:
        head_grad = to_send.pop(0)(head_grad)
    d_picked_all = jnp.dot(d_logits, slice_table, preferred_element_type=jnp.float32)
    d_picked = jnp.sum(
        exchange(
            d_picked_all.astype(jnp.bfloat16).reshape(groups, rows * picks, width), 6, whole=False
        ).astype(jnp.float32),
        0,
    )
    picked_wide = picked.astype(jnp.float32)
    target_logit = jnp.sum(picked_wide * label_rows, -1)
    own_start = place * rows * picks
    own_total = lax.dynamic_slice_in_dim(log_total, own_start, rows * picks, 0)
    own_cross = lax.dynamic_slice_in_dim(cross / t_sum, own_start, rows * picks, 0)
    predict_sum = jnp.sum(2.0 * own_total - own_cross - target_logit) / predict_denom
    d_picked = d_picked - label_rows / predict_denom
    d_hidden = pick_exact(pick_marks, d_picked, True) + back_last

    matrix_grads = [None] * layers
    vector_grads = [None] * layers
    attention_sum = jnp.float32(0.0)
    d_hidden, head_grad = lax.optimization_barrier((d_hidden, head_grad))
    head_grad = to_send.pop(0)(head_grad)
    for layer_index in reversed(range(layers)):
        d_hidden, *others = student_backward(
            d_hidden,
            vectors[layer_index],
            biases[layer_index],
            mask,
            [matrix[layer_index] for matrix in matrices],
            [kept[layer_index] for kept in saved],
            [t_scores, count.reshape(1, 1)] if layer_index == layers - 1 else [],
        )
        matrix_grads[layer_index] = others[:6]
        d_vectors, d_bias_up, square = others[6], others[7], others[8:]
        d_vectors = d_vectors.reshape(-1)
        vector_grads[layer_index] = jnp.concatenate(
            [d_vectors[:cut], d_bias_up[0, :FS], d_vectors[cut:]]
        )
        if square:
            attention_sum = jnp.sum(square[0]) / count
    d_hidden, head_grad = lax.optimization_barrier((d_hidden, head_grad))
    d_token, d_gain, d_bias = norm_backward(
        d_hidden + back_zero, normed_zero, inverse_zero, misc_vec[:DS]
    )
    grad_places = jnp.sum(d_token.reshape(rows, length, width), 0)

    row_grads = jnp.concatenate([d_token, -picked_wide / predict_denom])
    def more_grads(state):
        turn, so_far = state
        marks_now, wanted_now = ask(plan, turn, devices, extra)
        return (
            turn + 1,
            so_far + give_back(marks_now, wanted_now, row_grads, local_rows, devices),
        )

    grad_small = jnp.concatenate(vector_grads + [d_gain, d_bias, bias_zero + bias_last])
    small_local = -(-grad_small.shape[0] // devices)
    small_local = -(-small_local // DS) * DS
    small_padded = jnp.pad(grad_small, (0, devices * small_local - grad_small.shape[0]))
    rest = [grad_places, grad_proj, small_padded.reshape(-1, DS)]
    sizes = [flat_local] * layers + [part.size // devices for part in rest]
    lines = -(-sum(sizes) // line)
    block = (-(-lines // 8) * 8, line)
    sent = pick_exact(marks, row_grads).reshape(devices, SLOTS, width)
    if by_rows:
        amounts = [size // DS for size in sizes[layers:]]
        grad_parts = sum(matrix_grads, []) + rest
        block_rows_of = block_plan(devices, chunk, layers, amounts)
    else:
        wides = []
        for grads in matrix_grads:
            first = jnp.stack(grads[:3], 1).reshape(-1, width)
            wides.append(jnp.concatenate([first, *grads[3:]]))
        grad_parts = [pack([part.reshape(devices, -1) for part in wides + rest], *block[::-1])]
        block_rows_of = ()
    reduced, row_blocks = reduce(grad_parts, block_rows_of, block, sent, 7)
    g_table = pick_exact(
        wanted_marks(wanted, local_rows), row_blocks.reshape(devices * SLOTS, width), True
    )
    g_table = lax.while_loop(lambda state: state[0] < rounds, more_grads, (1, g_table))[1]
    g_table = g_table + head_grad
    if by_rows:
        pieces = []
        start = 0
        for size in sizes:
            pieces.append(reduced[start : start + size // DS])
            start += size // DS
    else:
        pieces = cut_pieces(reduced.reshape(-1), sizes)
    if by_rows:
        pieces[:layers] = [woven(piece, True) for piece in pieces[:layers]]
    layer_acc = jnp.stack([piece.reshape(-1) for piece in pieces[:layers]])
    g_places = pieces[layers].reshape(pos_local, DS)
    g_proj = pieces[layers + 1].reshape(proj_local, DS).T
    small_part = pieces[layers + 2].reshape(-1)
    squares = (
        jnp.sum(g_table * g_table)
        + jnp.sum(g_places * g_places)
        + jnp.sum(g_proj * g_proj)
        + jnp.sum(layer_acc * layer_acc)
        + jnp.sum(small_part * small_part)
    )
    note = jnp.concatenate(
        [small_part, jnp.stack([attention_sum + hidden_sum + predict_sum, squares])]
    )
    note = jnp.pad(note, (0, -(-note.shape[0] // 128) * 128 - note.shape[0])).reshape(1, -1)
    notes_all = exchange(note, 8, spread=True)[:, 0]
    small = notes_all[:, :small_local].reshape(-1)
    loss = jnp.sum(notes_all[:, small_local])
    norm = jnp.sqrt(jnp.sum(notes_all[:, small_local + 1]))
    g_vec = small[: layer_vec.size].reshape(layer_vec.shape)
    g_misc = small[layer_vec.size : layer_vec.size + misc_vec.shape[0]]
    factor = CLIP_NORM / jnp.maximum(norm, CLIP_NORM)
    return (
        loss,
        count,
        norm,
        *adam_update(emb_table, emb_first, emb_second, g_table * factor),
        *adam_update(pos_table, pos_first, pos_second, g_places * factor),
        *adam_update(layer_flat, layer_first, layer_second, layer_acc * factor),
        *adam_update(proj_weight, proj_first, proj_second, g_proj * factor),
        *adam_update(layer_vec, vec_first, vec_second, g_vec * factor),
        *adam_update(misc_vec, misc_first, misc_second, g_misc * factor),
    )


def solution(mesh):
    rows, lines, flat, tail, every = (
        P(None, BOTH),
        P(BOTH, None),
        P(BOTH),
        P(None, BOTH),
        P(),
    )
    placed = (
        *[rows] * 6,
        flat,
        every,
        P("fsdp", None),
        *[lines] * 6,
        *[tail] * 6,
        *[every] * 6,
    )
    return jax.shard_map(
        local,
        mesh=mesh,
        in_specs=placed,
        out_specs=(*[every] * 3, *[lines] * 6, *[tail] * 6, *[every] * 6),
        check_vma=False,
    )
```

```python
import math
from functools import partial

import jax
import jax.numpy as jnp
from jax import lax
from jax.experimental import pallas as pl
from jax.experimental.pallas import tpu as pltpu
from jax.sharding import PartitionSpec as P

DS = 312
HS = 12
FS = 1200
DT = 768
HT = 12
FT = 3072
STEP = 5


NORM_EPS = 1e-06
CLIP_NORM = 0.05
LEARN_RATE = 0.05
BETA_ONE = 0.9
BETA_TWO = 0.999
ADAM_EPS = 1e-06
WEIGHT_DECAY = 0.01
NEG_LARGE = -1e30

BOTH = ("dp", "fsdp")
MESH = pl.DeviceIdType.MESH
SLOTS = 48
WIDE = 3 * DS + DS + 2 * FS


def z_size_of(fsdp):
    return 4 if fsdp % 4 == 0 else 1


def place_of():
    fsdp = lax.axis_size("fsdp")
    return lax.axis_index("dp") * fsdp + lax.axis_index("fsdp")


def member(index, whole):
    fsdp = lax.axis_size("fsdp")
    if whole:
        return (index // fsdp, index % fsdp)
    return (lax.axis_index("dp"), index)


def greet(count, me, whole):
    barrier = pltpu.get_barrier_semaphore()

    def signal(step, carry):
        pl.semaphore_signal(
            barrier, inc=1, device_id=member((me + step) % count, whole), device_id_type=MESH
        )
        return carry

    lax.fori_loop(1, count, signal, 0)
    pl.semaphore_wait(barrier, count - 1)


def exchange_kernel(count, whole, spread, x_ref, o_ref, send, recv, local_sem):
    me = place_of() if whole else lax.axis_index("fsdp")
    own = pltpu.make_async_copy(x_ref if spread else x_ref.at[me], o_ref.at[me], local_sem)
    own.start()
    greet(count, me, whole)

    def copy(step):
        peer = (me + step) % count
        return pltpu.make_async_remote_copy(
            x_ref if spread else x_ref.at[peer],
            o_ref.at[me],
            send.at[step],
            recv.at[step],
            device_id=member(peer, whole),
            device_id_type=MESH,
        )

    def start(step, carry):
        copy(step).start()
        return carry

    def finish(step, carry):
        copy(step).wait()
        return carry

    lax.fori_loop(1, count, start, 0)
    own.wait()
    lax.fori_loop(1, count, finish, 0)


def exchange(x, number, whole=True, spread=False):
    count = lax.axis_size("fsdp") * (lax.axis_size("dp") if whole else 1)
    return pl.pallas_call(
        partial(exchange_kernel, count, whole, spread),
        out_shape=jax.ShapeDtypeStruct(((count,) if spread else ()) + x.shape, x.dtype),
        in_specs=[pl.BlockSpec(memory_space=pl.ANY)],
        out_specs=pl.BlockSpec(memory_space=pl.ANY),
        scratch_shapes=[
            pltpu.SemaphoreType.DMA((count,)),
            pltpu.SemaphoreType.DMA((count,)),
            pltpu.SemaphoreType.DMA,
        ],
        compiler_params=pltpu.CompilerParams(collective_id=number, has_side_effects=True),
    )(x)


class Grid:
    def __init__(self):
        self.fsdp = lax.axis_size("fsdp")
        self.z_size = z_size_of(self.fsdp)
        self.side = self.fsdp // self.z_size
        assert lax.axis_size("dp") == 2 * self.side
        dp, fsdp = lax.axis_index("dp"), lax.axis_index("fsdp")
        self.x, self.core = dp // 2, dp % 2
        self.z, self.y = fsdp // self.side, fsdp % self.side
        side, z_size = self.side, self.z_size
        self.keys = [(g, b, a) for g in range(side) for b in range(side) for a in range(z_size)]
        self.rank = {key: index for index, key in enumerate(self.keys)}
        self.count = len(self.keys)

    def at(self, third, second, z, other=0):
        core = (self.core + other) % 2
        x = (self.x + third * (1 - core) + second * core) % self.side
        y = (self.y + second * (1 - core) + third * core) % self.side
        return (x * 2 + core, ((self.z + z) % self.z_size) * self.side + y)

    def index(self, third, second, z, other=0):
        dp, fsdp = self.at(third, second, z, other)
        return dp * self.fsdp + fsdp

    def neighbours(self):
        return (
            [(0, 0, a, 0) for a in range(1, self.z_size)]
            + [(0, b, 0, 0) for b in range(1, self.side)]
            + [(g, 0, 0, 0) for g in range(1, self.side)]
            + [(0, 0, 0, 1)]
        )

    def greet(self):
        barrier = pltpu.get_barrier_semaphore()
        around = self.neighbours()
        for where in around:
            pl.semaphore_signal(barrier, inc=1, device_id=self.at(*where), device_id_type=MESH)
        pl.semaphore_wait(barrier, len(around))


class Spread:
    def __init__(self, grid, x_ref, o_ref, send, recv, local_sem):
        self.grid, self.x_ref, self.o_ref = grid, x_ref, o_ref
        self.send, self.recv = send, recv
        self.started = []
        self.own = pltpu.make_async_copy(x_ref, o_ref.at[self.slot((0, 0, 0))], local_sem)
        self.own.start()

    def slot(self, key, other=0):
        grid = self.grid
        third, second, z = key
        return grid.index(grid.side - third, grid.side - second, grid.z_size - z, other)

    def push(self, key, name, where):
        grid = self.grid
        index = grid.rank[name] + (grid.count if where[3] else 0)
        copy = pltpu.make_async_remote_copy(
            self.x_ref if key == (0, 0, 0) else self.o_ref.at[self.slot(key)],
            self.o_ref.at[self.slot(key)],
            self.send.at[index],
            self.recv.at[index],
            device_id=grid.at(*where),
            device_id_type=MESH,
        )
        copy.start()
        self.started.append(copy)

    def forward(self, key):
        grid = self.grid
        third, second, z = key
        if key == (0, 0, 0):
            for step in range(1, grid.z_size):
                self.push(key, (0, 0, step), (0, 0, step, 0))
        if third == 0 and second == 0:
            for step in range(1, grid.side):
                self.push(key, (0, step, z), (0, step, 0, 0))
        if third == 0:
            for step in range(1, grid.side):
                self.push(key, (step, second, z), (step, 0, 0, 0))
        self.push(key, key, (0, 0, 0, 1))

    def arrived(self, key, other=0):
        grid = self.grid
        index = grid.rank[key] + (grid.count if other else 0)
        pltpu.make_async_remote_copy(
            self.o_ref.at[self.slot(key, other)],
            self.o_ref.at[self.slot(key, other)],
            self.send.at[index],
            self.recv.at[index],
            device_id=grid.at(0, 0, 0, 1),
            device_id_type=MESH,
        ).wait_recv()

    def start(self):
        self.forward((0, 0, 0))

    def middle(self):
        for key in self.grid.keys[1:]:
            self.arrived(key)
            self.forward(key)

    def finish(self):
        for key in self.grid.keys:
            self.arrived(key, 1)
        self.own.wait()
        for copy in self.started:
            copy.wait_send()


def entry_kernel(
    ask_ref, w_ref, table_ref, got_ref, all_ref, rows_ref, sent, asks, *sems
):
    ask_send, ask_recv, ask_local, w_send, w_recv, w_local, row_send, row_recv, row_local, out_sem = sems
    grid = Grid()
    count = 2 * grid.count
    me = place_of()
    own = pltpu.make_async_copy(ask_ref.at[me], asks.at[me], ask_local)
    own.start()
    greet(count, me, True)

    def ask_copy(step):
        peer = (me + step) % count
        return pltpu.make_async_remote_copy(
            ask_ref.at[peer],
            asks.at[me],
            ask_send.at[step],
            ask_recv.at[step],
            device_id=member(peer, True),
            device_id_type=MESH,
        )

    def row_copy(step):
        peer = (me + step) % count
        return pltpu.make_async_remote_copy(
            sent.at[peer],
            rows_ref.at[me],
            row_send.at[step],
            row_recv.at[step],
            device_id=member(peer, True),
            device_id_type=MESH,
        )

    def each(first, action):
        def body(step, carry):
            action(step)
            return carry

        lax.fori_loop(first, count, body, 0)

    each(1, lambda step: ask_copy(step).start())
    spread = Spread(grid, w_ref, all_ref, w_send, w_recv, w_local)
    spread.start()
    own.wait()
    table = table_ref[...]
    line = lax.broadcasted_iota(jnp.int32, (table.shape[0], 128), 0)

    def answer(source):
        marks = jnp.where(line == asks[source], 1.0, 0.0).astype(jnp.bfloat16)
        sent[source] = outer_product(marks, table)[:SLOTS].astype(jnp.bfloat16)

    answer(me)
    mine = pltpu.make_async_copy(sent.at[me], rows_ref.at[me], row_local)
    mine.start()

    def serve(step):
        ask_copy(step).wait_recv()
        answer((me + count - step) % count)

    each(1, serve)
    each(1, lambda step: row_copy(step).start())
    keep = pltpu.make_async_copy(asks, got_ref, out_sem)
    keep.start()
    spread.middle()
    spread.finish()
    mine.wait()
    keep.wait()
    each(1, lambda step: row_copy(step).wait())
    each(1, lambda step: ask_copy(step).wait_send())


def entry(asked, weights, table_low, number):
    count = asked.shape[0]
    width = table_low.shape[1]
    anywhere = pl.BlockSpec(memory_space=pl.ANY)
    dma = pltpu.SemaphoreType.DMA
    return pl.pallas_call(
        entry_kernel,
        out_shape=(
            jax.ShapeDtypeStruct(asked.shape, asked.dtype),
            jax.ShapeDtypeStruct((count,) + weights.shape, weights.dtype),
            jax.ShapeDtypeStruct((count, SLOTS, width), table_low.dtype),
        ),
        in_specs=[anywhere, anywhere, pl.BlockSpec(memory_space=pltpu.VMEM)],
        out_specs=(anywhere, anywhere, anywhere),
        scratch_shapes=[
            pltpu.VMEM((count, SLOTS, width), table_low.dtype),
            pltpu.VMEM(asked.shape, asked.dtype),
            *[dma((count,)), dma((count,)), dma] * 3,
            dma,
        ],
        compiler_params=pltpu.CompilerParams(
            collective_id=number, has_side_effects=True, vmem_limit_bytes=32 * 1024 * 1024
        ),
    )(asked, weights, table_low)


def reduce_kernel(plan, sources, *refs):
    ins, rest = refs[:sources], refs[sources:]
    row_ref, o_ref, got_ref = rest[:3]
    if plan:
        x_ref, rest = rest[3], rest[1:]
    else:
        x_ref = ins[0]
    held, third_in, second_in, z_in, send, recv, row_send, row_recv, row_local = rest[3:]
    grid = Grid()
    side, z_size, count, rank = grid.side, grid.z_size, grid.count, grid.rank
    order = sorted(grid.keys, key=lambda key: (key[0] == 0, key[1] == 0, key[2] == 0))
    devices = 2 * count
    me = place_of()
    own = pltpu.make_async_copy(row_ref.at[me], got_ref.at[me], row_local)
    own.start()
    greet(devices, me, True)

    def row_copy(step):
        peer = (me + step) % devices
        return pltpu.make_async_remote_copy(
            row_ref.at[peer],
            got_ref.at[me],
            row_send.at[step],
            row_recv.at[step],
            device_id=member(peer, True),
            device_id_type=MESH,
        )

    def row_start(step, carry):
        row_copy(step).start()
        return carry

    def row_finish(step, carry):
        row_copy(step).wait()
        return carry

    started = []

    def push(source, target, index, where):
        copy = pltpu.make_async_remote_copy(
            source,
            target,
            send.at[index],
            recv.at[index],
            device_id=grid.at(*where),
            device_id_type=MESH,
        )
        copy.start()
        started.append(copy)

    def arrived(target, index):
        pltpu.make_async_remote_copy(
            target,
            target,
            send.at[index],
            recv.at[index],
            device_id=grid.at(0, 0, 0, 1),
            device_id_type=MESH,
        ).wait_recv()

    for source, at, rows, block, line in plan:
        value = jnp.zeros((rows, x_ref.shape[2]), x_ref.dtype)
        if source >= 0:
            value = ins[source][at : at + rows, :]
        x_ref[block, line : line + rows, :] = value
    for key in order:
        push(x_ref.at[grid.index(*key, 1)], held.at[rank[key]], rank[key], (0, 0, 0, 1))
    from_third = {}
    from_second = {}
    from_z = {}
    index = count
    for step in range(1, side):
        for second in range(side):
            for z in range(z_size):
                from_third[step, second, z] = (
                    third_in.at[((step - 1) * side + second) * z_size + z],
                    index,
                )
                index += 1
    for step in range(1, side):
        for z in range(z_size):
            from_second[step, z] = (second_in.at[(step - 1) * z_size + z], index)
            index += 1
    for way in (1, -1):
        for distance in range(z_size - 1):
            from_z[way, distance] = (z_in.at[len(from_z)], index)
            index += 1

    def gathered(key):
        third, second, z = key
        arrived(held.at[rank[key]], rank[key])
        total = held[rank[key]] + x_ref[grid.index(*key)]
        if third == 0:
            for step in range(1, side):
                arrived(*from_third[step, second, z])
                total = total + from_third[step, second, z][0][...]
        if third == 0 and second == 0:
            for step in range(1, side):
                arrived(*from_second[step, z])
                total = total + from_second[step, z][0][...]
        return total

    for number, key in enumerate(order):
        third, second, z = key
        if third == 0 and second == 0:
            continue
        held[rank[key]] = gathered(key)
        if third:
            target, where = from_third[third, second, z], (third, 0, 0, 0)
        else:
            target, where = from_second[second, z], (0, second, 0, 0)
        push(held.at[rank[key]], target[0], target[1], where)
        if number == 0:
            lax.fori_loop(1, devices, row_start, 0)

    def behind(way):
        return (grid.z > 0) if way > 0 else (grid.z < z_size - 1)

    def hop(way, distance):
        target = from_z[way, distance - 1]
        return pltpu.make_async_remote_copy(
            held.at[rank[0, 0, way * distance % z_size]],
            target[0],
            send.at[target[1]],
            recv.at[target[1]],
            device_id=grid.at(0, 0, way % z_size),
            device_id_type=MESH,
        )

    def reaches(way, distance):
        return (grid.z + way * distance >= 0) & (grid.z + way * distance < z_size)

    for distance in range(z_size - 1, 0, -1):
        for way in (1, -1):

            @pl.when(reaches(way, distance))
            def _(way=way, distance=distance):
                key = (0, 0, way * distance % z_size)
                held[rank[key]] = gathered(key)
                if distance < z_size - 1:

                    @pl.when(behind(way))
                    def _():
                        arrived(*from_z[way, distance])
                        held[rank[key]] += from_z[way, distance][0][...]

                hop(way, distance).start()

    o_ref[...] = gathered((0, 0, 0))
    for way in (1, -1):

        @pl.when(behind(way))
        def _(way=way):
            arrived(*from_z[way, 0])
            o_ref[...] += from_z[way, 0][0][...]

    for distance in range(z_size - 1, 0, -1):
        for way in (1, -1):
            pl.when(reaches(way, distance))(hop(way, distance).wait_send)
    for copy in started:
        copy.wait_send()
    own.wait()
    lax.fori_loop(1, devices, row_finish, 0)


def reduce(parts, plan, block, rows, number):
    count = lax.axis_size("dp") * lax.axis_size("fsdp")
    side = lax.axis_size("dp") // 2
    z_size = count // 2 // side // side
    kind = parts[0].dtype
    vmem, anywhere = pl.BlockSpec(memory_space=pltpu.VMEM), pl.BlockSpec(memory_space=pl.ANY)
    dma = pltpu.SemaphoreType.DMA
    return pl.pallas_call(
        partial(reduce_kernel, plan, len(parts)),
        out_shape=(
            jax.ShapeDtypeStruct(block, kind),
            jax.ShapeDtypeStruct(rows.shape, rows.dtype),
        ),
        in_specs=[vmem] * len(parts) + [anywhere],
        out_specs=(vmem, anywhere),
        scratch_shapes=[
            *([pltpu.VMEM((count,) + block, kind)] if plan else []),
            pltpu.VMEM((count // 2,) + block, kind),
            pltpu.VMEM(((side - 1) * side * z_size,) + block, kind),
            pltpu.VMEM(((side - 1) * z_size,) + block, kind),
            pltpu.VMEM((2 * (z_size - 1),) + block, kind),
            *[dma((count + z_size,))] * 2,
            *[dma((count,))] * 2,
            dma,
        ],
        compiler_params=pltpu.CompilerParams(
            collective_id=number, has_side_effects=True, vmem_limit_bytes=58 * 1024 * 1024
        ),
    )(*parts, rows)


def woven(block, weave):
    chunk = block.shape[0]
    me = place_of()
    made = block
    for index in range(-(-3 * DS // chunk)):
        amount = min(chunk, 3 * DS - index * chunk)
        head = block[:amount].reshape((3, amount // 3, DS) if weave else (amount // 3, 3, DS))
        head = head.transpose(1, 0, 2).reshape(amount, DS)
        if index == 0:
            made = jnp.where(me < 3 * DS // chunk, head, made)
        elif amount < chunk:
            made = jnp.where(me == index, jnp.concatenate([head, block[amount:]]), made)
    return made


def block_plan(devices, chunk, layers, others):
    plan = []
    for block in range(devices):
        for layer in range(layers):
            base = 6 * layer
            row, end, line = block * chunk, (block + 1) * chunk, layer * chunk
            first = row
            if row < 3 * DS:
                stop = min(end, 3 * DS)
                amount = (stop - row) // 3
                for part in range(3):
                    plan.append((base + part, row // 3, amount, block, line + part * amount))
                row = stop
            for part, start, size in ((3, 3 * DS, DS), (4, 4 * DS, FS), (5, 4 * DS + FS, FS)):
                stop = min(end, start + size)
                if row < stop:
                    where = line + row - first
                    plan.append((base + part, row - start, stop - row, block, where))
                    row = stop
        line = layers * chunk
        for index, amount in enumerate(others):
            plan.append((6 * layers + index, block * amount, amount, block, line))
            line += amount
        spare = -line % 8
        if spare:
            plan.append((-1, 0, spare, block, line))
    return tuple(plan)


def pack(parts, width, rows):
    count = parts[0].shape[0]
    if all(part.ndim == 3 for part in parts):
        joined = jnp.concatenate(parts, 1)
        return jnp.pad(joined, ((0, 0), (0, rows - joined.shape[1]), (0, 0)))
    joined = jnp.concatenate([part.reshape(count, -1) for part in parts], 1)
    joined = jnp.pad(joined, ((0, 0), (0, rows * width - joined.shape[1])))
    return joined.reshape(count, rows, width)


def outer_product(left, right):
    return lax.dot_general(
        left, right, (((0,), (0,)), ((), ())), preferred_element_type=jnp.float32
    )


def back_product(grad, weight):
    return lax.dot_general(
        grad, weight, (((1,), (1,)), ((), ())), preferred_element_type=jnp.float32
    )


def norm_forward(value, gain, bias):
    average = jnp.mean(value, -1, keepdims=True)
    centered = value - average
    inverse = lax.rsqrt(jnp.mean(centered * centered, -1, keepdims=True) + NORM_EPS)
    normed = centered * inverse
    return (normed * gain + bias, normed, inverse)


def norm_backward(grad, normed, inverse, gain):
    d_normed = grad * gain
    d_value = inverse * (
        d_normed
        - jnp.mean(d_normed, -1, keepdims=True)
        - normed * jnp.mean(d_normed * normed, -1, keepdims=True)
    )
    return (d_value, jnp.sum(grad * normed, 0), jnp.sum(grad, 0))


def cut_pieces(vector, sizes):
    pieces = []
    start = 0
    for amount in sizes:
        pieces.append(vector[..., start : start + amount])
        start += amount
    return pieces


def split_rows(wide, width, hidden):
    first, second, third = 3 * width, 4 * width, 4 * width + hidden
    return (
        wide[:first].reshape(width, 3 * width),
        wide[first:second],
        wide[second:third].reshape(width, hidden),
        wide[third:],
    )


def hidden_term(source, target, proj_turned, proj_bias, weight, denom):
    source_low = source.astype(jnp.bfloat16)
    mapped = back_product(source_low, proj_turned) + proj_bias
    spread = mapped - target
    d_mapped = (2.0 * weight * spread / denom).astype(jnp.bfloat16)
    return (
        jnp.sum(weight * spread * spread) / denom,
        outer_product(d_mapped, source_low),
        jnp.sum(d_mapped.astype(jnp.float32), 0),
        jnp.dot(d_mapped, proj_turned, preferred_element_type=jnp.float32),
    )


def own_parts_of(value):
    parts = value.reshape(2, 2, -1, value.shape[1])
    return jnp.where(lax.axis_index("dp") % 2 == 0, parts[:, 0], parts[:, 1])


def sum_along_x(parts):
    first = lax.axis_index("dp") // 2 == 0
    given = jnp.where(first, parts[1], parts[0])
    kept = jnp.where(first, parts[0], parts[1])
    return kept + lax.ppermute(given, "dp", [(0, 2), (2, 0), (1, 3), (3, 1)])


def adam_update(value, first, second, grad):
    first = BETA_ONE * first + (1.0 - BETA_ONE) * grad
    second = BETA_TWO * second + (1.0 - BETA_TWO) * grad * grad
    ratio = first / (1.0 - BETA_ONE**STEP) / (jnp.sqrt(second / (1.0 - BETA_TWO**STEP)) + ADAM_EPS)
    return (first, second, value - LEARN_RATE * (ratio + WEIGHT_DECAY * value))


def gelu(value):
    return 0.5 * value * (1.0 + jnp.tanh(0.7978845608028654 * (value + 0.044715 * value * value * value)))


def regroup(weights, group):
    amount = weights.shape[0]
    made = lax.broadcasted_iota(jnp.int32, (amount, amount), 0)
    taken = lax.broadcasted_iota(jnp.int32, (amount, amount), 1)
    inner = amount // group
    marks = jnp.where((made % inner) * group + made // inner == taken, 1.0, 0.0)
    return jnp.dot(
        marks.astype(jnp.bfloat16), weights, preferred_element_type=jnp.float32
    ).astype(jnp.bfloat16)


def softmax_low(scores, mask):
    masked = jnp.where(mask > 0.0, scores, NEG_LARGE)
    expo = jnp.exp(masked - jnp.max(masked, -1, keepdims=True))
    return (expo * (1.0 / jnp.sum(expo, -1, keepdims=True))).astype(jnp.bfloat16)


TILE = 256
CHUNK = 96


def teacher_kernel(x_ref, w_ref, vec_ref, mask_ref, y_ref, s_ref, qkv_ref, up_ref, context_ref):
    size = DT // HT
    for index in range(3 * DT // CHUNK):
        made = regroup(w_ref[index], 3)
        for part in range(3):
            rows = CHUNK // 3
            qkv_ref[part, index * rows : (index + 1) * rows, :] = made[part * rows : (part + 1) * rows]
    first_up, first_down = 4 * DT // CHUNK, (4 * DT + FT) // CHUNK
    many = FT // DT
    for index in range(FT // CHUNK // 2):
        at = first_up + 2 * index
        made = regroup(w_ref[at : at + 2].reshape(2 * CHUNK, DT), many)
        rows = 2 * CHUNK // many
        for part in range(many):
            up_ref[part, index * rows : (index + 1) * rows, :] = made[part * rows : (part + 1) * rows]
    line = lax.broadcasted_iota(jnp.int32, (1, 2 * size), 1)
    low_half = line < size
    length = mask_ref.shape[1]

    def vector(index, amount=1):
        return vec_ref[:, index * DT : (index + amount) * DT]

    def tile(step, carry):
        at = pl.ds(pl.multiple_of(step * TILE, TILE), TILE)
        x_low = x_ref[at, :]
        q, k, v = (
            (
                jnp.dot(x_low, qkv_ref[part], preferred_element_type=jnp.float32) + vector(part)
            ).astype(jnp.bfloat16)
            for part in range(3)
        )
        nothing = jnp.zeros((length, 2 * size), jnp.bfloat16)
        for row in range(TILE // length):
            span = slice(row * length, (row + 1) * length)
            here = pl.ds(pl.multiple_of(step * TILE + row * length, length), length)
            mask = mask_ref[here, :]
            for pair in range(HT // 2):
                lanes = slice(pair * 2 * size, (pair + 1) * 2 * size)
                k_pair, v_pair = k[span, lanes], v[span, lanes]
                k_both = jnp.concatenate(
                    [jnp.where(low_half, k_pair, nothing), jnp.where(low_half, nothing, k_pair)]
                )
                v_both = jnp.concatenate(
                    [jnp.where(low_half, v_pair, nothing), jnp.where(low_half, nothing, v_pair)]
                )
                scores = back_product(q[span, lanes], k_both) * size ** (-0.5)
                s_ref[here, pair * 2 * length : (pair + 1) * 2 * length] = scores
                weights = jnp.concatenate(
                    [softmax_low(scores[:, :length], mask), softmax_low(scores[:, length:], mask)], 1
                )
                context_ref[span, lanes] = jnp.dot(
                    weights, v_both, preferred_element_type=jnp.float32
                ).astype(jnp.bfloat16)
        w_out = w_ref[3 * DT // CHUNK : first_up].reshape(DT, DT)
        attended = jnp.dot(context_ref[...], w_out, preferred_element_type=jnp.float32) + vector(3)
        middle = norm_forward(x_low.astype(jnp.float32) + attended, vector(4), vector(5))[0]
        middle_low = middle.astype(jnp.bfloat16)
        outer = jnp.zeros((TILE, DT), jnp.float32)
        for part in range(many):
            inner = jnp.dot(middle_low, up_ref[part], preferred_element_type=jnp.float32) + vector(
                6 + part
            )
            begin = first_down + part * (DT // CHUNK)
            w_down = w_ref[begin : begin + DT // CHUNK].reshape(DT, DT)
            outer = outer + jnp.dot(
                gelu(inner).astype(jnp.bfloat16), w_down, preferred_element_type=jnp.float32
            )
        y_ref[at, :] = norm_forward(
            middle + outer + vector(6 + many), vector(7 + many), vector(8 + many)
        )[0]
        return carry

    lax.fori_loop(0, x_ref.shape[0] // TILE, tile, 0)


def teacher_forward(x_low, blocks, vectors, mask):
    tokens, length = mask.shape
    vmem = pl.BlockSpec(memory_space=pltpu.VMEM)
    return pl.pallas_call(
        teacher_kernel,
        out_shape=(
            jax.ShapeDtypeStruct((tokens, DT), jnp.float32),
            jax.ShapeDtypeStruct((tokens, HT * length), jnp.float32),
        ),
        in_specs=[vmem] * 4,
        out_specs=(vmem, vmem),
        scratch_shapes=[
            pltpu.VMEM((3, DT, DT), jnp.bfloat16),
            pltpu.VMEM((FT // DT, DT, DT), jnp.bfloat16),
            pltpu.VMEM((TILE, DT), jnp.bfloat16),
        ],
        compiler_params=pltpu.CompilerParams(vmem_limit_bytes=58 * 1024 * 1024),
        cost_estimate=pl.CostEstimate(
            flops=20 * 10**9, bytes_accessed=25 * 10**6, transcendentals=5 * 10**6
        ),
    )(x_low, blocks, vectors, mask)


WIDER = -(-FS // 128) * 128
VMEM_SPEC = pl.BlockSpec(memory_space=pltpu.VMEM)


def refold(source, target, source_width, target_width):
    period = math.lcm(source_width, target_width)
    groups = source.shape[1] * source_width // period
    step_in, step_out = period // source_width, period // target_width
    lane = lax.broadcasted_iota(jnp.int32, (groups, 128), 1)
    for row in range(step_out):
        for tile in range(-(-target_width // 128)):
            begin = row * target_width + 128 * tile
            amount = min(128, target_width - 128 * tile)
            made, at = jnp.zeros((groups, 128), source.dtype), 0
            while at < amount:
                line, column = divmod(begin + at, source_width)
                where, lanes = divmod(column, 128)
                piece = source[where, pl.ds(line, groups, stride=step_in), :]
                if (at - lanes) % 128:
                    piece = pltpu.roll(piece, (at - lanes) % 128, 1)
                length = min(128 - lanes, source_width - column, amount - at)
                made = jnp.where((lane >= at) & (lane < at + length), piece, made)
                at += length
            target[tile, pl.ds(row, groups, stride=step_out), :] = made


def unpack_kernel(plan, layers, w_ref, *refs):
    place_ref, proj_ref, square, wide, folded, unfolded, small = refs[4 * layers :]
    for layer in range(layers):
        qkv_ref, out_ref, up_ref, down_ref = refs[4 * layer : 4 * layer + 4]
        for matrix, at, rows, block, line in plan:
            part = matrix - 6 * layer
            if not 0 <= part < 6:
                continue
            value = w_ref[block].astype(jnp.float32)[line : line + rows]
            if part < 4:
                square[part, at : at + rows, :] = value
            elif part == 4:
                for tile in range(-(-DS // 128)):
                    lanes = min(128, DS - 128 * tile)
                    folded[tile, at : at + rows, :lanes] = value[:, 128 * tile : 128 * tile + lanes]
            else:
                wide[at : at + rows, :] = value
        for part in range(3):
            qkv_ref[part] = square[part].astype(jnp.bfloat16)
        out_ref[...] = square[3].astype(jnp.bfloat16)
        refold(folded, unfolded, DS, FS)
        for tile in range(WIDER // 128):
            up_ref[:, 128 * tile : 128 * tile + 128] = unfolded[tile].astype(jnp.bfloat16)
        down_ref[:FS, :] = wide[...].astype(jnp.bfloat16)
        down_ref[FS:, :] = jnp.zeros((WIDER - FS, DS), jnp.bfloat16)
    for matrix, at, rows, block, line in plan:
        if matrix >= 6 * layers:
            value = w_ref[block].astype(jnp.float32)[line : line + rows]
            small[matrix - 6 * layers, at : at + rows, :] = value
    place_ref[...] = small[0, : place_ref.shape[0]].astype(jnp.bfloat16)
    proj_ref[...] = small[1].astype(jnp.bfloat16)


def unpack(blocks, plan, layers, length):
    low = partial(jax.ShapeDtypeStruct, dtype=jnp.bfloat16)
    full = jnp.float32
    return pl.pallas_call(
        partial(unpack_kernel, plan, layers),
        out_shape=(
            *[low((3, DS, DS)), low((DS, DS)), low((DS, WIDER)), low((WIDER, DS))] * layers,
            low((length, DS)),
            low((DT, DS)),
        ),
        in_specs=[VMEM_SPEC],
        out_specs=(VMEM_SPEC,) * (4 * layers + 2),
        scratch_shapes=[
            pltpu.VMEM((4, DS, DS), full),
            pltpu.VMEM((FS, DS), full),
            pltpu.VMEM((-(-DS // 128), FS, 128), full),
            pltpu.VMEM((WIDER // 128, DS, 128), full),
            pltpu.VMEM((2, DT, DS), full),
        ],
        compiler_params=pltpu.CompilerParams(vmem_limit_bytes=50 * 1024 * 1024),
        cost_estimate=pl.CostEstimate(flops=0, bytes_accessed=20 * 10**6, transcendentals=0),
    )(blocks)


def by_heads(value, heads):
    width = value.shape[1]
    size = width // heads
    lane = lax.broadcasted_iota(jnp.int32, (1, width), 1)
    nothing = jnp.zeros_like(value)
    return jnp.concatenate(
        [
            jnp.where((lane >= head * size) & (lane < (head + 1) * size), value, nothing)
            for head in range(heads)
        ]
    )


def student_kernel(
    layers, token_ref, place_ref, evec_ref, vec_ref, bias_ref, mask_ref,
    *refs,
):
    matrices, refs = refs[: 4 * layers], refs[4 * layers :]
    emb_ref, zero_ref, zero_inv, last_ref = refs[:4]
    length = mask_ref.shape[1]
    size = DS // HS

    def tile(step, carry):
        at = pl.ds(pl.multiple_of(step * TILE, TILE), TILE)
        places = jnp.concatenate([place_ref[...].astype(jnp.float32)] * (TILE // length))
        hidden, normed, inverse = norm_forward(
            token_ref[at, :] + places, evec_ref[0:1, :], evec_ref[1:2, :]
        )
        emb_ref[at, :] = hidden
        zero_ref[at, :] = normed
        zero_inv[at, :] = inverse
        for layer in range(layers):
            qkv_w, out_w, up_w, down_w = matrices[4 * layer : 4 * layer + 4]
            low_ref, qkv_ref, context_ref, one_ref, one_inv, two_ref, two_inv = refs[
                4 + 7 * layer : 11 + 7 * layer
            ]

            def vector(index, layer=layer):
                return vec_ref[layer, index : index + 1, :]

            low = hidden.astype(jnp.bfloat16)
            low_ref[at, :] = low
            parts = []
            for part in range(3):
                made = jnp.dot(low, qkv_w[part], preferred_element_type=jnp.float32)
                if part != 1:
                    made = made + vector(part // 2)
                parts.append(made.astype(jnp.bfloat16))
                qkv_ref[part, at, :] = parts[part]
            contexts = []
            for row in range(TILE // length):
                span = slice(row * length, (row + 1) * length)
                here = pl.ds(pl.multiple_of(step * TILE + row * length, length), length)
                mask = mask_ref[here, :]
                q, k, v = (part[span] for part in parts)
                scores = back_product(q, by_heads(k, HS)) * size ** (-0.5)
                weights = jnp.concatenate(
                    [
                        softmax_low(scores[:, head * length : (head + 1) * length], mask)
                        for head in range(HS)
                    ],
                    1,
                )
                contexts.append(
                    jnp.dot(weights, by_heads(v, HS), preferred_element_type=jnp.float32)
                )
            context = jnp.concatenate(contexts).astype(jnp.bfloat16)
            context_ref[at, :] = context
            attended = jnp.dot(context, out_w[...], preferred_element_type=jnp.float32) + vector(2)
            middle, normed, inverse = norm_forward(hidden + attended, vector(3), vector(4))
            one_ref[at, :] = normed
            one_inv[at, :] = inverse
            inner = jnp.dot(
                middle.astype(jnp.bfloat16), up_w[...], preferred_element_type=jnp.float32
            ) + bias_ref[layer]
            outer = jnp.dot(
                gelu(inner).astype(jnp.bfloat16), down_w[...], preferred_element_type=jnp.float32
            ) + vector(5)
            hidden, normed, inverse = norm_forward(middle + outer, vector(6), vector(7))
            two_ref[at, :] = normed
            two_inv[at, :] = inverse
        last_ref[at, :] = hidden
        return carry

    lax.fori_loop(0, token_ref.shape[0] // TILE, tile, 0)


def student_forward(token_rows, places, evec, vectors, biases, mask, matrices):
    tokens = token_rows.shape[0]
    layers = vectors.shape[0]
    full = partial(jax.ShapeDtypeStruct, dtype=jnp.float32)
    low = partial(jax.ShapeDtypeStruct, dtype=jnp.bfloat16)
    made = (
        full((tokens, DS)),
        full((tokens, DS)),
        full((tokens, 1)),
        full((tokens, DS)),
        *[
            low((tokens, DS)),
            low((3, tokens, DS)),
            low((tokens, DS)),
            full((tokens, DS)),
            full((tokens, 1)),
            full((tokens, DS)),
            full((tokens, 1)),
        ]
        * layers,
    )
    return pl.pallas_call(
        partial(student_kernel, layers),
        out_shape=made,
        in_specs=[VMEM_SPEC] * (6 + len(matrices)),
        out_specs=(VMEM_SPEC,) * len(made),
        compiler_params=pltpu.CompilerParams(vmem_limit_bytes=58 * 1024 * 1024),
        cost_estimate=pl.CostEstimate(
            flops=8 * 10**9, bytes_accessed=40 * 10**6, transcendentals=6 * 10**6
        ),
    )(token_rows, places, evec, vectors, biases, mask, *matrices)


def back_kernel(
    last, grad_ref, vec_ref, bias_ref, mask_ref, qkv_w, out_w, up_w, down_w,
    low_ref, qkv_ref, context_ref, one_ref, one_inv, two_ref, two_inv, *refs,
):
    if last:
        score_ref, count_ref, refs = refs[0], refs[1], refs[2:]
    hidden_ref, *weight_refs, vec_out, bias_out, refs = (*refs[:9], refs[9:])
    dq_ref, dk_ref, dv_ref, do_ref, du_ref, dd_ref = weight_refs
    if last:
        loss_ref, refs = refs[0], refs[1:]
        loss_ref[...] = jnp.zeros_like(loss_ref)
    outer_s, attended_s, q_s, k_s, v_s, middle_s, active_s, inner_s, unfolded, folded = refs
    length = mask_ref.shape[1]
    size = DS // HS
    vec_out[...] = jnp.zeros_like(vec_out)
    bias_out[...] = jnp.zeros_like(bias_out)
    many = 256

    def vector(index):
        return vec_ref[index : index + 1, :]

    def note(index, value):
        vec_out[index : index + 1, :] += jnp.sum(value.astype(jnp.float32), 0, keepdims=True)

    def norm_back(grad, normed, inverse, gain, index):
        d_normed = grad * gain
        note(index, grad * normed)
        note(index + 1, grad)
        return inverse * (
            d_normed
            - jnp.mean(d_normed, -1, keepdims=True)
            - normed * jnp.mean(d_normed * normed, -1, keepdims=True)
        )

    def tile(step, carry):
        at = pl.ds(pl.multiple_of(step * TILE, TILE), TILE)
        d_sum = norm_back(grad_ref[at, :], two_ref[at, :], two_inv[at, :], vector(6), 6)
        d_outer = d_sum.astype(jnp.bfloat16)
        outer_s[at, :] = d_outer
        note(5, d_outer)
        middle = (one_ref[at, :] * vector(3) + vector(4)).astype(jnp.bfloat16)
        middle_s[at, :] = middle
        d_middle = d_sum
        for first in range(0, WIDER, many):
            lanes = slice(first, first + many)
            inner = jnp.dot(
                middle, up_w[:, lanes], preferred_element_type=jnp.float32
            ) + bias_ref[:, lanes]
            squared = inner * inner
            bent = jnp.tanh(0.7978845608028654 * (inner + 0.044715 * squared * inner))
            active_s[at, lanes] = (0.5 * inner * (1.0 + bent)).astype(jnp.bfloat16)
            slope = 0.5 * (1.0 + bent) + 0.5 * inner * (1.0 - bent * bent) * (
                0.7978845608028654 * (1.0 + 3.0 * 0.044715 * squared)
            )
            d_inner = (back_product(d_outer, down_w[lanes, :]) * slope).astype(jnp.bfloat16)
            inner_s[at, lanes] = d_inner
            bias_out[:, lanes] += jnp.sum(d_inner.astype(jnp.float32), 0, keepdims=True)
            d_middle = d_middle + back_product(d_inner, up_w[:, lanes])
        d_one = norm_back(d_middle, one_ref[at, :], one_inv[at, :], vector(3), 3)
        d_attended = d_one.astype(jnp.bfloat16)
        attended_s[at, :] = d_attended
        note(2, d_attended)
        d_context = back_product(d_attended, out_w[...]).astype(jnp.bfloat16)
        for row in range(TILE // length):
            here = pl.ds(pl.multiple_of(step * TILE + row * length, length), length)
            mask = mask_ref[here, :]
            d_row = d_context[row * length : (row + 1) * length]
            q, k, v = (qkv_ref[part, here, :] for part in range(3))
            keys = by_heads(k, HS)
            scores = back_product(q, keys) * size ** (-0.5)
            d_weights = back_product(d_row, by_heads(v, HS))
            low_weights, d_scores = [], []
            for head in range(HS):
                lanes = slice(head * length, (head + 1) * length)
                masked = jnp.where(mask > 0.0, scores[:, lanes], NEG_LARGE)
                expo = jnp.exp(masked - jnp.max(masked, -1, keepdims=True))
                weights = expo * (1.0 / jnp.sum(expo, -1, keepdims=True))
                low_weights.append(weights.astype(jnp.bfloat16))
                turned = weights * d_weights[:, lanes]
                made = turned - weights * jnp.sum(turned, -1, keepdims=True)
                if last:
                    differ = jnp.where(mask > 1.0, scores[:, lanes] - score_ref[here, lanes], 0.0)
                    loss_ref[...] += jnp.sum(differ * differ, 0, keepdims=True)
                    made = made + differ * (2.0 / count_ref[...])
                d_scores.append(made.astype(jnp.bfloat16))
            scale = size ** (-0.5)
            q_s[here, :] = (
                jnp.dot(jnp.concatenate(d_scores, 1), keys, preferred_element_type=jnp.float32)
                * scale
            ).astype(jnp.bfloat16)
            k_s[here, :] = (
                outer_product(jnp.concatenate(d_scores), by_heads(q, HS)) * scale
            ).astype(jnp.bfloat16)
            v_s[here, :] = outer_product(
                jnp.concatenate(low_weights), by_heads(d_row, HS)
            ).astype(jnp.bfloat16)
        d_hidden = d_one
        for part, held in enumerate((q_s, k_s, v_s)):
            d_part = held[at, :]
            if part != 1:
                note(part // 2, d_part)
            d_hidden = d_hidden + back_product(d_part, qkv_w[part])
        hidden_ref[at, :] = d_hidden
        return carry

    lax.fori_loop(0, grad_ref.shape[0] // TILE, tile, 0)
    low = low_ref[...]
    dq_ref[...] = outer_product(low, q_s[...])
    dk_ref[...] = outer_product(low, k_s[...])
    dv_ref[...] = outer_product(low, v_s[...])
    do_ref[...] = outer_product(context_ref[...], attended_s[...])
    for first in range(0, WIDER, many):
        lanes = slice(first, first + many)
        stop = min(first + many, FS)
        dd_ref[first:stop, :] = outer_product(active_s[:, lanes], outer_s[...])[: stop - first]
        made = outer_product(middle_s[...], inner_s[:, lanes])
        for tile_at in range(many // 128):
            unfolded[first // 128 + tile_at] = made[:, 128 * tile_at : 128 * tile_at + 128]
    refold(unfolded, folded, FS, DS)
    for tile_at in range(-(-DS // 128)):
        lanes = min(128, DS - 128 * tile_at)
        du_ref[:, 128 * tile_at : 128 * tile_at + lanes] = folded[tile_at, :, :lanes]


def student_backward(grad, vectors, biases, mask, matrices, saved, last):
    tokens, length = mask.shape
    full = partial(jax.ShapeDtypeStruct, dtype=jnp.float32)
    made = [
        full((tokens, DS)),
        *[full((DS, DS))] * 4,
        full((FS, DS)),
        full((FS, DS)),
        full((8, DS)),
        full((1, WIDER)),
    ]
    given = [grad, vectors, biases, mask, *matrices, *saved]
    if last:
        given += last
        made.append(full((1, length)))
    low = partial(pltpu.VMEM, dtype=jnp.bfloat16)
    return pl.pallas_call(
        partial(back_kernel, bool(last)),
        out_shape=tuple(made),
        in_specs=[VMEM_SPEC] * len(given),
        out_specs=(VMEM_SPEC,) * len(made),
        scratch_shapes=[
            *[low((tokens, DS))] * 6,
            *[low((tokens, WIDER))] * 2,
            pltpu.VMEM((WIDER // 128, DS, 128), jnp.float32),
            pltpu.VMEM((-(-DS // 128), FS, 128), jnp.float32),
        ],
        compiler_params=pltpu.CompilerParams(vmem_limit_bytes=58 * 1024 * 1024),
        cost_estimate=pl.CostEstimate(
            flops=10**9, bytes_accessed=4 * 10**6, transcendentals=3 * 10**5
        ),
    )(*given)


def d_all_width(width):
    return -(-width // 128) * 128


def head_kernel(
    groups, pair, denom, p_ref, t_ref, table_ref, head_ref, d_ref, own_ref, w_ref, *refs
):
    inbox_ref, refs = (refs[0], refs[1:]) if pair else (None, refs)
    (
        p_all, t_all, p_turned, t_turned, s_logits, t_logits, stats, rows_of, low_grads, tiles, total,
        send, recv, stat_send, stat_recv, d_send, d_recv, tile_sem, pair_send, pair_recv,
    ) = refs
    amount, width = p_ref.shape
    vocab = table_ref.shape[0]
    z_size = z_size_of(groups)
    side = groups // z_size
    across = z_size * amount
    half = d_all_width(width)
    dp, me = lax.axis_index("dp"), lax.axis_index("fsdp")
    z, y = me // side, me % side
    sibling = (dp // 2 * 2 + 1 - dp % 2, me)
    barrier = pltpu.get_barrier_semaphore()
    for step in range(1, groups):
        pl.semaphore_signal(
            barrier, inc=1, device_id=(dp, (me + step) % groups), device_id_type=MESH
        )
    if pair:
        pl.semaphore_signal(barrier, inc=1, device_id=sibling, device_id_type=MESH)
    pl.semaphore_wait(barrier, groups - 1 + (1 if pair else 0))

    def both(at, rank, target, own=False):
        return [
            pltpu.make_async_remote_copy(
                given if own else held.at[at],
                held.at[at],
                send.at[2 * rank + index],
                recv.at[2 * rank + index],
                device_id=(dp, target),
                device_id_type=MESH,
            )
            for index, (given, held) in enumerate(((p_ref, p_all), (t_ref, t_all)))
        ]

    def begin(copies):
        for copy in copies:
            copy.start()

    def received(copies):
        for copy in copies:
            copy.wait_recv()

    def sent(copies):
        for copy in copies:
            copy.wait_send()

    def line(step):
        return z + step, (z + step >= 0) & (z + step < z_size)

    def inside(position):
        return jnp.minimum(jnp.maximum(position, 0), z_size - 1) * side

    def z_copies(step, way, arriving):
        origin, known = line(-way * (step + (1 if arriving else 0)))
        target, there = line(way)
        rank = 2 * step + (1 if way > 0 else 0)
        made = both(inside(origin) + y, rank, inside(target) + y, own=step == 0 and not arriving)
        return made, known if arriving else known & there

    def y_copies(back, step, at, own=False):
        return both(
            at, 2 * z_size + (back - 1) * z_size + step, z * side + (y + back) % side, own
        )

    wide = next(size for size in (384, 320, 128) if vocab % size == 0)

    def measure(back):
        at_y = (y + side - back) % side
        slots = [line * side + at_y for line in range(z_size)]
        t_turned[...] = jnp.concatenate([t_all[at] for at in slots]).astype(jnp.float32).T.astype(
            jnp.bfloat16
        )
        p_turned[...] = jnp.concatenate([p_all[at] for at in slots]).astype(jnp.float32).T.astype(
            jnp.bfloat16
        )

        def step(index, carry):
            s_top, s_sum, t_top, t_sum, cross = carry
            lines = pl.ds(pl.multiple_of(index * wide, 64), wide)
            t_now = jnp.dot(head_ref[lines, :], t_turned[...], preferred_element_type=jnp.float32)
            s_now = jnp.dot(table_ref[lines, :], p_turned[...], preferred_element_type=jnp.float32)
            t_logits[back, lines, :] = t_now
            s_logits[back, lines, :] = s_now
            s_next = jnp.maximum(s_top, jnp.max(s_now, 0, keepdims=True))
            t_next = jnp.maximum(t_top, jnp.max(t_now, 0, keepdims=True))
            t_exp = jnp.exp(t_now - t_next)
            scale = jnp.exp(t_top - t_next)
            s_sum = s_sum * jnp.exp(s_top - s_next) + jnp.sum(
                jnp.exp(s_now - s_next), 0, keepdims=True
            )
            t_sum = t_sum * scale + jnp.sum(t_exp, 0, keepdims=True)
            cross = cross * scale + jnp.sum(t_exp * s_now, 0, keepdims=True)
            return (s_next, s_sum, t_next, t_sum, cross)

        lowest = jnp.full((1, across), -jnp.inf, jnp.float32)
        zero = jnp.zeros((1, across), jnp.float32)
        made = lax.fori_loop(0, vocab // wide, step, (lowest, zero, lowest, zero, zero))
        for index, value in enumerate(made):
            stats[me, at_y, index : index + 1, :] = value

    p_all[me] = p_ref[...]
    t_all[me] = t_ref[...]
    for way in (1, -1):
        made, wanted = z_copies(0, way, False)
        pl.when(wanted)(partial(begin, made))
    for back in range(1, side):
        begin(y_copies(back, z, me, own=True))
    for step in range(z_size - 1):
        for way in (1, -1):
            made, wanted = z_copies(step, way, True)
            onward, further = z_copies(step + 1, way, False) if step + 2 < z_size else (None, None)

            @pl.when(wanted)
            def _(made=made, onward=onward, further=further, step=step, way=way):
                received(made)
                if onward is not None:
                    pl.when(further)(partial(begin, onward))
                origin = z - way * (step + 1)
                for back in range(1, side):
                    begin(y_copies(back, origin, origin * side + y))

    for back in range(side):
        if back:
            for step in range(z_size):
                received(y_copies(back, step, step * side + (y + side - back) % side))
        measure(back)
    for step in range(z_size - 1):
        for way in (1, -1):
            made, wanted = z_copies(step, way, False)
            pl.when(wanted)(partial(sent, made))
    for back in range(1, side):
        for step in range(z_size):
            sent(y_copies(back, step, step * side + y))

    def stat_copy(step):
        return pltpu.make_async_remote_copy(
            stats.at[me],
            stats.at[me],
            stat_send.at[step],
            stat_recv.at[step],
            device_id=(dp, (me + step) % groups),
            device_id_type=MESH,
        )

    for step in range(1, groups):
        stat_copy(step).start()
    for step in range(1, groups):
        stat_copy(step).wait_recv()
    for back in range(side):
        at_y = (y + side - back) % side
        parts = [stats[other, at_y] for other in range(groups)]
        s_top, t_top = parts[0][0:1], parts[0][2:3]
        for part in parts[1:]:
            s_top = jnp.maximum(s_top, part[0:1])
            t_top = jnp.maximum(t_top, part[2:3])
        s_sum, t_sum, cross = (jnp.zeros_like(s_top) for unused in range(3))
        for part in parts:
            s_sum = s_sum + part[1:2] * jnp.exp(part[0:1] - s_top)
            scale = jnp.exp(part[2:3] - t_top)
            t_sum = t_sum + part[3:4] * scale
            cross = cross + part[4:5] * scale
        rows_of[back, 0:1, :] = s_top + jnp.log(s_sum)
        rows_of[back, 1:2, :] = t_top
        rows_of[back, 2:3, :] = 1.0 / t_sum
        rows_of[back, 3:4, :] = cross / t_sum
        total[back] = jnp.zeros((half, across), jnp.float32)
    own_ref[...] = rows_of[0]
    narrow = next(size for size in (384, 320, 128) if vocab % size == 0)
    outs = []
    for index in range(vocab // narrow):
        lines = slice(index * narrow, (index + 1) * narrow)
        table = table_ref[lines, :]

        def differ(back, carry, lines=lines, table=table):
            row = rows_of[back]
            made = 2.0 * jnp.exp(s_logits[back, lines, :] - row[0:1])
            made = made - jnp.exp(t_logits[back, lines, :] - row[1:2]) * row[2:3]
            low = (made * (1.0 / denom)).astype(jnp.bfloat16)
            low_grads[back] = low
            total[back, :width, :] += outer_product(table, low)
            return carry

        lax.fori_loop(0, side, differ, 0)
        if index >= 2:
            outs[index - 2].wait()
        made = jnp.zeros((narrow, width), jnp.float32)
        for back in range(side):
            at_y = (y + side - back) % side
            states = jnp.concatenate([p_all[line * side + at_y] for line in range(z_size)])
            made = made + jnp.dot(low_grads[back], states, preferred_element_type=jnp.float32)
        tiles[index % 2] = made
        outs.append(
            pltpu.make_async_copy(tiles.at[index % 2], w_ref.at[lines, :], tile_sem.at[index % 2])
        )
        outs[-1].start()
    for back in range(side):
        turned = total[back].T.astype(jnp.bfloat16)
        for line in range(z_size):
            at = line * side + (y + side - back) % side
            t_all[at, :, half : 2 * half] = turned[line * amount : (line + 1) * amount]

    def d_copy(step):
        peer = (me + step) % groups
        return pltpu.make_async_remote_copy(
            t_all.at[peer, :, half : 2 * half],
            t_all.at[me, :, 0:half],
            d_send.at[step],
            d_recv.at[step],
            device_id=(dp, peer),
            device_id_type=MESH,
        )

    for step in range(1, groups):
        d_copy(step).start()
    for out in outs[-2:]:
        out.wait()
    given = []
    if pair:
        part = vocab // 4
        for index in range(2):
            start = pl.multiple_of((2 * index + 1 - dp % 2) * part, 8)
            given.append(
                pltpu.make_async_remote_copy(
                    w_ref.at[pl.ds(start, part), :],
                    inbox_ref.at[index],
                    pair_send.at[index],
                    pair_recv.at[index],
                    device_id=sibling,
                    device_id_type=MESH,
                )
            )
            given[-1].start()
    made = t_all[me, :, half : 2 * half].astype(jnp.float32)
    for step in range(1, groups):
        d_copy(step).wait_recv()
        made = made + t_all[(me + groups - step) % groups, :, 0:half].astype(jnp.float32)
    d_ref[...] = made
    for step in range(1, groups):
        stat_copy(step).wait_send()
        d_copy(step).wait_send()
    for copy in given:
        copy.wait()


def head(picked, t_picked, table, teacher_head, denom, number):
    groups, n_dp = lax.axis_size("fsdp"), lax.axis_size("dp")
    pair = n_dp == 4
    amount, width = picked.shape
    vocab = table.shape[0]
    z_size = z_size_of(groups)
    side, across = groups // z_size, z_size * amount
    half = d_all_width(width)
    assert 2 * half <= DT
    narrow = next(size for size in (384, 320, 128) if vocab % size == 0)
    full, low = jnp.float32, jnp.bfloat16
    anywhere = pl.BlockSpec(memory_space=pl.ANY)
    dma = pltpu.SemaphoreType.DMA
    made = [
        jax.ShapeDtypeStruct((amount, half), full),
        jax.ShapeDtypeStruct((8, across), full),
        jax.ShapeDtypeStruct((vocab, width), full),
    ]
    if pair:
        made.append(jax.ShapeDtypeStruct((2, vocab // 4, width), full))
    return pl.pallas_call(
        partial(head_kernel, groups, pair, denom),
        out_shape=tuple(made),
        in_specs=[VMEM_SPEC] * 4,
        out_specs=(VMEM_SPEC, VMEM_SPEC) + (anywhere,) * (len(made) - 2),
        scratch_shapes=[
            pltpu.VMEM((groups, amount, width), low),
            pltpu.VMEM((groups, amount, DT), low),
            pltpu.VMEM((width, across), low),
            pltpu.VMEM((DT, across), low),
            pltpu.VMEM((side, vocab, across), full),
            pltpu.VMEM((side, vocab, across), full),
            pltpu.VMEM((groups, side, 8, across), full),
            pltpu.VMEM((side, 8, across), full),
            pltpu.VMEM((side, narrow, across), low),
            pltpu.VMEM((2, narrow, width), full),
            pltpu.VMEM((side, half, across), full),
            *[dma((2 * (2 * z_size + (side - 1) * z_size),))] * 2,
            *[dma((groups,))] * 4,
            *[dma((2,))] * 3,
        ],
        compiler_params=pltpu.CompilerParams(
            collective_id=number, has_side_effects=True, vmem_limit_bytes=60 * 1024 * 1024
        ),
    )(picked, t_picked, table, teacher_head)


def three_parts(value):
    high = lax.reduce_precision(value, 8, 7)
    rest = value - high
    middle = lax.reduce_precision(rest, 8, 7)
    low = rest - middle
    return jnp.concatenate([high, middle, low], -1).astype(jnp.bfloat16)


def pick_exact(marks, value, turned=False):
    width = value.shape[1]
    terms = three_parts(value)
    made = outer_product(marks, terms) if turned else jnp.dot(
        marks, terms, preferred_element_type=jnp.float32
    )
    return made[:, :width] + made[:, width : 2 * width] + made[:, 2 * width :]


def plan_requests(ids, local_rows):
    order = lax.broadcasted_iota(jnp.int32, (ids.shape[0],), 0)
    same = ids[:, None] == ids[None, :]
    leader = jnp.min(jnp.where(same, order[None, :], ids.shape[0]), 1)
    leads = leader == order
    owner = ids // local_rows
    before = (
        (owner[:, None] == owner[None, :]) & leads[None, :] & (order[None, :] < leader[:, None])
    )
    rank = jnp.sum(before.astype(jnp.int32), 1)
    return (leads, owner, ids - owner * local_rows, rank)


def round_marks(plan, turn, devices):
    leads, owner, local_id, rank = plan
    inside = (rank >= turn * SLOTS) & (rank < (turn + 1) * SLOTS)
    slot = jnp.where(inside, owner * SLOTS + rank - turn * SLOTS, -1)
    line = lax.broadcasted_iota(jnp.int32, (devices * SLOTS, 1), 0)
    hit = line == slot[None, :]
    asked = jnp.max(jnp.where(hit & leads[None, :], local_id[None, :], -1), 1)
    return (hit.astype(jnp.bfloat16), asked.reshape(devices, 1, SLOTS))


def question(plan, turn, devices, extra):
    marks, asked = round_marks(plan, turn, devices)
    fill = jnp.full((devices, 1, 128 - SLOTS - extra.shape[0]), -1, jnp.int32)
    note = jnp.broadcast_to(extra[None, None, :], (devices, 1, extra.shape[0]))
    return (marks, jnp.concatenate([asked, note, fill], 2))


def ask(plan, turn, devices, extra):
    marks, asked = question(plan, turn, devices, extra)
    return (marks, exchange(asked, 0)[:, 0, :SLOTS].reshape(-1))


def wanted_marks(wanted, local_rows):
    return (wanted[:, None] == lax.broadcasted_iota(jnp.int32, (1, local_rows), 1)).astype(
        jnp.bfloat16
    )


def fetch(marks, wanted, table_low, devices):
    rows = jnp.dot(
        wanted_marks(wanted, table_low.shape[0]), table_low, preferred_element_type=jnp.float32
    ).astype(jnp.bfloat16)
    got = exchange(rows.reshape(devices, SLOTS, -1), 1)
    return outer_product(marks, got.reshape(devices * SLOTS, -1))


def give_back(marks, wanted, grads, local_rows, devices):
    sent = pick_exact(marks, grads)
    got = exchange(sent.reshape(devices, SLOTS, -1), 2)
    return pick_exact(wanted_marks(wanted, local_rows), got.reshape(devices * SLOTS, -1), True)


def local(
    token_ids,
    valid_mask,
    seq_ids,
    mask_pos,
    mask_labels,
    teacher_in,
    teacher_flat,
    teacher_vec,
    teacher_head,
    emb_table,
    emb_first,
    emb_second,
    pos_table,
    pos_first,
    pos_second,
    layer_flat,
    layer_first,
    layer_second,
    proj_weight,
    proj_first,
    proj_second,
    layer_vec,
    vec_first,
    vec_second,
    misc_vec,
    misc_first,
    misc_second,
):
    micro, micro_rows, length = token_ids.shape
    rows = micro * micro_rows
    local_rows, width = emb_table.shape
    layers = layer_vec.shape[0]
    picks = mask_pos.shape[2]
    tokens = rows * length
    n_dp, groups = lax.axis_size("dp"), lax.axis_size("fsdp")
    place = lax.axis_index("fsdp")
    devices = n_dp * groups
    hidden_denom = float(rows * devices * length * DT)
    predict_denom = float(rows * devices * picks)
    flat_local = layer_flat.shape[1]
    by_rows = flat_local % DS == 0

    to_owner = [
        (d * groups + f, f * n_dp + d) for d in range(n_dp) for f in range(groups)
    ]
    from_owner = [(owner, holder) for holder, owner in to_owner]
    table_low = emb_table.astype(jnp.bfloat16)

    usable = valid_mask.reshape(rows, length) > 0
    docs = seq_ids.reshape(rows, length)
    same_doc = docs[:, :, None] == docs[:, None, :]
    pair_mask = same_doc & usable[:, :, None] & usable[:, None, :]
    allowed = pair_mask | jnp.eye(length, dtype=bool)
    ids = jnp.concatenate([token_ids.reshape(-1), mask_labels.reshape(-1)])
    plan = plan_requests(ids, local_rows)
    extra = jnp.stack([-1 - jnp.sum(pair_mask.astype(jnp.int32)), -1 - jnp.max(plan[3])])
    teacher_lines = teacher_flat.reshape(-1, DT)
    teacher_all = lax.all_gather(teacher_lines, BOTH, axis=0, tiled=True).reshape(-1, CHUNK, DT)
    own_parts = [
        layer_flat.astype(jnp.bfloat16),
        pos_table.astype(jnp.bfloat16),
        proj_weight.astype(jnp.bfloat16).T,
    ]
    if by_rows:
        chunk = flat_local // DS
        own_layers = [woven(part.reshape(-1, DS), False) for part in own_parts[0]]
        own_parts = [part.reshape(1, -1, DS) for part in own_layers + own_parts[1:]]
        line, lines = DS, sum(part.shape[1] for part in own_parts)
    else:
        own_parts = [part.reshape(1, -1) for part in own_parts]
        line, lines = 128, -(-sum(part.shape[1] for part in own_parts) // 128)
    block_rows = -(-lines // 16) * 16
    marks, asked = question(plan, 0, devices, extra)
    got, weights_all, token_blocks = entry(asked, pack(own_parts, line, block_rows)[0], table_low, 3)
    table_then = lax.optimization_barrier((table_low, got))[0]
    slice_part = lax.ppermute(table_then, BOTH, from_owner)
    wanted = got[:, 0, :SLOTS].reshape(-1)
    notes = got[:, 0, SLOTS : SLOTS + 2]
    count = jnp.sum(-1 - notes[:, 0]).astype(jnp.float32)
    rounds = jnp.max(-1 - notes[:, 1]) // SLOTS + 1
    all_rows = outer_product(marks, token_blocks.reshape(devices * SLOTS, width))

    def more_rows(state):
        turn, so_far = state
        marks_now, wanted_now = ask(plan, turn, devices, extra)
        return (turn + 1, so_far + fetch(marks_now, wanted_now, table_low, devices))

    all_rows = lax.while_loop(lambda state: state[0] < rounds, more_rows, (1, all_rows))[1]
    token_rows, label_rows = (all_rows[:tokens], all_rows[tokens:])
    pos_local, proj_local = pos_table.shape[0], proj_weight.shape[1]
    if by_rows:
        where = block_plan(devices, chunk, layers, (pos_local, proj_local))
        *matrices, places_all, proj_all = unpack(weights_all, where, layers, length)
    else:
        flat_all = weights_all.reshape(devices, -1)
        split = []
        for index in range(layers):
            wide = flat_all[:, index * flat_local : (index + 1) * flat_local].reshape(WIDE, DS)
            qkv, out, up, down = split_rows(wide, DS, FS)
            split.append(
                (
                    qkv.reshape(DS, 3, DS).transpose(1, 0, 2),
                    out,
                    jnp.pad(up, ((0, 0), (0, WIDER - FS))),
                    jnp.pad(down, ((0, WIDER - FS), (0, 0))),
                )
            )
        matrices = sum(map(list, split), [])
        start = layers * flat_local
        places_all = flat_all[:, start : start + pos_local * DS].reshape(length, DS)
        start += pos_local * DS
        proj_all = flat_all[:, start : start + proj_local * DS].reshape(DT, DS)

    slice_part = lax.optimization_barrier((slice_part, teacher_all))[0]
    slice_table = lax.all_gather(slice_part, "dp", axis=0, tiled=True)

    proj_bias = misc_vec[2 * DS :]
    evec = misc_vec[: 2 * DS].reshape(2, DS)
    cut = 5 * DS
    vectors = jnp.concatenate([layer_vec[:, :cut], layer_vec[:, cut + FS :]], 1).reshape(
        layers, 8, DS
    )
    biases = jnp.pad(layer_vec[:, cut : cut + FS], ((0, 0), (0, WIDER - FS)))[:, None]

    mask = jnp.where(pair_mask, 2.0, jnp.where(allowed, 1.0, 0.0)).reshape(tokens, length)
    embedded, normed_zero, inverse_zero, hidden, *saved = student_forward(
        token_rows, places_all, evec, vectors, biases, mask, matrices
    )
    t_input = teacher_in.reshape(tokens, DT).astype(jnp.float32)
    t_out, t_scores = teacher_forward(
        teacher_in.reshape(tokens, DT), teacher_all, teacher_vec.astype(jnp.float32)[None], mask
    )
    weight = valid_mask.reshape(tokens, 1).astype(jnp.float32)
    loss_zero, proj_zero, bias_zero, back_zero = hidden_term(
        embedded, t_input, proj_all, proj_bias, weight, hidden_denom
    )
    loss_last, proj_last, bias_last, back_last = hidden_term(
        hidden, t_out, proj_all, proj_bias, weight, hidden_denom
    )
    hidden_sum = loss_zero + loss_last
    grad_proj = proj_zero + proj_last

    flat_pick = (
        jnp.arange(rows, dtype=jnp.int32)[:, None] * length + mask_pos.reshape(rows, picks)
    ).reshape(-1)
    pick_marks = (flat_pick[:, None] == lax.broadcasted_iota(jnp.int32, (1, tokens), 1)).astype(
        jnp.bfloat16
    )
    picked = jnp.dot(
        pick_marks, hidden.astype(jnp.bfloat16), preferred_element_type=jnp.float32
    ).astype(jnp.bfloat16)
    t_picked = jnp.dot(
        pick_marks, t_out.astype(jnp.bfloat16), preferred_element_type=jnp.float32
    ).astype(jnp.bfloat16)
    d_picked, own_stats, head_grad, *inbox = head(
        picked, t_picked, slice_table, teacher_head, predict_denom, 4
    )
    own_z = place // (groups // z_size_of(groups))
    own_stats = lax.dynamic_slice_in_dim(own_stats, own_z * rows * picks, rows * picks, 1)
    picked_wide = picked.astype(jnp.float32)
    target_logit = jnp.sum(picked_wide * label_rows, -1)
    predict_sum = (
        jnp.sum(2.0 * own_stats[0] - own_stats[3] - target_logit) / predict_denom
    )
    d_picked = d_picked[:, :width] - label_rows / predict_denom
    d_hidden = pick_exact(pick_marks, d_picked, True) + back_last

    if inbox:
        head_grad = sum_along_x(own_parts_of(head_grad) + inbox[0])
    else:
        head_grad = lax.psum_scatter(head_grad, "dp", scatter_dimension=0, tiled=True)

    matrix_grads = [None] * layers
    vector_grads = [None] * layers
    attention_sum = jnp.float32(0.0)
    head_grad = lax.ppermute(head_grad, BOTH, to_owner)
    for layer_index in reversed(range(layers)):
        d_hidden, *others = student_backward(
            d_hidden,
            vectors[layer_index],
            biases[layer_index],
            mask,
            matrices[4 * layer_index : 4 * layer_index + 4],
            saved[7 * layer_index : 7 * layer_index + 7],
            [t_scores, count.reshape(1, 1)] if layer_index == layers - 1 else [],
        )
        matrix_grads[layer_index] = others[:6]
        d_vectors, d_bias_up, square = others[6], others[7], others[8:]
        d_vectors = d_vectors.reshape(-1)
        vector_grads[layer_index] = jnp.concatenate(
            [d_vectors[:cut], d_bias_up[0, :FS], d_vectors[cut:]]
        )
        if square:
            attention_sum = jnp.sum(square[0]) / count
    d_hidden, head_grad = lax.optimization_barrier((d_hidden, head_grad))
    d_token, d_gain, d_bias = norm_backward(
        d_hidden + back_zero, normed_zero, inverse_zero, misc_vec[:DS]
    )
    grad_places = jnp.sum(d_token.reshape(rows, length, width), 0)

    row_grads = jnp.concatenate([d_token, -picked_wide / predict_denom])
    def more_grads(state):
        turn, so_far = state
        marks_now, wanted_now = ask(plan, turn, devices, extra)
        return (
            turn + 1,
            so_far + give_back(marks_now, wanted_now, row_grads, local_rows, devices),
        )

    grad_small = jnp.concatenate(vector_grads + [d_gain, d_bias, bias_zero + bias_last])
    small_local = -(-grad_small.shape[0] // devices)
    small_local = -(-small_local // DS) * DS
    small_padded = jnp.pad(grad_small, (0, devices * small_local - grad_small.shape[0]))
    rest = [grad_places, grad_proj, small_padded.reshape(-1, DS)]
    sizes = [flat_local] * layers + [part.size // devices for part in rest]
    lines = -(-sum(sizes) // line)
    block = (-(-lines // 8) * 8, line)
    sent = pick_exact(marks, row_grads).reshape(devices, SLOTS, width)
    if by_rows:
        amounts = [size // DS for size in sizes[layers:]]
        grad_parts = sum(matrix_grads, []) + rest
        block_rows_of = block_plan(devices, chunk, layers, amounts)
    else:
        wides = []
        for grads in matrix_grads:
            first = jnp.stack(grads[:3], 1).reshape(-1, width)
            wides.append(jnp.concatenate([first, *grads[3:]]))
        grad_parts = [pack([part.reshape(devices, -1) for part in wides + rest], *block[::-1])]
        block_rows_of = ()
    reduced, row_blocks = reduce(grad_parts, block_rows_of, block, sent, 7)
    g_table = pick_exact(
        wanted_marks(wanted, local_rows), row_blocks.reshape(devices * SLOTS, width), True
    )
    g_table = lax.while_loop(lambda state: state[0] < rounds, more_grads, (1, g_table))[1]
    g_table = g_table + head_grad
    if by_rows:
        pieces = []
        start = 0
        for size in sizes:
            pieces.append(reduced[start : start + size // DS])
            start += size // DS
    else:
        pieces = cut_pieces(reduced.reshape(-1), sizes)
    if by_rows:
        pieces[:layers] = [woven(piece, True) for piece in pieces[:layers]]
    layer_acc = jnp.stack([piece.reshape(-1) for piece in pieces[:layers]])
    g_places = pieces[layers].reshape(pos_local, DS)
    g_proj = pieces[layers + 1].reshape(proj_local, DS).T
    small_part = pieces[layers + 2].reshape(-1)
    squares = (
        jnp.sum(g_table * g_table)
        + jnp.sum(g_places * g_places)
        + jnp.sum(g_proj * g_proj)
        + jnp.sum(layer_acc * layer_acc)
        + jnp.sum(small_part * small_part)
    )
    note = jnp.concatenate(
        [small_part, jnp.stack([attention_sum + hidden_sum + predict_sum, squares])]
    )
    note = jnp.pad(note, (0, -(-note.shape[0] // 128) * 128 - note.shape[0])).reshape(1, -1)
    notes_all = exchange(note, 8, spread=True)[:, 0]
    small = notes_all[:, :small_local].reshape(-1)
    loss = jnp.sum(notes_all[:, small_local])
    norm = jnp.sqrt(jnp.sum(notes_all[:, small_local + 1]))
    g_vec = small[: layer_vec.size].reshape(layer_vec.shape)
    g_misc = small[layer_vec.size : layer_vec.size + misc_vec.shape[0]]
    factor = CLIP_NORM / jnp.maximum(norm, CLIP_NORM)
    return (
        loss,
        count,
        norm,
        *adam_update(emb_table, emb_first, emb_second, g_table * factor),
        *adam_update(pos_table, pos_first, pos_second, g_places * factor),
        *adam_update(layer_flat, layer_first, layer_second, layer_acc * factor),
        *adam_update(proj_weight, proj_first, proj_second, g_proj * factor),
        *adam_update(layer_vec, vec_first, vec_second, g_vec * factor),
        *adam_update(misc_vec, misc_first, misc_second, g_misc * factor),
    )


def solution(mesh):
    rows, lines, flat, tail, every = (
        P(None, BOTH),
        P(BOTH, None),
        P(BOTH),
        P(None, BOTH),
        P(),
    )
    placed = (
        *[rows] * 6,
        flat,
        every,
        P("fsdp", None),
        *[lines] * 6,
        *[tail] * 6,
        *[every] * 6,
    )
    return jax.shard_map(
        local,
        mesh=mesh,
        in_specs=placed,
        out_specs=(*[every] * 3, *[lines] * 6, *[tail] * 6, *[every] * 6),
        check_vma=False,
    )
```

```python
import math
from functools import partial

import jax
import jax.numpy as jnp
from jax import lax
from jax.experimental import pallas as pl
from jax.experimental.pallas import tpu as pltpu
from jax.sharding import PartitionSpec as P

DS = 312
HS = 12
FS = 1200
DT = 768
HT = 12
FT = 3072
STEP = 5


NORM_EPS = 1e-06
CLIP_NORM = 0.05
LEARN_RATE = 0.05
BETA_ONE = 0.9
BETA_TWO = 0.999
ADAM_EPS = 1e-06
WEIGHT_DECAY = 0.01
NEG_LARGE = -1e30

BOTH = ("dp", "fsdp")
MESH = pl.DeviceIdType.MESH
SLOTS = 48
WIDE = 3 * DS + DS + 2 * FS


def z_size_of(fsdp):
    return 4 if fsdp % 4 == 0 else 1


def place_of():
    fsdp = lax.axis_size("fsdp")
    return lax.axis_index("dp") * fsdp + lax.axis_index("fsdp")


def member(index, whole):
    fsdp = lax.axis_size("fsdp")
    if whole:
        return (index // fsdp, index % fsdp)
    return (lax.axis_index("dp"), index)


def greet(count, me, whole):
    barrier = pltpu.get_barrier_semaphore()

    def signal(step, carry):
        pl.semaphore_signal(
            barrier, inc=1, device_id=member((me + step) % count, whole), device_id_type=MESH
        )
        return carry

    lax.fori_loop(1, count, signal, 0)
    pl.semaphore_wait(barrier, count - 1)


def exchange_kernel(count, whole, spread, x_ref, o_ref, send, recv, local_sem):
    me = place_of() if whole else lax.axis_index("fsdp")
    own = pltpu.make_async_copy(x_ref if spread else x_ref.at[me], o_ref.at[me], local_sem)
    own.start()
    greet(count, me, whole)

    def copy(step):
        peer = (me + step) % count
        return pltpu.make_async_remote_copy(
            x_ref if spread else x_ref.at[peer],
            o_ref.at[me],
            send.at[step],
            recv.at[step],
            device_id=member(peer, whole),
            device_id_type=MESH,
        )

    def start(step, carry):
        copy(step).start()
        return carry

    def finish(step, carry):
        copy(step).wait()
        return carry

    lax.fori_loop(1, count, start, 0)
    own.wait()
    lax.fori_loop(1, count, finish, 0)


def exchange(x, number, whole=True, spread=False):
    count = lax.axis_size("fsdp") * (lax.axis_size("dp") if whole else 1)
    return pl.pallas_call(
        partial(exchange_kernel, count, whole, spread),
        out_shape=jax.ShapeDtypeStruct(((count,) if spread else ()) + x.shape, x.dtype),
        in_specs=[pl.BlockSpec(memory_space=pl.ANY)],
        out_specs=pl.BlockSpec(memory_space=pl.ANY),
        scratch_shapes=[
            pltpu.SemaphoreType.DMA((count,)),
            pltpu.SemaphoreType.DMA((count,)),
            pltpu.SemaphoreType.DMA,
        ],
        compiler_params=pltpu.CompilerParams(collective_id=number, has_side_effects=True),
    )(x)


VMEM_SPEC = pl.BlockSpec(memory_space=pltpu.VMEM)


class Grid:
    def __init__(self):
        self.fsdp = lax.axis_size("fsdp")
        self.z_size = z_size_of(self.fsdp)
        self.side = self.fsdp // self.z_size
        assert lax.axis_size("dp") == 2 * self.side
        dp, fsdp = lax.axis_index("dp"), lax.axis_index("fsdp")
        self.x, self.core = dp // 2, dp % 2
        self.z, self.y = fsdp // self.side, fsdp % self.side
        side, z_size = self.side, self.z_size
        self.keys = [(g, b, a) for g in range(side) for b in range(side) for a in range(z_size)]
        self.rank = {key: index for index, key in enumerate(self.keys)}
        self.count = len(self.keys)

    def at(self, third, second, z, other=0):
        core = (self.core + other) % 2
        x = (self.x + third * (1 - core) + second * core) % self.side
        y = (self.y + second * (1 - core) + third * core) % self.side
        return (x * 2 + core, ((self.z + z) % self.z_size) * self.side + y)

    def index(self, third, second, z, other=0):
        dp, fsdp = self.at(third, second, z, other)
        return dp * self.fsdp + fsdp

    def neighbours(self):
        return (
            [(0, 0, a, 0) for a in range(1, self.z_size)]
            + [(0, b, 0, 0) for b in range(1, self.side)]
            + [(g, 0, 0, 0) for g in range(1, self.side)]
            + [(0, 0, 0, 1)]
        )

    def greet(self):
        barrier = pltpu.get_barrier_semaphore()
        around = self.neighbours()
        for where in around:
            pl.semaphore_signal(barrier, inc=1, device_id=self.at(*where), device_id_type=MESH)
        pl.semaphore_wait(barrier, len(around))


class Spread:
    def __init__(self, grid, x_ref, o_ref, send, recv, local_sem):
        self.grid, self.x_ref, self.o_ref = grid, x_ref, o_ref
        self.send, self.recv = send, recv
        self.started = []
        self.own = pltpu.make_async_copy(x_ref, o_ref.at[self.slot((0, 0, 0))], local_sem)
        self.own.start()

    def slot(self, key, other=0):
        grid = self.grid
        third, second, z = key
        return grid.index(grid.side - third, grid.side - second, grid.z_size - z, other)

    def push(self, key, name, where):
        grid = self.grid
        index = grid.rank[name] + (grid.count if where[3] else 0)
        copy = pltpu.make_async_remote_copy(
            self.x_ref if key == (0, 0, 0) else self.o_ref.at[self.slot(key)],
            self.o_ref.at[self.slot(key)],
            self.send.at[index],
            self.recv.at[index],
            device_id=grid.at(*where),
            device_id_type=MESH,
        )
        copy.start()
        self.started.append(copy)

    def forward(self, key):
        grid = self.grid
        third, second, z = key
        if key == (0, 0, 0):
            for step in range(1, grid.z_size):
                self.push(key, (0, 0, step), (0, 0, step, 0))
        if third == 0 and second == 0:
            for step in range(1, grid.side):
                self.push(key, (0, step, z), (0, step, 0, 0))
        if third == 0:
            for step in range(1, grid.side):
                self.push(key, (step, second, z), (step, 0, 0, 0))
        self.push(key, key, (0, 0, 0, 1))

    def arrived(self, key, other=0):
        grid = self.grid
        index = grid.rank[key] + (grid.count if other else 0)
        pltpu.make_async_remote_copy(
            self.o_ref.at[self.slot(key, other)],
            self.o_ref.at[self.slot(key, other)],
            self.send.at[index],
            self.recv.at[index],
            device_id=grid.at(0, 0, 0, 1),
            device_id_type=MESH,
        ).wait_recv()

    def start(self):
        self.forward((0, 0, 0))

    def middle(self):
        for key in self.grid.keys[1:]:
            self.arrived(key)
            self.forward(key)

    def finish(self):
        for key in self.grid.keys:
            self.arrived(key, 1)
        self.own.wait()
        for copy in self.started:
            copy.wait_send()


def entry_kernel(
    ask_ref, w_ref, table_ref, got_ref, all_ref, rows_ref, sent, asks, *sems
):
    ask_send, ask_recv, ask_local, w_send, w_recv, w_local, row_send, row_recv, row_local, out_sem = sems
    grid = Grid()
    count = 2 * grid.count
    me = place_of()
    own = pltpu.make_async_copy(ask_ref.at[me], asks.at[me], ask_local)
    own.start()
    greet(count, me, True)

    def ask_copy(step):
        peer = (me + step) % count
        return pltpu.make_async_remote_copy(
            ask_ref.at[peer],
            asks.at[me],
            ask_send.at[step],
            ask_recv.at[step],
            device_id=member(peer, True),
            device_id_type=MESH,
        )

    def row_copy(step):
        peer = (me + step) % count
        return pltpu.make_async_remote_copy(
            sent.at[peer],
            rows_ref.at[me],
            row_send.at[step],
            row_recv.at[step],
            device_id=member(peer, True),
            device_id_type=MESH,
        )

    def each(first, action):
        def body(step, carry):
            action(step)
            return carry

        lax.fori_loop(first, count, body, 0)

    each(1, lambda step: ask_copy(step).start())
    spread = Spread(grid, w_ref, all_ref, w_send, w_recv, w_local)
    spread.start()
    own.wait()
    table = table_ref[...]
    line = lax.broadcasted_iota(jnp.int32, (table.shape[0], 128), 0)

    def answer(source):
        marks = jnp.where(line == asks[source], 1.0, 0.0).astype(jnp.bfloat16)
        sent[source] = outer_product(marks, table)[:SLOTS].astype(jnp.bfloat16)

    answer(me)
    mine = pltpu.make_async_copy(sent.at[me], rows_ref.at[me], row_local)
    mine.start()

    def serve(step):
        ask_copy(step).wait_recv()
        answer((me + count - step) % count)

    each(1, serve)
    each(1, lambda step: row_copy(step).start())
    keep = pltpu.make_async_copy(asks, got_ref, out_sem)
    keep.start()
    spread.middle()
    spread.finish()
    mine.wait()
    keep.wait()
    each(1, lambda step: row_copy(step).wait())
    each(1, lambda step: ask_copy(step).wait_send())


def entry(asked, weights, table_low, number):
    count = asked.shape[0]
    width = table_low.shape[1]
    anywhere = pl.BlockSpec(memory_space=pl.ANY)
    dma = pltpu.SemaphoreType.DMA
    return pl.pallas_call(
        entry_kernel,
        out_shape=(
            jax.ShapeDtypeStruct(asked.shape, asked.dtype),
            jax.ShapeDtypeStruct((count,) + weights.shape, weights.dtype),
            jax.ShapeDtypeStruct((count, SLOTS, width), table_low.dtype),
        ),
        in_specs=[anywhere, anywhere, pl.BlockSpec(memory_space=pltpu.VMEM)],
        out_specs=(anywhere, VMEM_SPEC, VMEM_SPEC),
        scratch_shapes=[
            pltpu.VMEM((count, SLOTS, width), table_low.dtype),
            pltpu.VMEM(asked.shape, asked.dtype),
            *[dma((count,)), dma((count,)), dma] * 3,
            dma,
        ],
        compiler_params=pltpu.CompilerParams(
            collective_id=number, has_side_effects=True, vmem_limit_bytes=32 * 1024 * 1024
        ),
    )(asked, weights, table_low)


def reduce_kernel(plan, sources, *refs):
    ins, rest = refs[:sources], refs[sources:]
    row_ref, o_ref, got_ref = rest[:3]
    if plan:
        x_ref, rest = rest[3], rest[1:]
    else:
        x_ref = ins[0]
    held, third_in, second_in, z_in, send, recv, row_send, row_recv, row_local = rest[3:]
    grid = Grid()
    side, z_size, count, rank = grid.side, grid.z_size, grid.count, grid.rank
    order = sorted(grid.keys, key=lambda key: (key[0] == 0, key[1] == 0, key[2] == 0))
    devices = 2 * count
    me = place_of()
    own = pltpu.make_async_copy(row_ref.at[me], got_ref.at[me], row_local)
    own.start()
    greet(devices, me, True)

    def row_copy(step):
        peer = (me + step) % devices
        return pltpu.make_async_remote_copy(
            row_ref.at[peer],
            got_ref.at[me],
            row_send.at[step],
            row_recv.at[step],
            device_id=member(peer, True),
            device_id_type=MESH,
        )

    def row_start(step, carry):
        row_copy(step).start()
        return carry

    def row_finish(step, carry):
        row_copy(step).wait()
        return carry

    started = []

    def push(source, target, index, where):
        copy = pltpu.make_async_remote_copy(
            source,
            target,
            send.at[index],
            recv.at[index],
            device_id=grid.at(*where),
            device_id_type=MESH,
        )
        copy.start()
        started.append(copy)

    def arrived(target, index):
        pltpu.make_async_remote_copy(
            target,
            target,
            send.at[index],
            recv.at[index],
            device_id=grid.at(0, 0, 0, 1),
            device_id_type=MESH,
        ).wait_recv()

    for source, at, rows, block, line in plan:
        value = jnp.zeros((rows, x_ref.shape[2]), x_ref.dtype)
        if source >= 0:
            value = ins[source][at : at + rows, :]
        x_ref[block, line : line + rows, :] = value
    for key in order:
        push(x_ref.at[grid.index(*key, 1)], held.at[rank[key]], rank[key], (0, 0, 0, 1))
    from_third = {}
    from_second = {}
    from_z = {}
    index = count
    for step in range(1, side):
        for second in range(side):
            for z in range(z_size):
                from_third[step, second, z] = (
                    third_in.at[((step - 1) * side + second) * z_size + z],
                    index,
                )
                index += 1
    for step in range(1, side):
        for z in range(z_size):
            from_second[step, z] = (second_in.at[(step - 1) * z_size + z], index)
            index += 1
    for way in (1, -1):
        for distance in range(z_size - 1):
            from_z[way, distance] = (z_in.at[len(from_z)], index)
            index += 1

    def gathered(key):
        third, second, z = key
        arrived(held.at[rank[key]], rank[key])
        total = held[rank[key]] + x_ref[grid.index(*key)]
        if third == 0:
            for step in range(1, side):
                arrived(*from_third[step, second, z])
                total = total + from_third[step, second, z][0][...]
        if third == 0 and second == 0:
            for step in range(1, side):
                arrived(*from_second[step, z])
                total = total + from_second[step, z][0][...]
        return total

    for number, key in enumerate(order):
        third, second, z = key
        if third == 0 and second == 0:
            continue
        held[rank[key]] = gathered(key)
        if third:
            target, where = from_third[third, second, z], (third, 0, 0, 0)
        else:
            target, where = from_second[second, z], (0, second, 0, 0)
        push(held.at[rank[key]], target[0], target[1], where)
        if number == 0:
            lax.fori_loop(1, devices, row_start, 0)

    def behind(way):
        return (grid.z > 0) if way > 0 else (grid.z < z_size - 1)

    def hop(way, distance):
        target = from_z[way, distance - 1]
        return pltpu.make_async_remote_copy(
            held.at[rank[0, 0, way * distance % z_size]],
            target[0],
            send.at[target[1]],
            recv.at[target[1]],
            device_id=grid.at(0, 0, way % z_size),
            device_id_type=MESH,
        )

    def reaches(way, distance):
        return (grid.z + way * distance >= 0) & (grid.z + way * distance < z_size)

    for distance in range(z_size - 1, 0, -1):
        for way in (1, -1):

            @pl.when(reaches(way, distance))
            def _(way=way, distance=distance):
                key = (0, 0, way * distance % z_size)
                held[rank[key]] = gathered(key)
                if distance < z_size - 1:

                    @pl.when(behind(way))
                    def _():
                        arrived(*from_z[way, distance])
                        held[rank[key]] += from_z[way, distance][0][...]

                hop(way, distance).start()

    o_ref[...] = gathered((0, 0, 0))
    for way in (1, -1):

        @pl.when(behind(way))
        def _(way=way):
            arrived(*from_z[way, 0])
            o_ref[...] += from_z[way, 0][0][...]

    for distance in range(z_size - 1, 0, -1):
        for way in (1, -1):
            pl.when(reaches(way, distance))(hop(way, distance).wait_send)
    for copy in started:
        copy.wait_send()
    own.wait()
    lax.fori_loop(1, devices, row_finish, 0)


def reduce(parts, plan, block, rows, number):
    count = lax.axis_size("dp") * lax.axis_size("fsdp")
    side = lax.axis_size("dp") // 2
    z_size = count // 2 // side // side
    kind = parts[0].dtype
    vmem, anywhere = pl.BlockSpec(memory_space=pltpu.VMEM), pl.BlockSpec(memory_space=pl.ANY)
    dma = pltpu.SemaphoreType.DMA
    return pl.pallas_call(
        partial(reduce_kernel, plan, len(parts)),
        out_shape=(
            jax.ShapeDtypeStruct(block, kind),
            jax.ShapeDtypeStruct(rows.shape, rows.dtype),
        ),
        in_specs=[vmem] * len(parts) + [anywhere],
        out_specs=(vmem, anywhere),
        scratch_shapes=[
            *([pltpu.VMEM((count,) + block, kind)] if plan else []),
            pltpu.VMEM((count // 2,) + block, kind),
            pltpu.VMEM(((side - 1) * side * z_size,) + block, kind),
            pltpu.VMEM(((side - 1) * z_size,) + block, kind),
            pltpu.VMEM((2 * (z_size - 1),) + block, kind),
            *[dma((count + z_size,))] * 2,
            *[dma((count,))] * 2,
            dma,
        ],
        compiler_params=pltpu.CompilerParams(
            collective_id=number, has_side_effects=True, vmem_limit_bytes=58 * 1024 * 1024
        ),
    )(*parts, rows)


def woven(block, weave):
    chunk = block.shape[0]
    me = place_of()
    made = block
    for index in range(-(-3 * DS // chunk)):
        amount = min(chunk, 3 * DS - index * chunk)
        head = block[:amount].reshape((3, amount // 3, DS) if weave else (amount // 3, 3, DS))
        head = head.transpose(1, 0, 2).reshape(amount, DS)
        if index == 0:
            made = jnp.where(me < 3 * DS // chunk, head, made)
        elif amount < chunk:
            made = jnp.where(me == index, jnp.concatenate([head, block[amount:]]), made)
    return made


def block_plan(devices, chunk, layers, others):
    plan = []
    for block in range(devices):
        for layer in range(layers):
            base = 6 * layer
            row, end, line = block * chunk, (block + 1) * chunk, layer * chunk
            first = row
            if row < 3 * DS:
                stop = min(end, 3 * DS)
                amount = (stop - row) // 3
                for part in range(3):
                    plan.append((base + part, row // 3, amount, block, line + part * amount))
                row = stop
            for part, start, size in ((3, 3 * DS, DS), (4, 4 * DS, FS), (5, 4 * DS + FS, FS)):
                stop = min(end, start + size)
                if row < stop:
                    where = line + row - first
                    plan.append((base + part, row - start, stop - row, block, where))
                    row = stop
        line = layers * chunk
        for index, amount in enumerate(others):
            plan.append((6 * layers + index, block * amount, amount, block, line))
            line += amount
        spare = -line % 8
        if spare:
            plan.append((-1, 0, spare, block, line))
    return tuple(plan)


def pack(parts, width, rows):
    count = parts[0].shape[0]
    if all(part.ndim == 3 for part in parts):
        joined = jnp.concatenate(parts, 1)
        return jnp.pad(joined, ((0, 0), (0, rows - joined.shape[1]), (0, 0)))
    joined = jnp.concatenate([part.reshape(count, -1) for part in parts], 1)
    joined = jnp.pad(joined, ((0, 0), (0, rows * width - joined.shape[1])))
    return joined.reshape(count, rows, width)


def outer_product(left, right):
    return lax.dot_general(
        left, right, (((0,), (0,)), ((), ())), preferred_element_type=jnp.float32
    )


def back_product(grad, weight):
    return lax.dot_general(
        grad, weight, (((1,), (1,)), ((), ())), preferred_element_type=jnp.float32
    )


def norm_forward(value, gain, bias):
    average = jnp.mean(value, -1, keepdims=True)
    centered = value - average
    inverse = lax.rsqrt(jnp.mean(centered * centered, -1, keepdims=True) + NORM_EPS)
    normed = centered * inverse
    return (normed * gain + bias, normed, inverse)


def cut_pieces(vector, sizes):
    pieces = []
    start = 0
    for amount in sizes:
        pieces.append(vector[..., start : start + amount])
        start += amount
    return pieces


def split_rows(wide, width, hidden):
    first, second, third = 3 * width, 4 * width, 4 * width + hidden
    return (
        wide[:first].reshape(width, 3 * width),
        wide[first:second],
        wide[second:third].reshape(width, hidden),
        wide[third:],
    )


def adam_update(value, first, second, grad):
    first = BETA_ONE * first + (1.0 - BETA_ONE) * grad
    second = BETA_TWO * second + (1.0 - BETA_TWO) * grad * grad
    ratio = first / (1.0 - BETA_ONE**STEP) / (jnp.sqrt(second / (1.0 - BETA_TWO**STEP)) + ADAM_EPS)
    return (first, second, value - LEARN_RATE * (ratio + WEIGHT_DECAY * value))


def gelu(value):
    return 0.5 * value * (1.0 + jnp.tanh(0.7978845608028654 * (value + 0.044715 * value * value * value)))


def regroup(weights, group):
    amount = weights.shape[0]
    made = lax.broadcasted_iota(jnp.int32, (amount, amount), 0)
    taken = lax.broadcasted_iota(jnp.int32, (amount, amount), 1)
    inner = amount // group
    marks = jnp.where((made % inner) * group + made // inner == taken, 1.0, 0.0)
    return jnp.dot(
        marks.astype(jnp.bfloat16), weights, preferred_element_type=jnp.float32
    ).astype(jnp.bfloat16)


def softmax_low(scores, mask):
    masked = jnp.where(mask > 0.0, scores, NEG_LARGE)
    expo = jnp.exp(masked - jnp.max(masked, -1, keepdims=True))
    return (expo * (1.0 / jnp.sum(expo, -1, keepdims=True))).astype(jnp.bfloat16)


TILE = 256
CHUNK = 96


def teacher_kernel(
    denom, x_ref, w_ref, vec_ref, mask_ref, zero_ref, last_ref, proj_ref, bias_ref, weight_ref, pick_ref,
    s_ref, back_zero, back_last, proj_out, bias_out, loss_ref, picked_ref, t_picked_ref,
    low_ref, qkv_ref, up_ref, context_ref,
):
    size = DT // HT
    for ref in (proj_out, bias_out, loss_ref):
        ref[...] = jnp.zeros_like(ref)
    for index in range(3 * DT // CHUNK):
        made = regroup(w_ref[index], 3)
        for part in range(3):
            rows = CHUNK // 3
            qkv_ref[part, index * rows : (index + 1) * rows, :] = made[part * rows : (part + 1) * rows]
    first_up, first_down = 4 * DT // CHUNK, (4 * DT + FT) // CHUNK
    many = FT // DT
    for index in range(FT // CHUNK // 2):
        at = first_up + 2 * index
        made = regroup(w_ref[at : at + 2].reshape(2 * CHUNK, DT), many)
        rows = 2 * CHUNK // many
        for part in range(many):
            up_ref[part, index * rows : (index + 1) * rows, :] = made[part * rows : (part + 1) * rows]
    line = lax.broadcasted_iota(jnp.int32, (1, 2 * size), 1)
    low_half = line < size
    length = mask_ref.shape[1]

    def vector(index, amount=1):
        return vec_ref[:, index * DT : (index + amount) * DT]

    def tile(step, carry):
        at = pl.ds(pl.multiple_of(step * TILE, TILE), TILE)
        x_low = x_ref[at, :]
        q, k, v = (
            (
                jnp.dot(x_low, qkv_ref[part], preferred_element_type=jnp.float32) + vector(part)
            ).astype(jnp.bfloat16)
            for part in range(3)
        )
        nothing = jnp.zeros((length, 2 * size), jnp.bfloat16)
        for row in range(TILE // length):
            span = slice(row * length, (row + 1) * length)
            here = pl.ds(pl.multiple_of(step * TILE + row * length, length), length)
            mask = mask_ref[here, :]
            for pair in range(HT // 2):
                lanes = slice(pair * 2 * size, (pair + 1) * 2 * size)
                k_pair, v_pair = k[span, lanes], v[span, lanes]
                k_both = jnp.concatenate(
                    [jnp.where(low_half, k_pair, nothing), jnp.where(low_half, nothing, k_pair)]
                )
                v_both = jnp.concatenate(
                    [jnp.where(low_half, v_pair, nothing), jnp.where(low_half, nothing, v_pair)]
                )
                scores = back_product(q[span, lanes], k_both) * size ** (-0.5)
                s_ref[here, pair * 2 * length : (pair + 1) * 2 * length] = scores
                weights = jnp.concatenate(
                    [softmax_low(scores[:, :length], mask), softmax_low(scores[:, length:], mask)], 1
                )
                context_ref[span, lanes] = jnp.dot(
                    weights, v_both, preferred_element_type=jnp.float32
                ).astype(jnp.bfloat16)
        w_out = w_ref[3 * DT // CHUNK : first_up].reshape(DT, DT)
        attended = jnp.dot(context_ref[...], w_out, preferred_element_type=jnp.float32) + vector(3)
        middle = norm_forward(x_low.astype(jnp.float32) + attended, vector(4), vector(5))[0]
        middle_low = middle.astype(jnp.bfloat16)
        outer = jnp.zeros((TILE, DT), jnp.float32)
        for part in range(many):
            inner = jnp.dot(middle_low, up_ref[part], preferred_element_type=jnp.float32) + vector(
                6 + part
            )
            begin = first_down + part * (DT // CHUNK)
            w_down = w_ref[begin : begin + DT // CHUNK].reshape(DT, DT)
            outer = outer + jnp.dot(
                gelu(inner).astype(jnp.bfloat16), w_down, preferred_element_type=jnp.float32
            )
        made = norm_forward(
            middle + outer + vector(6 + many), vector(7 + many), vector(8 + many)
        )[0]
        low_ref[at, :] = made.astype(jnp.bfloat16)
        pairs = ((zero_ref, x_low.astype(jnp.float32), back_zero), (last_ref, made, back_last))
        for source_ref, target, back_ref in pairs:
            source = source_ref[at, :].astype(jnp.bfloat16)
            spread = back_product(source, proj_ref[...]) + bias_ref[...] - target
            weighted = spread * weight_ref[at, :]
            loss_ref[...] += jnp.sum(weighted * spread, 0, keepdims=True)
            d_mapped = (weighted * (2.0 / denom)).astype(jnp.bfloat16)
            back_ref[at, :] = jnp.dot(d_mapped, proj_ref[...], preferred_element_type=jnp.float32)
            proj_out[...] += outer_product(d_mapped, source)
            bias_out[...] += jnp.sum(d_mapped.astype(jnp.float32), 0, keepdims=True)
        return carry

    tokens = x_ref.shape[0]
    lax.fori_loop(0, tokens // TILE, tile, 0)
    line = lax.broadcasted_iota(jnp.int32, (pick_ref.shape[0], tokens), 1)
    marks = jnp.where(pick_ref[...] == line, 1.0, 0.0).astype(jnp.bfloat16)
    picked_ref[...] = jnp.dot(
        marks, last_ref[...].astype(jnp.bfloat16), preferred_element_type=jnp.float32
    ).astype(jnp.bfloat16)
    t_picked_ref[...] = jnp.dot(
        marks, low_ref[...], preferred_element_type=jnp.float32
    ).astype(jnp.bfloat16)


def teacher_forward(x_low, blocks, vectors, mask, embedded, last, proj, bias, weight, picks, denom):
    tokens, length = mask.shape
    full = partial(jax.ShapeDtypeStruct, dtype=jnp.float32)
    low = partial(jax.ShapeDtypeStruct, dtype=jnp.bfloat16)
    amount = picks.shape[0]
    made = (
        full((tokens, HT * length)),
        full((tokens, DS)),
        full((tokens, DS)),
        full((DT, DS)),
        full((1, DT)),
        full((1, DT)),
        low((amount, DS)),
        low((amount, DT)),
    )
    given = (x_low, blocks, vectors, mask, embedded, last, proj, bias, weight, picks)
    return pl.pallas_call(
        partial(teacher_kernel, denom),
        out_shape=made,
        in_specs=[VMEM_SPEC] * len(given),
        out_specs=(VMEM_SPEC,) * len(made),
        scratch_shapes=[
            pltpu.VMEM((tokens, DT), jnp.bfloat16),
            pltpu.VMEM((3, DT, DT), jnp.bfloat16),
            pltpu.VMEM((FT // DT, DT, DT), jnp.bfloat16),
            pltpu.VMEM((TILE, DT), jnp.bfloat16),
        ],
        compiler_params=pltpu.CompilerParams(vmem_limit_bytes=58 * 1024 * 1024),
        cost_estimate=pl.CostEstimate(
            flops=20 * 10**9, bytes_accessed=25 * 10**6, transcendentals=5 * 10**6
        ),
    )(*given)


WIDER = -(-FS // 128) * 128


def refold(source, target, source_width, target_width):
    period = math.lcm(source_width, target_width)
    groups = source.shape[1] * source_width // period
    step_in, step_out = period // source_width, period // target_width
    lane = lax.broadcasted_iota(jnp.int32, (groups, 128), 1)
    for row in range(step_out):
        for tile in range(-(-target_width // 128)):
            begin = row * target_width + 128 * tile
            amount = min(128, target_width - 128 * tile)
            made, at = jnp.zeros((groups, 128), source.dtype), 0
            while at < amount:
                line, column = divmod(begin + at, source_width)
                where, lanes = divmod(column, 128)
                piece = source[where, pl.ds(line, groups, stride=step_in), :]
                if (at - lanes) % 128:
                    piece = pltpu.roll(piece, (at - lanes) % 128, 1)
                length = min(128 - lanes, source_width - column, amount - at)
                made = jnp.where((lane >= at) & (lane < at + length), piece, made)
                at += length
            target[tile, pl.ds(row, groups, stride=step_out), :] = made


def unpack_kernel(plan, layers, w_ref, *refs):
    place_ref, proj_ref, square, wide, folded, unfolded, small = refs[4 * layers :]
    for layer in range(layers):
        qkv_ref, out_ref, up_ref, down_ref = refs[4 * layer : 4 * layer + 4]
        for matrix, at, rows, block, line in plan:
            part = matrix - 6 * layer
            if not 0 <= part < 6:
                continue
            value = w_ref[block].astype(jnp.float32)[line : line + rows]
            if part < 4:
                square[part, at : at + rows, :] = value
            elif part == 4:
                for tile in range(-(-DS // 128)):
                    lanes = min(128, DS - 128 * tile)
                    folded[tile, at : at + rows, :lanes] = value[:, 128 * tile : 128 * tile + lanes]
            else:
                wide[at : at + rows, :] = value
        for part in range(3):
            qkv_ref[part] = square[part].astype(jnp.bfloat16)
        out_ref[...] = square[3].astype(jnp.bfloat16)
        refold(folded, unfolded, DS, FS)
        for tile in range(WIDER // 128):
            up_ref[:, 128 * tile : 128 * tile + 128] = unfolded[tile].astype(jnp.bfloat16)
        down_ref[:FS, :] = wide[...].astype(jnp.bfloat16)
        down_ref[FS:, :] = jnp.zeros((WIDER - FS, DS), jnp.bfloat16)
    for matrix, at, rows, block, line in plan:
        if matrix >= 6 * layers:
            value = w_ref[block].astype(jnp.float32)[line : line + rows]
            small[matrix - 6 * layers, at : at + rows, :] = value
    place_ref[...] = small[0, : place_ref.shape[0]].astype(jnp.bfloat16)
    proj_ref[...] = small[1].astype(jnp.bfloat16)


def unpack(blocks, plan, layers, length):
    low = partial(jax.ShapeDtypeStruct, dtype=jnp.bfloat16)
    full = jnp.float32
    return pl.pallas_call(
        partial(unpack_kernel, plan, layers),
        out_shape=(
            *[low((3, DS, DS)), low((DS, DS)), low((DS, WIDER)), low((WIDER, DS))] * layers,
            low((length, DS)),
            low((DT, DS)),
        ),
        in_specs=[VMEM_SPEC],
        out_specs=(VMEM_SPEC,) * (4 * layers + 2),
        scratch_shapes=[
            pltpu.VMEM((4, DS, DS), full),
            pltpu.VMEM((FS, DS), full),
            pltpu.VMEM((-(-DS // 128), FS, 128), full),
            pltpu.VMEM((WIDER // 128, DS, 128), full),
            pltpu.VMEM((2, DT, DS), full),
        ],
        compiler_params=pltpu.CompilerParams(vmem_limit_bytes=50 * 1024 * 1024),
        cost_estimate=pl.CostEstimate(flops=0, bytes_accessed=20 * 10**6, transcendentals=0),
    )(blocks)


def by_heads(value, heads):
    width = value.shape[1]
    size = width // heads
    lane = lax.broadcasted_iota(jnp.int32, (1, width), 1)
    nothing = jnp.zeros_like(value)
    return jnp.concatenate(
        [
            jnp.where((lane >= head * size) & (lane < (head + 1) * size), value, nothing)
            for head in range(heads)
        ]
    )


def student_kernel(
    layers, token_ref, place_ref, evec_ref, vec_ref, bias_ref, mask_ref,
    *refs,
):
    matrices, refs = refs[: 4 * layers], refs[4 * layers :]
    emb_ref, zero_ref, zero_inv, last_ref = refs[:4]
    length = mask_ref.shape[1]
    size = DS // HS

    def tile(step, carry):
        at = pl.ds(pl.multiple_of(step * TILE, TILE), TILE)
        places = jnp.concatenate([place_ref[...].astype(jnp.float32)] * (TILE // length))
        hidden, normed, inverse = norm_forward(
            token_ref[at, :] + places, evec_ref[0:1, :], evec_ref[1:2, :]
        )
        emb_ref[at, :] = hidden
        zero_ref[at, :] = normed
        zero_inv[at, :] = inverse
        for layer in range(layers):
            qkv_w, out_w, up_w, down_w = matrices[4 * layer : 4 * layer + 4]
            low_ref, qkv_ref, context_ref, one_ref, one_inv, two_ref, two_inv = refs[
                4 + 7 * layer : 11 + 7 * layer
            ]

            def vector(index, layer=layer):
                return vec_ref[layer, index : index + 1, :]

            low = hidden.astype(jnp.bfloat16)
            low_ref[at, :] = low
            parts = []
            for part in range(3):
                made = jnp.dot(low, qkv_w[part], preferred_element_type=jnp.float32)
                if part != 1:
                    made = made + vector(part // 2)
                parts.append(made.astype(jnp.bfloat16))
                qkv_ref[part, at, :] = parts[part]
            contexts = []
            for row in range(TILE // length):
                span = slice(row * length, (row + 1) * length)
                here = pl.ds(pl.multiple_of(step * TILE + row * length, length), length)
                mask = mask_ref[here, :]
                q, k, v = (part[span] for part in parts)
                scores = back_product(q, by_heads(k, HS)) * size ** (-0.5)
                weights = jnp.concatenate(
                    [
                        softmax_low(scores[:, head * length : (head + 1) * length], mask)
                        for head in range(HS)
                    ],
                    1,
                )
                contexts.append(
                    jnp.dot(weights, by_heads(v, HS), preferred_element_type=jnp.float32)
                )
            context = jnp.concatenate(contexts).astype(jnp.bfloat16)
            context_ref[at, :] = context
            attended = jnp.dot(context, out_w[...], preferred_element_type=jnp.float32) + vector(2)
            middle, normed, inverse = norm_forward(hidden + attended, vector(3), vector(4))
            one_ref[at, :] = normed
            one_inv[at, :] = inverse
            inner = jnp.dot(
                middle.astype(jnp.bfloat16), up_w[...], preferred_element_type=jnp.float32
            ) + bias_ref[layer]
            outer = jnp.dot(
                gelu(inner).astype(jnp.bfloat16), down_w[...], preferred_element_type=jnp.float32
            ) + vector(5)
            hidden, normed, inverse = norm_forward(middle + outer, vector(6), vector(7))
            two_ref[at, :] = normed
            two_inv[at, :] = inverse
        last_ref[at, :] = hidden
        return carry

    lax.fori_loop(0, token_ref.shape[0] // TILE, tile, 0)


def student_forward(token_rows, places, evec, vectors, biases, mask, matrices):
    tokens = token_rows.shape[0]
    layers = vectors.shape[0]
    full = partial(jax.ShapeDtypeStruct, dtype=jnp.float32)
    low = partial(jax.ShapeDtypeStruct, dtype=jnp.bfloat16)
    made = (
        full((tokens, DS)),
        full((tokens, DS)),
        full((tokens, 1)),
        full((tokens, DS)),
        *[
            low((tokens, DS)),
            low((3, tokens, DS)),
            low((tokens, DS)),
            full((tokens, DS)),
            full((tokens, 1)),
            full((tokens, DS)),
            full((tokens, 1)),
        ]
        * layers,
    )
    return pl.pallas_call(
        partial(student_kernel, layers),
        out_shape=made,
        in_specs=[VMEM_SPEC] * (6 + len(matrices)),
        out_specs=(VMEM_SPEC,) * len(made),
        compiler_params=pltpu.CompilerParams(vmem_limit_bytes=58 * 1024 * 1024),
        cost_estimate=pl.CostEstimate(
            flops=8 * 10**9, bytes_accessed=40 * 10**6, transcendentals=6 * 10**6
        ),
    )(token_rows, places, evec, vectors, biases, mask, *matrices)


def back_kernel(
    last, first_layer, grad_ref, vec_ref, bias_ref, mask_ref, qkv_w, out_w, up_w, down_w,
    low_ref, qkv_ref, context_ref, one_ref, one_inv, two_ref, two_inv, *refs,
):
    if first_layer:
        (more_ref, zero_ref, zero_inv, evec_ref), refs = refs[:4], refs[4:]
    if last:
        score_ref, count_ref, refs = refs[0], refs[1], refs[2:]
    hidden_ref, *weight_refs, vec_out, bias_out, refs = (*refs[:9], refs[9:])
    dq_ref, dk_ref, dv_ref, do_ref, du_ref, dd_ref = weight_refs
    if last:
        loss_ref, refs = refs[0], refs[1:]
        loss_ref[...] = jnp.zeros_like(loss_ref)
    if first_layer:
        (place_ref, edge_ref), refs = refs[:2], refs[2:]
        place_ref[...] = jnp.zeros_like(place_ref)
        edge_ref[...] = jnp.zeros_like(edge_ref)
    outer_s, attended_s, q_s, k_s, v_s, middle_s, active_s, inner_s, unfolded, folded = refs
    length = mask_ref.shape[1]
    size = DS // HS
    vec_out[...] = jnp.zeros_like(vec_out)
    bias_out[...] = jnp.zeros_like(bias_out)
    many = 256

    def vector(index):
        return vec_ref[index : index + 1, :]

    def note(index, value, to=vec_out):
        to[index : index + 1, :] += jnp.sum(value.astype(jnp.float32), 0, keepdims=True)

    def norm_back(grad, normed, inverse, gain, index, to=vec_out):
        d_normed = grad * gain
        note(index, grad * normed, to)
        note(index + 1, grad, to)
        return inverse * (
            d_normed
            - jnp.mean(d_normed, -1, keepdims=True)
            - normed * jnp.mean(d_normed * normed, -1, keepdims=True)
        )

    def tile(step, carry):
        at = pl.ds(pl.multiple_of(step * TILE, TILE), TILE)
        d_sum = norm_back(grad_ref[at, :], two_ref[at, :], two_inv[at, :], vector(6), 6)
        d_outer = d_sum.astype(jnp.bfloat16)
        outer_s[at, :] = d_outer
        note(5, d_outer)
        middle = (one_ref[at, :] * vector(3) + vector(4)).astype(jnp.bfloat16)
        middle_s[at, :] = middle
        d_middle = d_sum
        for first in range(0, WIDER, many):
            lanes = slice(first, first + many)
            inner = jnp.dot(
                middle, up_w[:, lanes], preferred_element_type=jnp.float32
            ) + bias_ref[:, lanes]
            squared = inner * inner
            bent = jnp.tanh(0.7978845608028654 * (inner + 0.044715 * squared * inner))
            active_s[at, lanes] = (0.5 * inner * (1.0 + bent)).astype(jnp.bfloat16)
            slope = 0.5 * (1.0 + bent) + 0.5 * inner * (1.0 - bent * bent) * (
                0.7978845608028654 * (1.0 + 3.0 * 0.044715 * squared)
            )
            d_inner = (back_product(d_outer, down_w[lanes, :]) * slope).astype(jnp.bfloat16)
            inner_s[at, lanes] = d_inner
            bias_out[:, lanes] += jnp.sum(d_inner.astype(jnp.float32), 0, keepdims=True)
            d_middle = d_middle + back_product(d_inner, up_w[:, lanes])
        d_one = norm_back(d_middle, one_ref[at, :], one_inv[at, :], vector(3), 3)
        d_attended = d_one.astype(jnp.bfloat16)
        attended_s[at, :] = d_attended
        note(2, d_attended)
        d_context = back_product(d_attended, out_w[...]).astype(jnp.bfloat16)
        for row in range(TILE // length):
            here = pl.ds(pl.multiple_of(step * TILE + row * length, length), length)
            mask = mask_ref[here, :]
            d_row = d_context[row * length : (row + 1) * length]
            q, k, v = (qkv_ref[part, here, :] for part in range(3))
            keys = by_heads(k, HS)
            scores = back_product(q, keys) * size ** (-0.5)
            d_weights = back_product(d_row, by_heads(v, HS))
            low_weights, d_scores = [], []
            for head in range(HS):
                lanes = slice(head * length, (head + 1) * length)
                masked = jnp.where(mask > 0.0, scores[:, lanes], NEG_LARGE)
                expo = jnp.exp(masked - jnp.max(masked, -1, keepdims=True))
                weights = expo * (1.0 / jnp.sum(expo, -1, keepdims=True))
                low_weights.append(weights.astype(jnp.bfloat16))
                turned = weights * d_weights[:, lanes]
                made = turned - weights * jnp.sum(turned, -1, keepdims=True)
                if last:
                    differ = jnp.where(mask > 1.0, scores[:, lanes] - score_ref[here, lanes], 0.0)
                    loss_ref[...] += jnp.sum(differ * differ, 0, keepdims=True)
                    made = made + differ * (2.0 / count_ref[...])
                d_scores.append(made.astype(jnp.bfloat16))
            scale = size ** (-0.5)
            q_s[here, :] = (
                jnp.dot(jnp.concatenate(d_scores, 1), keys, preferred_element_type=jnp.float32)
                * scale
            ).astype(jnp.bfloat16)
            k_s[here, :] = (
                outer_product(jnp.concatenate(d_scores), by_heads(q, HS)) * scale
            ).astype(jnp.bfloat16)
            v_s[here, :] = outer_product(
                jnp.concatenate(low_weights), by_heads(d_row, HS)
            ).astype(jnp.bfloat16)
        d_hidden = d_one
        for part, held in enumerate((q_s, k_s, v_s)):
            d_part = held[at, :]
            if part != 1:
                note(part // 2, d_part)
            d_hidden = d_hidden + back_product(d_part, qkv_w[part])
        if first_layer:
            d_hidden = norm_back(
                d_hidden + more_ref[at, :],
                zero_ref[at, :],
                zero_inv[at, :],
                evec_ref[0:1, :],
                0,
                edge_ref,
            )
            for row in range(TILE // length):
                place_ref[...] += d_hidden[row * length : (row + 1) * length]
        hidden_ref[at, :] = d_hidden
        return carry

    lax.fori_loop(0, grad_ref.shape[0] // TILE, tile, 0)
    low = low_ref[...]
    dq_ref[...] = outer_product(low, q_s[...])
    dk_ref[...] = outer_product(low, k_s[...])
    dv_ref[...] = outer_product(low, v_s[...])
    do_ref[...] = outer_product(context_ref[...], attended_s[...])
    for first in range(0, WIDER, many):
        lanes = slice(first, first + many)
        stop = min(first + many, FS)
        dd_ref[first:stop, :] = outer_product(active_s[:, lanes], outer_s[...])[: stop - first]
        made = outer_product(middle_s[...], inner_s[:, lanes])
        for tile_at in range(many // 128):
            unfolded[first // 128 + tile_at] = made[:, 128 * tile_at : 128 * tile_at + 128]
    refold(unfolded, folded, FS, DS)
    for tile_at in range(-(-DS // 128)):
        lanes = min(128, DS - 128 * tile_at)
        du_ref[:, 128 * tile_at : 128 * tile_at + lanes] = folded[tile_at, :, :lanes]


def student_backward(grad, vectors, biases, mask, matrices, saved, last, first_layer):
    tokens, length = mask.shape
    full = partial(jax.ShapeDtypeStruct, dtype=jnp.float32)
    made = [
        full((tokens, DS)),
        *[full((DS, DS))] * 4,
        full((FS, DS)),
        full((FS, DS)),
        full((8, DS)),
        full((1, WIDER)),
    ]
    given = [grad, vectors, biases, mask, *matrices, *saved]
    given += first_layer
    if last:
        given += last
        made.append(full((1, length)))
    if first_layer:
        made += [full((length, DS)), full((8, DS))]
    low = partial(pltpu.VMEM, dtype=jnp.bfloat16)
    return pl.pallas_call(
        partial(back_kernel, bool(last), bool(first_layer)),
        out_shape=tuple(made),
        in_specs=[VMEM_SPEC] * len(given),
        out_specs=(VMEM_SPEC,) * len(made),
        scratch_shapes=[
            *[low((tokens, DS))] * 6,
            *[low((tokens, WIDER))] * 2,
            pltpu.VMEM((WIDER // 128, DS, 128), jnp.float32),
            pltpu.VMEM((-(-DS // 128), FS, 128), jnp.float32),
        ],
        compiler_params=pltpu.CompilerParams(vmem_limit_bytes=58 * 1024 * 1024),
        cost_estimate=pl.CostEstimate(
            flops=10**9, bytes_accessed=4 * 10**6, transcendentals=3 * 10**5
        ),
    )(*given)


def d_all_width(width):
    return -(-width // 128) * 128


def head_kernel(
    groups, pair, denom, p_ref, t_ref, table_ref, head_ref, d_ref, own_ref, w_ref, *refs
):
    (
        p_all, t_all, p_turned, t_turned, s_logits, t_logits, stats, rows_of, inbox, total,
        send, recv, stat_send, stat_recv, d_send, d_recv, pair_send, pair_recv, out_sem,
    ) = refs
    amount, width = p_ref.shape
    vocab = table_ref.shape[0]
    z_size = z_size_of(groups)
    side = groups // z_size
    across = z_size * amount
    half = d_all_width(width)
    dp, me = lax.axis_index("dp"), lax.axis_index("fsdp")
    z, y = me // side, me % side
    sibling = (dp // 2 * 2 + 1 - dp % 2, me)
    beside = ((dp + 2) % lax.axis_size("dp"), me)
    barrier = pltpu.get_barrier_semaphore()
    for step in range(1, groups):
        pl.semaphore_signal(
            barrier, inc=1, device_id=(dp, (me + step) % groups), device_id_type=MESH
        )
    if pair:
        for other in (sibling, beside):
            pl.semaphore_signal(barrier, inc=1, device_id=other, device_id_type=MESH)
    pl.semaphore_wait(barrier, groups - 1 + (2 if pair else 0))

    def both(at, rank, target, own=False):
        return [
            pltpu.make_async_remote_copy(
                given if own else held.at[at],
                held.at[at],
                send.at[2 * rank + index],
                recv.at[2 * rank + index],
                device_id=(dp, target),
                device_id_type=MESH,
            )
            for index, (given, held) in enumerate(((p_ref, p_all), (t_ref, t_all)))
        ]

    def begin(copies):
        for copy in copies:
            copy.start()

    def received(copies):
        for copy in copies:
            copy.wait_recv()

    def sent(copies):
        for copy in copies:
            copy.wait_send()

    def line(step):
        return z + step, (z + step >= 0) & (z + step < z_size)

    def inside(position):
        return jnp.minimum(jnp.maximum(position, 0), z_size - 1) * side

    def z_copies(step, way, arriving):
        origin, known = line(-way * (step + (1 if arriving else 0)))
        target, there = line(way)
        rank = 2 * step + (1 if way > 0 else 0)
        made = both(inside(origin) + y, rank, inside(target) + y, own=step == 0 and not arriving)
        return made, known if arriving else known & there

    def y_copies(back, step, at, own=False):
        return both(
            at, 2 * z_size + (back - 1) * z_size + step, z * side + (y + back) % side, own
        )

    wide = next(size for size in (384, 320, 128) if vocab % size == 0)

    def measure(back):
        at_y = (y + side - back) % side
        slots = [line * side + at_y for line in range(z_size)]
        t_turned[...] = jnp.concatenate([t_all[at] for at in slots]).astype(jnp.float32).T.astype(
            jnp.bfloat16
        )
        p_turned[...] = jnp.concatenate([p_all[at] for at in slots]).astype(jnp.float32).T.astype(
            jnp.bfloat16
        )

        def step(index, carry):
            s_top, s_sum, t_top, t_sum, cross = carry
            lines = pl.ds(pl.multiple_of(index * wide, 64), wide)
            t_now = jnp.dot(head_ref[lines, :], t_turned[...], preferred_element_type=jnp.float32)
            s_now = jnp.dot(table_ref[lines, :], p_turned[...], preferred_element_type=jnp.float32)
            t_logits[back, lines, :] = t_now
            s_logits[back, lines, :] = s_now
            s_next = jnp.maximum(s_top, jnp.max(s_now, 0, keepdims=True))
            t_next = jnp.maximum(t_top, jnp.max(t_now, 0, keepdims=True))
            t_exp = jnp.exp(t_now - t_next)
            scale = jnp.exp(t_top - t_next)
            s_sum = s_sum * jnp.exp(s_top - s_next) + jnp.sum(
                jnp.exp(s_now - s_next), 0, keepdims=True
            )
            t_sum = t_sum * scale + jnp.sum(t_exp, 0, keepdims=True)
            cross = cross * scale + jnp.sum(t_exp * s_now, 0, keepdims=True)
            return (s_next, s_sum, t_next, t_sum, cross)

        lowest = jnp.full((1, across), -jnp.inf, jnp.float32)
        zero = jnp.zeros((1, across), jnp.float32)
        made = lax.fori_loop(0, vocab // wide, step, (lowest, zero, lowest, zero, zero))
        for index, value in enumerate(made):
            stats[me, at_y, index : index + 1, :] = value

    p_all[me] = p_ref[...]
    t_all[me] = t_ref[...]
    for way in (1, -1):
        made, wanted = z_copies(0, way, False)
        pl.when(wanted)(partial(begin, made))
    for back in range(1, side):
        begin(y_copies(back, z, me, own=True))
    for step in range(z_size - 1):
        for way in (1, -1):
            made, wanted = z_copies(step, way, True)
            onward, further = z_copies(step + 1, way, False) if step + 2 < z_size else (None, None)

            @pl.when(wanted)
            def _(made=made, onward=onward, further=further, step=step, way=way):
                received(made)
                if onward is not None:
                    pl.when(further)(partial(begin, onward))
                origin = z - way * (step + 1)
                for back in range(1, side):
                    begin(y_copies(back, origin, origin * side + y))

    for back in range(side):
        if back:
            for step in range(z_size):
                received(y_copies(back, step, step * side + (y + side - back) % side))
        measure(back)
    for step in range(z_size - 1):
        for way in (1, -1):
            made, wanted = z_copies(step, way, False)
            pl.when(wanted)(partial(sent, made))
    for back in range(1, side):
        for step in range(z_size):
            sent(y_copies(back, step, step * side + y))

    def stat_copy(step):
        return pltpu.make_async_remote_copy(
            stats.at[me],
            stats.at[me],
            stat_send.at[step],
            stat_recv.at[step],
            device_id=(dp, (me + step) % groups),
            device_id_type=MESH,
        )

    for step in range(1, groups):
        stat_copy(step).start()
    for step in range(1, groups):
        stat_copy(step).wait_recv()
    for back in range(side):
        at_y = (y + side - back) % side
        parts = [stats[other, at_y] for other in range(groups)]
        s_top, t_top = parts[0][0:1], parts[0][2:3]
        for part in parts[1:]:
            s_top = jnp.maximum(s_top, part[0:1])
            t_top = jnp.maximum(t_top, part[2:3])
        s_sum, t_sum, cross = (jnp.zeros_like(s_top) for unused in range(3))
        for part in parts:
            s_sum = s_sum + part[1:2] * jnp.exp(part[0:1] - s_top)
            scale = jnp.exp(part[2:3] - t_top)
            t_sum = t_sum + part[3:4] * scale
            cross = cross + part[4:5] * scale
        rows_of[back, 0:1, :] = s_top + jnp.log(s_sum)
        rows_of[back, 1:2, :] = t_top
        rows_of[back, 2:3, :] = 1.0 / t_sum
        rows_of[back, 3:4, :] = cross / t_sum
        total[back] = jnp.zeros((half, across), jnp.float32)
    own_ref[...] = rows_of[0]
    narrow = next(size for size in (320, 128) if vocab % size == 0)
    part = vocab // 4 if pair else vocab

    def rows_at(start, amount):
        return t_logits.at[0, pl.ds(pl.multiple_of(start, 64), amount), 0:half]

    def grade(first):
        def chunk(index, carry):
            lines = pl.ds(pl.multiple_of(first + index * narrow, 64), narrow)
            table = table_ref[lines, :]
            made = jnp.zeros((narrow, width), jnp.float32)
            for back in range(side):
                row = rows_of[back]
                grads = 2.0 * jnp.exp(s_logits[back, lines, :] - row[0:1])
                grads = grads - jnp.exp(t_logits[back, lines, :] - row[1:2]) * row[2:3]
                low = (grads * (1.0 / denom)).astype(jnp.bfloat16)
                total[back, :width, :] += outer_product(table, low)
                at_y = (y + side - back) % side
                states = jnp.concatenate([p_all[line * side + at_y] for line in range(z_size)])
                made = made + jnp.dot(low, states, preferred_element_type=jnp.float32)
            t_logits[0, lines, 0:width] = made
            return carry

        lax.fori_loop(0, part // narrow, chunk, 0)

    def pair_copy(index, source, target):
        return pltpu.make_async_remote_copy(
            source,
            inbox.at[index],
            pair_send.at[index],
            pair_recv.at[index],
            device_id=target,
            device_id_type=MESH,
        )

    given = []
    if pair:
        x, core = dp // 2, dp % 2
        far, near = 1 - x, x

        def start_of(along, other):
            return (2 * along + (core + other) % 2) * part

        for index, (along, other) in enumerate(((far, 1), (far, 0), (near, 1), (near, 0))):
            grade(start_of(along, other))
            if other:
                given.append(pair_copy(index // 2, rows_at(start_of(along, other), part), sibling))
                given[-1].start()
            elif along is far:
                given[0].wait_recv()
                lines = pl.ds(pl.multiple_of(start_of(far, 0), 64), part)
                t_logits[0, lines, 0:half] += inbox[0]
                given.append(pair_copy(2, rows_at(start_of(far, 0), part), beside))
                given[-1].start()
    else:
        grade(0)
    for back in range(side):
        turned = total[back].T.astype(jnp.bfloat16)
        for line in range(z_size):
            at = line * side + (y + side - back) % side
            t_all[at, :, half : 2 * half] = turned[line * amount : (line + 1) * amount]

    def d_copy(step):
        peer = (me + step) % groups
        return pltpu.make_async_remote_copy(
            t_all.at[peer, :, half : 2 * half],
            t_all.at[me, :, 0:half],
            d_send.at[step],
            d_recv.at[step],
            device_id=(dp, peer),
            device_id_type=MESH,
        )

    for step in range(1, groups):
        d_copy(step).start()
    made = t_all[me, :, half : 2 * half].astype(jnp.float32)
    for step in range(1, groups):
        d_copy(step).wait_recv()
        made = made + t_all[(me + groups - step) % groups, :, 0:half].astype(jnp.float32)
    d_ref[...] = made
    kept = 0
    if pair:
        kept = start_of(near, 0)
        lines = pl.ds(pl.multiple_of(kept, 64), part)
        given[2].wait_recv()
        t_logits[0, lines, 0:half] += inbox[1]
        given[1].wait_recv()
        t_logits[0, lines, 0:half] += inbox[2]
    out = pltpu.make_async_copy(rows_at(kept, part), w_ref, out_sem)
    out.start()
    for step in range(1, groups):
        stat_copy(step).wait_send()
        d_copy(step).wait_send()
    for copy in given:
        copy.wait_send()
    out.wait()


def head(picked, t_picked, table, teacher_head, denom, number):
    groups, n_dp = lax.axis_size("fsdp"), lax.axis_size("dp")
    pair = n_dp == 4
    amount, width = picked.shape
    vocab = table.shape[0]
    z_size = z_size_of(groups)
    side, across = groups // z_size, z_size * amount
    half = d_all_width(width)
    assert 2 * half <= DT
    full, low = jnp.float32, jnp.bfloat16
    anywhere = pl.BlockSpec(memory_space=pl.ANY)
    dma = pltpu.SemaphoreType.DMA
    made = [
        jax.ShapeDtypeStruct((amount, half), full),
        jax.ShapeDtypeStruct((8, across), full),
        jax.ShapeDtypeStruct((vocab // 4 if pair else vocab, half), full),
    ]
    return pl.pallas_call(
        partial(head_kernel, groups, pair, denom),
        out_shape=tuple(made),
        in_specs=[VMEM_SPEC] * 4,
        out_specs=(VMEM_SPEC, VMEM_SPEC) + (anywhere,) * (len(made) - 2),
        scratch_shapes=[
            pltpu.VMEM((groups, amount, width), low),
            pltpu.VMEM((groups, amount, DT), low),
            pltpu.VMEM((width, across), low),
            pltpu.VMEM((DT, across), low),
            pltpu.VMEM((side, vocab, across), full),
            pltpu.VMEM((side, vocab, across), full),
            pltpu.VMEM((groups, side, 8, across), full),
            pltpu.VMEM((side, 8, across), full),
            pltpu.VMEM((3, vocab // 4, half) if pair else (1, 8, 128), full),
            pltpu.VMEM((side, half, across), full),
            *[dma((2 * (2 * z_size + (side - 1) * z_size),))] * 2,
            *[dma((groups,))] * 4,
            *[dma((3,))] * 2,
            dma,
        ],
        compiler_params=pltpu.CompilerParams(
            collective_id=number, has_side_effects=True, vmem_limit_bytes=61 * 1024 * 1024
        ),
    )(picked, t_picked, table, teacher_head)


def three_parts(value):
    high = lax.reduce_precision(value, 8, 7)
    rest = value - high
    middle = lax.reduce_precision(rest, 8, 7)
    low = rest - middle
    return jnp.concatenate([high, middle, low], -1).astype(jnp.bfloat16)


def pick_exact(marks, value, turned=False):
    width = value.shape[1]
    terms = three_parts(value)
    made = outer_product(marks, terms) if turned else jnp.dot(
        marks, terms, preferred_element_type=jnp.float32
    )
    return made[:, :width] + made[:, width : 2 * width] + made[:, 2 * width :]


def plan_requests(ids, local_rows):
    order = lax.broadcasted_iota(jnp.int32, (ids.shape[0],), 0)
    same = ids[:, None] == ids[None, :]
    leader = jnp.min(jnp.where(same, order[None, :], ids.shape[0]), 1)
    leads = leader == order
    owner = ids // local_rows
    before = (
        (owner[:, None] == owner[None, :]) & leads[None, :] & (order[None, :] < leader[:, None])
    )
    rank = jnp.sum(before.astype(jnp.int32), 1)
    return (leads, owner, ids - owner * local_rows, rank)


def round_marks(plan, turn, devices):
    leads, owner, local_id, rank = plan
    inside = (rank >= turn * SLOTS) & (rank < (turn + 1) * SLOTS)
    slot = jnp.where(inside, owner * SLOTS + rank - turn * SLOTS, -1)
    line = lax.broadcasted_iota(jnp.int32, (devices * SLOTS, 1), 0)
    hit = line == slot[None, :]
    asked = jnp.max(jnp.where(hit & leads[None, :], local_id[None, :], -1), 1)
    return (hit.astype(jnp.bfloat16), asked.reshape(devices, 1, SLOTS))


def question(plan, turn, devices, extra):
    marks, asked = round_marks(plan, turn, devices)
    fill = jnp.full((devices, 1, 128 - SLOTS - extra.shape[0]), -1, jnp.int32)
    note = jnp.broadcast_to(extra[None, None, :], (devices, 1, extra.shape[0]))
    return (marks, jnp.concatenate([asked, note, fill], 2))


def ask(plan, turn, devices, extra):
    marks, asked = question(plan, turn, devices, extra)
    return (marks, exchange(asked, 0)[:, 0, :SLOTS].reshape(-1))


def wanted_marks(wanted, local_rows):
    return (wanted[:, None] == lax.broadcasted_iota(jnp.int32, (1, local_rows), 1)).astype(
        jnp.bfloat16
    )


def fetch(marks, wanted, table_low, devices):
    rows = jnp.dot(
        wanted_marks(wanted, table_low.shape[0]), table_low, preferred_element_type=jnp.float32
    ).astype(jnp.bfloat16)
    got = exchange(rows.reshape(devices, SLOTS, -1), 1)
    return outer_product(marks, got.reshape(devices * SLOTS, -1))


def give_back(marks, wanted, grads, local_rows, devices):
    sent = pick_exact(marks, grads)
    got = exchange(sent.reshape(devices, SLOTS, -1), 2)
    return pick_exact(wanted_marks(wanted, local_rows), got.reshape(devices * SLOTS, -1), True)


def local(
    token_ids,
    valid_mask,
    seq_ids,
    mask_pos,
    mask_labels,
    teacher_in,
    teacher_flat,
    teacher_vec,
    teacher_head,
    emb_table,
    emb_first,
    emb_second,
    pos_table,
    pos_first,
    pos_second,
    layer_flat,
    layer_first,
    layer_second,
    proj_weight,
    proj_first,
    proj_second,
    layer_vec,
    vec_first,
    vec_second,
    misc_vec,
    misc_first,
    misc_second,
):
    micro, micro_rows, length = token_ids.shape
    rows = micro * micro_rows
    local_rows, width = emb_table.shape
    layers = layer_vec.shape[0]
    picks = mask_pos.shape[2]
    tokens = rows * length
    n_dp, groups = lax.axis_size("dp"), lax.axis_size("fsdp")
    place = lax.axis_index("fsdp")
    devices = n_dp * groups
    hidden_denom = float(rows * devices * length * DT)
    predict_denom = float(rows * devices * picks)
    flat_local = layer_flat.shape[1]
    by_rows = flat_local % DS == 0

    to_owner = [
        (d * groups + f, f * n_dp + d) for d in range(n_dp) for f in range(groups)
    ]
    from_owner = [(owner, holder) for holder, owner in to_owner]
    table_low = emb_table.astype(jnp.bfloat16)

    usable = valid_mask.reshape(rows, length) > 0
    docs = seq_ids.reshape(rows, length)
    same_doc = docs[:, :, None] == docs[:, None, :]
    pair_mask = same_doc & usable[:, :, None] & usable[:, None, :]
    allowed = pair_mask | jnp.eye(length, dtype=bool)
    ids = jnp.concatenate([token_ids.reshape(-1), mask_labels.reshape(-1)])
    plan = plan_requests(ids, local_rows)
    extra = jnp.stack([-1 - jnp.sum(pair_mask.astype(jnp.int32)), -1 - jnp.max(plan[3])])
    teacher_lines = teacher_flat.reshape(-1, DT)
    teacher_all = lax.all_gather(teacher_lines, BOTH, axis=0, tiled=True).reshape(-1, CHUNK, DT)
    own_parts = [
        layer_flat.astype(jnp.bfloat16),
        pos_table.astype(jnp.bfloat16),
        proj_weight.astype(jnp.bfloat16).T,
    ]
    if by_rows:
        chunk = flat_local // DS
        own_layers = [woven(part.reshape(-1, DS), False) for part in own_parts[0]]
        own_parts = [part.reshape(1, -1, DS) for part in own_layers + own_parts[1:]]
        line, lines = DS, sum(part.shape[1] for part in own_parts)
    else:
        own_parts = [part.reshape(1, -1) for part in own_parts]
        line, lines = 128, -(-sum(part.shape[1] for part in own_parts) // 128)
    block_rows = -(-lines // 16) * 16
    marks, asked = question(plan, 0, devices, extra)
    got, weights_all, token_blocks = entry(asked, pack(own_parts, line, block_rows)[0], table_low, 3)
    table_then = lax.optimization_barrier((table_low, got))[0]
    slice_part = lax.ppermute(table_then, BOTH, from_owner)
    wanted = got[:, 0, :SLOTS].reshape(-1)
    notes = got[:, 0, SLOTS : SLOTS + 2]
    count = jnp.sum(-1 - notes[:, 0]).astype(jnp.float32)
    rounds = jnp.max(-1 - notes[:, 1]) // SLOTS + 1
    all_rows = outer_product(marks, token_blocks.reshape(devices * SLOTS, width))

    def more_rows(state):
        turn, so_far = state
        marks_now, wanted_now = ask(plan, turn, devices, extra)
        return (turn + 1, so_far + fetch(marks_now, wanted_now, table_low, devices))

    all_rows = lax.while_loop(lambda state: state[0] < rounds, more_rows, (1, all_rows))[1]
    token_rows, label_rows = (all_rows[:tokens], all_rows[tokens:])
    pos_local, proj_local = pos_table.shape[0], proj_weight.shape[1]
    if by_rows:
        where = block_plan(devices, chunk, layers, (pos_local, proj_local))
        *matrices, places_all, proj_all = unpack(weights_all, where, layers, length)
    else:
        flat_all = weights_all.reshape(devices, -1)
        split = []
        for index in range(layers):
            wide = flat_all[:, index * flat_local : (index + 1) * flat_local].reshape(WIDE, DS)
            qkv, out, up, down = split_rows(wide, DS, FS)
            split.append(
                (
                    qkv.reshape(DS, 3, DS).transpose(1, 0, 2),
                    out,
                    jnp.pad(up, ((0, 0), (0, WIDER - FS))),
                    jnp.pad(down, ((0, WIDER - FS), (0, 0))),
                )
            )
        matrices = sum(map(list, split), [])
        start = layers * flat_local
        places_all = flat_all[:, start : start + pos_local * DS].reshape(length, DS)
        start += pos_local * DS
        proj_all = flat_all[:, start : start + proj_local * DS].reshape(DT, DS)

    proj_bias = misc_vec[2 * DS :]
    evec = misc_vec[: 2 * DS].reshape(2, DS)
    cut = 5 * DS
    vectors = jnp.concatenate([layer_vec[:, :cut], layer_vec[:, cut + FS :]], 1).reshape(
        layers, 8, DS
    )
    biases = jnp.pad(layer_vec[:, cut : cut + FS], ((0, 0), (0, WIDER - FS)))[:, None]

    mask = jnp.where(pair_mask, 2.0, jnp.where(allowed, 1.0, 0.0)).reshape(tokens, length)
    embedded, normed_zero, inverse_zero, hidden, *saved = student_forward(
        token_rows, places_all, evec, vectors, biases, mask, matrices
    )
    slice_part = lax.optimization_barrier((slice_part, teacher_all, hidden))[0]
    slice_table = lax.all_gather(slice_part, "dp", axis=0, tiled=True)

    flat_pick = (
        jnp.arange(rows, dtype=jnp.int32)[:, None] * length + mask_pos.reshape(rows, picks)
    ).reshape(-1)
    weight = valid_mask.reshape(tokens, 1).astype(jnp.float32)
    t_scores, back_zero, back_last, grad_proj, grad_bias, squares_of, picked, t_picked = (
        teacher_forward(
            teacher_in.reshape(tokens, DT),
            teacher_all,
            teacher_vec.astype(jnp.float32)[None],
            mask,
            embedded,
            hidden,
            proj_all,
            proj_bias[None],
            weight,
            flat_pick[:, None],
            hidden_denom,
        )
    )
    hidden_sum = jnp.sum(squares_of) / hidden_denom
    pick_marks = (flat_pick[:, None] == lax.broadcasted_iota(jnp.int32, (1, tokens), 1)).astype(
        jnp.bfloat16
    )
    d_picked, own_stats, head_grad = head(
        picked, t_picked, slice_table, teacher_head, predict_denom, 4
    )
    own_z = place // (groups // z_size_of(groups))
    own_stats = lax.dynamic_slice_in_dim(own_stats, own_z * rows * picks, rows * picks, 1)
    picked_wide = picked.astype(jnp.float32)
    target_logit = jnp.sum(picked_wide * label_rows, -1)
    predict_sum = (
        jnp.sum(2.0 * own_stats[0] - own_stats[3] - target_logit) / predict_denom
    )
    d_picked = d_picked[:, :width] - label_rows / predict_denom
    d_hidden = pick_exact(pick_marks, d_picked, True) + back_last

    if n_dp != 4:
        head_grad = lax.psum_scatter(head_grad, "dp", scatter_dimension=0, tiled=True)

    matrix_grads = [None] * layers
    vector_grads = [None] * layers
    attention_sum = jnp.float32(0.0)
    head_grad = lax.ppermute(head_grad, BOTH, to_owner)
    for layer_index in reversed(range(layers)):
        d_hidden, *others = student_backward(
            d_hidden,
            vectors[layer_index],
            biases[layer_index],
            mask,
            matrices[4 * layer_index : 4 * layer_index + 4],
            saved[7 * layer_index : 7 * layer_index + 7],
            [t_scores, count.reshape(1, 1)] if layer_index == layers - 1 else [],
            [] if layer_index else [back_zero, normed_zero, inverse_zero, evec],
        )
        matrix_grads[layer_index] = others[:6]
        d_vectors, d_bias_up, more = others[6], others[7], others[8:]
        d_vectors = d_vectors.reshape(-1)
        vector_grads[layer_index] = jnp.concatenate(
            [d_vectors[:cut], d_bias_up[0, :FS], d_vectors[cut:]]
        )
        if layer_index == layers - 1:
            attention_sum = jnp.sum(more.pop(0)) / count
    d_hidden, head_grad = lax.optimization_barrier((d_hidden, head_grad))
    head_grad = head_grad[:, :width]
    d_token, (grad_places, d_edge) = d_hidden, more

    row_grads = jnp.concatenate([d_token, -picked_wide / predict_denom])
    def more_grads(state):
        turn, so_far = state
        marks_now, wanted_now = ask(plan, turn, devices, extra)
        return (
            turn + 1,
            so_far + give_back(marks_now, wanted_now, row_grads, local_rows, devices),
        )

    grad_small = jnp.concatenate(vector_grads + [d_edge[0], d_edge[1], grad_bias[0]])
    small_local = -(-grad_small.shape[0] // devices)
    small_local = -(-small_local // DS) * DS
    small_padded = jnp.pad(grad_small, (0, devices * small_local - grad_small.shape[0]))
    rest = [grad_places, grad_proj, small_padded.reshape(-1, DS)]
    sizes = [flat_local] * layers + [part.size // devices for part in rest]
    lines = -(-sum(sizes) // line)
    block = (-(-lines // 8) * 8, line)
    sent = pick_exact(marks, row_grads).reshape(devices, SLOTS, width)
    if by_rows:
        amounts = [size // DS for size in sizes[layers:]]
        grad_parts = sum(matrix_grads, []) + rest
        block_rows_of = block_plan(devices, chunk, layers, amounts)
    else:
        wides = []
        for grads in matrix_grads:
            first = jnp.stack(grads[:3], 1).reshape(-1, width)
            wides.append(jnp.concatenate([first, *grads[3:]]))
        grad_parts = [pack([part.reshape(devices, -1) for part in wides + rest], *block[::-1])]
        block_rows_of = ()
    reduced, row_blocks = reduce(grad_parts, block_rows_of, block, sent, 7)
    g_table = pick_exact(
        wanted_marks(wanted, local_rows), row_blocks.reshape(devices * SLOTS, width), True
    )
    g_table = lax.while_loop(lambda state: state[0] < rounds, more_grads, (1, g_table))[1]
    g_table = g_table + head_grad
    if by_rows:
        pieces = []
        start = 0
        for size in sizes:
            pieces.append(reduced[start : start + size // DS])
            start += size // DS
    else:
        pieces = cut_pieces(reduced.reshape(-1), sizes)
    if by_rows:
        pieces[:layers] = [woven(piece, True) for piece in pieces[:layers]]
    layer_acc = jnp.stack([piece.reshape(-1) for piece in pieces[:layers]])
    g_places = pieces[layers].reshape(pos_local, DS)
    g_proj = pieces[layers + 1].reshape(proj_local, DS).T
    small_part = pieces[layers + 2].reshape(-1)
    squares = (
        jnp.sum(g_table * g_table)
        + jnp.sum(g_places * g_places)
        + jnp.sum(g_proj * g_proj)
        + jnp.sum(layer_acc * layer_acc)
        + jnp.sum(small_part * small_part)
    )
    note = jnp.concatenate(
        [small_part, jnp.stack([attention_sum + hidden_sum + predict_sum, squares])]
    )
    note = jnp.pad(note, (0, -(-note.shape[0] // 128) * 128 - note.shape[0])).reshape(1, -1)
    notes_all = exchange(note, 8, spread=True)[:, 0]
    small = notes_all[:, :small_local].reshape(-1)
    loss = jnp.sum(notes_all[:, small_local])
    norm = jnp.sqrt(jnp.sum(notes_all[:, small_local + 1]))
    g_vec = small[: layer_vec.size].reshape(layer_vec.shape)
    g_misc = small[layer_vec.size : layer_vec.size + misc_vec.shape[0]]
    factor = CLIP_NORM / jnp.maximum(norm, CLIP_NORM)
    return (
        loss,
        count,
        norm,
        *adam_update(emb_table, emb_first, emb_second, g_table * factor),
        *adam_update(pos_table, pos_first, pos_second, g_places * factor),
        *adam_update(layer_flat, layer_first, layer_second, layer_acc * factor),
        *adam_update(proj_weight, proj_first, proj_second, g_proj * factor),
        *adam_update(layer_vec, vec_first, vec_second, g_vec * factor),
        *adam_update(misc_vec, misc_first, misc_second, g_misc * factor),
    )


def solution(mesh):
    rows, lines, flat, tail, every = (
        P(None, BOTH),
        P(BOTH, None),
        P(BOTH),
        P(None, BOTH),
        P(),
    )
    placed = (
        *[rows] * 6,
        flat,
        every,
        P("fsdp", None),
        *[lines] * 6,
        *[tail] * 6,
        *[every] * 6,
    )
    return jax.shard_map(
        local,
        mesh=mesh,
        in_specs=placed,
        out_specs=(*[every] * 3, *[lines] * 6, *[tail] * 6, *[every] * 6),
        check_vma=False,
    )
```

```python
import math
from functools import partial

import jax
import jax.numpy as jnp
from jax import lax
from jax.experimental import pallas as pl
from jax.experimental.pallas import tpu as pltpu
from jax.sharding import PartitionSpec as P

DS = 312
HS = 12
FS = 1200
DT = 768
HT = 12
FT = 3072
STEP = 5


NORM_EPS = 1e-06
CLIP_NORM = 0.05
LEARN_RATE = 0.05
BETA_ONE = 0.9
BETA_TWO = 0.999
ADAM_EPS = 1e-06
WEIGHT_DECAY = 0.01
NEG_LARGE = -1e30

BOTH = ("dp", "fsdp")
MESH = pl.DeviceIdType.MESH
SLOTS = 48
WIDE = 3 * DS + DS + 2 * FS


def z_size_of(fsdp):
    return 4 if fsdp % 4 == 0 else 1


def place_of():
    fsdp = lax.axis_size("fsdp")
    return lax.axis_index("dp") * fsdp + lax.axis_index("fsdp")


def member(index, whole):
    fsdp = lax.axis_size("fsdp")
    if whole:
        return (index // fsdp, index % fsdp)
    return (lax.axis_index("dp"), index)


def greet(count, me, whole):
    barrier = pltpu.get_barrier_semaphore()

    def signal(step, carry):
        pl.semaphore_signal(
            barrier, inc=1, device_id=member((me + step) % count, whole), device_id_type=MESH
        )
        return carry

    lax.fori_loop(1, count, signal, 0)
    pl.semaphore_wait(barrier, count - 1)


def exchange_kernel(count, whole, spread, x_ref, o_ref, send, recv, local_sem):
    me = place_of() if whole else lax.axis_index("fsdp")
    own = pltpu.make_async_copy(x_ref if spread else x_ref.at[me], o_ref.at[me], local_sem)
    own.start()
    greet(count, me, whole)

    def copy(step):
        peer = (me + step) % count
        return pltpu.make_async_remote_copy(
            x_ref if spread else x_ref.at[peer],
            o_ref.at[me],
            send.at[step],
            recv.at[step],
            device_id=member(peer, whole),
            device_id_type=MESH,
        )

    def start(step, carry):
        copy(step).start()
        return carry

    def finish(step, carry):
        copy(step).wait()
        return carry

    lax.fori_loop(1, count, start, 0)
    own.wait()
    lax.fori_loop(1, count, finish, 0)


def exchange(x, number, whole=True, spread=False):
    count = lax.axis_size("fsdp") * (lax.axis_size("dp") if whole else 1)
    return pl.pallas_call(
        partial(exchange_kernel, count, whole, spread),
        out_shape=jax.ShapeDtypeStruct(((count,) if spread else ()) + x.shape, x.dtype),
        in_specs=[pl.BlockSpec(memory_space=pl.ANY)],
        out_specs=pl.BlockSpec(memory_space=pl.ANY),
        scratch_shapes=[
            pltpu.SemaphoreType.DMA((count,)),
            pltpu.SemaphoreType.DMA((count,)),
            pltpu.SemaphoreType.DMA,
        ],
        compiler_params=pltpu.CompilerParams(collective_id=number, has_side_effects=True),
    )(x)


VMEM_SPEC = pl.BlockSpec(memory_space=pltpu.VMEM)


class Grid:
    def __init__(self):
        self.fsdp = lax.axis_size("fsdp")
        self.z_size = z_size_of(self.fsdp)
        self.side = self.fsdp // self.z_size
        assert lax.axis_size("dp") == 2 * self.side
        dp, fsdp = lax.axis_index("dp"), lax.axis_index("fsdp")
        self.x, self.core = dp // 2, dp % 2
        self.z, self.y = fsdp // self.side, fsdp % self.side
        side, z_size = self.side, self.z_size
        self.keys = [(g, b, a) for g in range(side) for b in range(side) for a in range(z_size)]
        self.rank = {key: index for index, key in enumerate(self.keys)}
        self.count = len(self.keys)

    def at(self, third, second, z, other=0):
        core = (self.core + other) % 2
        x = (self.x + third * (1 - core) + second * core) % self.side
        y = (self.y + second * (1 - core) + third * core) % self.side
        return (x * 2 + core, ((self.z + z) % self.z_size) * self.side + y)

    def index(self, third, second, z, other=0):
        dp, fsdp = self.at(third, second, z, other)
        return dp * self.fsdp + fsdp

    def neighbours(self):
        return (
            [(0, 0, a, 0) for a in range(1, self.z_size)]
            + [(0, b, 0, 0) for b in range(1, self.side)]
            + [(g, 0, 0, 0) for g in range(1, self.side)]
            + [(0, 0, 0, 1)]
        )

    def greet(self):
        barrier = pltpu.get_barrier_semaphore()
        around = self.neighbours()
        for where in around:
            pl.semaphore_signal(barrier, inc=1, device_id=self.at(*where), device_id_type=MESH)
        pl.semaphore_wait(barrier, len(around))


class Spread:
    def __init__(self, grid, x_ref, o_ref, send, recv, local_sem):
        self.grid, self.x_ref, self.o_ref = grid, x_ref, o_ref
        self.send, self.recv = send, recv
        self.started = []
        self.own = pltpu.make_async_copy(x_ref, o_ref.at[self.slot((0, 0, 0))], local_sem)
        self.own.start()

    def slot(self, key, other=0):
        grid = self.grid
        third, second, z = key
        return grid.index(grid.side - third, grid.side - second, grid.z_size - z, other)

    def push(self, key, name, where):
        grid = self.grid
        index = grid.rank[name] + (grid.count if where[3] else 0)
        copy = pltpu.make_async_remote_copy(
            self.x_ref if key == (0, 0, 0) else self.o_ref.at[self.slot(key)],
            self.o_ref.at[self.slot(key)],
            self.send.at[index],
            self.recv.at[index],
            device_id=grid.at(*where),
            device_id_type=MESH,
        )
        copy.start()
        self.started.append(copy)

    def forward(self, key):
        grid = self.grid
        third, second, z = key
        if key == (0, 0, 0):
            for step in range(1, grid.z_size):
                self.push(key, (0, 0, step), (0, 0, step, 0))
        if third == 0 and second == 0:
            for step in range(1, grid.side):
                self.push(key, (0, step, z), (0, step, 0, 0))
        if third == 0:
            for step in range(1, grid.side):
                self.push(key, (step, second, z), (step, 0, 0, 0))
        self.push(key, key, (0, 0, 0, 1))

    def arrived(self, key, other=0):
        grid = self.grid
        index = grid.rank[key] + (grid.count if other else 0)
        pltpu.make_async_remote_copy(
            self.o_ref.at[self.slot(key, other)],
            self.o_ref.at[self.slot(key, other)],
            self.send.at[index],
            self.recv.at[index],
            device_id=grid.at(0, 0, 0, 1),
            device_id_type=MESH,
        ).wait_recv()

    def start(self):
        self.forward((0, 0, 0))

    def middle(self):
        for key in self.grid.keys[1:]:
            self.arrived(key)
            self.forward(key)

    def finish(self):
        for key in self.grid.keys:
            self.arrived(key, 1)
        self.own.wait()
        for copy in self.started:
            copy.wait_send()


def entry_kernel(
    ask_ref, w_ref, table_ref, got_ref, all_ref, rows_ref, sent, asks, *sems
):
    ask_send, ask_recv, ask_local, w_send, w_recv, w_local, row_send, row_recv, row_local, out_sem = sems
    grid = Grid()
    count = 2 * grid.count
    me = place_of()
    own = pltpu.make_async_copy(ask_ref.at[me], asks.at[me], ask_local)
    own.start()
    greet(count, me, True)

    def ask_copy(step):
        peer = (me + step) % count
        return pltpu.make_async_remote_copy(
            ask_ref.at[peer],
            asks.at[me],
            ask_send.at[step],
            ask_recv.at[step],
            device_id=member(peer, True),
            device_id_type=MESH,
        )

    def row_copy(step):
        peer = (me + step) % count
        return pltpu.make_async_remote_copy(
            sent.at[peer],
            rows_ref.at[me],
            row_send.at[step],
            row_recv.at[step],
            device_id=member(peer, True),
            device_id_type=MESH,
        )

    def each(first, action):
        def body(step, carry):
            action(step)
            return carry

        lax.fori_loop(first, count, body, 0)

    each(1, lambda step: ask_copy(step).start())
    spread = Spread(grid, w_ref, all_ref, w_send, w_recv, w_local)
    spread.start()
    own.wait()
    table = table_ref[...]
    line = lax.broadcasted_iota(jnp.int32, (table.shape[0], 128), 0)

    def answer(source):
        marks = jnp.where(line == asks[source], 1.0, 0.0).astype(jnp.bfloat16)
        sent[source] = outer_product(marks, table)[:SLOTS].astype(jnp.bfloat16)

    answer(me)
    mine = pltpu.make_async_copy(sent.at[me], rows_ref.at[me], row_local)
    mine.start()

    def serve(step):
        ask_copy(step).wait_recv()
        answer((me + count - step) % count)

    each(1, serve)
    each(1, lambda step: row_copy(step).start())
    keep = pltpu.make_async_copy(asks, got_ref, out_sem)
    keep.start()
    spread.middle()
    spread.finish()
    mine.wait()
    keep.wait()
    each(1, lambda step: row_copy(step).wait())
    each(1, lambda step: ask_copy(step).wait_send())


def entry(asked, weights, table_low, number):
    count = asked.shape[0]
    width = table_low.shape[1]
    anywhere = pl.BlockSpec(memory_space=pl.ANY)
    dma = pltpu.SemaphoreType.DMA
    return pl.pallas_call(
        entry_kernel,
        out_shape=(
            jax.ShapeDtypeStruct(asked.shape, asked.dtype),
            jax.ShapeDtypeStruct((count,) + weights.shape, weights.dtype),
            jax.ShapeDtypeStruct((count, SLOTS, width), table_low.dtype),
        ),
        in_specs=[anywhere, anywhere, pl.BlockSpec(memory_space=pltpu.VMEM)],
        out_specs=(anywhere, VMEM_SPEC, VMEM_SPEC),
        scratch_shapes=[
            pltpu.VMEM((count, SLOTS, width), table_low.dtype),
            pltpu.VMEM(asked.shape, asked.dtype),
            *[dma((count,)), dma((count,)), dma] * 3,
            dma,
        ],
        compiler_params=pltpu.CompilerParams(
            collective_id=number, has_side_effects=True, vmem_limit_bytes=32 * 1024 * 1024
        ),
    )(asked, weights, table_low)


def reduce_kernel(plan, sources, *refs):
    ins, rest = refs[:sources], refs[sources:]
    row_ref, o_ref, got_ref = rest[:3]
    if plan:
        x_ref, rest = rest[3], rest[1:]
    else:
        x_ref = ins[0]
    held, third_in, second_in, z_in, send, recv, row_send, row_recv, row_local = rest[3:]
    grid = Grid()
    side, z_size, count, rank = grid.side, grid.z_size, grid.count, grid.rank
    order = sorted(grid.keys, key=lambda key: (key[0] == 0, key[1] == 0, key[2] == 0))
    devices = 2 * count
    me = place_of()
    own = pltpu.make_async_copy(row_ref.at[me], got_ref.at[me], row_local)
    own.start()
    greet(devices, me, True)

    def row_copy(step):
        peer = (me + step) % devices
        return pltpu.make_async_remote_copy(
            row_ref.at[peer],
            got_ref.at[me],
            row_send.at[step],
            row_recv.at[step],
            device_id=member(peer, True),
            device_id_type=MESH,
        )

    def row_start(step, carry):
        row_copy(step).start()
        return carry

    def row_finish(step, carry):
        row_copy(step).wait()
        return carry

    lax.fori_loop(1, devices, row_start, 0)
    started = []

    def push(source, target, index, where):
        copy = pltpu.make_async_remote_copy(
            source,
            target,
            send.at[index],
            recv.at[index],
            device_id=grid.at(*where),
            device_id_type=MESH,
        )
        copy.start()
        started.append(copy)

    def arrived(target, index):
        pltpu.make_async_remote_copy(
            target,
            target,
            send.at[index],
            recv.at[index],
            device_id=grid.at(0, 0, 0, 1),
            device_id_type=MESH,
        ).wait_recv()

    for source, at, rows, block, line in plan:
        value = jnp.zeros((rows, x_ref.shape[2]), x_ref.dtype)
        if source >= 0:
            value = ins[source][at : at + rows, :]
        x_ref[block, line : line + rows, :] = value
    for key in order:
        push(x_ref.at[grid.index(*key, 1)], held.at[rank[key]], rank[key], (0, 0, 0, 1))
    from_third = {}
    from_second = {}
    from_z = {}
    index = count
    for step in range(1, side):
        for second in range(side):
            for z in range(z_size):
                from_third[step, second, z] = (
                    third_in.at[((step - 1) * side + second) * z_size + z],
                    index,
                )
                index += 1
    for step in range(1, side):
        for z in range(z_size):
            from_second[step, z] = (second_in.at[(step - 1) * z_size + z], index)
            index += 1
    for way in (1, -1):
        for distance in range(z_size - 1):
            from_z[way, distance] = (z_in.at[len(from_z)], index)
            index += 1

    def gathered(key):
        third, second, z = key
        arrived(held.at[rank[key]], rank[key])
        total = held[rank[key]] + x_ref[grid.index(*key)]
        if third == 0:
            for step in range(1, side):
                arrived(*from_third[step, second, z])
                total = total + from_third[step, second, z][0][...]
        if third == 0 and second == 0:
            for step in range(1, side):
                arrived(*from_second[step, z])
                total = total + from_second[step, z][0][...]
        return total

    for key in order:
        third, second, z = key
        if third == 0 and second == 0:
            continue
        held[rank[key]] = gathered(key)
        if third:
            target, where = from_third[third, second, z], (third, 0, 0, 0)
        else:
            target, where = from_second[second, z], (0, second, 0, 0)
        push(held.at[rank[key]], target[0], target[1], where)

    def behind(way):
        return (grid.z > 0) if way > 0 else (grid.z < z_size - 1)

    def hop(way, distance):
        target = from_z[way, distance - 1]
        return pltpu.make_async_remote_copy(
            held.at[rank[0, 0, way * distance % z_size]],
            target[0],
            send.at[target[1]],
            recv.at[target[1]],
            device_id=grid.at(0, 0, way % z_size),
            device_id_type=MESH,
        )

    def reaches(way, distance):
        return (grid.z + way * distance >= 0) & (grid.z + way * distance < z_size)

    for distance in range(z_size - 1, 0, -1):
        for way in (1, -1):

            @pl.when(reaches(way, distance))
            def _(way=way, distance=distance):
                key = (0, 0, way * distance % z_size)
                held[rank[key]] = gathered(key)
                if distance < z_size - 1:

                    @pl.when(behind(way))
                    def _():
                        arrived(*from_z[way, distance])
                        held[rank[key]] += from_z[way, distance][0][...]

                hop(way, distance).start()

    o_ref[...] = gathered((0, 0, 0))
    for way in (1, -1):

        @pl.when(behind(way))
        def _(way=way):
            arrived(*from_z[way, 0])
            o_ref[...] += from_z[way, 0][0][...]

    for distance in range(z_size - 1, 0, -1):
        for way in (1, -1):
            pl.when(reaches(way, distance))(hop(way, distance).wait_send)
    for copy in started:
        copy.wait_send()
    own.wait()
    lax.fori_loop(1, devices, row_finish, 0)


def reduce(parts, plan, block, rows, number):
    count = lax.axis_size("dp") * lax.axis_size("fsdp")
    side = lax.axis_size("dp") // 2
    z_size = count // 2 // side // side
    kind = parts[0].dtype
    vmem, anywhere = pl.BlockSpec(memory_space=pltpu.VMEM), pl.BlockSpec(memory_space=pl.ANY)
    dma = pltpu.SemaphoreType.DMA
    return pl.pallas_call(
        partial(reduce_kernel, plan, len(parts)),
        out_shape=(
            jax.ShapeDtypeStruct(block, kind),
            jax.ShapeDtypeStruct(rows.shape, rows.dtype),
        ),
        in_specs=[vmem] * len(parts) + [anywhere],
        out_specs=(vmem, anywhere),
        scratch_shapes=[
            *([pltpu.VMEM((count,) + block, kind)] if plan else []),
            pltpu.VMEM((count // 2,) + block, kind),
            pltpu.VMEM(((side - 1) * side * z_size,) + block, kind),
            pltpu.VMEM(((side - 1) * z_size,) + block, kind),
            pltpu.VMEM((2 * (z_size - 1),) + block, kind),
            *[dma((count + z_size,))] * 2,
            *[dma((count,))] * 2,
            dma,
        ],
        compiler_params=pltpu.CompilerParams(
            collective_id=number, has_side_effects=True, vmem_limit_bytes=58 * 1024 * 1024
        ),
    )(*parts, rows)


def woven(block, weave):
    chunk = block.shape[0]
    me = place_of()
    made = block
    for index in range(-(-3 * DS // chunk)):
        amount = min(chunk, 3 * DS - index * chunk)
        head = block[:amount].reshape((3, amount // 3, DS) if weave else (amount // 3, 3, DS))
        head = head.transpose(1, 0, 2).reshape(amount, DS)
        if index == 0:
            made = jnp.where(me < 3 * DS // chunk, head, made)
        elif amount < chunk:
            made = jnp.where(me == index, jnp.concatenate([head, block[amount:]]), made)
    return made


def block_plan(devices, chunk, layers, others):
    plan = []
    for block in range(devices):
        for layer in range(layers):
            base = 6 * layer
            row, end, line = block * chunk, (block + 1) * chunk, layer * chunk
            first = row
            if row < 3 * DS:
                stop = min(end, 3 * DS)
                amount = (stop - row) // 3
                for part in range(3):
                    plan.append((base + part, row // 3, amount, block, line + part * amount))
                row = stop
            for part, start, size in ((3, 3 * DS, DS), (4, 4 * DS, FS), (5, 4 * DS + FS, FS)):
                stop = min(end, start + size)
                if row < stop:
                    where = line + row - first
                    plan.append((base + part, row - start, stop - row, block, where))
                    row = stop
        line = layers * chunk
        for index, amount in enumerate(others):
            plan.append((6 * layers + index, block * amount, amount, block, line))
            line += amount
        spare = -line % 8
        if spare:
            plan.append((-1, 0, spare, block, line))
    return tuple(plan)


def pack(parts, width, rows):
    count = parts[0].shape[0]
    if all(part.ndim == 3 for part in parts):
        joined = jnp.concatenate(parts, 1)
        return jnp.pad(joined, ((0, 0), (0, rows - joined.shape[1]), (0, 0)))
    joined = jnp.concatenate([part.reshape(count, -1) for part in parts], 1)
    joined = jnp.pad(joined, ((0, 0), (0, rows * width - joined.shape[1])))
    return joined.reshape(count, rows, width)


def outer_product(left, right):
    return lax.dot_general(
        left, right, (((0,), (0,)), ((), ())), preferred_element_type=jnp.float32
    )


def back_product(grad, weight):
    return lax.dot_general(
        grad, weight, (((1,), (1,)), ((), ())), preferred_element_type=jnp.float32
    )


def norm_forward(value, gain, bias):
    average = jnp.mean(value, -1, keepdims=True)
    centered = value - average
    inverse = lax.rsqrt(jnp.mean(centered * centered, -1, keepdims=True) + NORM_EPS)
    normed = centered * inverse
    return (normed * gain + bias, normed, inverse)


def cut_pieces(vector, sizes):
    pieces = []
    start = 0
    for amount in sizes:
        pieces.append(vector[..., start : start + amount])
        start += amount
    return pieces


def split_rows(wide, width, hidden):
    first, second, third = 3 * width, 4 * width, 4 * width + hidden
    return (
        wide[:first].reshape(width, 3 * width),
        wide[first:second],
        wide[second:third].reshape(width, hidden),
        wide[third:],
    )


def adam_update(value, first, second, grad):
    first = BETA_ONE * first + (1.0 - BETA_ONE) * grad
    second = BETA_TWO * second + (1.0 - BETA_TWO) * grad * grad
    ratio = first / (1.0 - BETA_ONE**STEP) / (jnp.sqrt(second / (1.0 - BETA_TWO**STEP)) + ADAM_EPS)
    return (first, second, value - LEARN_RATE * (ratio + WEIGHT_DECAY * value))


def gelu(value):
    return 0.5 * value * (1.0 + jnp.tanh(0.7978845608028654 * (value + 0.044715 * value * value * value)))


def regroup(weights, group):
    amount = weights.shape[0]
    made = lax.broadcasted_iota(jnp.int32, (amount, amount), 0)
    taken = lax.broadcasted_iota(jnp.int32, (amount, amount), 1)
    inner = amount // group
    marks = jnp.where((made % inner) * group + made // inner == taken, 1.0, 0.0)
    return jnp.dot(
        marks.astype(jnp.bfloat16), weights, preferred_element_type=jnp.float32
    ).astype(jnp.bfloat16)


def softmax_low(scores, mask):
    masked = jnp.where(mask > 0.0, scores, NEG_LARGE)
    expo = jnp.exp(masked - jnp.max(masked, -1, keepdims=True))
    return (expo * (1.0 / jnp.sum(expo, -1, keepdims=True))).astype(jnp.bfloat16)


TILE = 256
CHUNK = 96


def teacher_kernel(
    denom, x_ref, w_ref, vec_ref, mask_ref, zero_ref, last_ref, proj_ref, bias_ref, weight_ref, pick_ref,
    s_ref, back_zero, back_last, proj_out, bias_out, loss_ref, picked_ref, t_picked_ref,
    low_ref, qkv_ref, up_ref, context_ref, sent, send, recv,
):
    size = DT // HT
    tokens = x_ref.shape[0]
    line = lax.broadcasted_iota(jnp.int32, (pick_ref.shape[0], tokens), 1)
    marks = jnp.where(pick_ref[...] == line, 1.0, 0.0).astype(jnp.bfloat16)
    me, groups = lax.axis_index("fsdp"), lax.axis_size("fsdp")
    own = jnp.dot(
        marks, last_ref[...].astype(jnp.bfloat16), preferred_element_type=jnp.float32
    ).astype(jnp.bfloat16)
    sent[...] = own
    picked_ref[me] = own
    greet(groups, me, False)

    def copy(step):
        return pltpu.make_async_remote_copy(
            sent,
            picked_ref.at[me],
            send.at[step],
            recv.at[step],
            device_id=member((me + step) % groups, False),
            device_id_type=MESH,
        )

    for step in range(1, groups):
        copy(step).start()
    for ref in (proj_out, bias_out, loss_ref):
        ref[...] = jnp.zeros_like(ref)
    for index in range(3 * DT // CHUNK):
        made = regroup(w_ref[index], 3)
        for part in range(3):
            rows = CHUNK // 3
            qkv_ref[part, index * rows : (index + 1) * rows, :] = made[part * rows : (part + 1) * rows]
    first_up, first_down = 4 * DT // CHUNK, (4 * DT + FT) // CHUNK
    many = FT // DT
    for index in range(FT // CHUNK // 2):
        at = first_up + 2 * index
        made = regroup(w_ref[at : at + 2].reshape(2 * CHUNK, DT), many)
        rows = 2 * CHUNK // many
        for part in range(many):
            up_ref[part, index * rows : (index + 1) * rows, :] = made[part * rows : (part + 1) * rows]
    line = lax.broadcasted_iota(jnp.int32, (1, 2 * size), 1)
    low_half = line < size
    length = mask_ref.shape[1]

    def vector(index, amount=1):
        return vec_ref[:, index * DT : (index + amount) * DT]

    def tile(step, carry):
        at = pl.ds(pl.multiple_of(step * TILE, TILE), TILE)
        x_low = x_ref[at, :]
        q, k, v = (
            (
                jnp.dot(x_low, qkv_ref[part], preferred_element_type=jnp.float32) + vector(part)
            ).astype(jnp.bfloat16)
            for part in range(3)
        )
        nothing = jnp.zeros((length, 2 * size), jnp.bfloat16)
        for row in range(TILE // length):
            span = slice(row * length, (row + 1) * length)
            here = pl.ds(pl.multiple_of(step * TILE + row * length, length), length)
            mask = mask_ref[here, :]
            for pair in range(HT // 2):
                lanes = slice(pair * 2 * size, (pair + 1) * 2 * size)
                k_pair, v_pair = k[span, lanes], v[span, lanes]
                k_both = jnp.concatenate(
                    [jnp.where(low_half, k_pair, nothing), jnp.where(low_half, nothing, k_pair)]
                )
                v_both = jnp.concatenate(
                    [jnp.where(low_half, v_pair, nothing), jnp.where(low_half, nothing, v_pair)]
                )
                scores = back_product(q[span, lanes], k_both) * size ** (-0.5)
                s_ref[here, pair * 2 * length : (pair + 1) * 2 * length] = scores
                weights = jnp.concatenate(
                    [softmax_low(scores[:, :length], mask), softmax_low(scores[:, length:], mask)], 1
                )
                context_ref[span, lanes] = jnp.dot(
                    weights, v_both, preferred_element_type=jnp.float32
                ).astype(jnp.bfloat16)
        w_out = w_ref[3 * DT // CHUNK : first_up].reshape(DT, DT)
        attended = jnp.dot(context_ref[...], w_out, preferred_element_type=jnp.float32) + vector(3)
        middle = norm_forward(x_low.astype(jnp.float32) + attended, vector(4), vector(5))[0]
        middle_low = middle.astype(jnp.bfloat16)
        outer = jnp.zeros((TILE, DT), jnp.float32)
        for part in range(many):
            inner = jnp.dot(middle_low, up_ref[part], preferred_element_type=jnp.float32) + vector(
                6 + part
            )
            begin = first_down + part * (DT // CHUNK)
            w_down = w_ref[begin : begin + DT // CHUNK].reshape(DT, DT)
            outer = outer + jnp.dot(
                gelu(inner).astype(jnp.bfloat16), w_down, preferred_element_type=jnp.float32
            )
        made = norm_forward(
            middle + outer + vector(6 + many), vector(7 + many), vector(8 + many)
        )[0]
        low_ref[at, :] = made.astype(jnp.bfloat16)
        pairs = ((zero_ref, x_low.astype(jnp.float32), back_zero), (last_ref, made, back_last))
        for source_ref, target, back_ref in pairs:
            source = source_ref[at, :].astype(jnp.bfloat16)
            spread = back_product(source, proj_ref[...]) + bias_ref[...] - target
            weighted = spread * weight_ref[at, :]
            loss_ref[...] += jnp.sum(weighted * spread, 0, keepdims=True)
            d_mapped = (weighted * (2.0 / denom)).astype(jnp.bfloat16)
            back_ref[at, :] = jnp.dot(d_mapped, proj_ref[...], preferred_element_type=jnp.float32)
            proj_out[...] += outer_product(d_mapped, source)
            bias_out[...] += jnp.sum(d_mapped.astype(jnp.float32), 0, keepdims=True)
        return carry

    lax.fori_loop(0, tokens // TILE, tile, 0)
    t_picked_ref[...] = jnp.dot(
        marks, low_ref[...], preferred_element_type=jnp.float32
    ).astype(jnp.bfloat16)
    for step in range(1, groups):
        copy(step).wait()


def teacher_forward(x_low, blocks, vectors, mask, embedded, last, proj, bias, weight, picks, denom):
    tokens, length = mask.shape
    full = partial(jax.ShapeDtypeStruct, dtype=jnp.float32)
    low = partial(jax.ShapeDtypeStruct, dtype=jnp.bfloat16)
    amount, groups = picks.shape[0], lax.axis_size("fsdp")
    made = (
        full((tokens, HT * length)),
        full((tokens, DS)),
        full((tokens, DS)),
        full((DT, DS)),
        full((1, DT)),
        full((1, DT)),
        low((groups, amount, DS)),
        low((amount, DT)),
    )
    given = (x_low, blocks, vectors, mask, embedded, last, proj, bias, weight, picks)
    return pl.pallas_call(
        partial(teacher_kernel, denom),
        out_shape=made,
        in_specs=[VMEM_SPEC] * len(given),
        out_specs=(VMEM_SPEC,) * len(made),
        scratch_shapes=[
            pltpu.VMEM((tokens, DT), jnp.bfloat16),
            pltpu.VMEM((3, DT, DT), jnp.bfloat16),
            pltpu.VMEM((FT // DT, DT, DT), jnp.bfloat16),
            pltpu.VMEM((TILE, DT), jnp.bfloat16),
            pltpu.VMEM((amount, DS), jnp.bfloat16),
            *[pltpu.SemaphoreType.DMA((groups,))] * 2,
        ],
        compiler_params=pltpu.CompilerParams(
            collective_id=5, has_side_effects=True, vmem_limit_bytes=58 * 1024 * 1024
        ),
        cost_estimate=pl.CostEstimate(
            flops=20 * 10**9, bytes_accessed=25 * 10**6, transcendentals=5 * 10**6
        ),
    )(*given)


WIDER = -(-FS // 128) * 128


def refold(source, target, source_width, target_width):
    period = math.lcm(source_width, target_width)
    groups = source.shape[1] * source_width // period
    step_in, step_out = period // source_width, period // target_width
    lane = lax.broadcasted_iota(jnp.int32, (groups, 128), 1)
    for row in range(step_out):
        for tile in range(-(-target_width // 128)):
            begin = row * target_width + 128 * tile
            amount = min(128, target_width - 128 * tile)
            made, at = jnp.zeros((groups, 128), source.dtype), 0
            while at < amount:
                line, column = divmod(begin + at, source_width)
                where, lanes = divmod(column, 128)
                piece = source[where, pl.ds(line, groups, stride=step_in), :]
                if (at - lanes) % 128:
                    piece = pltpu.roll(piece, (at - lanes) % 128, 1)
                length = min(128 - lanes, source_width - column, amount - at)
                made = jnp.where((lane >= at) & (lane < at + length), piece, made)
                at += length
            target[tile, pl.ds(row, groups, stride=step_out), :] = made


def unpack_into(plan, layers, w_ref, *refs):
    place_ref, proj_ref, square, wide, folded, unfolded, small = refs[4 * layers :]
    for layer in range(layers):
        qkv_ref, out_ref, up_ref, down_ref = refs[4 * layer : 4 * layer + 4]
        for matrix, at, rows, block, line in plan:
            part = matrix - 6 * layer
            if not 0 <= part < 6:
                continue
            value = w_ref[block].astype(jnp.float32)[line : line + rows]
            if part < 4:
                square[part, at : at + rows, :] = value
            elif part == 4:
                for tile in range(-(-DS // 128)):
                    lanes = min(128, DS - 128 * tile)
                    folded[tile, at : at + rows, :lanes] = value[:, 128 * tile : 128 * tile + lanes]
            else:
                wide[at : at + rows, :] = value
        for part in range(3):
            qkv_ref[part] = square[part].astype(jnp.bfloat16)
        out_ref[...] = square[3].astype(jnp.bfloat16)
        refold(folded, unfolded, DS, FS)
        for tile in range(WIDER // 128):
            up_ref[:, 128 * tile : 128 * tile + 128] = unfolded[tile].astype(jnp.bfloat16)
        down_ref[:FS, :] = wide[...].astype(jnp.bfloat16)
        down_ref[FS:, :] = jnp.zeros((WIDER - FS, DS), jnp.bfloat16)
    for matrix, at, rows, block, line in plan:
        if matrix >= 6 * layers:
            value = w_ref[block].astype(jnp.float32)[line : line + rows]
            small[matrix - 6 * layers, at : at + rows, :] = value
    place_ref[...] = small[0, : place_ref.shape[0]].astype(jnp.bfloat16)
    proj_ref[...] = small[1].astype(jnp.bfloat16)


def unpack_shapes(layers, length):
    low = partial(jax.ShapeDtypeStruct, dtype=jnp.bfloat16)
    return (
        *[low((3, DS, DS)), low((DS, DS)), low((DS, WIDER)), low((WIDER, DS))] * layers,
        low((length, DS)),
        low((DT, DS)),
    )


def by_heads(value, heads):
    width = value.shape[1]
    size = width // heads
    lane = lax.broadcasted_iota(jnp.int32, (1, width), 1)
    nothing = jnp.zeros_like(value)
    return jnp.concatenate(
        [
            jnp.where((lane >= head * size) & (lane < (head + 1) * size), value, nothing)
            for head in range(heads)
        ]
    )


def student_kernel(
    plan, layers, token_ref, evec_ref, vec_ref, bias_ref, mask_ref, *refs,
):
    ready = 4 * layers + 2
    if plan:
        w_ref, *refs = refs
        unpack_into(plan, layers, w_ref, *refs[:ready], *refs[-5:])
    matrices, place_ref, refs = refs[: 4 * layers], refs[4 * layers], refs[ready:]
    emb_ref, zero_ref, zero_inv, last_ref = refs[:4]
    length = mask_ref.shape[1]
    size = DS // HS

    def tile(step, carry):
        at = pl.ds(pl.multiple_of(step * TILE, TILE), TILE)
        places = jnp.concatenate([place_ref[...].astype(jnp.float32)] * (TILE // length))
        hidden, normed, inverse = norm_forward(
            token_ref[at, :] + places, evec_ref[0:1, :], evec_ref[1:2, :]
        )
        emb_ref[at, :] = hidden
        zero_ref[at, :] = normed
        zero_inv[at, :] = inverse
        for layer in range(layers):
            qkv_w, out_w, up_w, down_w = matrices[4 * layer : 4 * layer + 4]
            low_ref, qkv_ref, context_ref, one_ref, one_inv, two_ref, two_inv = refs[
                4 + 7 * layer : 11 + 7 * layer
            ]

            def vector(index, layer=layer):
                return vec_ref[layer, index : index + 1, :]

            low = hidden.astype(jnp.bfloat16)
            low_ref[at, :] = low
            parts = []
            for part in range(3):
                made = jnp.dot(low, qkv_w[part], preferred_element_type=jnp.float32)
                if part != 1:
                    made = made + vector(part // 2)
                parts.append(made.astype(jnp.bfloat16))
                qkv_ref[part, at, :] = parts[part]
            contexts = []
            for row in range(TILE // length):
                span = slice(row * length, (row + 1) * length)
                here = pl.ds(pl.multiple_of(step * TILE + row * length, length), length)
                mask = mask_ref[here, :]
                q, k, v = (part[span] for part in parts)
                scores = back_product(q, by_heads(k, HS)) * size ** (-0.5)
                weights = jnp.concatenate(
                    [
                        softmax_low(scores[:, head * length : (head + 1) * length], mask)
                        for head in range(HS)
                    ],
                    1,
                )
                contexts.append(
                    jnp.dot(weights, by_heads(v, HS), preferred_element_type=jnp.float32)
                )
            context = jnp.concatenate(contexts).astype(jnp.bfloat16)
            context_ref[at, :] = context
            attended = jnp.dot(context, out_w[...], preferred_element_type=jnp.float32) + vector(2)
            middle, normed, inverse = norm_forward(hidden + attended, vector(3), vector(4))
            one_ref[at, :] = normed
            one_inv[at, :] = inverse
            inner = jnp.dot(
                middle.astype(jnp.bfloat16), up_w[...], preferred_element_type=jnp.float32
            ) + bias_ref[layer]
            outer = jnp.dot(
                gelu(inner).astype(jnp.bfloat16), down_w[...], preferred_element_type=jnp.float32
            ) + vector(5)
            hidden, normed, inverse = norm_forward(middle + outer, vector(6), vector(7))
            two_ref[at, :] = normed
            two_inv[at, :] = inverse
        last_ref[at, :] = hidden
        return carry

    lax.fori_loop(0, token_ref.shape[0] // TILE, tile, 0)


def student_forward(token_rows, evec, vectors, biases, mask, plan, blocks, matrices):
    tokens = token_rows.shape[0]
    layers = vectors.shape[0]
    full = partial(jax.ShapeDtypeStruct, dtype=jnp.float32)
    low = partial(jax.ShapeDtypeStruct, dtype=jnp.bfloat16)
    length = mask.shape[1]
    shapes = () if matrices else unpack_shapes(layers, length)
    made = (
        *shapes,
        full((tokens, DS)),
        full((tokens, DS)),
        full((tokens, 1)),
        full((tokens, DS)),
        *[
            low((tokens, DS)),
            low((3, tokens, DS)),
            low((tokens, DS)),
            full((tokens, DS)),
            full((tokens, 1)),
            full((tokens, DS)),
            full((tokens, 1)),
        ]
        * layers,
    )
    given = (token_rows, evec, vectors, biases, mask, *(matrices or [blocks]))
    all_of = pl.pallas_call(
        partial(student_kernel, plan, layers),
        out_shape=made,
        in_specs=[VMEM_SPEC] * len(given),
        out_specs=(VMEM_SPEC,) * len(made),
        scratch_shapes=(
            []
            if matrices
            else [
                pltpu.VMEM((4, DS, DS), jnp.float32),
                pltpu.VMEM((FS, DS), jnp.float32),
                pltpu.VMEM((-(-DS // 128), FS, 128), jnp.float32),
                pltpu.VMEM((WIDER // 128, DS, 128), jnp.float32),
                pltpu.VMEM((2, DT, DS), jnp.float32),
            ]
        ),
        compiler_params=pltpu.CompilerParams(vmem_limit_bytes=58 * 1024 * 1024),
        cost_estimate=pl.CostEstimate(
            flops=8 * 10**9, bytes_accessed=40 * 10**6, transcendentals=6 * 10**6
        ),
    )(*given)
    return list(all_of[: len(shapes)] or matrices), all_of[len(shapes) :]


def back_kernel(
    last, first_layer, grad_ref, vec_ref, bias_ref, mask_ref, qkv_w, out_w, up_w, down_w,
    low_ref, qkv_ref, context_ref, one_ref, one_inv, two_ref, two_inv, *refs,
):
    if first_layer:
        (more_ref, zero_ref, zero_inv, evec_ref), refs = refs[:4], refs[4:]
    if last:
        score_ref, count_ref, refs = refs[0], refs[1], refs[2:]
    hidden_ref, *weight_refs, vec_out, bias_out, refs = (*refs[:9], refs[9:])
    dq_ref, dk_ref, dv_ref, do_ref, du_ref, dd_ref = weight_refs
    if last:
        loss_ref, refs = refs[0], refs[1:]
        loss_ref[...] = jnp.zeros_like(loss_ref)
    if first_layer:
        (place_ref, edge_ref), refs = refs[:2], refs[2:]
        place_ref[...] = jnp.zeros_like(place_ref)
        edge_ref[...] = jnp.zeros_like(edge_ref)
    outer_s, attended_s, q_s, k_s, v_s, middle_s, active_s, inner_s, unfolded, folded = refs
    length = mask_ref.shape[1]
    size = DS // HS
    vec_out[...] = jnp.zeros_like(vec_out)
    bias_out[...] = jnp.zeros_like(bias_out)
    many = 256

    def vector(index):
        return vec_ref[index : index + 1, :]

    def note(index, value, to=vec_out):
        to[index : index + 1, :] += jnp.sum(value.astype(jnp.float32), 0, keepdims=True)

    def norm_back(grad, normed, inverse, gain, index, to=vec_out):
        d_normed = grad * gain
        note(index, grad * normed, to)
        note(index + 1, grad, to)
        return inverse * (
            d_normed
            - jnp.mean(d_normed, -1, keepdims=True)
            - normed * jnp.mean(d_normed * normed, -1, keepdims=True)
        )

    def tile(step, carry):
        at = pl.ds(pl.multiple_of(step * TILE, TILE), TILE)
        d_sum = norm_back(grad_ref[at, :], two_ref[at, :], two_inv[at, :], vector(6), 6)
        d_outer = d_sum.astype(jnp.bfloat16)
        outer_s[at, :] = d_outer
        note(5, d_outer)
        middle = (one_ref[at, :] * vector(3) + vector(4)).astype(jnp.bfloat16)
        middle_s[at, :] = middle
        d_middle = d_sum
        for first in range(0, WIDER, many):
            lanes = slice(first, first + many)
            inner = jnp.dot(
                middle, up_w[:, lanes], preferred_element_type=jnp.float32
            ) + bias_ref[:, lanes]
            squared = inner * inner
            bent = jnp.tanh(0.7978845608028654 * (inner + 0.044715 * squared * inner))
            active_s[at, lanes] = (0.5 * inner * (1.0 + bent)).astype(jnp.bfloat16)
            slope = 0.5 * (1.0 + bent) + 0.5 * inner * (1.0 - bent * bent) * (
                0.7978845608028654 * (1.0 + 3.0 * 0.044715 * squared)
            )
            d_inner = (back_product(d_outer, down_w[lanes, :]) * slope).astype(jnp.bfloat16)
            inner_s[at, lanes] = d_inner
            bias_out[:, lanes] += jnp.sum(d_inner.astype(jnp.float32), 0, keepdims=True)
            d_middle = d_middle + back_product(d_inner, up_w[:, lanes])
        d_one = norm_back(d_middle, one_ref[at, :], one_inv[at, :], vector(3), 3)
        d_attended = d_one.astype(jnp.bfloat16)
        attended_s[at, :] = d_attended
        note(2, d_attended)
        d_context = back_product(d_attended, out_w[...]).astype(jnp.bfloat16)
        for row in range(TILE // length):
            here = pl.ds(pl.multiple_of(step * TILE + row * length, length), length)
            mask = mask_ref[here, :]
            d_row = d_context[row * length : (row + 1) * length]
            q, k, v = (qkv_ref[part, here, :] for part in range(3))
            keys = by_heads(k, HS)
            scores = back_product(q, keys) * size ** (-0.5)
            d_weights = back_product(d_row, by_heads(v, HS))
            low_weights, d_scores = [], []
            for head in range(HS):
                lanes = slice(head * length, (head + 1) * length)
                masked = jnp.where(mask > 0.0, scores[:, lanes], NEG_LARGE)
                expo = jnp.exp(masked - jnp.max(masked, -1, keepdims=True))
                weights = expo * (1.0 / jnp.sum(expo, -1, keepdims=True))
                low_weights.append(weights.astype(jnp.bfloat16))
                turned = weights * d_weights[:, lanes]
                made = turned - weights * jnp.sum(turned, -1, keepdims=True)
                if last:
                    differ = jnp.where(mask > 1.0, scores[:, lanes] - score_ref[here, lanes], 0.0)
                    loss_ref[...] += jnp.sum(differ * differ, 0, keepdims=True)
                    made = made + differ * (2.0 / count_ref[...])
                d_scores.append(made.astype(jnp.bfloat16))
            scale = size ** (-0.5)
            q_s[here, :] = (
                jnp.dot(jnp.concatenate(d_scores, 1), keys, preferred_element_type=jnp.float32)
                * scale
            ).astype(jnp.bfloat16)
            k_s[here, :] = (
                outer_product(jnp.concatenate(d_scores), by_heads(q, HS)) * scale
            ).astype(jnp.bfloat16)
            v_s[here, :] = outer_product(
                jnp.concatenate(low_weights), by_heads(d_row, HS)
            ).astype(jnp.bfloat16)
        d_hidden = d_one
        for part, held in enumerate((q_s, k_s, v_s)):
            d_part = held[at, :]
            if part != 1:
                note(part // 2, d_part)
            d_hidden = d_hidden + back_product(d_part, qkv_w[part])
        if first_layer:
            d_hidden = norm_back(
                d_hidden + more_ref[at, :],
                zero_ref[at, :],
                zero_inv[at, :],
                evec_ref[0:1, :],
                0,
                edge_ref,
            )
            for row in range(TILE // length):
                place_ref[...] += d_hidden[row * length : (row + 1) * length]
        hidden_ref[at, :] = d_hidden
        return carry

    lax.fori_loop(0, grad_ref.shape[0] // TILE, tile, 0)
    low = low_ref[...]
    dq_ref[...] = outer_product(low, q_s[...])
    dk_ref[...] = outer_product(low, k_s[...])
    dv_ref[...] = outer_product(low, v_s[...])
    do_ref[...] = outer_product(context_ref[...], attended_s[...])
    for first in range(0, WIDER, many):
        lanes = slice(first, first + many)
        stop = min(first + many, FS)
        dd_ref[first:stop, :] = outer_product(active_s[:, lanes], outer_s[...])[: stop - first]
        made = outer_product(middle_s[...], inner_s[:, lanes])
        for tile_at in range(many // 128):
            unfolded[first // 128 + tile_at] = made[:, 128 * tile_at : 128 * tile_at + 128]
    refold(unfolded, folded, FS, DS)
    for tile_at in range(-(-DS // 128)):
        lanes = min(128, DS - 128 * tile_at)
        du_ref[:, 128 * tile_at : 128 * tile_at + lanes] = folded[tile_at, :, :lanes]


def student_backward(grad, vectors, biases, mask, matrices, saved, last, first_layer):
    tokens, length = mask.shape
    full = partial(jax.ShapeDtypeStruct, dtype=jnp.float32)
    made = [
        full((tokens, DS)),
        *[full((DS, DS))] * 4,
        full((FS, DS)),
        full((FS, DS)),
        full((8, DS)),
        full((1, WIDER)),
    ]
    given = [grad, vectors, biases, mask, *matrices, *saved]
    given += first_layer
    if last:
        given += last
        made.append(full((1, length)))
    if first_layer:
        made += [full((length, DS)), full((8, DS))]
    low = partial(pltpu.VMEM, dtype=jnp.bfloat16)
    return pl.pallas_call(
        partial(back_kernel, bool(last), bool(first_layer)),
        out_shape=tuple(made),
        in_specs=[VMEM_SPEC] * len(given),
        out_specs=(VMEM_SPEC,) * len(made),
        scratch_shapes=[
            *[low((tokens, DS))] * 6,
            *[low((tokens, WIDER))] * 2,
            pltpu.VMEM((WIDER // 128, DS, 128), jnp.float32),
            pltpu.VMEM((-(-DS // 128), FS, 128), jnp.float32),
        ],
        compiler_params=pltpu.CompilerParams(vmem_limit_bytes=58 * 1024 * 1024),
        cost_estimate=pl.CostEstimate(
            flops=10**9, bytes_accessed=4 * 10**6, transcendentals=3 * 10**5
        ),
    )(*given)


def d_all_width(width):
    return -(-width // 128) * 128


def head_kernel(
    groups, pair, denom, p_all, t_ref, table_ref, head_ref, d_ref, own_ref, w_ref, *refs
):
    (
        t_all, p_turned, t_turned, s_logits, t_logits, stats, rows_of, inbox, total,
        send, recv, stat_send, stat_recv, d_send, d_recv, pair_send, pair_recv, out_sem,
    ) = refs
    amount, width = p_all.shape[1:]
    vocab = table_ref.shape[0]
    z_size = z_size_of(groups)
    side = groups // z_size
    across = z_size * amount
    half = d_all_width(width)
    dp, me = lax.axis_index("dp"), lax.axis_index("fsdp")
    z, y = me // side, me % side
    sibling = (dp // 2 * 2 + 1 - dp % 2, me)
    beside = ((dp + 2) % lax.axis_size("dp"), me)
    barrier = pltpu.get_barrier_semaphore()
    for step in range(1, groups):
        pl.semaphore_signal(
            barrier, inc=1, device_id=(dp, (me + step) % groups), device_id_type=MESH
        )
    if pair:
        for other in (sibling, beside):
            pl.semaphore_signal(barrier, inc=1, device_id=other, device_id_type=MESH)
    pl.semaphore_wait(barrier, groups - 1 + (2 if pair else 0))

    def both(at, rank, target, own=False):
        return [
            pltpu.make_async_remote_copy(
                t_ref if own else t_all.at[at],
                t_all.at[at],
                send.at[rank],
                recv.at[rank],
                device_id=(dp, target),
                device_id_type=MESH,
            )
        ]

    def begin(copies):
        for copy in copies:
            copy.start()

    def received(copies):
        for copy in copies:
            copy.wait_recv()

    def sent(copies):
        for copy in copies:
            copy.wait_send()

    def line(step):
        return z + step, (z + step >= 0) & (z + step < z_size)

    def inside(position):
        return jnp.minimum(jnp.maximum(position, 0), z_size - 1) * side

    def z_copies(step, way, arriving):
        origin, known = line(-way * (step + (1 if arriving else 0)))
        target, there = line(way)
        rank = 2 * step + (1 if way > 0 else 0)
        made = both(inside(origin) + y, rank, inside(target) + y, own=step == 0 and not arriving)
        return made, known if arriving else known & there

    def y_copies(back, step, at, own=False):
        return both(
            at, 2 * z_size + (back - 1) * z_size + step, z * side + (y + back) % side, own
        )

    wide = next(size for size in (384, 320, 128) if vocab % size == 0)

    def measure(back):
        at_y = (y + side - back) % side
        slots = [line * side + at_y for line in range(z_size)]
        t_turned[...] = jnp.concatenate([t_all[at] for at in slots]).astype(jnp.float32).T.astype(
            jnp.bfloat16
        )
        p_turned[...] = jnp.concatenate([p_all[at] for at in slots]).astype(jnp.float32).T.astype(
            jnp.bfloat16
        )

        def step(index, carry):
            s_top, s_sum, t_top, t_sum, cross = carry
            lines = pl.ds(pl.multiple_of(index * wide, 64), wide)
            t_now = jnp.dot(head_ref[lines, :], t_turned[...], preferred_element_type=jnp.float32)
            s_now = jnp.dot(table_ref[lines, :], p_turned[...], preferred_element_type=jnp.float32)
            t_logits[back, lines, :] = t_now
            s_logits[back, lines, :] = s_now
            s_next = jnp.maximum(s_top, jnp.max(s_now, 0, keepdims=True))
            t_next = jnp.maximum(t_top, jnp.max(t_now, 0, keepdims=True))
            t_exp = jnp.exp(t_now - t_next)
            scale = jnp.exp(t_top - t_next)
            s_sum = s_sum * jnp.exp(s_top - s_next) + jnp.sum(
                jnp.exp(s_now - s_next), 0, keepdims=True
            )
            t_sum = t_sum * scale + jnp.sum(t_exp, 0, keepdims=True)
            cross = cross * scale + jnp.sum(t_exp * s_now, 0, keepdims=True)
            return (s_next, s_sum, t_next, t_sum, cross)

        lowest = jnp.full((1, across), -jnp.inf, jnp.float32)
        zero = jnp.zeros((1, across), jnp.float32)
        made = lax.fori_loop(0, vocab // wide, step, (lowest, zero, lowest, zero, zero))
        for index, value in enumerate(made):
            stats[me, at_y, index : index + 1, :] = value

    t_all[me] = t_ref[...]
    for way in (1, -1):
        made, wanted = z_copies(0, way, False)
        pl.when(wanted)(partial(begin, made))
    for back in range(1, side):
        begin(y_copies(back, z, me, own=True))
    for step in range(z_size - 1):
        for way in (1, -1):
            made, wanted = z_copies(step, way, True)
            onward, further = z_copies(step + 1, way, False) if step + 2 < z_size else (None, None)

            @pl.when(wanted)
            def _(made=made, onward=onward, further=further, step=step, way=way):
                received(made)
                if onward is not None:
                    pl.when(further)(partial(begin, onward))
                origin = z - way * (step + 1)
                for back in range(1, side):
                    begin(y_copies(back, origin, origin * side + y))

    for back in range(side):
        if back:
            for step in range(z_size):
                received(y_copies(back, step, step * side + (y + side - back) % side))
        measure(back)
    for step in range(z_size - 1):
        for way in (1, -1):
            made, wanted = z_copies(step, way, False)
            pl.when(wanted)(partial(sent, made))
    for back in range(1, side):
        for step in range(z_size):
            sent(y_copies(back, step, step * side + y))

    def stat_copy(step):
        return pltpu.make_async_remote_copy(
            stats.at[me],
            stats.at[me],
            stat_send.at[step],
            stat_recv.at[step],
            device_id=(dp, (me + step) % groups),
            device_id_type=MESH,
        )

    for step in range(1, groups):
        stat_copy(step).start()
    for step in range(1, groups):
        stat_copy(step).wait_recv()
    for back in range(side):
        at_y = (y + side - back) % side
        parts = [stats[other, at_y] for other in range(groups)]
        s_top, t_top = parts[0][0:1], parts[0][2:3]
        for part in parts[1:]:
            s_top = jnp.maximum(s_top, part[0:1])
            t_top = jnp.maximum(t_top, part[2:3])
        s_sum, t_sum, cross = (jnp.zeros_like(s_top) for unused in range(3))
        for part in parts:
            s_sum = s_sum + part[1:2] * jnp.exp(part[0:1] - s_top)
            scale = jnp.exp(part[2:3] - t_top)
            t_sum = t_sum + part[3:4] * scale
            cross = cross + part[4:5] * scale
        rows_of[back, 0:1, :] = s_top + jnp.log(s_sum)
        rows_of[back, 1:2, :] = t_top
        rows_of[back, 2:3, :] = 1.0 / t_sum
        rows_of[back, 3:4, :] = cross / t_sum
        total[back] = jnp.zeros((half, across), jnp.float32)
    own_ref[...] = rows_of[0]
    narrow = next(size for size in (320, 128) if vocab % size == 0)
    part = vocab // 4 if pair else vocab

    def rows_at(start, amount):
        return t_logits.at[0, pl.ds(pl.multiple_of(start, 64), amount), 0:half]

    def grade(first):
        def chunk(index, carry):
            lines = pl.ds(pl.multiple_of(first + index * narrow, 64), narrow)
            table = table_ref[lines, :]
            made = jnp.zeros((narrow, width), jnp.float32)
            for back in range(side):
                row = rows_of[back]
                grads = 2.0 * jnp.exp(s_logits[back, lines, :] - row[0:1])
                grads = grads - jnp.exp(t_logits[back, lines, :] - row[1:2]) * row[2:3]
                low = (grads * (1.0 / denom)).astype(jnp.bfloat16)
                total[back, :width, :] += outer_product(table, low)
                at_y = (y + side - back) % side
                states = jnp.concatenate([p_all[line * side + at_y] for line in range(z_size)])
                made = made + jnp.dot(low, states, preferred_element_type=jnp.float32)
            t_logits[0, lines, 0:width] = made
            return carry

        lax.fori_loop(0, part // narrow, chunk, 0)

    def pair_copy(index, source, target):
        return pltpu.make_async_remote_copy(
            source,
            inbox.at[index],
            pair_send.at[index],
            pair_recv.at[index],
            device_id=target,
            device_id_type=MESH,
        )

    given = []
    if pair:
        x, core = dp // 2, dp % 2
        far, near = 1 - x, x

        def start_of(along, other):
            return (2 * along + (core + other) % 2) * part

        for index, (along, other) in enumerate(((far, 1), (far, 0), (near, 1), (near, 0))):
            grade(start_of(along, other))
            if other:
                given.append(pair_copy(index // 2, rows_at(start_of(along, other), part), sibling))
                given[-1].start()
            elif along is far:
                given[0].wait_recv()
                lines = pl.ds(pl.multiple_of(start_of(far, 0), 64), part)
                t_logits[0, lines, 0:half] += inbox[0]
                given.append(pair_copy(2, rows_at(start_of(far, 0), part), beside))
                given[-1].start()
    else:
        grade(0)
    for back in range(side):
        turned = total[back].T.astype(jnp.bfloat16)
        for line in range(z_size):
            at = line * side + (y + side - back) % side
            t_all[at, :, half : 2 * half] = turned[line * amount : (line + 1) * amount]

    def d_copy(step):
        peer = (me + step) % groups
        return pltpu.make_async_remote_copy(
            t_all.at[peer, :, half : 2 * half],
            t_all.at[me, :, 0:half],
            d_send.at[step],
            d_recv.at[step],
            device_id=(dp, peer),
            device_id_type=MESH,
        )

    for step in range(1, groups):
        d_copy(step).start()
    made = t_all[me, :, half : 2 * half].astype(jnp.float32)
    for step in range(1, groups):
        d_copy(step).wait_recv()
        made = made + t_all[(me + groups - step) % groups, :, 0:half].astype(jnp.float32)
    d_ref[...] = made
    kept = 0
    if pair:
        kept = start_of(near, 0)
        lines = pl.ds(pl.multiple_of(kept, 64), part)
        given[2].wait_recv()
        t_logits[0, lines, 0:half] += inbox[1]
        given[1].wait_recv()
        t_logits[0, lines, 0:half] += inbox[2]
    out = pltpu.make_async_copy(rows_at(kept, part), w_ref, out_sem)
    out.start()
    for step in range(1, groups):
        stat_copy(step).wait_send()
        d_copy(step).wait_send()
    for copy in given:
        copy.wait_send()
    out.wait()


def head(picked, t_picked, table, teacher_head, denom, number):
    groups, n_dp = lax.axis_size("fsdp"), lax.axis_size("dp")
    pair = n_dp == 4
    amount, width = picked.shape[1:]
    vocab = table.shape[0]
    z_size = z_size_of(groups)
    side, across = groups // z_size, z_size * amount
    half = d_all_width(width)
    assert 2 * half <= DT
    full, low = jnp.float32, jnp.bfloat16
    anywhere = pl.BlockSpec(memory_space=pl.ANY)
    dma = pltpu.SemaphoreType.DMA
    made = [
        jax.ShapeDtypeStruct((amount, half), full),
        jax.ShapeDtypeStruct((8, across), full),
        jax.ShapeDtypeStruct((vocab // 4 if pair else vocab, half), full),
    ]
    return pl.pallas_call(
        partial(head_kernel, groups, pair, denom),
        out_shape=tuple(made),
        in_specs=[VMEM_SPEC] * 4,
        out_specs=(VMEM_SPEC, VMEM_SPEC) + (anywhere,) * (len(made) - 2),
        scratch_shapes=[
            pltpu.VMEM((groups, amount, DT), low),
            pltpu.VMEM((width, across), low),
            pltpu.VMEM((DT, across), low),
            pltpu.VMEM((side, vocab, across), full),
            pltpu.VMEM((side, vocab, across), full),
            pltpu.VMEM((groups, side, 8, across), full),
            pltpu.VMEM((side, 8, across), full),
            pltpu.VMEM((3, vocab // 4, half) if pair else (1, 8, 128), full),
            pltpu.VMEM((side, half, across), full),
            *[dma((2 * z_size + (side - 1) * z_size,))] * 2,
            *[dma((groups,))] * 4,
            *[dma((3,))] * 2,
            dma,
        ],
        compiler_params=pltpu.CompilerParams(
            collective_id=number, has_side_effects=True, vmem_limit_bytes=61 * 1024 * 1024
        ),
    )(picked, t_picked, table, teacher_head)


def three_parts(value):
    high = lax.reduce_precision(value, 8, 7)
    rest = value - high
    middle = lax.reduce_precision(rest, 8, 7)
    low = rest - middle
    return jnp.concatenate([high, middle, low], -1).astype(jnp.bfloat16)


def pick_exact(marks, value, turned=False):
    width = value.shape[1]
    terms = three_parts(value)
    made = outer_product(marks, terms) if turned else jnp.dot(
        marks, terms, preferred_element_type=jnp.float32
    )
    return made[:, :width] + made[:, width : 2 * width] + made[:, 2 * width :]


def plan_requests(ids, local_rows):
    order = lax.broadcasted_iota(jnp.int32, (ids.shape[0],), 0)
    same = ids[:, None] == ids[None, :]
    leader = jnp.min(jnp.where(same, order[None, :], ids.shape[0]), 1)
    leads = leader == order
    owner = ids // local_rows
    before = (
        (owner[:, None] == owner[None, :]) & leads[None, :] & (order[None, :] < leader[:, None])
    )
    rank = jnp.sum(before.astype(jnp.int32), 1)
    return (leads, owner, ids - owner * local_rows, rank)


def round_marks(plan, turn, devices):
    leads, owner, local_id, rank = plan
    inside = (rank >= turn * SLOTS) & (rank < (turn + 1) * SLOTS)
    slot = jnp.where(inside, owner * SLOTS + rank - turn * SLOTS, -1)
    line = lax.broadcasted_iota(jnp.int32, (devices * SLOTS, 1), 0)
    hit = line == slot[None, :]
    asked = jnp.max(jnp.where(hit & leads[None, :], local_id[None, :], -1), 1)
    return (hit.astype(jnp.bfloat16), asked.reshape(devices, 1, SLOTS))


def question(plan, turn, devices, extra):
    marks, asked = round_marks(plan, turn, devices)
    fill = jnp.full((devices, 1, 128 - SLOTS - extra.shape[0]), -1, jnp.int32)
    note = jnp.broadcast_to(extra[None, None, :], (devices, 1, extra.shape[0]))
    return (marks, jnp.concatenate([asked, note, fill], 2))


def ask(plan, turn, devices, extra):
    marks, asked = question(plan, turn, devices, extra)
    return (marks, exchange(asked, 0)[:, 0, :SLOTS].reshape(-1))


def wanted_marks(wanted, local_rows):
    return (wanted[:, None] == lax.broadcasted_iota(jnp.int32, (1, local_rows), 1)).astype(
        jnp.bfloat16
    )


def fetch(marks, wanted, table_low, devices):
    rows = jnp.dot(
        wanted_marks(wanted, table_low.shape[0]), table_low, preferred_element_type=jnp.float32
    ).astype(jnp.bfloat16)
    got = exchange(rows.reshape(devices, SLOTS, -1), 1)
    return outer_product(marks, got.reshape(devices * SLOTS, -1))


def give_back(marks, wanted, grads, local_rows, devices):
    sent = pick_exact(marks, grads)
    got = exchange(sent.reshape(devices, SLOTS, -1), 2)
    return pick_exact(wanted_marks(wanted, local_rows), got.reshape(devices * SLOTS, -1), True)


def finish_kernel(
    at, rows_ref, wanted_ref, more_ref, head_ref, reduced_ref, note_ref, g_ref, notes_ref, sent, send, recv
):
    count, me = notes_ref.shape[0], place_of()
    greet(count, me, True)
    value = rows_ref[...]
    width = value.shape[1]
    high = value.astype(jnp.bfloat16)
    rest = value - high.astype(jnp.float32)
    middle = rest.astype(jnp.bfloat16)
    low = (rest - middle.astype(jnp.float32)).astype(jnp.bfloat16)
    rows = g_ref.shape[0]
    step = next(size for size in (192, 120, 8) if rows % size == 0)
    squares = jnp.sum(reduced_ref[...] * reduced_ref[...], 0, keepdims=True)
    squares = jnp.sum(squares, 1, keepdims=True)
    line = lax.broadcasted_iota(jnp.int32, (step, value.shape[0]), 0)
    for first in range(0, rows, step):
        marks = jnp.where(line + first == wanted_ref[...], 1.0, 0.0).astype(jnp.bfloat16)
        made = more_ref[first : first + step, :] + head_ref[first : first + step, :width]
        for term in (high, middle, low):
            made = made + jnp.dot(marks, term, preferred_element_type=jnp.float32)
        g_ref[first : first + step, :] = made
        squares = squares + jnp.sum(jnp.sum(made * made, 0, keepdims=True), 1, keepdims=True)
    lane = lax.broadcasted_iota(jnp.int32, sent.shape, 1)
    note = jnp.where(lane == at, squares, note_ref[...])
    sent[...] = note
    notes_ref[me] = note

    def copy(step):
        return pltpu.make_async_remote_copy(
            sent,
            notes_ref.at[me],
            send.at[step],
            recv.at[step],
            device_id=member((me + step) % count, True),
            device_id_type=MESH,
        )

    def start(step, carry):
        copy(step).start()
        return carry

    def finish(step, carry):
        copy(step).wait()
        return carry

    lax.fori_loop(1, count, start, 0)
    lax.fori_loop(1, count, finish, 0)


def finish(row_blocks, wanted, more, head_grad, reduced, note, at, number):
    count = lax.axis_size("dp") * lax.axis_size("fsdp")
    dma = pltpu.SemaphoreType.DMA
    return pl.pallas_call(
        partial(finish_kernel, at),
        out_shape=(
            jax.ShapeDtypeStruct(more.shape, more.dtype),
            jax.ShapeDtypeStruct((count,) + note.shape, note.dtype),
        ),
        in_specs=[VMEM_SPEC] * 6,
        out_specs=(VMEM_SPEC,) * 2,
        scratch_shapes=[pltpu.VMEM(note.shape, note.dtype), dma((count,)), dma((count,))],
        compiler_params=pltpu.CompilerParams(
            collective_id=number, has_side_effects=True, vmem_limit_bytes=40 * 1024 * 1024
        ),
    )(row_blocks, wanted[None], more, head_grad, reduced, note)


def local(
    token_ids,
    valid_mask,
    seq_ids,
    mask_pos,
    mask_labels,
    teacher_in,
    teacher_flat,
    teacher_vec,
    teacher_head,
    emb_table,
    emb_first,
    emb_second,
    pos_table,
    pos_first,
    pos_second,
    layer_flat,
    layer_first,
    layer_second,
    proj_weight,
    proj_first,
    proj_second,
    layer_vec,
    vec_first,
    vec_second,
    misc_vec,
    misc_first,
    misc_second,
):
    micro, micro_rows, length = token_ids.shape
    rows = micro * micro_rows
    local_rows, width = emb_table.shape
    layers = layer_vec.shape[0]
    picks = mask_pos.shape[2]
    tokens = rows * length
    n_dp, groups = lax.axis_size("dp"), lax.axis_size("fsdp")
    place = lax.axis_index("fsdp")
    devices = n_dp * groups
    hidden_denom = float(rows * devices * length * DT)
    predict_denom = float(rows * devices * picks)
    flat_local = layer_flat.shape[1]
    by_rows = flat_local % DS == 0

    to_owner = [
        (d * groups + f, f * n_dp + d) for d in range(n_dp) for f in range(groups)
    ]
    from_owner = [(owner, holder) for holder, owner in to_owner]
    table_low = emb_table.astype(jnp.bfloat16)

    usable = valid_mask.reshape(rows, length) > 0
    docs = seq_ids.reshape(rows, length)
    same_doc = docs[:, :, None] == docs[:, None, :]
    pair_mask = same_doc & usable[:, :, None] & usable[:, None, :]
    allowed = pair_mask | jnp.eye(length, dtype=bool)
    ids = jnp.concatenate([token_ids.reshape(-1), mask_labels.reshape(-1)])
    plan = plan_requests(ids, local_rows)
    extra = jnp.stack([-1 - jnp.sum(pair_mask.astype(jnp.int32)), -1 - jnp.max(plan[3])])
    teacher_lines = teacher_flat.reshape(-1, DT)
    teacher_all = lax.all_gather(teacher_lines, BOTH, axis=0, tiled=True).reshape(-1, CHUNK, DT)
    own_parts = [
        layer_flat.astype(jnp.bfloat16),
        pos_table.astype(jnp.bfloat16),
        proj_weight.astype(jnp.bfloat16).T,
    ]
    if by_rows:
        chunk = flat_local // DS
        own_layers = [woven(part.reshape(-1, DS), False) for part in own_parts[0]]
        own_parts = [part.reshape(1, -1, DS) for part in own_layers + own_parts[1:]]
        line, lines = DS, sum(part.shape[1] for part in own_parts)
    else:
        own_parts = [part.reshape(1, -1) for part in own_parts]
        line, lines = 128, -(-sum(part.shape[1] for part in own_parts) // 128)
    block_rows = -(-lines // 16) * 16
    marks, asked = question(plan, 0, devices, extra)
    got, weights_all, token_blocks = entry(asked, pack(own_parts, line, block_rows)[0], table_low, 3)
    table_then = lax.optimization_barrier((table_low, got))[0]
    slice_part = lax.ppermute(table_then, BOTH, from_owner)
    wanted = got[:, 0, :SLOTS].reshape(-1)
    notes = got[:, 0, SLOTS : SLOTS + 2]
    count = jnp.sum(-1 - notes[:, 0]).astype(jnp.float32)
    rounds = jnp.max(-1 - notes[:, 1]) // SLOTS + 1
    all_rows = outer_product(marks, token_blocks.reshape(devices * SLOTS, width))

    def more_rows(state):
        turn, so_far = state
        marks_now, wanted_now = ask(plan, turn, devices, extra)
        return (turn + 1, so_far + fetch(marks_now, wanted_now, table_low, devices))

    all_rows = lax.while_loop(lambda state: state[0] < rounds, more_rows, (1, all_rows))[1]
    token_rows, label_rows = (all_rows[:tokens], all_rows[tokens:])
    pos_local, proj_local = pos_table.shape[0], proj_weight.shape[1]
    if by_rows:
        where, matrices = block_plan(devices, chunk, layers, (pos_local, proj_local)), []
    else:
        where = ()
        flat_all = weights_all.reshape(devices, -1)
        split = []
        for index in range(layers):
            wide = flat_all[:, index * flat_local : (index + 1) * flat_local].reshape(WIDE, DS)
            qkv, out, up, down = split_rows(wide, DS, FS)
            split.append(
                (
                    qkv.reshape(DS, 3, DS).transpose(1, 0, 2),
                    out,
                    jnp.pad(up, ((0, 0), (0, WIDER - FS))),
                    jnp.pad(down, ((0, WIDER - FS), (0, 0))),
                )
            )
        matrices = sum(map(list, split), [])
        start = layers * flat_local
        places_all = flat_all[:, start : start + pos_local * DS].reshape(length, DS)
        start += pos_local * DS
        matrices += [places_all, flat_all[:, start : start + proj_local * DS].reshape(DT, DS)]

    proj_bias = misc_vec[2 * DS :]
    evec = misc_vec[: 2 * DS].reshape(2, DS)
    cut = 5 * DS
    vectors = jnp.concatenate([layer_vec[:, :cut], layer_vec[:, cut + FS :]], 1).reshape(
        layers, 8, DS
    )
    biases = jnp.pad(layer_vec[:, cut : cut + FS], ((0, 0), (0, WIDER - FS)))[:, None]

    mask = jnp.where(pair_mask, 2.0, jnp.where(allowed, 1.0, 0.0)).reshape(tokens, length)
    matrices, made = student_forward(
        token_rows, evec, vectors, biases, mask, where, weights_all, matrices
    )
    embedded, normed_zero, inverse_zero, hidden, *saved = made
    proj_all = matrices[-1]
    slice_part = lax.optimization_barrier((slice_part, teacher_all, hidden))[0]
    slice_table = lax.all_gather(slice_part, "dp", axis=0, tiled=True)

    flat_pick = (
        jnp.arange(rows, dtype=jnp.int32)[:, None] * length + mask_pos.reshape(rows, picks)
    ).reshape(-1)
    weight = valid_mask.reshape(tokens, 1).astype(jnp.float32)
    t_scores, back_zero, back_last, grad_proj, grad_bias, squares_of, picked_all, t_picked = (
        teacher_forward(
            teacher_in.reshape(tokens, DT),
            teacher_all,
            teacher_vec.astype(jnp.float32)[None],
            mask,
            embedded,
            hidden,
            proj_all,
            proj_bias[None],
            weight,
            flat_pick[:, None],
            hidden_denom,
        )
    )
    hidden_sum = jnp.sum(squares_of) / hidden_denom
    pick_marks = (flat_pick[:, None] == lax.broadcasted_iota(jnp.int32, (1, tokens), 1)).astype(
        jnp.bfloat16
    )
    picked = lax.dynamic_index_in_dim(picked_all, place, 0, False)
    d_picked, own_stats, head_grad = head(
        picked_all, t_picked, slice_table, teacher_head, predict_denom, 4
    )
    own_z = place // (groups // z_size_of(groups))
    own_stats = lax.dynamic_slice_in_dim(own_stats, own_z * rows * picks, rows * picks, 1)
    picked_wide = picked.astype(jnp.float32)
    target_logit = jnp.sum(picked_wide * label_rows, -1)
    predict_sum = (
        jnp.sum(2.0 * own_stats[0] - own_stats[3] - target_logit) / predict_denom
    )
    d_picked = d_picked[:, :width] - label_rows / predict_denom
    d_hidden = pick_exact(pick_marks, d_picked, True) + back_last

    if n_dp != 4:
        head_grad = lax.psum_scatter(head_grad, "dp", scatter_dimension=0, tiled=True)

    matrix_grads = [None] * layers
    vector_grads = [None] * layers
    attention_sum = jnp.float32(0.0)
    head_grad = lax.ppermute(head_grad, BOTH, to_owner)
    for layer_index in reversed(range(layers)):
        d_hidden, *others = student_backward(
            d_hidden,
            vectors[layer_index],
            biases[layer_index],
            mask,
            matrices[4 * layer_index : 4 * layer_index + 4],
            saved[7 * layer_index : 7 * layer_index + 7],
            [t_scores, count.reshape(1, 1)] if layer_index == layers - 1 else [],
            [] if layer_index else [back_zero, normed_zero, inverse_zero, evec],
        )
        matrix_grads[layer_index] = others[:6]
        d_vectors, d_bias_up, more = others[6], others[7], others[8:]
        d_vectors = d_vectors.reshape(-1)
        vector_grads[layer_index] = jnp.concatenate(
            [d_vectors[:cut], d_bias_up[0, :FS], d_vectors[cut:]]
        )
        if layer_index == layers - 1:
            attention_sum = jnp.sum(more.pop(0)) / count
    d_hidden, head_grad = lax.optimization_barrier((d_hidden, head_grad))
    d_token, (grad_places, d_edge) = d_hidden, more

    row_grads = jnp.concatenate([d_token, -picked_wide / predict_denom])
    def more_grads(state):
        turn, so_far = state
        marks_now, wanted_now = ask(plan, turn, devices, extra)
        return (
            turn + 1,
            so_far + give_back(marks_now, wanted_now, row_grads, local_rows, devices),
        )

    grad_small = jnp.concatenate(vector_grads + [d_edge[0], d_edge[1], grad_bias[0]])
    small_local = -(-grad_small.shape[0] // devices)
    small_local = -(-small_local // DS) * DS
    small_padded = jnp.pad(grad_small, (0, devices * small_local - grad_small.shape[0]))
    rest = [grad_places, grad_proj, small_padded.reshape(-1, DS)]
    sizes = [flat_local] * layers + [part.size // devices for part in rest]
    lines = -(-sum(sizes) // line)
    block = (-(-lines // 8) * 8, line)
    sent = pick_exact(marks, row_grads).reshape(devices, SLOTS, width)
    if by_rows:
        amounts = [size // DS for size in sizes[layers:]]
        grad_parts = sum(matrix_grads, []) + rest
        block_rows_of = block_plan(devices, chunk, layers, amounts)
    else:
        wides = []
        for grads in matrix_grads:
            first = jnp.stack(grads[:3], 1).reshape(-1, width)
            wides.append(jnp.concatenate([first, *grads[3:]]))
        grad_parts = [pack([part.reshape(devices, -1) for part in wides + rest], *block[::-1])]
        block_rows_of = ()
    reduced, row_blocks = reduce(grad_parts, block_rows_of, block, sent, 7)
    more = jnp.zeros((local_rows, width), jnp.float32)
    more = lax.while_loop(lambda state: state[0] < rounds, more_grads, (1, more))[1]
    if by_rows:
        pieces = []
        start = 0
        for size in sizes:
            pieces.append(reduced[start : start + size // DS])
            start += size // DS
    else:
        pieces = cut_pieces(reduced.reshape(-1), sizes)
    if by_rows:
        pieces[:layers] = [woven(piece, True) for piece in pieces[:layers]]
    layer_acc = jnp.stack([piece.reshape(-1) for piece in pieces[:layers]])
    g_places = pieces[layers].reshape(pos_local, DS)
    g_proj = pieces[layers + 1].reshape(proj_local, DS).T
    small_part = pieces[layers + 2].reshape(-1)
    note = jnp.concatenate(
        [small_part, (attention_sum + hidden_sum + predict_sum).reshape(1)]
    )
    note = jnp.pad(note, (0, -(-(small_local + 2) // 128) * 128 - note.shape[0])).reshape(1, -1)
    g_table, notes_all = finish(
        row_blocks.reshape(devices * SLOTS, width),
        wanted,
        more,
        head_grad,
        reduced,
        note,
        small_local + 1,
        8,
    )
    notes_all = notes_all[:, 0]
    small = notes_all[:, :small_local].reshape(-1)
    loss = jnp.sum(notes_all[:, small_local])
    norm = jnp.sqrt(jnp.sum(notes_all[:, small_local + 1]))
    g_vec = small[: layer_vec.size].reshape(layer_vec.shape)
    g_misc = small[layer_vec.size : layer_vec.size + misc_vec.shape[0]]
    factor = CLIP_NORM / jnp.maximum(norm, CLIP_NORM)
    return (
        loss,
        count,
        norm,
        *adam_update(emb_table, emb_first, emb_second, g_table * factor),
        *adam_update(pos_table, pos_first, pos_second, g_places * factor),
        *adam_update(layer_flat, layer_first, layer_second, layer_acc * factor),
        *adam_update(proj_weight, proj_first, proj_second, g_proj * factor),
        *adam_update(layer_vec, vec_first, vec_second, g_vec * factor),
        *adam_update(misc_vec, misc_first, misc_second, g_misc * factor),
    )


def solution(mesh):
    rows, lines, flat, tail, every = (
        P(None, BOTH),
        P(BOTH, None),
        P(BOTH),
        P(None, BOTH),
        P(),
    )
    placed = (
        *[rows] * 6,
        flat,
        every,
        P("fsdp", None),
        *[lines] * 6,
        *[tail] * 6,
        *[every] * 6,
    )
    return jax.shard_map(
        local,
        mesh=mesh,
        in_specs=placed,
        out_specs=(*[every] * 3, *[lines] * 6, *[tail] * 6, *[every] * 6),
        check_vma=False,
    )
```

```python
import math
from functools import partial

import jax
import jax.numpy as jnp
from jax import lax
from jax.experimental import pallas as pl
from jax.experimental.pallas import tpu as pltpu
from jax.sharding import PartitionSpec as P

DS = 312
HS = 12
FS = 1200
DT = 768
HT = 12
FT = 3072
STEP = 5


NORM_EPS = 1e-06
CLIP_NORM = 0.05
LEARN_RATE = 0.05
BETA_ONE = 0.9
BETA_TWO = 0.999
ADAM_EPS = 1e-06
WEIGHT_DECAY = 0.01
NEG_LARGE = -1e30

BOTH = ("dp", "fsdp")
MESH = pl.DeviceIdType.MESH
SLOTS = 48
WIDE = 3 * DS + DS + 2 * FS


def z_size_of(fsdp):
    return 4 if fsdp % 4 == 0 else 1


def place_of():
    fsdp = lax.axis_size("fsdp")
    return lax.axis_index("dp") * fsdp + lax.axis_index("fsdp")


def member(index, whole):
    fsdp = lax.axis_size("fsdp")
    if whole:
        return (index // fsdp, index % fsdp)
    return (lax.axis_index("dp"), index)


def greet(count, me, whole):
    barrier = pltpu.get_barrier_semaphore()

    def signal(step, carry):
        pl.semaphore_signal(
            barrier, inc=1, device_id=member((me + step) % count, whole), device_id_type=MESH
        )
        return carry

    lax.fori_loop(1, count, signal, 0)
    pl.semaphore_wait(barrier, count - 1)


def exchange_kernel(count, whole, spread, x_ref, o_ref, send, recv, local_sem):
    me = place_of() if whole else lax.axis_index("fsdp")
    own = pltpu.make_async_copy(x_ref if spread else x_ref.at[me], o_ref.at[me], local_sem)
    own.start()
    greet(count, me, whole)

    def copy(step):
        peer = (me + step) % count
        return pltpu.make_async_remote_copy(
            x_ref if spread else x_ref.at[peer],
            o_ref.at[me],
            send.at[step],
            recv.at[step],
            device_id=member(peer, whole),
            device_id_type=MESH,
        )

    def start(step, carry):
        copy(step).start()
        return carry

    def finish(step, carry):
        copy(step).wait()
        return carry

    lax.fori_loop(1, count, start, 0)
    own.wait()
    lax.fori_loop(1, count, finish, 0)


def exchange(x, number, whole=True, spread=False):
    count = lax.axis_size("fsdp") * (lax.axis_size("dp") if whole else 1)
    return pl.pallas_call(
        partial(exchange_kernel, count, whole, spread),
        out_shape=jax.ShapeDtypeStruct(((count,) if spread else ()) + x.shape, x.dtype),
        in_specs=[pl.BlockSpec(memory_space=pl.ANY)],
        out_specs=pl.BlockSpec(memory_space=pl.ANY),
        scratch_shapes=[
            pltpu.SemaphoreType.DMA((count,)),
            pltpu.SemaphoreType.DMA((count,)),
            pltpu.SemaphoreType.DMA,
        ],
        compiler_params=pltpu.CompilerParams(collective_id=number, has_side_effects=True),
    )(x)


VMEM_SPEC = pl.BlockSpec(memory_space=pltpu.VMEM)


class Grid:
    def __init__(self):
        self.fsdp = lax.axis_size("fsdp")
        self.z_size = z_size_of(self.fsdp)
        self.side = self.fsdp // self.z_size
        assert lax.axis_size("dp") == 2 * self.side
        dp, fsdp = lax.axis_index("dp"), lax.axis_index("fsdp")
        self.x, self.core = dp // 2, dp % 2
        self.z, self.y = fsdp // self.side, fsdp % self.side
        side, z_size = self.side, self.z_size
        self.keys = [(g, b, a) for g in range(side) for b in range(side) for a in range(z_size)]
        self.rank = {key: index for index, key in enumerate(self.keys)}
        self.count = len(self.keys)

    def at(self, third, second, z, other=0):
        core = (self.core + other) % 2
        x = (self.x + third * (1 - core) + second * core) % self.side
        y = (self.y + second * (1 - core) + third * core) % self.side
        return (x * 2 + core, ((self.z + z) % self.z_size) * self.side + y)

    def index(self, third, second, z, other=0):
        dp, fsdp = self.at(third, second, z, other)
        return dp * self.fsdp + fsdp

    def neighbours(self):
        return (
            [(0, 0, a, 0) for a in range(1, self.z_size)]
            + [(0, b, 0, 0) for b in range(1, self.side)]
            + [(g, 0, 0, 0) for g in range(1, self.side)]
            + [(0, 0, 0, 1)]
        )

    def greet(self):
        barrier = pltpu.get_barrier_semaphore()
        around = self.neighbours()
        for where in around:
            pl.semaphore_signal(barrier, inc=1, device_id=self.at(*where), device_id_type=MESH)
        pl.semaphore_wait(barrier, len(around))


class Spread:
    def __init__(self, grid, x_ref, o_ref, send, recv, local_sem):
        self.grid, self.x_ref, self.o_ref = grid, x_ref, o_ref
        self.send, self.recv = send, recv
        self.started = []
        self.own = pltpu.make_async_copy(x_ref, o_ref.at[self.slot((0, 0, 0))], local_sem)
        self.own.start()

    def slot(self, key, other=0):
        grid = self.grid
        third, second, z = key
        return grid.index(grid.side - third, grid.side - second, grid.z_size - z, other)

    def push(self, key, name, where):
        grid = self.grid
        index = grid.rank[name] + (grid.count if where[3] else 0)
        copy = pltpu.make_async_remote_copy(
            self.x_ref if key == (0, 0, 0) else self.o_ref.at[self.slot(key)],
            self.o_ref.at[self.slot(key)],
            self.send.at[index],
            self.recv.at[index],
            device_id=grid.at(*where),
            device_id_type=MESH,
        )
        copy.start()
        self.started.append(copy)

    def forward(self, key):
        grid = self.grid
        third, second, z = key
        if key == (0, 0, 0):
            for step in range(1, grid.z_size):
                self.push(key, (0, 0, step), (0, 0, step, 0))
        if third == 0 and second == 0:
            for step in range(1, grid.side):
                self.push(key, (0, step, z), (0, step, 0, 0))
        if third == 0:
            for step in range(1, grid.side):
                self.push(key, (step, second, z), (step, 0, 0, 0))
        self.push(key, key, (0, 0, 0, 1))

    def arrived(self, key, other=0):
        grid = self.grid
        index = grid.rank[key] + (grid.count if other else 0)
        pltpu.make_async_remote_copy(
            self.o_ref.at[self.slot(key, other)],
            self.o_ref.at[self.slot(key, other)],
            self.send.at[index],
            self.recv.at[index],
            device_id=grid.at(0, 0, 0, 1),
            device_id_type=MESH,
        ).wait_recv()

    def start(self):
        self.forward((0, 0, 0))

    def middle(self):
        for key in self.grid.keys[1:]:
            self.arrived(key)
            self.forward(key)

    def finish(self):
        for key in self.grid.keys:
            self.arrived(key, 1)
        self.own.wait()
        for copy in self.started:
            copy.wait_send()


def entry_kernel(
    ask_ref, w_ref, table_ref, got_ref, all_ref, rows_ref, sent, asks, *sems
):
    ask_send, ask_recv, ask_local, w_send, w_recv, w_local, row_send, row_recv, row_local, out_sem = sems
    grid = Grid()
    count = 2 * grid.count
    me = place_of()
    own = pltpu.make_async_copy(ask_ref.at[me], asks.at[me], ask_local)
    own.start()
    greet(count, me, True)

    def ask_copy(step):
        peer = (me + step) % count
        return pltpu.make_async_remote_copy(
            ask_ref.at[peer],
            asks.at[me],
            ask_send.at[step],
            ask_recv.at[step],
            device_id=member(peer, True),
            device_id_type=MESH,
        )

    def row_copy(step):
        peer = (me + step) % count
        return pltpu.make_async_remote_copy(
            sent.at[peer],
            rows_ref.at[me],
            row_send.at[step],
            row_recv.at[step],
            device_id=member(peer, True),
            device_id_type=MESH,
        )

    def each(first, action):
        def body(step, carry):
            action(step)
            return carry

        lax.fori_loop(first, count, body, 0)

    each(1, lambda step: ask_copy(step).start())
    spread = Spread(grid, w_ref, all_ref, w_send, w_recv, w_local)
    spread.start()
    own.wait()
    table = table_ref[...]
    line = lax.broadcasted_iota(jnp.int32, (table.shape[0], 128), 0)

    def answer(source):
        marks = jnp.where(line == asks[source], 1.0, 0.0).astype(jnp.bfloat16)
        sent[source] = outer_product(marks, table)[:SLOTS].astype(jnp.bfloat16)

    answer(me)
    mine = pltpu.make_async_copy(sent.at[me], rows_ref.at[me], row_local)
    mine.start()

    def serve(step):
        ask_copy(step).wait_recv()
        answer((me + count - step) % count)

    each(1, serve)
    each(1, lambda step: row_copy(step).start())
    keep = pltpu.make_async_copy(asks, got_ref, out_sem)
    keep.start()
    spread.middle()
    spread.finish()
    mine.wait()
    keep.wait()
    each(1, lambda step: row_copy(step).wait())
    each(1, lambda step: ask_copy(step).wait_send())


def entry(asked, weights, table_low, number):
    count = asked.shape[0]
    width = table_low.shape[1]
    anywhere = pl.BlockSpec(memory_space=pl.ANY)
    dma = pltpu.SemaphoreType.DMA
    return pl.pallas_call(
        entry_kernel,
        out_shape=(
            jax.ShapeDtypeStruct(asked.shape, asked.dtype),
            jax.ShapeDtypeStruct((count,) + weights.shape, weights.dtype),
            jax.ShapeDtypeStruct((count, SLOTS, width), table_low.dtype),
        ),
        in_specs=[anywhere, anywhere, pl.BlockSpec(memory_space=pltpu.VMEM)],
        out_specs=(anywhere, VMEM_SPEC, VMEM_SPEC),
        scratch_shapes=[
            pltpu.VMEM((count, SLOTS, width), table_low.dtype),
            pltpu.VMEM(asked.shape, asked.dtype),
            *[dma((count,)), dma((count,)), dma] * 3,
            dma,
        ],
        compiler_params=pltpu.CompilerParams(
            collective_id=number, has_side_effects=True, vmem_limit_bytes=32 * 1024 * 1024
        ),
    )(asked, weights, table_low)


def reduce_kernel(plan, sources, *refs):
    ins, rest = refs[:sources], refs[sources:]
    row_ref, o_ref, got_ref = rest[:3]
    if plan:
        x_ref, rest = rest[3], rest[1:]
    else:
        x_ref = ins[0]
    held, third_in, second_in, z_in, send, recv, row_send, row_recv, row_local = rest[3:]
    grid = Grid()
    side, z_size, count, rank = grid.side, grid.z_size, grid.count, grid.rank
    order = sorted(grid.keys, key=lambda key: (key[0] == 0, key[1] == 0, key[2] == 0))
    devices = 2 * count
    me = place_of()
    own = pltpu.make_async_copy(row_ref.at[me], got_ref.at[me], row_local)
    own.start()
    greet(devices, me, True)

    def row_copy(step):
        peer = (me + step) % devices
        return pltpu.make_async_remote_copy(
            row_ref.at[peer],
            got_ref.at[me],
            row_send.at[step],
            row_recv.at[step],
            device_id=member(peer, True),
            device_id_type=MESH,
        )

    def row_start(step, carry):
        row_copy(step).start()
        return carry

    def row_finish(step, carry):
        row_copy(step).wait()
        return carry

    lax.fori_loop(1, devices, row_start, 0)
    started = []

    def push(source, target, index, where):
        copy = pltpu.make_async_remote_copy(
            source,
            target,
            send.at[index],
            recv.at[index],
            device_id=grid.at(*where),
            device_id_type=MESH,
        )
        copy.start()
        started.append(copy)

    def arrived(target, index):
        pltpu.make_async_remote_copy(
            target,
            target,
            send.at[index],
            recv.at[index],
            device_id=grid.at(0, 0, 0, 1),
            device_id_type=MESH,
        ).wait_recv()

    for source, at, rows, block, line in plan:
        value = jnp.zeros((rows, x_ref.shape[2]), x_ref.dtype)
        if source >= 0:
            value = ins[source][at : at + rows, :]
        x_ref[block, line : line + rows, :] = value
    for key in order:
        push(x_ref.at[grid.index(*key, 1)], held.at[rank[key]], rank[key], (0, 0, 0, 1))
    from_third = {}
    from_second = {}
    from_z = {}
    index = count
    for step in range(1, side):
        for second in range(side):
            for z in range(z_size):
                from_third[step, second, z] = (
                    third_in.at[((step - 1) * side + second) * z_size + z],
                    index,
                )
                index += 1
    for step in range(1, side):
        for z in range(z_size):
            from_second[step, z] = (second_in.at[(step - 1) * z_size + z], index)
            index += 1
    for way in (1, -1):
        for distance in range(z_size - 1):
            from_z[way, distance] = (z_in.at[len(from_z)], index)
            index += 1

    def gathered(key):
        third, second, z = key
        arrived(held.at[rank[key]], rank[key])
        total = held[rank[key]] + x_ref[grid.index(*key)]
        if third == 0:
            for step in range(1, side):
                arrived(*from_third[step, second, z])
                total = total + from_third[step, second, z][0][...]
        if third == 0 and second == 0:
            for step in range(1, side):
                arrived(*from_second[step, z])
                total = total + from_second[step, z][0][...]
        return total

    for key in order:
        third, second, z = key
        if third == 0 and second == 0:
            continue
        held[rank[key]] = gathered(key)
        if third:
            target, where = from_third[third, second, z], (third, 0, 0, 0)
        else:
            target, where = from_second[second, z], (0, second, 0, 0)
        push(held.at[rank[key]], target[0], target[1], where)

    def behind(way):
        return (grid.z > 0) if way > 0 else (grid.z < z_size - 1)

    def hop(way, distance):
        target = from_z[way, distance - 1]
        return pltpu.make_async_remote_copy(
            held.at[rank[0, 0, way * distance % z_size]],
            target[0],
            send.at[target[1]],
            recv.at[target[1]],
            device_id=grid.at(0, 0, way % z_size),
            device_id_type=MESH,
        )

    def reaches(way, distance):
        return (grid.z + way * distance >= 0) & (grid.z + way * distance < z_size)

    for distance in range(z_size - 1, 0, -1):
        for way in (1, -1):

            @pl.when(reaches(way, distance))
            def _(way=way, distance=distance):
                key = (0, 0, way * distance % z_size)
                held[rank[key]] = gathered(key)
                if distance < z_size - 1:

                    @pl.when(behind(way))
                    def _():
                        arrived(*from_z[way, distance])
                        held[rank[key]] += from_z[way, distance][0][...]

                hop(way, distance).start()

    o_ref[...] = gathered((0, 0, 0))
    for way in (1, -1):

        @pl.when(behind(way))
        def _(way=way):
            arrived(*from_z[way, 0])
            o_ref[...] += from_z[way, 0][0][...]

    for distance in range(z_size - 1, 0, -1):
        for way in (1, -1):
            pl.when(reaches(way, distance))(hop(way, distance).wait_send)
    for copy in started:
        copy.wait_send()
    own.wait()
    lax.fori_loop(1, devices, row_finish, 0)


def reduce(parts, plan, block, rows, number):
    count = lax.axis_size("dp") * lax.axis_size("fsdp")
    side = lax.axis_size("dp") // 2
    z_size = count // 2 // side // side
    kind = parts[0].dtype
    vmem, anywhere = pl.BlockSpec(memory_space=pltpu.VMEM), pl.BlockSpec(memory_space=pl.ANY)
    dma = pltpu.SemaphoreType.DMA
    return pl.pallas_call(
        partial(reduce_kernel, plan, len(parts)),
        out_shape=(
            jax.ShapeDtypeStruct(block, kind),
            jax.ShapeDtypeStruct(rows.shape, rows.dtype),
        ),
        in_specs=[vmem] * len(parts) + [anywhere],
        out_specs=(vmem, anywhere),
        scratch_shapes=[
            *([pltpu.VMEM((count,) + block, kind)] if plan else []),
            pltpu.VMEM((count // 2,) + block, kind),
            pltpu.VMEM(((side - 1) * side * z_size,) + block, kind),
            pltpu.VMEM(((side - 1) * z_size,) + block, kind),
            pltpu.VMEM((2 * (z_size - 1),) + block, kind),
            *[dma((count + z_size,))] * 2,
            *[dma((count,))] * 2,
            dma,
        ],
        compiler_params=pltpu.CompilerParams(
            collective_id=number, has_side_effects=True, vmem_limit_bytes=58 * 1024 * 1024
        ),
    )(*parts, rows)


def woven(block, weave):
    chunk = block.shape[0]
    me = place_of()
    made = block
    for index in range(-(-3 * DS // chunk)):
        amount = min(chunk, 3 * DS - index * chunk)
        head = block[:amount].reshape((3, amount // 3, DS) if weave else (amount // 3, 3, DS))
        head = head.transpose(1, 0, 2).reshape(amount, DS)
        if index == 0:
            made = jnp.where(me < 3 * DS // chunk, head, made)
        elif amount < chunk:
            made = jnp.where(me == index, jnp.concatenate([head, block[amount:]]), made)
    return made


def block_plan(devices, chunk, layers, others):
    plan = []
    for block in range(devices):
        for layer in range(layers):
            base = 6 * layer
            row, end, line = block * chunk, (block + 1) * chunk, layer * chunk
            first = row
            if row < 3 * DS:
                stop = min(end, 3 * DS)
                amount = (stop - row) // 3
                for part in range(3):
                    plan.append((base + part, row // 3, amount, block, line + part * amount))
                row = stop
            for part, start, size in ((3, 3 * DS, DS), (4, 4 * DS, FS), (5, 4 * DS + FS, FS)):
                stop = min(end, start + size)
                if row < stop:
                    where = line + row - first
                    plan.append((base + part, row - start, stop - row, block, where))
                    row = stop
        line = layers * chunk
        for index, amount in enumerate(others):
            plan.append((6 * layers + index, block * amount, amount, block, line))
            line += amount
        spare = -line % 8
        if spare:
            plan.append((-1, 0, spare, block, line))
    return tuple(plan)


def pack(parts, width, rows):
    count = parts[0].shape[0]
    if all(part.ndim == 3 for part in parts):
        joined = jnp.concatenate(parts, 1)
        return jnp.pad(joined, ((0, 0), (0, rows - joined.shape[1]), (0, 0)))
    joined = jnp.concatenate([part.reshape(count, -1) for part in parts], 1)
    joined = jnp.pad(joined, ((0, 0), (0, rows * width - joined.shape[1])))
    return joined.reshape(count, rows, width)


def outer_product(left, right):
    return lax.dot_general(
        left, right, (((0,), (0,)), ((), ())), preferred_element_type=jnp.float32
    )


def back_product(grad, weight):
    return lax.dot_general(
        grad, weight, (((1,), (1,)), ((), ())), preferred_element_type=jnp.float32
    )


def norm_forward(value, gain, bias):
    average = jnp.mean(value, -1, keepdims=True)
    centered = value - average
    inverse = lax.rsqrt(jnp.mean(centered * centered, -1, keepdims=True) + NORM_EPS)
    normed = centered * inverse
    return (normed * gain + bias, normed, inverse)


def cut_pieces(vector, sizes):
    pieces = []
    start = 0
    for amount in sizes:
        pieces.append(vector[..., start : start + amount])
        start += amount
    return pieces


def split_rows(wide, width, hidden):
    first, second, third = 3 * width, 4 * width, 4 * width + hidden
    return (
        wide[:first].reshape(width, 3 * width),
        wide[first:second],
        wide[second:third].reshape(width, hidden),
        wide[third:],
    )


def adam_update(value, first, second, grad):
    first = BETA_ONE * first + (1.0 - BETA_ONE) * grad
    second = BETA_TWO * second + (1.0 - BETA_TWO) * grad * grad
    ratio = first / (1.0 - BETA_ONE**STEP) / (jnp.sqrt(second / (1.0 - BETA_TWO**STEP)) + ADAM_EPS)
    return (first, second, value - LEARN_RATE * (ratio + WEIGHT_DECAY * value))


def gelu(value):
    return 0.5 * value * (1.0 + jnp.tanh(0.7978845608028654 * (value + 0.044715 * value * value * value)))


def regroup(weights, group):
    amount = weights.shape[0]
    made = lax.broadcasted_iota(jnp.int32, (amount, amount), 0)
    taken = lax.broadcasted_iota(jnp.int32, (amount, amount), 1)
    inner = amount // group
    marks = jnp.where((made % inner) * group + made // inner == taken, 1.0, 0.0)
    return jnp.dot(
        marks.astype(jnp.bfloat16), weights, preferred_element_type=jnp.float32
    ).astype(jnp.bfloat16)


def softmax_low(scores, mask):
    masked = jnp.where(mask > 0.0, scores, NEG_LARGE)
    expo = jnp.exp(masked - jnp.max(masked, -1, keepdims=True))
    return (expo * (1.0 / jnp.sum(expo, -1, keepdims=True))).astype(jnp.bfloat16)


TILE = 256
CHUNK = 96


def teacher_kernel(
    denom, x_ref, w_ref, vec_ref, mask_ref, zero_ref, last_ref, proj_ref, bias_ref, weight_ref, pick_ref,
    s_ref, back_zero, back_last, proj_out, bias_out, loss_ref, picked_ref, t_picked_ref,
    low_ref, qkv_ref, up_ref, context_ref, sent, send, recv,
):
    size = DT // HT
    tokens = x_ref.shape[0]
    line = lax.broadcasted_iota(jnp.int32, (pick_ref.shape[0], tokens), 1)
    marks = jnp.where(pick_ref[...] == line, 1.0, 0.0).astype(jnp.bfloat16)
    me, groups = lax.axis_index("fsdp"), lax.axis_size("fsdp")
    own = jnp.dot(
        marks, last_ref[...].astype(jnp.bfloat16), preferred_element_type=jnp.float32
    ).astype(jnp.bfloat16)
    sent[...] = own
    picked_ref[me] = own
    greet(groups, me, False)

    def copy(step):
        return pltpu.make_async_remote_copy(
            sent,
            picked_ref.at[me],
            send.at[step],
            recv.at[step],
            device_id=member((me + step) % groups, False),
            device_id_type=MESH,
        )

    for step in range(1, groups):
        copy(step).start()
    for ref in (proj_out, bias_out, loss_ref):
        ref[...] = jnp.zeros_like(ref)
    for index in range(3 * DT // CHUNK):
        made = regroup(w_ref[index], 3)
        for part in range(3):
            rows = CHUNK // 3
            qkv_ref[part, index * rows : (index + 1) * rows, :] = made[part * rows : (part + 1) * rows]
    first_up, first_down = 4 * DT // CHUNK, (4 * DT + FT) // CHUNK
    many = FT // DT
    for index in range(FT // CHUNK // 2):
        at = first_up + 2 * index
        made = regroup(w_ref[at : at + 2].reshape(2 * CHUNK, DT), many)
        rows = 2 * CHUNK // many
        for part in range(many):
            up_ref[part, index * rows : (index + 1) * rows, :] = made[part * rows : (part + 1) * rows]
    line = lax.broadcasted_iota(jnp.int32, (1, 2 * size), 1)
    low_half = line < size
    length = mask_ref.shape[1]

    def vector(index, amount=1):
        return vec_ref[:, index * DT : (index + amount) * DT]

    def tile(step, carry):
        at = pl.ds(pl.multiple_of(step * TILE, TILE), TILE)
        x_low = x_ref[at, :]
        q, k, v = (
            (
                jnp.dot(x_low, qkv_ref[part], preferred_element_type=jnp.float32) + vector(part)
            ).astype(jnp.bfloat16)
            for part in range(3)
        )
        nothing = jnp.zeros((length, 2 * size), jnp.bfloat16)
        for row in range(TILE // length):
            span = slice(row * length, (row + 1) * length)
            here = pl.ds(pl.multiple_of(step * TILE + row * length, length), length)
            mask = mask_ref[here, :]
            for pair in range(HT // 2):
                lanes = slice(pair * 2 * size, (pair + 1) * 2 * size)
                k_pair, v_pair = k[span, lanes], v[span, lanes]
                k_both = jnp.concatenate(
                    [jnp.where(low_half, k_pair, nothing), jnp.where(low_half, nothing, k_pair)]
                )
                v_both = jnp.concatenate(
                    [jnp.where(low_half, v_pair, nothing), jnp.where(low_half, nothing, v_pair)]
                )
                scores = back_product(q[span, lanes], k_both) * size ** (-0.5)
                s_ref[here, pair * 2 * length : (pair + 1) * 2 * length] = scores
                weights = jnp.concatenate(
                    [softmax_low(scores[:, :length], mask), softmax_low(scores[:, length:], mask)], 1
                )
                context_ref[span, lanes] = jnp.dot(
                    weights, v_both, preferred_element_type=jnp.float32
                ).astype(jnp.bfloat16)
        w_out = w_ref[3 * DT // CHUNK : first_up].reshape(DT, DT)
        attended = jnp.dot(context_ref[...], w_out, preferred_element_type=jnp.float32) + vector(3)
        middle = norm_forward(x_low.astype(jnp.float32) + attended, vector(4), vector(5))[0]
        middle_low = middle.astype(jnp.bfloat16)
        outer = jnp.zeros((TILE, DT), jnp.float32)
        for part in range(many):
            inner = jnp.dot(middle_low, up_ref[part], preferred_element_type=jnp.float32) + vector(
                6 + part
            )
            begin = first_down + part * (DT // CHUNK)
            w_down = w_ref[begin : begin + DT // CHUNK].reshape(DT, DT)
            outer = outer + jnp.dot(
                gelu(inner).astype(jnp.bfloat16), w_down, preferred_element_type=jnp.float32
            )
        made = norm_forward(
            middle + outer + vector(6 + many), vector(7 + many), vector(8 + many)
        )[0]
        low_ref[at, :] = made.astype(jnp.bfloat16)
        pairs = ((zero_ref, x_low.astype(jnp.float32), back_zero), (last_ref, made, back_last))
        for source_ref, target, back_ref in pairs:
            source = source_ref[at, :].astype(jnp.bfloat16)
            spread = back_product(source, proj_ref[...]) + bias_ref[...] - target
            weighted = spread * weight_ref[at, :]
            loss_ref[...] += jnp.sum(weighted * spread, 0, keepdims=True)
            d_mapped = (weighted * (2.0 / denom)).astype(jnp.bfloat16)
            back_ref[at, :] = jnp.dot(d_mapped, proj_ref[...], preferred_element_type=jnp.float32)
            proj_out[...] += outer_product(d_mapped, source)
            bias_out[...] += jnp.sum(d_mapped.astype(jnp.float32), 0, keepdims=True)
        return carry

    lax.fori_loop(0, tokens // TILE, tile, 0)
    t_picked_ref[...] = jnp.dot(
        marks, low_ref[...], preferred_element_type=jnp.float32
    ).astype(jnp.bfloat16)
    for step in range(1, groups):
        copy(step).wait()


def teacher_forward(x_low, blocks, vectors, mask, embedded, last, proj, bias, weight, picks, denom):
    tokens, length = mask.shape
    full = partial(jax.ShapeDtypeStruct, dtype=jnp.float32)
    low = partial(jax.ShapeDtypeStruct, dtype=jnp.bfloat16)
    amount, groups = picks.shape[0], lax.axis_size("fsdp")
    made = (
        full((tokens, HT * length)),
        full((tokens, DS)),
        full((tokens, DS)),
        full((DT, DS)),
        full((1, DT)),
        full((1, DT)),
        low((groups, amount, DS)),
        low((amount, DT)),
    )
    given = (x_low, blocks, vectors, mask, embedded, last, proj, bias, weight, picks)
    return pl.pallas_call(
        partial(teacher_kernel, denom),
        out_shape=made,
        in_specs=[VMEM_SPEC] * len(given),
        out_specs=(VMEM_SPEC,) * len(made),
        scratch_shapes=[
            pltpu.VMEM((tokens, DT), jnp.bfloat16),
            pltpu.VMEM((3, DT, DT), jnp.bfloat16),
            pltpu.VMEM((FT // DT, DT, DT), jnp.bfloat16),
            pltpu.VMEM((TILE, DT), jnp.bfloat16),
            pltpu.VMEM((amount, DS), jnp.bfloat16),
            *[pltpu.SemaphoreType.DMA((groups,))] * 2,
        ],
        compiler_params=pltpu.CompilerParams(
            collective_id=5, has_side_effects=True, vmem_limit_bytes=58 * 1024 * 1024
        ),
        cost_estimate=pl.CostEstimate(
            flops=20 * 10**9, bytes_accessed=25 * 10**6, transcendentals=5 * 10**6
        ),
    )(*given)


WIDER = -(-FS // 128) * 128


def refold(source, target, source_width, target_width):
    period = math.lcm(source_width, target_width)
    groups = source.shape[1] * source_width // period
    step_in, step_out = period // source_width, period // target_width
    lane = lax.broadcasted_iota(jnp.int32, (groups, 128), 1)
    for row in range(step_out):
        for tile in range(-(-target_width // 128)):
            begin = row * target_width + 128 * tile
            amount = min(128, target_width - 128 * tile)
            made, at = jnp.zeros((groups, 128), source.dtype), 0
            while at < amount:
                line, column = divmod(begin + at, source_width)
                where, lanes = divmod(column, 128)
                piece = source[where, pl.ds(line, groups, stride=step_in), :]
                if (at - lanes) % 128:
                    piece = pltpu.roll(piece, (at - lanes) % 128, 1)
                length = min(128 - lanes, source_width - column, amount - at)
                made = jnp.where((lane >= at) & (lane < at + length), piece, made)
                at += length
            target[tile, pl.ds(row, groups, stride=step_out), :] = made


def unpack_into(plan, layers, w_ref, *refs):
    place_ref, proj_ref, square, wide, folded, unfolded, small = refs[4 * layers :]
    for layer in range(layers):
        qkv_ref, out_ref, up_ref, down_ref = refs[4 * layer : 4 * layer + 4]
        for matrix, at, rows, block, line in plan:
            part = matrix - 6 * layer
            if not 0 <= part < 6:
                continue
            value = w_ref[block].astype(jnp.float32)[line : line + rows]
            if part < 4:
                square[part, at : at + rows, :] = value
            elif part == 4:
                for tile in range(-(-DS // 128)):
                    lanes = min(128, DS - 128 * tile)
                    folded[tile, at : at + rows, :lanes] = value[:, 128 * tile : 128 * tile + lanes]
            else:
                wide[at : at + rows, :] = value
        for part in range(3):
            qkv_ref[part] = square[part].astype(jnp.bfloat16)
        out_ref[...] = square[3].astype(jnp.bfloat16)
        refold(folded, unfolded, DS, FS)
        for tile in range(WIDER // 128):
            up_ref[:, 128 * tile : 128 * tile + 128] = unfolded[tile].astype(jnp.bfloat16)
        down_ref[:FS, :] = wide[...].astype(jnp.bfloat16)
        down_ref[FS:, :] = jnp.zeros((WIDER - FS, DS), jnp.bfloat16)
    for matrix, at, rows, block, line in plan:
        if matrix >= 6 * layers:
            value = w_ref[block].astype(jnp.float32)[line : line + rows]
            small[matrix - 6 * layers, at : at + rows, :] = value
    place_ref[...] = small[0, : place_ref.shape[0]].astype(jnp.bfloat16)
    proj_ref[...] = small[1].astype(jnp.bfloat16)


def unpack_shapes(layers, length):
    low = partial(jax.ShapeDtypeStruct, dtype=jnp.bfloat16)
    return (
        *[low((3, DS, DS)), low((DS, DS)), low((DS, WIDER)), low((WIDER, DS))] * layers,
        low((length, DS)),
        low((DT, DS)),
    )


def by_heads(value, heads):
    width = value.shape[1]
    size = width // heads
    lane = lax.broadcasted_iota(jnp.int32, (1, width), 1)
    nothing = jnp.zeros_like(value)
    return jnp.concatenate(
        [
            jnp.where((lane >= head * size) & (lane < (head + 1) * size), value, nothing)
            for head in range(heads)
        ]
    )


def student_kernel(
    plan, layers, token_ref, evec_ref, vec_ref, bias_ref, mask_ref, *refs,
):
    ready = 4 * layers + 2
    if plan:
        w_ref, *refs = refs
        unpack_into(plan, layers, w_ref, *refs[:ready], *refs[-5:])
    matrices, place_ref, refs = refs[: 4 * layers], refs[4 * layers], refs[ready:]
    emb_ref, zero_ref, zero_inv, last_ref = refs[:4]
    length = mask_ref.shape[1]
    size = DS // HS

    def tile(step, carry):
        at = pl.ds(pl.multiple_of(step * TILE, TILE), TILE)
        places = jnp.concatenate([place_ref[...].astype(jnp.float32)] * (TILE // length))
        hidden, normed, inverse = norm_forward(
            token_ref[at, :] + places, evec_ref[0:1, :], evec_ref[1:2, :]
        )
        emb_ref[at, :] = hidden
        zero_ref[at, :] = normed
        zero_inv[at, :] = inverse
        for layer in range(layers):
            qkv_w, out_w, up_w, down_w = matrices[4 * layer : 4 * layer + 4]
            low_ref, qkv_ref, context_ref, one_ref, one_inv, two_ref, two_inv = refs[
                4 + 7 * layer : 11 + 7 * layer
            ]

            def vector(index, layer=layer):
                return vec_ref[layer, index : index + 1, :]

            low = hidden.astype(jnp.bfloat16)
            low_ref[at, :] = low
            parts = []
            for part in range(3):
                made = jnp.dot(low, qkv_w[part], preferred_element_type=jnp.float32)
                if part != 1:
                    made = made + vector(part // 2)
                parts.append(made.astype(jnp.bfloat16))
                qkv_ref[part, at, :] = parts[part]
            contexts = []
            for row in range(TILE // length):
                span = slice(row * length, (row + 1) * length)
                here = pl.ds(pl.multiple_of(step * TILE + row * length, length), length)
                mask = mask_ref[here, :]
                q, k, v = (part[span] for part in parts)
                scores = back_product(q, by_heads(k, HS)) * size ** (-0.5)
                weights = jnp.concatenate(
                    [
                        softmax_low(scores[:, head * length : (head + 1) * length], mask)
                        for head in range(HS)
                    ],
                    1,
                )
                contexts.append(
                    jnp.dot(weights, by_heads(v, HS), preferred_element_type=jnp.float32)
                )
            context = jnp.concatenate(contexts).astype(jnp.bfloat16)
            context_ref[at, :] = context
            attended = jnp.dot(context, out_w[...], preferred_element_type=jnp.float32) + vector(2)
            middle, normed, inverse = norm_forward(hidden + attended, vector(3), vector(4))
            one_ref[at, :] = normed
            one_inv[at, :] = inverse
            inner = jnp.dot(
                middle.astype(jnp.bfloat16), up_w[...], preferred_element_type=jnp.float32
            ) + bias_ref[layer]
            outer = jnp.dot(
                gelu(inner).astype(jnp.bfloat16), down_w[...], preferred_element_type=jnp.float32
            ) + vector(5)
            hidden, normed, inverse = norm_forward(middle + outer, vector(6), vector(7))
            two_ref[at, :] = normed
            two_inv[at, :] = inverse
        last_ref[at, :] = hidden
        return carry

    lax.fori_loop(0, token_ref.shape[0] // TILE, tile, 0)


def student_forward(token_rows, evec, vectors, biases, mask, plan, blocks, matrices):
    tokens = token_rows.shape[0]
    layers = vectors.shape[0]
    full = partial(jax.ShapeDtypeStruct, dtype=jnp.float32)
    low = partial(jax.ShapeDtypeStruct, dtype=jnp.bfloat16)
    length = mask.shape[1]
    shapes = () if matrices else unpack_shapes(layers, length)
    made = (
        *shapes,
        full((tokens, DS)),
        full((tokens, DS)),
        full((tokens, 1)),
        full((tokens, DS)),
        *[
            low((tokens, DS)),
            low((3, tokens, DS)),
            low((tokens, DS)),
            full((tokens, DS)),
            full((tokens, 1)),
            full((tokens, DS)),
            full((tokens, 1)),
        ]
        * layers,
    )
    given = (token_rows, evec, vectors, biases, mask, *(matrices or [blocks]))
    all_of = pl.pallas_call(
        partial(student_kernel, plan, layers),
        out_shape=made,
        in_specs=[VMEM_SPEC] * len(given),
        out_specs=(VMEM_SPEC,) * len(made),
        scratch_shapes=(
            []
            if matrices
            else [
                pltpu.VMEM((4, DS, DS), jnp.float32),
                pltpu.VMEM((FS, DS), jnp.float32),
                pltpu.VMEM((-(-DS // 128), FS, 128), jnp.float32),
                pltpu.VMEM((WIDER // 128, DS, 128), jnp.float32),
                pltpu.VMEM((2, DT, DS), jnp.float32),
            ]
        ),
        compiler_params=pltpu.CompilerParams(vmem_limit_bytes=58 * 1024 * 1024),
        cost_estimate=pl.CostEstimate(
            flops=8 * 10**9, bytes_accessed=40 * 10**6, transcendentals=6 * 10**6
        ),
    )(*given)
    return list(all_of[: len(shapes)] or matrices), all_of[len(shapes) :]


def back_kernel(
    last, first_layer, grad_ref, vec_ref, bias_ref, mask_ref, qkv_w, out_w, up_w, down_w,
    low_ref, qkv_ref, context_ref, one_ref, one_inv, two_ref, two_inv, *refs,
):
    if first_layer:
        (more_ref, zero_ref, zero_inv, evec_ref), refs = refs[:4], refs[4:]
    if last:
        score_ref, count_ref, refs = refs[0], refs[1], refs[2:]
    hidden_ref, *weight_refs, vec_out, bias_out, refs = (*refs[:9], refs[9:])
    dq_ref, dk_ref, dv_ref, do_ref, du_ref, dd_ref = weight_refs
    if last:
        loss_ref, refs = refs[0], refs[1:]
        loss_ref[...] = jnp.zeros_like(loss_ref)
    if first_layer:
        (place_ref, edge_ref), refs = refs[:2], refs[2:]
        place_ref[...] = jnp.zeros_like(place_ref)
        edge_ref[...] = jnp.zeros_like(edge_ref)
    outer_s, attended_s, q_s, k_s, v_s, middle_s, active_s, inner_s, unfolded, folded = refs
    length = mask_ref.shape[1]
    size = DS // HS
    vec_out[...] = jnp.zeros_like(vec_out)
    bias_out[...] = jnp.zeros_like(bias_out)
    many = 256

    def vector(index):
        return vec_ref[index : index + 1, :]

    def note(index, value, to=vec_out):
        to[index : index + 1, :] += jnp.sum(value.astype(jnp.float32), 0, keepdims=True)

    def norm_back(grad, normed, inverse, gain, index, to=vec_out):
        d_normed = grad * gain
        note(index, grad * normed, to)
        note(index + 1, grad, to)
        return inverse * (
            d_normed
            - jnp.mean(d_normed, -1, keepdims=True)
            - normed * jnp.mean(d_normed * normed, -1, keepdims=True)
        )

    def tile(step, carry):
        at = pl.ds(pl.multiple_of(step * TILE, TILE), TILE)
        d_sum = norm_back(grad_ref[at, :], two_ref[at, :], two_inv[at, :], vector(6), 6)
        d_outer = d_sum.astype(jnp.bfloat16)
        outer_s[at, :] = d_outer
        note(5, d_outer)
        middle = (one_ref[at, :] * vector(3) + vector(4)).astype(jnp.bfloat16)
        middle_s[at, :] = middle
        d_middle = d_sum
        for first in range(0, WIDER, many):
            lanes = slice(first, first + many)
            inner = jnp.dot(
                middle, up_w[:, lanes], preferred_element_type=jnp.float32
            ) + bias_ref[:, lanes]
            squared = inner * inner
            bent = jnp.tanh(0.7978845608028654 * (inner + 0.044715 * squared * inner))
            active_s[at, lanes] = (0.5 * inner * (1.0 + bent)).astype(jnp.bfloat16)
            slope = 0.5 * (1.0 + bent) + 0.5 * inner * (1.0 - bent * bent) * (
                0.7978845608028654 * (1.0 + 3.0 * 0.044715 * squared)
            )
            d_inner = (back_product(d_outer, down_w[lanes, :]) * slope).astype(jnp.bfloat16)
            inner_s[at, lanes] = d_inner
            bias_out[:, lanes] += jnp.sum(d_inner.astype(jnp.float32), 0, keepdims=True)
            d_middle = d_middle + back_product(d_inner, up_w[:, lanes])
        d_one = norm_back(d_middle, one_ref[at, :], one_inv[at, :], vector(3), 3)
        d_attended = d_one.astype(jnp.bfloat16)
        attended_s[at, :] = d_attended
        note(2, d_attended)
        d_context = back_product(d_attended, out_w[...]).astype(jnp.bfloat16)
        for row in range(TILE // length):
            here = pl.ds(pl.multiple_of(step * TILE + row * length, length), length)
            mask = mask_ref[here, :]
            d_row = d_context[row * length : (row + 1) * length]
            q, k, v = (qkv_ref[part, here, :] for part in range(3))
            keys = by_heads(k, HS)
            scores = back_product(q, keys) * size ** (-0.5)
            d_weights = back_product(d_row, by_heads(v, HS))
            low_weights, d_scores = [], []
            for head in range(HS):
                lanes = slice(head * length, (head + 1) * length)
                masked = jnp.where(mask > 0.0, scores[:, lanes], NEG_LARGE)
                expo = jnp.exp(masked - jnp.max(masked, -1, keepdims=True))
                weights = expo * (1.0 / jnp.sum(expo, -1, keepdims=True))
                low_weights.append(weights.astype(jnp.bfloat16))
                turned = weights * d_weights[:, lanes]
                made = turned - weights * jnp.sum(turned, -1, keepdims=True)
                if last:
                    differ = jnp.where(mask > 1.0, scores[:, lanes] - score_ref[here, lanes], 0.0)
                    loss_ref[...] += jnp.sum(differ * differ, 0, keepdims=True)
                    made = made + differ * (2.0 / count_ref[...])
                d_scores.append(made.astype(jnp.bfloat16))
            scale = size ** (-0.5)
            q_s[here, :] = (
                jnp.dot(jnp.concatenate(d_scores, 1), keys, preferred_element_type=jnp.float32)
                * scale
            ).astype(jnp.bfloat16)
            k_s[here, :] = (
                outer_product(jnp.concatenate(d_scores), by_heads(q, HS)) * scale
            ).astype(jnp.bfloat16)
            v_s[here, :] = outer_product(
                jnp.concatenate(low_weights), by_heads(d_row, HS)
            ).astype(jnp.bfloat16)
        d_hidden = d_one
        for part, held in enumerate((q_s, k_s, v_s)):
            d_part = held[at, :]
            if part != 1:
                note(part // 2, d_part)
            d_hidden = d_hidden + back_product(d_part, qkv_w[part])
        if first_layer:
            d_hidden = norm_back(
                d_hidden + more_ref[at, :],
                zero_ref[at, :],
                zero_inv[at, :],
                evec_ref[0:1, :],
                0,
                edge_ref,
            )
            for row in range(TILE // length):
                place_ref[...] += d_hidden[row * length : (row + 1) * length]
        hidden_ref[at, :] = d_hidden
        return carry

    lax.fori_loop(0, grad_ref.shape[0] // TILE, tile, 0)
    low = low_ref[...]
    dq_ref[...] = outer_product(low, q_s[...])
    dk_ref[...] = outer_product(low, k_s[...])
    dv_ref[...] = outer_product(low, v_s[...])
    do_ref[...] = outer_product(context_ref[...], attended_s[...])
    for first in range(0, WIDER, many):
        lanes = slice(first, first + many)
        stop = min(first + many, FS)
        dd_ref[first:stop, :] = outer_product(active_s[:, lanes], outer_s[...])[: stop - first]
        made = outer_product(middle_s[...], inner_s[:, lanes])
        for tile_at in range(many // 128):
            unfolded[first // 128 + tile_at] = made[:, 128 * tile_at : 128 * tile_at + 128]
    refold(unfolded, folded, FS, DS)
    for tile_at in range(-(-DS // 128)):
        lanes = min(128, DS - 128 * tile_at)
        du_ref[:, 128 * tile_at : 128 * tile_at + lanes] = folded[tile_at, :, :lanes]


def student_backward(grad, vectors, biases, mask, matrices, saved, last, first_layer):
    tokens, length = mask.shape
    full = partial(jax.ShapeDtypeStruct, dtype=jnp.float32)
    made = [
        full((tokens, DS)),
        *[full((DS, DS))] * 4,
        full((FS, DS)),
        full((FS, DS)),
        full((8, DS)),
        full((1, WIDER)),
    ]
    given = [grad, vectors, biases, mask, *matrices, *saved]
    given += first_layer
    if last:
        given += last
        made.append(full((1, length)))
    if first_layer:
        made += [full((length, DS)), full((8, DS))]
    low = partial(pltpu.VMEM, dtype=jnp.bfloat16)
    return pl.pallas_call(
        partial(back_kernel, bool(last), bool(first_layer)),
        out_shape=tuple(made),
        in_specs=[VMEM_SPEC] * len(given),
        out_specs=(VMEM_SPEC,) * len(made),
        scratch_shapes=[
            *[low((tokens, DS))] * 6,
            *[low((tokens, WIDER))] * 2,
            pltpu.VMEM((WIDER // 128, DS, 128), jnp.float32),
            pltpu.VMEM((-(-DS // 128), FS, 128), jnp.float32),
        ],
        compiler_params=pltpu.CompilerParams(vmem_limit_bytes=58 * 1024 * 1024),
        cost_estimate=pl.CostEstimate(
            flops=10**9, bytes_accessed=4 * 10**6, transcendentals=3 * 10**5
        ),
    )(*given)


def d_all_width(width):
    return -(-width // 128) * 128


def head_kernel(
    groups, pair, denom, p_all, t_ref, table_ref, head_ref, d_ref, own_ref, w_ref, *refs
):
    (
        t_all, p_turned, t_turned, s_logits, t_logits, stats, rows_of, inbox, total,
        send, recv, stat_send, stat_recv, d_send, d_recv, pair_send, pair_recv, out_sem,
    ) = refs
    amount, width = p_all.shape[1:]
    vocab = table_ref.shape[0]
    z_size = z_size_of(groups)
    side = groups // z_size
    across = z_size * amount
    half = d_all_width(width)
    dp, me = lax.axis_index("dp"), lax.axis_index("fsdp")
    z, y = me // side, me % side
    sibling = (dp // 2 * 2 + 1 - dp % 2, me)
    beside = ((dp + 2) % lax.axis_size("dp"), me)
    barrier = pltpu.get_barrier_semaphore()
    for step in range(1, groups):
        pl.semaphore_signal(
            barrier, inc=1, device_id=(dp, (me + step) % groups), device_id_type=MESH
        )
    if pair:
        for other in (sibling, beside):
            pl.semaphore_signal(barrier, inc=1, device_id=other, device_id_type=MESH)
    pl.semaphore_wait(barrier, groups - 1 + (2 if pair else 0))

    def both(at, rank, target, own=False):
        return [
            pltpu.make_async_remote_copy(
                t_ref if own else t_all.at[at],
                t_all.at[at],
                send.at[rank],
                recv.at[rank],
                device_id=(dp, target),
                device_id_type=MESH,
            )
        ]

    def begin(copies):
        for copy in copies:
            copy.start()

    def received(copies):
        for copy in copies:
            copy.wait_recv()

    def sent(copies):
        for copy in copies:
            copy.wait_send()

    def line(step):
        return z + step, (z + step >= 0) & (z + step < z_size)

    def inside(position):
        return jnp.minimum(jnp.maximum(position, 0), z_size - 1) * side

    def z_copies(step, way, arriving):
        origin, known = line(-way * (step + (1 if arriving else 0)))
        target, there = line(way)
        rank = 2 * step + (1 if way > 0 else 0)
        made = both(inside(origin) + y, rank, inside(target) + y, own=step == 0 and not arriving)
        return made, known if arriving else known & there

    def y_copies(back, step, at, own=False):
        return both(
            at, 2 * z_size + (back - 1) * z_size + step, z * side + (y + back) % side, own
        )

    wide = next(size for size in (384, 320, 128) if vocab % size == 0)

    def measure(back):
        at_y = (y + side - back) % side
        slots = [line * side + at_y for line in range(z_size)]
        t_turned[...] = jnp.concatenate([t_all[at] for at in slots]).astype(jnp.float32).T.astype(
            jnp.bfloat16
        )
        p_turned[...] = jnp.concatenate([p_all[at] for at in slots]).astype(jnp.float32).T.astype(
            jnp.bfloat16
        )

        def step(index, carry):
            s_top, s_sum, t_top, t_sum, cross = carry
            lines = pl.ds(pl.multiple_of(index * wide, 64), wide)
            t_now = jnp.dot(head_ref[lines, :], t_turned[...], preferred_element_type=jnp.float32)
            s_now = jnp.dot(table_ref[lines, 0:width], p_turned[...], preferred_element_type=jnp.float32)
            t_logits[back, lines, :] = t_now
            s_logits[back, lines, :] = s_now
            s_next = jnp.maximum(s_top, jnp.max(s_now, 0, keepdims=True))
            t_next = jnp.maximum(t_top, jnp.max(t_now, 0, keepdims=True))
            t_exp = jnp.exp(t_now - t_next)
            scale = jnp.exp(t_top - t_next)
            s_sum = s_sum * jnp.exp(s_top - s_next) + jnp.sum(
                jnp.exp(s_now - s_next), 0, keepdims=True
            )
            t_sum = t_sum * scale + jnp.sum(t_exp, 0, keepdims=True)
            cross = cross * scale + jnp.sum(t_exp * s_now, 0, keepdims=True)
            return (s_next, s_sum, t_next, t_sum, cross)

        lowest = jnp.full((1, across), -jnp.inf, jnp.float32)
        zero = jnp.zeros((1, across), jnp.float32)
        made = lax.fori_loop(0, vocab // wide, step, (lowest, zero, lowest, zero, zero))
        for index, value in enumerate(made):
            stats[me, at_y, index : index + 1, :] = value

    t_all[me] = t_ref[...]
    for way in (1, -1):
        made, wanted = z_copies(0, way, False)
        pl.when(wanted)(partial(begin, made))
    for back in range(1, side):
        begin(y_copies(back, z, me, own=True))
    for step in range(z_size - 1):
        for way in (1, -1):
            made, wanted = z_copies(step, way, True)
            onward, further = z_copies(step + 1, way, False) if step + 2 < z_size else (None, None)

            @pl.when(wanted)
            def _(made=made, onward=onward, further=further, step=step, way=way):
                received(made)
                if onward is not None:
                    pl.when(further)(partial(begin, onward))
                origin = z - way * (step + 1)
                for back in range(1, side):
                    begin(y_copies(back, origin, origin * side + y))

    for back in range(side):
        if back:
            for step in range(z_size):
                received(y_copies(back, step, step * side + (y + side - back) % side))
        measure(back)
    for step in range(z_size - 1):
        for way in (1, -1):
            made, wanted = z_copies(step, way, False)
            pl.when(wanted)(partial(sent, made))
    for back in range(1, side):
        for step in range(z_size):
            sent(y_copies(back, step, step * side + y))

    def stat_copy(step):
        return pltpu.make_async_remote_copy(
            stats.at[me],
            stats.at[me],
            stat_send.at[step],
            stat_recv.at[step],
            device_id=(dp, (me + step) % groups),
            device_id_type=MESH,
        )

    for step in range(1, groups):
        stat_copy(step).start()
    for step in range(1, groups):
        stat_copy(step).wait_recv()
    for back in range(side):
        at_y = (y + side - back) % side
        parts = [stats[other, at_y] for other in range(groups)]
        s_top, t_top = parts[0][0:1], parts[0][2:3]
        for part in parts[1:]:
            s_top = jnp.maximum(s_top, part[0:1])
            t_top = jnp.maximum(t_top, part[2:3])
        s_sum, t_sum, cross = (jnp.zeros_like(s_top) for unused in range(3))
        for part in parts:
            s_sum = s_sum + part[1:2] * jnp.exp(part[0:1] - s_top)
            scale = jnp.exp(part[2:3] - t_top)
            t_sum = t_sum + part[3:4] * scale
            cross = cross + part[4:5] * scale
        rows_of[back, 0:1, :] = s_top + jnp.log(s_sum)
        rows_of[back, 1:2, :] = t_top
        rows_of[back, 2:3, :] = 1.0 / t_sum
        rows_of[back, 3:4, :] = cross / t_sum
        total[back] = jnp.zeros((half, across), jnp.float32)
    own_ref[...] = rows_of[0]
    narrow = next(size for size in (320, 128) if vocab % size == 0)
    part = vocab // 4 if pair else vocab

    def rows_at(start, amount):
        return t_logits.at[0, pl.ds(pl.multiple_of(start, 64), amount), 0:half]

    def grade(first):
        def chunk(index, carry):
            lines = pl.ds(pl.multiple_of(first + index * narrow, 64), narrow)
            table = table_ref[lines, 0:width]
            made = jnp.zeros((narrow, width), jnp.float32)
            for back in range(side):
                row = rows_of[back]
                grads = 2.0 * jnp.exp(s_logits[back, lines, :] - row[0:1])
                grads = grads - jnp.exp(t_logits[back, lines, :] - row[1:2]) * row[2:3]
                low = (grads * (1.0 / denom)).astype(jnp.bfloat16)
                total[back, :width, :] += outer_product(table, low)
                at_y = (y + side - back) % side
                states = jnp.concatenate([p_all[line * side + at_y] for line in range(z_size)])
                made = made + jnp.dot(low, states, preferred_element_type=jnp.float32)
            t_logits[0, lines, 0:width] = made
            return carry

        lax.fori_loop(0, part // narrow, chunk, 0)

    def pair_copy(index, source, target):
        return pltpu.make_async_remote_copy(
            source,
            inbox.at[index],
            pair_send.at[index],
            pair_recv.at[index],
            device_id=target,
            device_id_type=MESH,
        )

    given = []
    if pair:
        x, core = dp // 2, dp % 2
        far, near = 1 - x, x

        def start_of(along, other):
            return (2 * along + (core + other) % 2) * part

        for index, (along, other) in enumerate(((far, 1), (far, 0), (near, 1), (near, 0))):
            grade(start_of(along, other))
            if other:
                given.append(pair_copy(index // 2, rows_at(start_of(along, other), part), sibling))
                given[-1].start()
            elif along is far:
                given[0].wait_recv()
                lines = pl.ds(pl.multiple_of(start_of(far, 0), 64), part)
                t_logits[0, lines, 0:half] += inbox[0]
                given.append(pair_copy(2, rows_at(start_of(far, 0), part), beside))
                given[-1].start()
    else:
        grade(0)
    for back in range(side):
        turned = total[back].T.astype(jnp.bfloat16)
        for line in range(z_size):
            at = line * side + (y + side - back) % side
            t_all[at, :, half : 2 * half] = turned[line * amount : (line + 1) * amount]

    def d_copy(step):
        peer = (me + step) % groups
        return pltpu.make_async_remote_copy(
            t_all.at[peer, :, half : 2 * half],
            t_all.at[me, :, 0:half],
            d_send.at[step],
            d_recv.at[step],
            device_id=(dp, peer),
            device_id_type=MESH,
        )

    for step in range(1, groups):
        d_copy(step).start()
    made = t_all[me, :, half : 2 * half].astype(jnp.float32)
    for step in range(1, groups):
        d_copy(step).wait_recv()
        made = made + t_all[(me + groups - step) % groups, :, 0:half].astype(jnp.float32)
    d_ref[...] = made
    kept = 0
    if pair:
        kept = start_of(near, 0)
        lines = pl.ds(pl.multiple_of(kept, 64), part)
        given[2].wait_recv()
        t_logits[0, lines, 0:half] += inbox[1]
        given[1].wait_recv()
        t_logits[0, lines, 0:half] += inbox[2]
    out = pltpu.make_async_copy(rows_at(kept, part), w_ref, out_sem)
    out.start()
    for step in range(1, groups):
        stat_copy(step).wait_send()
        d_copy(step).wait_send()
    for copy in given:
        copy.wait_send()
    out.wait()


def head(picked, t_picked, table, teacher_head, denom, number):
    groups, n_dp = lax.axis_size("fsdp"), lax.axis_size("dp")
    pair = n_dp == 4
    amount, width = picked.shape[1:]
    vocab = table.shape[0]
    z_size = z_size_of(groups)
    side, across = groups // z_size, z_size * amount
    half = d_all_width(width)
    assert 2 * half <= DT
    full, low = jnp.float32, jnp.bfloat16
    anywhere = pl.BlockSpec(memory_space=pl.ANY)
    dma = pltpu.SemaphoreType.DMA
    made = [
        jax.ShapeDtypeStruct((amount, half), full),
        jax.ShapeDtypeStruct((8, across), full),
        jax.ShapeDtypeStruct((vocab // 4 if pair else vocab, half), full),
    ]
    return pl.pallas_call(
        partial(head_kernel, groups, pair, denom),
        out_shape=tuple(made),
        in_specs=[VMEM_SPEC] * 4,
        out_specs=(VMEM_SPEC, VMEM_SPEC) + (anywhere,) * (len(made) - 2),
        scratch_shapes=[
            pltpu.VMEM((groups, amount, DT), low),
            pltpu.VMEM((width, across), low),
            pltpu.VMEM((DT, across), low),
            pltpu.VMEM((side, vocab, across), full),
            pltpu.VMEM((side, vocab, across), full),
            pltpu.VMEM((groups, side, 8, across), full),
            pltpu.VMEM((side, 8, across), full),
            pltpu.VMEM((3, vocab // 4, half) if pair else (1, 8, 128), full),
            pltpu.VMEM((side, half, across), full),
            *[dma((2 * z_size + (side - 1) * z_size,))] * 2,
            *[dma((groups,))] * 4,
            *[dma((3,))] * 2,
            dma,
        ],
        compiler_params=pltpu.CompilerParams(
            collective_id=number, has_side_effects=True, vmem_limit_bytes=61 * 1024 * 1024
        ),
    )(picked, t_picked, table, teacher_head)


def three_parts(value):
    high = lax.reduce_precision(value, 8, 7)
    rest = value - high
    middle = lax.reduce_precision(rest, 8, 7)
    low = rest - middle
    return jnp.concatenate([high, middle, low], -1).astype(jnp.bfloat16)


def pick_exact(marks, value, turned=False):
    width = value.shape[1]
    terms = three_parts(value)
    made = outer_product(marks, terms) if turned else jnp.dot(
        marks, terms, preferred_element_type=jnp.float32
    )
    return made[:, :width] + made[:, width : 2 * width] + made[:, 2 * width :]


def plan_requests(ids, local_rows):
    order = lax.broadcasted_iota(jnp.int32, (ids.shape[0],), 0)
    same = ids[:, None] == ids[None, :]
    leader = jnp.min(jnp.where(same, order[None, :], ids.shape[0]), 1)
    leads = leader == order
    owner = ids // local_rows
    before = (
        (owner[:, None] == owner[None, :]) & leads[None, :] & (order[None, :] < leader[:, None])
    )
    rank = jnp.sum(before.astype(jnp.int32), 1)
    return (leads, owner, ids - owner * local_rows, rank)


def round_marks(plan, turn, devices):
    leads, owner, local_id, rank = plan
    inside = (rank >= turn * SLOTS) & (rank < (turn + 1) * SLOTS)
    slot = jnp.where(inside, owner * SLOTS + rank - turn * SLOTS, -1)
    line = lax.broadcasted_iota(jnp.int32, (devices * SLOTS, 1), 0)
    hit = line == slot[None, :]
    asked = jnp.max(jnp.where(hit & leads[None, :], local_id[None, :], -1), 1)
    return (hit.astype(jnp.bfloat16), asked.reshape(devices, 1, SLOTS))


def question(plan, turn, devices, extra):
    marks, asked = round_marks(plan, turn, devices)
    fill = jnp.full((devices, 1, 128 - SLOTS - extra.shape[0]), -1, jnp.int32)
    note = jnp.broadcast_to(extra[None, None, :], (devices, 1, extra.shape[0]))
    return (marks, jnp.concatenate([asked, note, fill], 2))


def ask(plan, turn, devices, extra):
    marks, asked = question(plan, turn, devices, extra)
    return (marks, exchange(asked, 0)[:, 0, :SLOTS].reshape(-1))


def wanted_marks(wanted, local_rows):
    return (wanted[:, None] == lax.broadcasted_iota(jnp.int32, (1, local_rows), 1)).astype(
        jnp.bfloat16
    )


def fetch(marks, wanted, table_low, devices):
    rows = jnp.dot(
        wanted_marks(wanted, table_low.shape[0]), table_low, preferred_element_type=jnp.float32
    ).astype(jnp.bfloat16)
    got = exchange(rows.reshape(devices, SLOTS, -1), 1)
    return outer_product(marks, got.reshape(devices * SLOTS, -1))


def give_back(marks, wanted, grads, local_rows, devices):
    sent = pick_exact(marks, grads)
    got = exchange(sent.reshape(devices, SLOTS, -1), 2)
    return pick_exact(wanted_marks(wanted, local_rows), got.reshape(devices * SLOTS, -1), True)


def finish_kernel(
    at, rows_ref, wanted_ref, more_ref, head_ref, reduced_ref, note_ref, g_ref, notes_ref, sent, send, recv
):
    count, me = notes_ref.shape[0], place_of()
    greet(count, me, True)
    value = rows_ref[...]
    width = value.shape[1]
    high = value.astype(jnp.bfloat16)
    rest = value - high.astype(jnp.float32)
    middle = rest.astype(jnp.bfloat16)
    low = (rest - middle.astype(jnp.float32)).astype(jnp.bfloat16)
    rows = more_ref.shape[0]
    squares = jnp.sum(reduced_ref[...] * reduced_ref[...], 0, keepdims=True)
    squares = jnp.sum(squares, 1, keepdims=True)
    for first in range(0, rows, 384):
        step = min(384, rows - first)
        line = lax.broadcasted_iota(jnp.int32, (step, value.shape[0]), 0)
        marks = jnp.where(line + first == wanted_ref[...], 1.0, 0.0).astype(jnp.bfloat16)
        made = more_ref[first : first + step, :] + head_ref[first : first + step, :width]
        for term in (high, middle, low):
            made = made + jnp.dot(marks, term, preferred_element_type=jnp.float32)
        g_ref[:, first : first + step] = made.T
        squares = squares + jnp.sum(jnp.sum(made * made, 0, keepdims=True), 1, keepdims=True)
    lane = lax.broadcasted_iota(jnp.int32, sent.shape, 1)
    note = jnp.where(lane == at, squares, note_ref[...])
    sent[...] = note
    notes_ref[me] = note

    def copy(step):
        return pltpu.make_async_remote_copy(
            sent,
            notes_ref.at[me],
            send.at[step],
            recv.at[step],
            device_id=member((me + step) % count, True),
            device_id_type=MESH,
        )

    def start(step, carry):
        copy(step).start()
        return carry

    def finish(step, carry):
        copy(step).wait()
        return carry

    lax.fori_loop(1, count, start, 0)
    lax.fori_loop(1, count, finish, 0)


def finish(row_blocks, wanted, more, head_grad, reduced, note, at, number):
    count = lax.axis_size("dp") * lax.axis_size("fsdp")
    dma = pltpu.SemaphoreType.DMA
    return pl.pallas_call(
        partial(finish_kernel, at),
        out_shape=(
            jax.ShapeDtypeStruct(more.shape[::-1], more.dtype),
            jax.ShapeDtypeStruct((count,) + note.shape, note.dtype),
        ),
        in_specs=[VMEM_SPEC] * 6,
        out_specs=(VMEM_SPEC,) * 2,
        scratch_shapes=[pltpu.VMEM(note.shape, note.dtype), dma((count,)), dma((count,))],
        compiler_params=pltpu.CompilerParams(
            collective_id=number, has_side_effects=True, vmem_limit_bytes=40 * 1024 * 1024
        ),
    )(row_blocks, wanted[None], more, head_grad, reduced, note)


def local(
    token_ids,
    valid_mask,
    seq_ids,
    mask_pos,
    mask_labels,
    teacher_in,
    teacher_flat,
    teacher_vec,
    teacher_head,
    emb_table,
    emb_first,
    emb_second,
    pos_table,
    pos_first,
    pos_second,
    layer_flat,
    layer_first,
    layer_second,
    proj_weight,
    proj_first,
    proj_second,
    layer_vec,
    vec_first,
    vec_second,
    misc_vec,
    misc_first,
    misc_second,
):
    micro, micro_rows, length = token_ids.shape
    rows = micro * micro_rows
    local_rows, width = emb_table.shape
    layers = layer_vec.shape[0]
    picks = mask_pos.shape[2]
    tokens = rows * length
    n_dp, groups = lax.axis_size("dp"), lax.axis_size("fsdp")
    place = lax.axis_index("fsdp")
    devices = n_dp * groups
    hidden_denom = float(rows * devices * length * DT)
    predict_denom = float(rows * devices * picks)
    flat_local = layer_flat.shape[1]
    by_rows = flat_local % DS == 0

    to_owner = [
        (d * groups + f, f * n_dp + d) for d in range(n_dp) for f in range(groups)
    ]
    from_owner = [(owner, holder) for holder, owner in to_owner]
    table_low = emb_table.astype(jnp.bfloat16)

    usable = valid_mask.reshape(rows, length) > 0
    docs = seq_ids.reshape(rows, length)
    same_doc = docs[:, :, None] == docs[:, None, :]
    pair_mask = same_doc & usable[:, :, None] & usable[:, None, :]
    allowed = pair_mask | jnp.eye(length, dtype=bool)
    ids = jnp.concatenate([token_ids.reshape(-1), mask_labels.reshape(-1)])
    plan = plan_requests(ids, local_rows)
    extra = jnp.stack([-1 - jnp.sum(pair_mask.astype(jnp.int32)), -1 - jnp.max(plan[3])])
    teacher_lines = teacher_flat.reshape(-1, DT)
    teacher_all = lax.all_gather(teacher_lines, BOTH, axis=0, tiled=True).reshape(-1, CHUNK, DT)
    own_parts = [
        layer_flat.astype(jnp.bfloat16),
        pos_table.astype(jnp.bfloat16),
        proj_weight.astype(jnp.bfloat16).T,
    ]
    if by_rows:
        chunk = flat_local // DS
        own_layers = [woven(part.reshape(-1, DS), False) for part in own_parts[0]]
        own_parts = [part.reshape(1, -1, DS) for part in own_layers + own_parts[1:]]
        line, lines = DS, sum(part.shape[1] for part in own_parts)
    else:
        own_parts = [part.reshape(1, -1) for part in own_parts]
        line, lines = 128, -(-sum(part.shape[1] for part in own_parts) // 128)
    block_rows = -(-lines // 16) * 16
    marks, asked = question(plan, 0, devices, extra)
    got, weights_all, token_blocks = entry(asked, pack(own_parts, line, block_rows)[0], table_low, 3)
    table_then = lax.optimization_barrier((table_low, got))[0]
    table_then = jnp.pad(table_then, ((0, 0), (0, d_all_width(width) - width)))
    slice_part = lax.ppermute(table_then, BOTH, from_owner)
    wanted = got[:, 0, :SLOTS].reshape(-1)
    notes = got[:, 0, SLOTS : SLOTS + 2]
    count = jnp.sum(-1 - notes[:, 0]).astype(jnp.float32)
    rounds = jnp.max(-1 - notes[:, 1]) // SLOTS + 1
    all_rows = outer_product(marks, token_blocks.reshape(devices * SLOTS, width))

    def more_rows(state):
        turn, so_far = state
        marks_now, wanted_now = ask(plan, turn, devices, extra)
        return (turn + 1, so_far + fetch(marks_now, wanted_now, table_low, devices))

    all_rows = lax.while_loop(lambda state: state[0] < rounds, more_rows, (1, all_rows))[1]
    token_rows, label_rows = (all_rows[:tokens], all_rows[tokens:])
    pos_local, proj_local = pos_table.shape[0], proj_weight.shape[1]
    if by_rows:
        where, matrices = block_plan(devices, chunk, layers, (pos_local, proj_local)), []
    else:
        where = ()
        flat_all = weights_all.reshape(devices, -1)
        split = []
        for index in range(layers):
            wide = flat_all[:, index * flat_local : (index + 1) * flat_local].reshape(WIDE, DS)
            qkv, out, up, down = split_rows(wide, DS, FS)
            split.append(
                (
                    qkv.reshape(DS, 3, DS).transpose(1, 0, 2),
                    out,
                    jnp.pad(up, ((0, 0), (0, WIDER - FS))),
                    jnp.pad(down, ((0, WIDER - FS), (0, 0))),
                )
            )
        matrices = sum(map(list, split), [])
        start = layers * flat_local
        places_all = flat_all[:, start : start + pos_local * DS].reshape(length, DS)
        start += pos_local * DS
        matrices += [places_all, flat_all[:, start : start + proj_local * DS].reshape(DT, DS)]

    proj_bias = misc_vec[2 * DS :]
    evec = misc_vec[: 2 * DS].reshape(2, DS)
    cut = 5 * DS
    vectors = jnp.concatenate([layer_vec[:, :cut], layer_vec[:, cut + FS :]], 1).reshape(
        layers, 8, DS
    )
    biases = jnp.pad(layer_vec[:, cut : cut + FS], ((0, 0), (0, WIDER - FS)))[:, None]

    mask = jnp.where(pair_mask, 2.0, jnp.where(allowed, 1.0, 0.0)).reshape(tokens, length)
    matrices, made = student_forward(
        token_rows, evec, vectors, biases, mask, where, weights_all, matrices
    )
    embedded, normed_zero, inverse_zero, hidden, *saved = made
    proj_all = matrices[-1]
    slice_part = lax.optimization_barrier((slice_part, teacher_all, hidden))[0]
    slice_table = lax.all_gather(slice_part, "dp", axis=0, tiled=True)

    flat_pick = (
        jnp.arange(rows, dtype=jnp.int32)[:, None] * length + mask_pos.reshape(rows, picks)
    ).reshape(-1)
    weight = valid_mask.reshape(tokens, 1).astype(jnp.float32)
    t_scores, back_zero, back_last, grad_proj, grad_bias, squares_of, picked_all, t_picked = (
        teacher_forward(
            teacher_in.reshape(tokens, DT),
            teacher_all,
            teacher_vec.astype(jnp.float32)[None],
            mask,
            embedded,
            hidden,
            proj_all,
            proj_bias[None],
            weight,
            flat_pick[:, None],
            hidden_denom,
        )
    )
    hidden_sum = jnp.sum(squares_of) / hidden_denom
    pick_marks = (flat_pick[:, None] == lax.broadcasted_iota(jnp.int32, (1, tokens), 1)).astype(
        jnp.bfloat16
    )
    picked = lax.dynamic_index_in_dim(picked_all, place, 0, False)
    d_picked, own_stats, head_grad = head(
        picked_all, t_picked, slice_table, teacher_head, predict_denom, 4
    )
    own_z = place // (groups // z_size_of(groups))
    own_stats = lax.dynamic_slice_in_dim(own_stats, own_z * rows * picks, rows * picks, 1)
    picked_wide = picked.astype(jnp.float32)
    target_logit = jnp.sum(picked_wide * label_rows, -1)
    predict_sum = (
        jnp.sum(2.0 * own_stats[0] - own_stats[3] - target_logit) / predict_denom
    )
    d_picked = d_picked[:, :width] - label_rows / predict_denom
    d_hidden = pick_exact(pick_marks, d_picked, True) + back_last

    if n_dp != 4:
        head_grad = lax.psum_scatter(head_grad, "dp", scatter_dimension=0, tiled=True)

    matrix_grads = [None] * layers
    vector_grads = [None] * layers
    attention_sum = jnp.float32(0.0)
    head_grad = lax.ppermute(head_grad, BOTH, to_owner)
    for layer_index in reversed(range(layers)):
        d_hidden, *others = student_backward(
            d_hidden,
            vectors[layer_index],
            biases[layer_index],
            mask,
            matrices[4 * layer_index : 4 * layer_index + 4],
            saved[7 * layer_index : 7 * layer_index + 7],
            [t_scores, count.reshape(1, 1)] if layer_index == layers - 1 else [],
            [] if layer_index else [back_zero, normed_zero, inverse_zero, evec],
        )
        matrix_grads[layer_index] = others[:6]
        d_vectors, d_bias_up, more = others[6], others[7], others[8:]
        d_vectors = d_vectors.reshape(-1)
        vector_grads[layer_index] = jnp.concatenate(
            [d_vectors[:cut], d_bias_up[0, :FS], d_vectors[cut:]]
        )
        if layer_index == layers - 1:
            attention_sum = jnp.sum(more.pop(0)) / count
    d_hidden, head_grad = lax.optimization_barrier((d_hidden, head_grad))
    d_token, (grad_places, d_edge) = d_hidden, more

    row_grads = jnp.concatenate([d_token, -picked_wide / predict_denom])
    def more_grads(state):
        turn, so_far = state
        marks_now, wanted_now = ask(plan, turn, devices, extra)
        return (
            turn + 1,
            so_far + give_back(marks_now, wanted_now, row_grads, local_rows, devices),
        )

    grad_small = jnp.concatenate(vector_grads + [d_edge[0], d_edge[1], grad_bias[0]])
    small_local = -(-grad_small.shape[0] // devices)
    small_local = -(-small_local // DS) * DS
    small_padded = jnp.pad(grad_small, (0, devices * small_local - grad_small.shape[0]))
    rest = [grad_places, grad_proj, small_padded.reshape(-1, DS)]
    sizes = [flat_local] * layers + [part.size // devices for part in rest]
    lines = -(-sum(sizes) // line)
    block = (-(-lines // 8) * 8, line)
    sent = pick_exact(marks, row_grads).reshape(devices, SLOTS, width)
    if by_rows:
        amounts = [size // DS for size in sizes[layers:]]
        grad_parts = sum(matrix_grads, []) + rest
        block_rows_of = block_plan(devices, chunk, layers, amounts)
    else:
        wides = []
        for grads in matrix_grads:
            first = jnp.stack(grads[:3], 1).reshape(-1, width)
            wides.append(jnp.concatenate([first, *grads[3:]]))
        grad_parts = [pack([part.reshape(devices, -1) for part in wides + rest], *block[::-1])]
        block_rows_of = ()
    reduced, row_blocks = reduce(grad_parts, block_rows_of, block, sent, 7)
    more = jnp.zeros((local_rows, width), jnp.float32)
    more = lax.while_loop(lambda state: state[0] < rounds, more_grads, (1, more))[1]
    if by_rows:
        pieces = []
        start = 0
        for size in sizes:
            pieces.append(reduced[start : start + size // DS])
            start += size // DS
    else:
        pieces = cut_pieces(reduced.reshape(-1), sizes)
    if by_rows:
        pieces[:layers] = [woven(piece, True) for piece in pieces[:layers]]
    layer_acc = jnp.stack([piece.reshape(-1) for piece in pieces[:layers]])
    g_places = pieces[layers].reshape(pos_local, DS)
    g_proj = pieces[layers + 1].reshape(proj_local, DS).T
    small_part = pieces[layers + 2].reshape(-1)
    note = jnp.concatenate(
        [small_part, (attention_sum + hidden_sum + predict_sum).reshape(1)]
    )
    note = jnp.pad(note, (0, -(-(small_local + 2) // 128) * 128 - note.shape[0])).reshape(1, -1)
    g_table, notes_all = finish(
        row_blocks.reshape(devices * SLOTS, width),
        wanted,
        more,
        head_grad,
        reduced,
        note,
        small_local + 1,
        8,
    )
    g_table, notes_all = g_table.T, notes_all[:, 0]
    small = notes_all[:, :small_local].reshape(-1)
    loss = jnp.sum(notes_all[:, small_local])
    norm = jnp.sqrt(jnp.sum(notes_all[:, small_local + 1]))
    g_vec = small[: layer_vec.size].reshape(layer_vec.shape)
    g_misc = small[layer_vec.size : layer_vec.size + misc_vec.shape[0]]
    factor = CLIP_NORM / jnp.maximum(norm, CLIP_NORM)
    return (
        loss,
        count,
        norm,
        *adam_update(emb_table, emb_first, emb_second, g_table * factor),
        *adam_update(pos_table, pos_first, pos_second, g_places * factor),
        *adam_update(layer_flat, layer_first, layer_second, layer_acc * factor),
        *adam_update(proj_weight, proj_first, proj_second, g_proj * factor),
        *adam_update(layer_vec, vec_first, vec_second, g_vec * factor),
        *adam_update(misc_vec, misc_first, misc_second, g_misc * factor),
    )


def solution(mesh):
    rows, lines, flat, tail, every = (
        P(None, BOTH),
        P(BOTH, None),
        P(BOTH),
        P(None, BOTH),
        P(),
    )
    placed = (
        *[rows] * 6,
        flat,
        every,
        P("fsdp", None),
        *[lines] * 6,
        *[tail] * 6,
        *[every] * 6,
    )
    return jax.shard_map(
        local,
        mesh=mesh,
        in_specs=placed,
        out_specs=(*[every] * 3, *[lines] * 6, *[tail] * 6, *[every] * 6),
        check_vma=False,
    )
```

```python
import math
from functools import partial

import jax
import jax.numpy as jnp
from jax import lax
from jax.experimental import pallas as pl
from jax.experimental.pallas import tpu as pltpu
from jax.sharding import PartitionSpec as P

DS = 312
HS = 12
FS = 1200
DT = 768
HT = 12
FT = 3072
STEP = 5


NORM_EPS = 1e-06
CLIP_NORM = 0.05
LEARN_RATE = 0.05
BETA_ONE = 0.9
BETA_TWO = 0.999
ADAM_EPS = 1e-06
WEIGHT_DECAY = 0.01
NEG_LARGE = -1e30

BOTH = ("dp", "fsdp")
MESH = pl.DeviceIdType.MESH
SLOTS = 48
WIDE = 3 * DS + DS + 2 * FS


def z_size_of(fsdp):
    return 4 if fsdp % 4 == 0 else 1


def place_of():
    fsdp = lax.axis_size("fsdp")
    return lax.axis_index("dp") * fsdp + lax.axis_index("fsdp")


def member(index, whole):
    fsdp = lax.axis_size("fsdp")
    if whole:
        return (index // fsdp, index % fsdp)
    return (lax.axis_index("dp"), index)


def greet(count, me, whole):
    barrier = pltpu.get_barrier_semaphore()

    def signal(step, carry):
        pl.semaphore_signal(
            barrier, inc=1, device_id=member((me + step) % count, whole), device_id_type=MESH
        )
        return carry

    lax.fori_loop(1, count, signal, 0)
    pl.semaphore_wait(barrier, count - 1)


def exchange_kernel(count, whole, spread, x_ref, o_ref, send, recv, local_sem):
    me = place_of() if whole else lax.axis_index("fsdp")
    own = pltpu.make_async_copy(x_ref if spread else x_ref.at[me], o_ref.at[me], local_sem)
    own.start()
    greet(count, me, whole)

    def copy(step):
        peer = (me + step) % count
        return pltpu.make_async_remote_copy(
            x_ref if spread else x_ref.at[peer],
            o_ref.at[me],
            send.at[step],
            recv.at[step],
            device_id=member(peer, whole),
            device_id_type=MESH,
        )

    def start(step, carry):
        copy(step).start()
        return carry

    def finish(step, carry):
        copy(step).wait()
        return carry

    lax.fori_loop(1, count, start, 0)
    own.wait()
    lax.fori_loop(1, count, finish, 0)


def exchange(x, number, whole=True, spread=False):
    count = lax.axis_size("fsdp") * (lax.axis_size("dp") if whole else 1)
    return pl.pallas_call(
        partial(exchange_kernel, count, whole, spread),
        out_shape=jax.ShapeDtypeStruct(((count,) if spread else ()) + x.shape, x.dtype),
        in_specs=[pl.BlockSpec(memory_space=pl.ANY)],
        out_specs=pl.BlockSpec(memory_space=pl.ANY),
        scratch_shapes=[
            pltpu.SemaphoreType.DMA((count,)),
            pltpu.SemaphoreType.DMA((count,)),
            pltpu.SemaphoreType.DMA,
        ],
        compiler_params=pltpu.CompilerParams(collective_id=number, has_side_effects=True),
    )(x)


VMEM_SPEC = pl.BlockSpec(memory_space=pltpu.VMEM)


class Grid:
    def __init__(self):
        self.fsdp = lax.axis_size("fsdp")
        self.z_size = z_size_of(self.fsdp)
        self.side = self.fsdp // self.z_size
        assert lax.axis_size("dp") == 2 * self.side
        dp, fsdp = lax.axis_index("dp"), lax.axis_index("fsdp")
        self.x, self.core = dp // 2, dp % 2
        self.z, self.y = fsdp // self.side, fsdp % self.side
        side, z_size = self.side, self.z_size
        self.keys = [(g, b, a) for g in range(side) for b in range(side) for a in range(z_size)]
        self.rank = {key: index for index, key in enumerate(self.keys)}
        self.count = len(self.keys)

    def at(self, third, second, z, other=0):
        core = (self.core + other) % 2
        x = (self.x + third * (1 - core) + second * core) % self.side
        y = (self.y + second * (1 - core) + third * core) % self.side
        return (x * 2 + core, ((self.z + z) % self.z_size) * self.side + y)

    def index(self, third, second, z, other=0):
        dp, fsdp = self.at(third, second, z, other)
        return dp * self.fsdp + fsdp

    def neighbours(self):
        return (
            [(0, 0, a, 0) for a in range(1, self.z_size)]
            + [(0, b, 0, 0) for b in range(1, self.side)]
            + [(g, 0, 0, 0) for g in range(1, self.side)]
            + [(0, 0, 0, 1)]
        )

    def greet(self):
        barrier = pltpu.get_barrier_semaphore()
        around = self.neighbours()
        for where in around:
            pl.semaphore_signal(barrier, inc=1, device_id=self.at(*where), device_id_type=MESH)
        pl.semaphore_wait(barrier, len(around))


class Spread:
    def __init__(self, grid, x_ref, o_ref, send, recv, local_sem):
        self.grid, self.x_ref, self.o_ref = grid, x_ref, o_ref
        self.send, self.recv = send, recv
        self.started = []
        self.own = pltpu.make_async_copy(x_ref, o_ref.at[self.slot((0, 0, 0))], local_sem)
        self.own.start()

    def slot(self, key, other=0):
        grid = self.grid
        third, second, z = key
        return grid.index(grid.side - third, grid.side - second, grid.z_size - z, other)

    def push(self, key, name, where):
        grid = self.grid
        index = grid.rank[name] + (grid.count if where[3] else 0)
        copy = pltpu.make_async_remote_copy(
            self.x_ref if key == (0, 0, 0) else self.o_ref.at[self.slot(key)],
            self.o_ref.at[self.slot(key)],
            self.send.at[index],
            self.recv.at[index],
            device_id=grid.at(*where),
            device_id_type=MESH,
        )
        copy.start()
        self.started.append(copy)

    def forward(self, key):
        grid = self.grid
        third, second, z = key
        if key == (0, 0, 0):
            for step in range(1, grid.z_size):
                self.push(key, (0, 0, step), (0, 0, step, 0))
        if third == 0 and second == 0:
            for step in range(1, grid.side):
                self.push(key, (0, step, z), (0, step, 0, 0))
        if third == 0:
            for step in range(1, grid.side):
                self.push(key, (step, second, z), (step, 0, 0, 0))
        self.push(key, key, (0, 0, 0, 1))

    def arrived(self, key, other=0):
        grid = self.grid
        index = grid.rank[key] + (grid.count if other else 0)
        pltpu.make_async_remote_copy(
            self.o_ref.at[self.slot(key, other)],
            self.o_ref.at[self.slot(key, other)],
            self.send.at[index],
            self.recv.at[index],
            device_id=grid.at(0, 0, 0, 1),
            device_id_type=MESH,
        ).wait_recv()

    def start(self):
        self.forward((0, 0, 0))

    def middle(self):
        for key in self.grid.keys[1:]:
            self.arrived(key)
            self.forward(key)

    def finish(self):
        for key in self.grid.keys:
            self.arrived(key, 1)
        self.own.wait()
        for copy in self.started:
            copy.wait_send()


def entry_kernel(
    ask_ref, w_ref, table_ref, got_ref, all_ref, rows_ref, sent, asks, *sems
):
    ask_send, ask_recv, ask_local, w_send, w_recv, w_local, row_send, row_recv, row_local, out_sem = sems
    grid = Grid()
    count = 2 * grid.count
    me = place_of()
    own = pltpu.make_async_copy(ask_ref.at[me], asks.at[me], ask_local)
    own.start()
    greet(count, me, True)

    def ask_copy(step):
        peer = (me + step) % count
        return pltpu.make_async_remote_copy(
            ask_ref.at[peer],
            asks.at[me],
            ask_send.at[step],
            ask_recv.at[step],
            device_id=member(peer, True),
            device_id_type=MESH,
        )

    def row_copy(step):
        peer = (me + step) % count
        return pltpu.make_async_remote_copy(
            sent.at[peer],
            rows_ref.at[me],
            row_send.at[step],
            row_recv.at[step],
            device_id=member(peer, True),
            device_id_type=MESH,
        )

    def each(first, action):
        def body(step, carry):
            action(step)
            return carry

        lax.fori_loop(first, count, body, 0)

    each(1, lambda step: ask_copy(step).start())
    spread = Spread(grid, w_ref, all_ref, w_send, w_recv, w_local)
    spread.start()
    own.wait()
    table = table_ref[...]
    line = lax.broadcasted_iota(jnp.int32, (table.shape[0], 128), 0)

    def answer(source):
        marks = jnp.where(line == asks[source], 1.0, 0.0).astype(jnp.bfloat16)
        sent[source] = outer_product(marks, table)[:SLOTS].astype(jnp.bfloat16)

    answer(me)
    mine = pltpu.make_async_copy(sent.at[me], rows_ref.at[me], row_local)
    mine.start()

    def serve(step):
        ask_copy(step).wait_recv()
        answer((me + count - step) % count)

    each(1, serve)
    each(1, lambda step: row_copy(step).start())
    keep = pltpu.make_async_copy(asks, got_ref, out_sem)
    keep.start()
    spread.middle()
    spread.finish()
    mine.wait()
    keep.wait()
    each(1, lambda step: row_copy(step).wait())
    each(1, lambda step: ask_copy(step).wait_send())


def entry(asked, weights, table_low, number):
    count = asked.shape[0]
    width = table_low.shape[1]
    anywhere = pl.BlockSpec(memory_space=pl.ANY)
    dma = pltpu.SemaphoreType.DMA
    return pl.pallas_call(
        entry_kernel,
        out_shape=(
            jax.ShapeDtypeStruct(asked.shape, asked.dtype),
            jax.ShapeDtypeStruct((count,) + weights.shape, weights.dtype),
            jax.ShapeDtypeStruct((count, SLOTS, width), table_low.dtype),
        ),
        in_specs=[anywhere, anywhere, pl.BlockSpec(memory_space=pltpu.VMEM)],
        out_specs=(anywhere, VMEM_SPEC, VMEM_SPEC),
        scratch_shapes=[
            pltpu.VMEM((count, SLOTS, width), table_low.dtype),
            pltpu.VMEM(asked.shape, asked.dtype),
            *[dma((count,)), dma((count,)), dma] * 3,
            dma,
        ],
        compiler_params=pltpu.CompilerParams(
            collective_id=number, has_side_effects=True, vmem_limit_bytes=32 * 1024 * 1024
        ),
    )(asked, weights, table_low)


def reduce_kernel(plan, sources, *refs):
    ins, rest = refs[:sources], refs[sources:]
    row_ref, o_ref, got_ref = rest[:3]
    if plan:
        x_ref, rest = rest[3], rest[1:]
    else:
        x_ref = ins[0]
    held, third_in, second_in, z_in, send, recv, row_send, row_recv, row_local = rest[3:]
    grid = Grid()
    side, z_size, count, rank = grid.side, grid.z_size, grid.count, grid.rank
    order = sorted(grid.keys, key=lambda key: (key[0] == 0, key[1] == 0, key[2] == 0))
    devices = 2 * count
    me = place_of()
    own = pltpu.make_async_copy(row_ref.at[me], got_ref.at[me], row_local)
    own.start()
    greet(devices, me, True)

    def row_copy(step):
        peer = (me + step) % devices
        return pltpu.make_async_remote_copy(
            row_ref.at[peer],
            got_ref.at[me],
            row_send.at[step],
            row_recv.at[step],
            device_id=member(peer, True),
            device_id_type=MESH,
        )

    def row_start(step, carry):
        row_copy(step).start()
        return carry

    def row_finish(step, carry):
        row_copy(step).wait()
        return carry

    lax.fori_loop(1, devices, row_start, 0)
    started = []

    def push(source, target, index, where):
        copy = pltpu.make_async_remote_copy(
            source,
            target,
            send.at[index],
            recv.at[index],
            device_id=grid.at(*where),
            device_id_type=MESH,
        )
        copy.start()
        started.append(copy)

    def arrived(target, index):
        pltpu.make_async_remote_copy(
            target,
            target,
            send.at[index],
            recv.at[index],
            device_id=grid.at(0, 0, 0, 1),
            device_id_type=MESH,
        ).wait_recv()

    for source, at, rows, block, line in plan:
        value = jnp.zeros((rows, x_ref.shape[2]), x_ref.dtype)
        if source >= 0:
            value = ins[source][at : at + rows, :]
        x_ref[block, line : line + rows, :] = value
    for key in order:
        push(x_ref.at[grid.index(*key, 1)], held.at[rank[key]], rank[key], (0, 0, 0, 1))
    from_third = {}
    from_second = {}
    from_z = {}
    index = count
    for step in range(1, side):
        for second in range(side):
            for z in range(z_size):
                from_third[step, second, z] = (
                    third_in.at[((step - 1) * side + second) * z_size + z],
                    index,
                )
                index += 1
    for step in range(1, side):
        for z in range(z_size):
            from_second[step, z] = (second_in.at[(step - 1) * z_size + z], index)
            index += 1
    for way in (1, -1):
        for distance in range(z_size - 1):
            from_z[way, distance] = (z_in.at[len(from_z)], index)
            index += 1

    def gathered(key):
        third, second, z = key
        arrived(held.at[rank[key]], rank[key])
        total = held[rank[key]] + x_ref[grid.index(*key)]
        if third == 0:
            for step in range(1, side):
                arrived(*from_third[step, second, z])
                total = total + from_third[step, second, z][0][...]
        if third == 0 and second == 0:
            for step in range(1, side):
                arrived(*from_second[step, z])
                total = total + from_second[step, z][0][...]
        return total

    for key in order:
        third, second, z = key
        if third == 0 and second == 0:
            continue
        held[rank[key]] = gathered(key)
        if third:
            target, where = from_third[third, second, z], (third, 0, 0, 0)
        else:
            target, where = from_second[second, z], (0, second, 0, 0)
        push(held.at[rank[key]], target[0], target[1], where)

    def behind(way):
        return (grid.z > 0) if way > 0 else (grid.z < z_size - 1)

    def hop(way, distance):
        target = from_z[way, distance - 1]
        return pltpu.make_async_remote_copy(
            held.at[rank[0, 0, way * distance % z_size]],
            target[0],
            send.at[target[1]],
            recv.at[target[1]],
            device_id=grid.at(0, 0, way % z_size),
            device_id_type=MESH,
        )

    def reaches(way, distance):
        return (grid.z + way * distance >= 0) & (grid.z + way * distance < z_size)

    for distance in range(z_size - 1, 0, -1):
        for way in (1, -1):

            @pl.when(reaches(way, distance))
            def _(way=way, distance=distance):
                key = (0, 0, way * distance % z_size)
                held[rank[key]] = gathered(key)
                if distance < z_size - 1:

                    @pl.when(behind(way))
                    def _():
                        arrived(*from_z[way, distance])
                        held[rank[key]] += from_z[way, distance][0][...]

                hop(way, distance).start()

    o_ref[...] = gathered((0, 0, 0))
    for way in (1, -1):

        @pl.when(behind(way))
        def _(way=way):
            arrived(*from_z[way, 0])
            o_ref[...] += from_z[way, 0][0][...]

    for distance in range(z_size - 1, 0, -1):
        for way in (1, -1):
            pl.when(reaches(way, distance))(hop(way, distance).wait_send)
    for copy in started:
        copy.wait_send()
    own.wait()
    lax.fori_loop(1, devices, row_finish, 0)


def reduce(parts, plan, block, rows, number):
    count = lax.axis_size("dp") * lax.axis_size("fsdp")
    side = lax.axis_size("dp") // 2
    z_size = count // 2 // side // side
    kind = parts[0].dtype
    vmem, anywhere = pl.BlockSpec(memory_space=pltpu.VMEM), pl.BlockSpec(memory_space=pl.ANY)
    dma = pltpu.SemaphoreType.DMA
    return pl.pallas_call(
        partial(reduce_kernel, plan, len(parts)),
        out_shape=(
            jax.ShapeDtypeStruct(block, kind),
            jax.ShapeDtypeStruct(rows.shape, rows.dtype),
        ),
        in_specs=[vmem] * len(parts) + [anywhere],
        out_specs=(vmem, anywhere),
        scratch_shapes=[
            *([pltpu.VMEM((count,) + block, kind)] if plan else []),
            pltpu.VMEM((count // 2,) + block, kind),
            pltpu.VMEM(((side - 1) * side * z_size,) + block, kind),
            pltpu.VMEM(((side - 1) * z_size,) + block, kind),
            pltpu.VMEM((2 * (z_size - 1),) + block, kind),
            *[dma((count + z_size,))] * 2,
            *[dma((count,))] * 2,
            dma,
        ],
        compiler_params=pltpu.CompilerParams(
            collective_id=number, has_side_effects=True, vmem_limit_bytes=58 * 1024 * 1024
        ),
    )(*parts, rows)


def woven(block, weave):
    chunk = block.shape[0]
    me = place_of()
    made = block
    for index in range(-(-3 * DS // chunk)):
        amount = min(chunk, 3 * DS - index * chunk)
        head = block[:amount].reshape((3, amount // 3, DS) if weave else (amount // 3, 3, DS))
        head = head.transpose(1, 0, 2).reshape(amount, DS)
        if index == 0:
            made = jnp.where(me < 3 * DS // chunk, head, made)
        elif amount < chunk:
            made = jnp.where(me == index, jnp.concatenate([head, block[amount:]]), made)
    return made


def block_plan(devices, chunk, layers, others):
    plan = []
    for block in range(devices):
        for layer in range(layers):
            base = 6 * layer
            row, end, line = block * chunk, (block + 1) * chunk, layer * chunk
            first = row
            if row < 3 * DS:
                stop = min(end, 3 * DS)
                amount = (stop - row) // 3
                for part in range(3):
                    plan.append((base + part, row // 3, amount, block, line + part * amount))
                row = stop
            for part, start, size in ((3, 3 * DS, DS), (4, 4 * DS, FS), (5, 4 * DS + FS, FS)):
                stop = min(end, start + size)
                if row < stop:
                    where = line + row - first
                    plan.append((base + part, row - start, stop - row, block, where))
                    row = stop
        line = layers * chunk
        for index, amount in enumerate(others):
            plan.append((6 * layers + index, block * amount, amount, block, line))
            line += amount
        spare = -line % 8
        if spare:
            plan.append((-1, 0, spare, block, line))
    return tuple(plan)


def pack(parts, width, rows):
    count = parts[0].shape[0]
    if all(part.ndim == 3 for part in parts):
        joined = jnp.concatenate(parts, 1)
        return jnp.pad(joined, ((0, 0), (0, rows - joined.shape[1]), (0, 0)))
    joined = jnp.concatenate([part.reshape(count, -1) for part in parts], 1)
    joined = jnp.pad(joined, ((0, 0), (0, rows * width - joined.shape[1])))
    return joined.reshape(count, rows, width)


def outer_product(left, right):
    return lax.dot_general(
        left, right, (((0,), (0,)), ((), ())), preferred_element_type=jnp.float32
    )


def back_product(grad, weight):
    return lax.dot_general(
        grad, weight, (((1,), (1,)), ((), ())), preferred_element_type=jnp.float32
    )


def norm_forward(value, gain, bias):
    average = jnp.mean(value, -1, keepdims=True)
    centered = value - average
    inverse = lax.rsqrt(jnp.mean(centered * centered, -1, keepdims=True) + NORM_EPS)
    normed = centered * inverse
    return (normed * gain + bias, normed, inverse)


def cut_pieces(vector, sizes):
    pieces = []
    start = 0
    for amount in sizes:
        pieces.append(vector[..., start : start + amount])
        start += amount
    return pieces


def split_rows(wide, width, hidden):
    first, second, third = 3 * width, 4 * width, 4 * width + hidden
    return (
        wide[:first].reshape(width, 3 * width),
        wide[first:second],
        wide[second:third].reshape(width, hidden),
        wide[third:],
    )


def adam_update(value, first, second, grad):
    first = BETA_ONE * first + (1.0 - BETA_ONE) * grad
    second = BETA_TWO * second + (1.0 - BETA_TWO) * grad * grad
    ratio = first / (1.0 - BETA_ONE**STEP) / (jnp.sqrt(second / (1.0 - BETA_TWO**STEP)) + ADAM_EPS)
    return (first, second, value - LEARN_RATE * (ratio + WEIGHT_DECAY * value))


def gelu(value):
    return 0.5 * value * (1.0 + jnp.tanh(0.7978845608028654 * (value + 0.044715 * value * value * value)))


def regroup(weights, group):
    amount = weights.shape[0]
    made = lax.broadcasted_iota(jnp.int32, (amount, amount), 0)
    taken = lax.broadcasted_iota(jnp.int32, (amount, amount), 1)
    inner = amount // group
    marks = jnp.where((made % inner) * group + made // inner == taken, 1.0, 0.0)
    return jnp.dot(
        marks.astype(jnp.bfloat16), weights, preferred_element_type=jnp.float32
    ).astype(jnp.bfloat16)


def softmax_low(scores, mask):
    masked = jnp.where(mask > 0.0, scores, NEG_LARGE)
    expo = jnp.exp(masked - jnp.max(masked, -1, keepdims=True))
    return (expo * (1.0 / jnp.sum(expo, -1, keepdims=True))).astype(jnp.bfloat16)


TILE = 256
CHUNK = 96


def teacher_kernel(
    denom, x_ref, w_ref, vec_ref, mask_ref, zero_ref, last_ref, proj_ref, bias_ref, weight_ref, pick_ref,
    s_ref, back_zero, back_last, proj_out, bias_out, loss_ref, picked_ref, t_picked_ref,
    low_ref, qkv_ref, up_ref, context_ref, sent, send, recv,
):
    size = DT // HT
    tokens = x_ref.shape[0]
    line = lax.broadcasted_iota(jnp.int32, (pick_ref.shape[0], tokens), 1)
    marks = jnp.where(pick_ref[...] == line, 1.0, 0.0).astype(jnp.bfloat16)
    me, groups = lax.axis_index("fsdp"), lax.axis_size("fsdp")
    own = jnp.dot(
        marks, last_ref[...].astype(jnp.bfloat16), preferred_element_type=jnp.float32
    ).astype(jnp.bfloat16)
    sent[...] = own
    picked_ref[me] = own
    greet(groups, me, False)

    def copy(step):
        return pltpu.make_async_remote_copy(
            sent,
            picked_ref.at[me],
            send.at[step],
            recv.at[step],
            device_id=member((me + step) % groups, False),
            device_id_type=MESH,
        )

    for step in range(1, groups):
        copy(step).start()
    for ref in (proj_out, bias_out, loss_ref):
        ref[...] = jnp.zeros_like(ref)
    for index in range(3 * DT // CHUNK):
        made = regroup(w_ref[index], 3)
        for part in range(3):
            rows = CHUNK // 3
            qkv_ref[part, index * rows : (index + 1) * rows, :] = made[part * rows : (part + 1) * rows]
    first_up, first_down = 4 * DT // CHUNK, (4 * DT + FT) // CHUNK
    many = FT // DT
    for index in range(FT // CHUNK // 2):
        at = first_up + 2 * index
        made = regroup(w_ref[at : at + 2].reshape(2 * CHUNK, DT), many)
        rows = 2 * CHUNK // many
        for part in range(many):
            up_ref[part, index * rows : (index + 1) * rows, :] = made[part * rows : (part + 1) * rows]
    line = lax.broadcasted_iota(jnp.int32, (1, 2 * size), 1)
    low_half = line < size
    length = mask_ref.shape[1]

    def vector(index, amount=1):
        return vec_ref[:, index * DT : (index + amount) * DT]

    def tile(step, carry):
        at = pl.ds(pl.multiple_of(step * TILE, TILE), TILE)
        x_low = x_ref[at, :]
        q, k, v = (
            (
                jnp.dot(x_low, qkv_ref[part], preferred_element_type=jnp.float32) + vector(part)
            ).astype(jnp.bfloat16)
            for part in range(3)
        )
        nothing = jnp.zeros((length, 2 * size), jnp.bfloat16)
        for row in range(TILE // length):
            span = slice(row * length, (row + 1) * length)
            here = pl.ds(pl.multiple_of(step * TILE + row * length, length), length)
            mask = mask_ref[here, :]
            for pair in range(HT // 2):
                lanes = slice(pair * 2 * size, (pair + 1) * 2 * size)
                k_pair, v_pair = k[span, lanes], v[span, lanes]
                k_both = jnp.concatenate(
                    [jnp.where(low_half, k_pair, nothing), jnp.where(low_half, nothing, k_pair)]
                )
                v_both = jnp.concatenate(
                    [jnp.where(low_half, v_pair, nothing), jnp.where(low_half, nothing, v_pair)]
                )
                scores = back_product(q[span, lanes], k_both) * size ** (-0.5)
                s_ref[here, pair * 2 * length : (pair + 1) * 2 * length] = scores
                weights = jnp.concatenate(
                    [softmax_low(scores[:, :length], mask), softmax_low(scores[:, length:], mask)], 1
                )
                context_ref[span, lanes] = jnp.dot(
                    weights, v_both, preferred_element_type=jnp.float32
                ).astype(jnp.bfloat16)
        w_out = w_ref[3 * DT // CHUNK : first_up].reshape(DT, DT)
        attended = jnp.dot(context_ref[...], w_out, preferred_element_type=jnp.float32) + vector(3)
        middle = norm_forward(x_low.astype(jnp.float32) + attended, vector(4), vector(5))[0]
        middle_low = middle.astype(jnp.bfloat16)
        outer = jnp.zeros((TILE, DT), jnp.float32)
        for part in range(many):
            inner = jnp.dot(middle_low, up_ref[part], preferred_element_type=jnp.float32) + vector(
                6 + part
            )
            begin = first_down + part * (DT // CHUNK)
            w_down = w_ref[begin : begin + DT // CHUNK].reshape(DT, DT)
            outer = outer + jnp.dot(
                gelu(inner).astype(jnp.bfloat16), w_down, preferred_element_type=jnp.float32
            )
        made = norm_forward(
            middle + outer + vector(6 + many), vector(7 + many), vector(8 + many)
        )[0]
        low_ref[at, :] = made.astype(jnp.bfloat16)
        pairs = ((zero_ref, x_low.astype(jnp.float32), back_zero), (last_ref, made, back_last))
        for source_ref, target, back_ref in pairs:
            source = source_ref[at, :].astype(jnp.bfloat16)
            spread = back_product(source, proj_ref[...]) + bias_ref[...] - target
            weighted = spread * weight_ref[at, :]
            loss_ref[...] += jnp.sum(weighted * spread, 0, keepdims=True)
            d_mapped = (weighted * (2.0 / denom)).astype(jnp.bfloat16)
            back_ref[at, :] = jnp.dot(d_mapped, proj_ref[...], preferred_element_type=jnp.float32)
            proj_out[...] += outer_product(d_mapped, source)
            bias_out[...] += jnp.sum(d_mapped.astype(jnp.float32), 0, keepdims=True)
        return carry

    lax.fori_loop(0, tokens // TILE, tile, 0)
    t_picked_ref[...] = jnp.dot(
        marks, low_ref[...], preferred_element_type=jnp.float32
    ).astype(jnp.bfloat16)
    for step in range(1, groups):
        copy(step).wait()


def teacher_forward(x_low, blocks, vectors, mask, embedded, last, proj, bias, weight, picks, denom):
    tokens, length = mask.shape
    full = partial(jax.ShapeDtypeStruct, dtype=jnp.float32)
    low = partial(jax.ShapeDtypeStruct, dtype=jnp.bfloat16)
    amount, groups = picks.shape[0], lax.axis_size("fsdp")
    made = (
        full((tokens, HT * length)),
        full((tokens, DS)),
        full((tokens, DS)),
        full((DT, DS)),
        full((1, DT)),
        full((1, DT)),
        low((groups, amount, DS)),
        low((amount, DT)),
    )
    given = (x_low, blocks, vectors, mask, embedded, last, proj, bias, weight, picks)
    return pl.pallas_call(
        partial(teacher_kernel, denom),
        out_shape=made,
        in_specs=[VMEM_SPEC] * len(given),
        out_specs=(VMEM_SPEC,) * len(made),
        scratch_shapes=[
            pltpu.VMEM((tokens, DT), jnp.bfloat16),
            pltpu.VMEM((3, DT, DT), jnp.bfloat16),
            pltpu.VMEM((FT // DT, DT, DT), jnp.bfloat16),
            pltpu.VMEM((TILE, DT), jnp.bfloat16),
            pltpu.VMEM((amount, DS), jnp.bfloat16),
            *[pltpu.SemaphoreType.DMA((groups,))] * 2,
        ],
        compiler_params=pltpu.CompilerParams(
            collective_id=5, has_side_effects=True, vmem_limit_bytes=58 * 1024 * 1024
        ),
        cost_estimate=pl.CostEstimate(
            flops=20 * 10**9, bytes_accessed=25 * 10**6, transcendentals=5 * 10**6
        ),
    )(*given)


WIDER = -(-FS // 128) * 128


def refold(source, target, source_width, target_width):
    period = math.lcm(source_width, target_width)
    groups = source.shape[1] * source_width // period
    step_in, step_out = period // source_width, period // target_width
    lane = lax.broadcasted_iota(jnp.int32, (groups, 128), 1)
    for row in range(step_out):
        for tile in range(-(-target_width // 128)):
            begin = row * target_width + 128 * tile
            amount = min(128, target_width - 128 * tile)
            made, at = jnp.zeros((groups, 128), source.dtype), 0
            while at < amount:
                line, column = divmod(begin + at, source_width)
                where, lanes = divmod(column, 128)
                piece = source[where, pl.ds(line, groups, stride=step_in), :]
                if (at - lanes) % 128:
                    piece = pltpu.roll(piece, (at - lanes) % 128, 1)
                length = min(128 - lanes, source_width - column, amount - at)
                made = jnp.where((lane >= at) & (lane < at + length), piece, made)
                at += length
            target[tile, pl.ds(row, groups, stride=step_out), :] = made


def unpack_into(plan, layers, w_ref, *refs):
    place_ref, proj_ref, square, wide, folded, unfolded, small = refs[4 * layers :]
    for layer in range(layers):
        qkv_ref, out_ref, up_ref, down_ref = refs[4 * layer : 4 * layer + 4]
        for matrix, at, rows, block, line in plan:
            part = matrix - 6 * layer
            if not 0 <= part < 6:
                continue
            value = w_ref[block].astype(jnp.float32)[line : line + rows]
            if part < 4:
                square[part, at : at + rows, :] = value
            elif part == 4:
                for tile in range(-(-DS // 128)):
                    lanes = min(128, DS - 128 * tile)
                    folded[tile, at : at + rows, :lanes] = value[:, 128 * tile : 128 * tile + lanes]
            else:
                wide[at : at + rows, :] = value
        for part in range(3):
            qkv_ref[part] = square[part].astype(jnp.bfloat16)
        out_ref[...] = square[3].astype(jnp.bfloat16)
        refold(folded, unfolded, DS, FS)
        for tile in range(WIDER // 128):
            up_ref[:, 128 * tile : 128 * tile + 128] = unfolded[tile].astype(jnp.bfloat16)
        down_ref[:FS, :] = wide[...].astype(jnp.bfloat16)
        down_ref[FS:, :] = jnp.zeros((WIDER - FS, DS), jnp.bfloat16)
    for matrix, at, rows, block, line in plan:
        if matrix >= 6 * layers:
            value = w_ref[block].astype(jnp.float32)[line : line + rows]
            small[matrix - 6 * layers, at : at + rows, :] = value
    place_ref[...] = small[0, : place_ref.shape[0]].astype(jnp.bfloat16)
    proj_ref[...] = small[1].astype(jnp.bfloat16)


def unpack_shapes(layers, length):
    low = partial(jax.ShapeDtypeStruct, dtype=jnp.bfloat16)
    return (
        *[low((3, DS, DS)), low((DS, DS)), low((DS, WIDER)), low((WIDER, DS))] * layers,
        low((length, DS)),
        low((DT, DS)),
    )


def by_heads(value, heads):
    width = value.shape[1]
    size = width // heads
    lane = lax.broadcasted_iota(jnp.int32, (1, width), 1)
    nothing = jnp.zeros_like(value)
    return jnp.concatenate(
        [
            jnp.where((lane >= head * size) & (lane < (head + 1) * size), value, nothing)
            for head in range(heads)
        ]
    )


def student_kernel(
    plan, layers, token_ref, evec_ref, vec_ref, bias_ref, mask_ref, *refs,
):
    ready = 4 * layers + 2
    if plan:
        w_ref, *refs = refs
        unpack_into(plan, layers, w_ref, *refs[:ready], *refs[-5:])
    matrices, place_ref, refs = refs[: 4 * layers], refs[4 * layers], refs[ready:]
    emb_ref, zero_ref, zero_inv, last_ref = refs[:4]
    length = mask_ref.shape[1]
    size = DS // HS

    def tile(step, carry):
        at = pl.ds(pl.multiple_of(step * TILE, TILE), TILE)
        places = jnp.concatenate([place_ref[...].astype(jnp.float32)] * (TILE // length))
        hidden, normed, inverse = norm_forward(
            token_ref[at, :] + places, evec_ref[0:1, :], evec_ref[1:2, :]
        )
        emb_ref[at, :] = hidden
        zero_ref[at, :] = normed
        zero_inv[at, :] = inverse
        for layer in range(layers):
            qkv_w, out_w, up_w, down_w = matrices[4 * layer : 4 * layer + 4]
            low_ref, qkv_ref, context_ref, one_ref, one_inv, two_ref, two_inv = refs[
                4 + 7 * layer : 11 + 7 * layer
            ]

            def vector(index, layer=layer):
                return vec_ref[layer, index : index + 1, :]

            low = hidden.astype(jnp.bfloat16)
            low_ref[at, :] = low
            parts = []
            for part in range(3):
                made = jnp.dot(low, qkv_w[part], preferred_element_type=jnp.float32)
                if part != 1:
                    made = made + vector(part // 2)
                parts.append(made.astype(jnp.bfloat16))
                qkv_ref[part, at, :] = parts[part]
            contexts = []
            for row in range(TILE // length):
                span = slice(row * length, (row + 1) * length)
                here = pl.ds(pl.multiple_of(step * TILE + row * length, length), length)
                mask = mask_ref[here, :]
                q, k, v = (part[span] for part in parts)
                scores = back_product(q, by_heads(k, HS)) * size ** (-0.5)
                weights = jnp.concatenate(
                    [
                        softmax_low(scores[:, head * length : (head + 1) * length], mask)
                        for head in range(HS)
                    ],
                    1,
                )
                contexts.append(
                    jnp.dot(weights, by_heads(v, HS), preferred_element_type=jnp.float32)
                )
            context = jnp.concatenate(contexts).astype(jnp.bfloat16)
            context_ref[at, :] = context
            attended = jnp.dot(context, out_w[...], preferred_element_type=jnp.float32) + vector(2)
            middle, normed, inverse = norm_forward(hidden + attended, vector(3), vector(4))
            one_ref[at, :] = normed
            one_inv[at, :] = inverse
            inner = jnp.dot(
                middle.astype(jnp.bfloat16), up_w[...], preferred_element_type=jnp.float32
            ) + bias_ref[layer]
            outer = jnp.dot(
                gelu(inner).astype(jnp.bfloat16), down_w[...], preferred_element_type=jnp.float32
            ) + vector(5)
            hidden, normed, inverse = norm_forward(middle + outer, vector(6), vector(7))
            two_ref[at, :] = normed
            two_inv[at, :] = inverse
        last_ref[at, :] = hidden
        return carry

    lax.fori_loop(0, token_ref.shape[0] // TILE, tile, 0)


def student_forward(token_rows, evec, vectors, biases, mask, plan, blocks, matrices):
    tokens = token_rows.shape[0]
    layers = vectors.shape[0]
    full = partial(jax.ShapeDtypeStruct, dtype=jnp.float32)
    low = partial(jax.ShapeDtypeStruct, dtype=jnp.bfloat16)
    length = mask.shape[1]
    shapes = () if matrices else unpack_shapes(layers, length)
    made = (
        *shapes,
        full((tokens, DS)),
        full((tokens, DS)),
        full((tokens, 1)),
        full((tokens, DS)),
        *[
            low((tokens, DS)),
            low((3, tokens, DS)),
            low((tokens, DS)),
            full((tokens, DS)),
            full((tokens, 1)),
            full((tokens, DS)),
            full((tokens, 1)),
        ]
        * layers,
    )
    given = (token_rows, evec, vectors, biases, mask, *(matrices or [blocks]))
    all_of = pl.pallas_call(
        partial(student_kernel, plan, layers),
        out_shape=made,
        in_specs=[VMEM_SPEC] * len(given),
        out_specs=(VMEM_SPEC,) * len(made),
        scratch_shapes=(
            []
            if matrices
            else [
                pltpu.VMEM((4, DS, DS), jnp.float32),
                pltpu.VMEM((FS, DS), jnp.float32),
                pltpu.VMEM((-(-DS // 128), FS, 128), jnp.float32),
                pltpu.VMEM((WIDER // 128, DS, 128), jnp.float32),
                pltpu.VMEM((2, DT, DS), jnp.float32),
            ]
        ),
        compiler_params=pltpu.CompilerParams(vmem_limit_bytes=58 * 1024 * 1024),
        cost_estimate=pl.CostEstimate(
            flops=8 * 10**9, bytes_accessed=40 * 10**6, transcendentals=6 * 10**6
        ),
    )(*given)
    return list(all_of[: len(shapes)] or matrices), all_of[len(shapes) :]


def back_kernel(
    last, first_layer, grad_ref, vec_ref, bias_ref, mask_ref, qkv_w, out_w, up_w, down_w,
    low_ref, qkv_ref, context_ref, one_ref, one_inv, two_ref, two_inv, *refs,
):
    if first_layer:
        (more_ref, zero_ref, zero_inv, evec_ref), refs = refs[:4], refs[4:]
    if last:
        score_ref, count_ref, refs = refs[0], refs[1], refs[2:]
    hidden_ref, *weight_refs, vec_out, bias_out, refs = (*refs[:9], refs[9:])
    dq_ref, dk_ref, dv_ref, do_ref, du_ref, dd_ref = weight_refs
    if last:
        loss_ref, refs = refs[0], refs[1:]
        loss_ref[...] = jnp.zeros_like(loss_ref)
    if first_layer:
        (place_ref, edge_ref), refs = refs[:2], refs[2:]
        place_ref[...] = jnp.zeros_like(place_ref)
        edge_ref[...] = jnp.zeros_like(edge_ref)
    outer_s, attended_s, q_s, k_s, v_s, middle_s, active_s, inner_s, unfolded, folded = refs
    length = mask_ref.shape[1]
    size = DS // HS
    vec_out[...] = jnp.zeros_like(vec_out)
    bias_out[...] = jnp.zeros_like(bias_out)
    many = 256

    def vector(index):
        return vec_ref[index : index + 1, :]

    def note(index, value, to=vec_out):
        to[index : index + 1, :] += jnp.sum(value.astype(jnp.float32), 0, keepdims=True)

    def norm_back(grad, normed, inverse, gain, index, to=vec_out):
        d_normed = grad * gain
        note(index, grad * normed, to)
        note(index + 1, grad, to)
        return inverse * (
            d_normed
            - jnp.mean(d_normed, -1, keepdims=True)
            - normed * jnp.mean(d_normed * normed, -1, keepdims=True)
        )

    def tile(step, carry):
        at = pl.ds(pl.multiple_of(step * TILE, TILE), TILE)
        d_sum = norm_back(grad_ref[at, :], two_ref[at, :], two_inv[at, :], vector(6), 6)
        d_outer = d_sum.astype(jnp.bfloat16)
        outer_s[at, :] = d_outer
        note(5, d_outer)
        middle = (one_ref[at, :] * vector(3) + vector(4)).astype(jnp.bfloat16)
        middle_s[at, :] = middle
        d_middle = d_sum
        for first in range(0, WIDER, many):
            lanes = slice(first, first + many)
            inner = jnp.dot(
                middle, up_w[:, lanes], preferred_element_type=jnp.float32
            ) + bias_ref[:, lanes]
            squared = inner * inner
            bent = jnp.tanh(0.7978845608028654 * (inner + 0.044715 * squared * inner))
            active_s[at, lanes] = (0.5 * inner * (1.0 + bent)).astype(jnp.bfloat16)
            slope = 0.5 * (1.0 + bent) + 0.5 * inner * (1.0 - bent * bent) * (
                0.7978845608028654 * (1.0 + 3.0 * 0.044715 * squared)
            )
            d_inner = (back_product(d_outer, down_w[lanes, :]) * slope).astype(jnp.bfloat16)
            inner_s[at, lanes] = d_inner
            bias_out[:, lanes] += jnp.sum(d_inner.astype(jnp.float32), 0, keepdims=True)
            d_middle = d_middle + back_product(d_inner, up_w[:, lanes])
        d_one = norm_back(d_middle, one_ref[at, :], one_inv[at, :], vector(3), 3)
        d_attended = d_one.astype(jnp.bfloat16)
        attended_s[at, :] = d_attended
        note(2, d_attended)
        d_context = back_product(d_attended, out_w[...]).astype(jnp.bfloat16)
        for row in range(TILE // length):
            here = pl.ds(pl.multiple_of(step * TILE + row * length, length), length)
            mask = mask_ref[here, :]
            d_row = d_context[row * length : (row + 1) * length]
            q, k, v = (qkv_ref[part, here, :] for part in range(3))
            keys = by_heads(k, HS)
            scores = back_product(q, keys) * size ** (-0.5)
            d_weights = back_product(d_row, by_heads(v, HS))
            low_weights, d_scores = [], []
            for head in range(HS):
                lanes = slice(head * length, (head + 1) * length)
                masked = jnp.where(mask > 0.0, scores[:, lanes], NEG_LARGE)
                expo = jnp.exp(masked - jnp.max(masked, -1, keepdims=True))
                weights = expo * (1.0 / jnp.sum(expo, -1, keepdims=True))
                low_weights.append(weights.astype(jnp.bfloat16))
                turned = weights * d_weights[:, lanes]
                made = turned - weights * jnp.sum(turned, -1, keepdims=True)
                if last:
                    differ = jnp.where(mask > 1.0, scores[:, lanes] - score_ref[here, lanes], 0.0)
                    loss_ref[...] += jnp.sum(differ * differ, 0, keepdims=True)
                    made = made + differ * (2.0 / count_ref[...])
                d_scores.append(made.astype(jnp.bfloat16))
            scale = size ** (-0.5)
            q_s[here, :] = (
                jnp.dot(jnp.concatenate(d_scores, 1), keys, preferred_element_type=jnp.float32)
                * scale
            ).astype(jnp.bfloat16)
            k_s[here, :] = (
                outer_product(jnp.concatenate(d_scores), by_heads(q, HS)) * scale
            ).astype(jnp.bfloat16)
            v_s[here, :] = outer_product(
                jnp.concatenate(low_weights), by_heads(d_row, HS)
            ).astype(jnp.bfloat16)
        d_hidden = d_one
        for part, held in enumerate((q_s, k_s, v_s)):
            d_part = held[at, :]
            if part != 1:
                note(part // 2, d_part)
            d_hidden = d_hidden + back_product(d_part, qkv_w[part])
        if first_layer:
            d_hidden = norm_back(
                d_hidden + more_ref[at, :],
                zero_ref[at, :],
                zero_inv[at, :],
                evec_ref[0:1, :],
                0,
                edge_ref,
            )
            for row in range(TILE // length):
                place_ref[...] += d_hidden[row * length : (row + 1) * length]
        hidden_ref[at, :] = d_hidden
        return carry

    lax.fori_loop(0, grad_ref.shape[0] // TILE, tile, 0)
    low = low_ref[...]
    dq_ref[...] = outer_product(low, q_s[...])
    dk_ref[...] = outer_product(low, k_s[...])
    dv_ref[...] = outer_product(low, v_s[...])
    do_ref[...] = outer_product(context_ref[...], attended_s[...])
    for first in range(0, WIDER, many):
        lanes = slice(first, first + many)
        stop = min(first + many, FS)
        dd_ref[first:stop, :] = outer_product(active_s[:, lanes], outer_s[...])[: stop - first]
        made = outer_product(middle_s[...], inner_s[:, lanes])
        for tile_at in range(many // 128):
            unfolded[first // 128 + tile_at] = made[:, 128 * tile_at : 128 * tile_at + 128]
    refold(unfolded, folded, FS, DS)
    for tile_at in range(-(-DS // 128)):
        lanes = min(128, DS - 128 * tile_at)
        du_ref[:, 128 * tile_at : 128 * tile_at + lanes] = folded[tile_at, :, :lanes]


def student_backward(grad, vectors, biases, mask, matrices, saved, last, first_layer):
    tokens, length = mask.shape
    full = partial(jax.ShapeDtypeStruct, dtype=jnp.float32)
    made = [
        full((tokens, DS)),
        *[full((DS, DS))] * 4,
        full((FS, DS)),
        full((FS, DS)),
        full((8, DS)),
        full((1, WIDER)),
    ]
    given = [grad, vectors, biases, mask, *matrices, *saved]
    given += first_layer
    if last:
        given += last
        made.append(full((1, length)))
    if first_layer:
        made += [full((length, DS)), full((8, DS))]
    low = partial(pltpu.VMEM, dtype=jnp.bfloat16)
    return pl.pallas_call(
        partial(back_kernel, bool(last), bool(first_layer)),
        out_shape=tuple(made),
        in_specs=[VMEM_SPEC] * len(given),
        out_specs=(VMEM_SPEC,) * len(made),
        scratch_shapes=[
            *[low((tokens, DS))] * 6,
            *[low((tokens, WIDER))] * 2,
            pltpu.VMEM((WIDER // 128, DS, 128), jnp.float32),
            pltpu.VMEM((-(-DS // 128), FS, 128), jnp.float32),
        ],
        compiler_params=pltpu.CompilerParams(vmem_limit_bytes=58 * 1024 * 1024),
        cost_estimate=pl.CostEstimate(
            flops=10**9, bytes_accessed=4 * 10**6, transcendentals=3 * 10**5
        ),
    )(*given)


def d_all_width(width):
    return -(-width // 128) * 128


def head_kernel(
    groups, pair, denom, p_all, t_ref, table_ref, head_ref, d_ref, own_ref, w_ref, *refs
):
    (
        t_all, p_turned, t_turned, s_logits, t_logits, stats, rows_of, inbox, total,
        send, recv, stat_send, stat_recv, d_send, d_recv, pair_send, pair_recv, out_sem,
    ) = refs
    amount, width = p_all.shape[1:]
    vocab = table_ref.shape[0]
    z_size = z_size_of(groups)
    side = groups // z_size
    across = z_size * amount
    half = d_all_width(width)
    dp, me = lax.axis_index("dp"), lax.axis_index("fsdp")
    z, y = me // side, me % side
    sibling = (dp // 2 * 2 + 1 - dp % 2, me)
    beside = ((dp + 2) % lax.axis_size("dp"), me)
    barrier = pltpu.get_barrier_semaphore()
    for step in range(1, groups):
        pl.semaphore_signal(
            barrier, inc=1, device_id=(dp, (me + step) % groups), device_id_type=MESH
        )
    if pair:
        for other in (sibling, beside):
            pl.semaphore_signal(barrier, inc=1, device_id=other, device_id_type=MESH)
    pl.semaphore_wait(barrier, groups - 1 + (2 if pair else 0))

    def both(at, rank, target, own=False):
        return [
            pltpu.make_async_remote_copy(
                t_ref if own else t_all.at[at],
                t_all.at[at],
                send.at[rank],
                recv.at[rank],
                device_id=(dp, target),
                device_id_type=MESH,
            )
        ]

    def begin(copies):
        for copy in copies:
            copy.start()

    def received(copies):
        for copy in copies:
            copy.wait_recv()

    def sent(copies):
        for copy in copies:
            copy.wait_send()

    def line(step):
        return z + step, (z + step >= 0) & (z + step < z_size)

    def inside(position):
        return jnp.minimum(jnp.maximum(position, 0), z_size - 1) * side

    def z_copies(step, way, arriving):
        origin, known = line(-way * (step + (1 if arriving else 0)))
        target, there = line(way)
        rank = 2 * step + (1 if way > 0 else 0)
        made = both(inside(origin) + y, rank, inside(target) + y, own=step == 0 and not arriving)
        return made, known if arriving else known & there

    def y_copies(back, step, at, own=False):
        return both(
            at, 2 * z_size + (back - 1) * z_size + step, z * side + (y + back) % side, own
        )

    wide = next(size for size in (384, 320, 128) if vocab % size == 0)

    def measure(back):
        at_y = (y + side - back) % side
        slots = [line * side + at_y for line in range(z_size)]
        t_turned[...] = jnp.concatenate([t_all[at] for at in slots]).astype(jnp.float32).T.astype(
            jnp.bfloat16
        )
        p_turned[...] = jnp.concatenate([p_all[at] for at in slots]).astype(jnp.float32).T.astype(
            jnp.bfloat16
        )

        def step(index, carry):
            s_top, s_sum, t_top, t_sum, cross = carry
            lines = pl.ds(pl.multiple_of(index * wide, 64), wide)
            t_now = jnp.dot(head_ref[lines, :], t_turned[...], preferred_element_type=jnp.float32)
            s_now = jnp.dot(table_ref[lines, 0:width], p_turned[...], preferred_element_type=jnp.float32)
            t_logits[back, lines, :] = t_now
            s_logits[back, lines, :] = s_now
            s_next = jnp.maximum(s_top, jnp.max(s_now, 0, keepdims=True))
            t_next = jnp.maximum(t_top, jnp.max(t_now, 0, keepdims=True))
            t_exp = jnp.exp(t_now - t_next)
            scale = jnp.exp(t_top - t_next)
            s_sum = s_sum * jnp.exp(s_top - s_next) + jnp.sum(
                jnp.exp(s_now - s_next), 0, keepdims=True
            )
            t_sum = t_sum * scale + jnp.sum(t_exp, 0, keepdims=True)
            cross = cross * scale + jnp.sum(t_exp * s_now, 0, keepdims=True)
            return (s_next, s_sum, t_next, t_sum, cross)

        lowest = jnp.full((1, across), -jnp.inf, jnp.float32)
        zero = jnp.zeros((1, across), jnp.float32)
        made = lax.fori_loop(0, vocab // wide, step, (lowest, zero, lowest, zero, zero))
        for index, value in enumerate(made):
            stats[me, at_y, index : index + 1, :] = value

    def stat_copy(step, back):
        at_y = (y + side - back) % side
        rank = back * groups + step
        return pltpu.make_async_remote_copy(
            stats.at[me, at_y],
            stats.at[me, at_y],
            stat_send.at[rank],
            stat_recv.at[rank],
            device_id=(dp, (me + step) % groups),
            device_id_type=MESH,
        )

    t_all[me] = t_ref[...]
    for way in (1, -1):
        made, wanted = z_copies(0, way, False)
        pl.when(wanted)(partial(begin, made))
    for back in range(1, side):
        begin(y_copies(back, z, me, own=True))
    for step in range(z_size - 1):
        for way in (1, -1):
            made, wanted = z_copies(step, way, True)
            onward, further = z_copies(step + 1, way, False) if step + 2 < z_size else (None, None)

            @pl.when(wanted)
            def _(made=made, onward=onward, further=further, step=step, way=way):
                received(made)
                if onward is not None:
                    pl.when(further)(partial(begin, onward))
                origin = z - way * (step + 1)
                for back in range(1, side):
                    begin(y_copies(back, origin, origin * side + y))

    for back in range(side):
        if back:
            for step in range(z_size):
                received(y_copies(back, step, step * side + (y + side - back) % side))
        measure(back)
        if back < side - 1:
            for step in range(1, groups):
                stat_copy(step, back).start()
    for step in range(z_size - 1):
        for way in (1, -1):
            made, wanted = z_copies(step, way, False)
            pl.when(wanted)(partial(sent, made))
    for back in range(1, side):
        for step in range(z_size):
            sent(y_copies(back, step, step * side + y))

    for step in range(1, groups):
        stat_copy(step, side - 1).start()
    for step in range(1, groups):
        for back in range(side):
            stat_copy(step, back).wait_recv()
    for back in range(side):
        at_y = (y + side - back) % side
        parts = [stats[other, at_y] for other in range(groups)]
        s_top, t_top = parts[0][0:1], parts[0][2:3]
        for part in parts[1:]:
            s_top = jnp.maximum(s_top, part[0:1])
            t_top = jnp.maximum(t_top, part[2:3])
        s_sum, t_sum, cross = (jnp.zeros_like(s_top) for unused in range(3))
        for part in parts:
            s_sum = s_sum + part[1:2] * jnp.exp(part[0:1] - s_top)
            scale = jnp.exp(part[2:3] - t_top)
            t_sum = t_sum + part[3:4] * scale
            cross = cross + part[4:5] * scale
        rows_of[back, 0:1, :] = s_top + jnp.log(s_sum)
        rows_of[back, 1:2, :] = t_top
        rows_of[back, 2:3, :] = 1.0 / t_sum
        rows_of[back, 3:4, :] = cross / t_sum
        total[back] = jnp.zeros((half, across), jnp.float32)
    own_ref[...] = rows_of[0]
    narrow = next(size for size in (320, 128) if vocab % size == 0)
    part = vocab // 4 if pair else vocab

    def rows_at(start, amount):
        return t_logits.at[0, pl.ds(pl.multiple_of(start, 64), amount), 0:half]

    def grade(first):
        def chunk(index, carry):
            lines = pl.ds(pl.multiple_of(first + index * narrow, 64), narrow)
            table = table_ref[lines, 0:width]
            made = jnp.zeros((narrow, width), jnp.float32)
            for back in range(side):
                row = rows_of[back]
                grads = 2.0 * jnp.exp(s_logits[back, lines, :] - row[0:1])
                grads = grads - jnp.exp(t_logits[back, lines, :] - row[1:2]) * row[2:3]
                low = (grads * (1.0 / denom)).astype(jnp.bfloat16)
                total[back, :width, :] += outer_product(table, low)
                at_y = (y + side - back) % side
                states = jnp.concatenate([p_all[line * side + at_y] for line in range(z_size)])
                made = made + jnp.dot(low, states, preferred_element_type=jnp.float32)
            t_logits[0, lines, 0:width] = made
            return carry

        lax.fori_loop(0, part // narrow, chunk, 0)

    def pair_copy(index, source, target):
        return pltpu.make_async_remote_copy(
            source,
            inbox.at[index],
            pair_send.at[index],
            pair_recv.at[index],
            device_id=target,
            device_id_type=MESH,
        )

    given = []
    if pair:
        x, core = dp // 2, dp % 2
        far, near = 1 - x, x

        def start_of(along, other):
            return (2 * along + (core + other) % 2) * part

        for index, (along, other) in enumerate(((far, 1), (far, 0), (near, 1), (near, 0))):
            grade(start_of(along, other))
            if other:
                given.append(pair_copy(index // 2, rows_at(start_of(along, other), part), sibling))
                given[-1].start()
            elif along is far:
                given[0].wait_recv()
                lines = pl.ds(pl.multiple_of(start_of(far, 0), 64), part)
                t_logits[0, lines, 0:half] += inbox[0]
                given.append(pair_copy(2, rows_at(start_of(far, 0), part), beside))
                given[-1].start()
    else:
        grade(0)
    for back in range(side):
        turned = total[back].T.astype(jnp.bfloat16)
        for line in range(z_size):
            at = line * side + (y + side - back) % side
            t_all[at, :, half : 2 * half] = turned[line * amount : (line + 1) * amount]

    def d_copy(step):
        peer = (me + step) % groups
        return pltpu.make_async_remote_copy(
            t_all.at[peer, :, half : 2 * half],
            t_all.at[me, :, 0:half],
            d_send.at[step],
            d_recv.at[step],
            device_id=(dp, peer),
            device_id_type=MESH,
        )

    for step in range(1, groups):
        d_copy(step).start()
    made = t_all[me, :, half : 2 * half].astype(jnp.float32)
    for step in range(1, groups):
        d_copy(step).wait_recv()
        made = made + t_all[(me + groups - step) % groups, :, 0:half].astype(jnp.float32)
    d_ref[...] = made
    kept = 0
    if pair:
        kept = start_of(near, 0)
        lines = pl.ds(pl.multiple_of(kept, 64), part)
        given[2].wait_recv()
        t_logits[0, lines, 0:half] += inbox[1]
        given[1].wait_recv()
        t_logits[0, lines, 0:half] += inbox[2]
    out = pltpu.make_async_copy(rows_at(kept, part), w_ref, out_sem)
    out.start()
    for step in range(1, groups):
        for back in range(side):
            stat_copy(step, back).wait_send()
        d_copy(step).wait_send()
    for copy in given:
        copy.wait_send()
    out.wait()


def head(picked, t_picked, table, teacher_head, denom, number):
    groups, n_dp = lax.axis_size("fsdp"), lax.axis_size("dp")
    pair = n_dp == 4
    amount, width = picked.shape[1:]
    vocab = table.shape[0]
    z_size = z_size_of(groups)
    side, across = groups // z_size, z_size * amount
    half = d_all_width(width)
    assert 2 * half <= DT
    full, low = jnp.float32, jnp.bfloat16
    anywhere = pl.BlockSpec(memory_space=pl.ANY)
    dma = pltpu.SemaphoreType.DMA
    made = [
        jax.ShapeDtypeStruct((amount, half), full),
        jax.ShapeDtypeStruct((8, across), full),
        jax.ShapeDtypeStruct((vocab // 4 if pair else vocab, half), full),
    ]
    return pl.pallas_call(
        partial(head_kernel, groups, pair, denom),
        out_shape=tuple(made),
        in_specs=[VMEM_SPEC] * 4,
        out_specs=(VMEM_SPEC, VMEM_SPEC) + (anywhere,) * (len(made) - 2),
        scratch_shapes=[
            pltpu.VMEM((groups, amount, DT), low),
            pltpu.VMEM((width, across), low),
            pltpu.VMEM((DT, across), low),
            pltpu.VMEM((side, vocab, across), full),
            pltpu.VMEM((side, vocab, across), full),
            pltpu.VMEM((groups, side, 8, across), full),
            pltpu.VMEM((side, 8, across), full),
            pltpu.VMEM((3, vocab // 4, half) if pair else (1, 8, 128), full),
            pltpu.VMEM((side, half, across), full),
            *[dma((2 * z_size + (side - 1) * z_size,))] * 2,
            *[dma((side * groups,))] * 2,
            *[dma((groups,))] * 2,
            *[dma((3,))] * 2,
            dma,
        ],
        compiler_params=pltpu.CompilerParams(
            collective_id=number, has_side_effects=True, vmem_limit_bytes=61 * 1024 * 1024
        ),
    )(picked, t_picked, table, teacher_head)


def three_parts(value):
    high = lax.reduce_precision(value, 8, 7)
    rest = value - high
    middle = lax.reduce_precision(rest, 8, 7)
    low = rest - middle
    return jnp.concatenate([high, middle, low], -1).astype(jnp.bfloat16)


def pick_exact(marks, value, turned=False):
    width = value.shape[1]
    terms = three_parts(value)
    made = outer_product(marks, terms) if turned else jnp.dot(
        marks, terms, preferred_element_type=jnp.float32
    )
    return made[:, :width] + made[:, width : 2 * width] + made[:, 2 * width :]


def plan_requests(ids, local_rows):
    order = lax.broadcasted_iota(jnp.int32, (ids.shape[0],), 0)
    same = ids[:, None] == ids[None, :]
    leader = jnp.min(jnp.where(same, order[None, :], ids.shape[0]), 1)
    leads = leader == order
    owner = ids // local_rows
    before = (
        (owner[:, None] == owner[None, :]) & leads[None, :] & (order[None, :] < leader[:, None])
    )
    rank = jnp.sum(before.astype(jnp.int32), 1)
    return (leads, owner, ids - owner * local_rows, rank)


def round_marks(plan, turn, devices):
    leads, owner, local_id, rank = plan
    inside = (rank >= turn * SLOTS) & (rank < (turn + 1) * SLOTS)
    slot = jnp.where(inside, owner * SLOTS + rank - turn * SLOTS, -1)
    line = lax.broadcasted_iota(jnp.int32, (devices * SLOTS, 1), 0)
    hit = line == slot[None, :]
    asked = jnp.max(jnp.where(hit & leads[None, :], local_id[None, :], -1), 1)
    return (hit.astype(jnp.bfloat16), asked.reshape(devices, 1, SLOTS))


def question(plan, turn, devices, extra):
    marks, asked = round_marks(plan, turn, devices)
    fill = jnp.full((devices, 1, 128 - SLOTS - extra.shape[0]), -1, jnp.int32)
    note = jnp.broadcast_to(extra[None, None, :], (devices, 1, extra.shape[0]))
    return (marks, jnp.concatenate([asked, note, fill], 2))


def ask(plan, turn, devices, extra):
    marks, asked = question(plan, turn, devices, extra)
    return (marks, exchange(asked, 0)[:, 0, :SLOTS].reshape(-1))


def wanted_marks(wanted, local_rows):
    return (wanted[:, None] == lax.broadcasted_iota(jnp.int32, (1, local_rows), 1)).astype(
        jnp.bfloat16
    )


def fetch(marks, wanted, table_low, devices):
    rows = jnp.dot(
        wanted_marks(wanted, table_low.shape[0]), table_low, preferred_element_type=jnp.float32
    ).astype(jnp.bfloat16)
    got = exchange(rows.reshape(devices, SLOTS, -1), 1)
    return outer_product(marks, got.reshape(devices * SLOTS, -1))


def give_back(marks, wanted, grads, local_rows, devices):
    sent = pick_exact(marks, grads)
    got = exchange(sent.reshape(devices, SLOTS, -1), 2)
    return pick_exact(wanted_marks(wanted, local_rows), got.reshape(devices * SLOTS, -1), True)


def finish_kernel(
    at, rows_ref, wanted_ref, more_ref, head_ref, reduced_ref, note_ref, g_ref, notes_ref, sent, send, recv
):
    count, me = notes_ref.shape[0], place_of()
    greet(count, me, True)
    value = rows_ref[...]
    width = value.shape[1]
    high = value.astype(jnp.bfloat16)
    rest = value - high.astype(jnp.float32)
    middle = rest.astype(jnp.bfloat16)
    low = (rest - middle.astype(jnp.float32)).astype(jnp.bfloat16)
    rows = more_ref.shape[0]
    squares = jnp.sum(reduced_ref[...] * reduced_ref[...], 0, keepdims=True)
    squares = jnp.sum(squares, 1, keepdims=True)
    for first in range(0, rows, 384):
        step = min(384, rows - first)
        line = lax.broadcasted_iota(jnp.int32, (step, value.shape[0]), 0)
        marks = jnp.where(line + first == wanted_ref[...], 1.0, 0.0).astype(jnp.bfloat16)
        made = more_ref[first : first + step, :] + head_ref[first : first + step, :width]
        for term in (high, middle, low):
            made = made + jnp.dot(marks, term, preferred_element_type=jnp.float32)
        g_ref[:, first : first + step] = made.T
        squares = squares + jnp.sum(jnp.sum(made * made, 0, keepdims=True), 1, keepdims=True)
    lane = lax.broadcasted_iota(jnp.int32, sent.shape, 1)
    note = jnp.where(lane == at, squares, note_ref[...])
    sent[...] = note
    notes_ref[me] = note

    def copy(step):
        return pltpu.make_async_remote_copy(
            sent,
            notes_ref.at[me],
            send.at[step],
            recv.at[step],
            device_id=member((me + step) % count, True),
            device_id_type=MESH,
        )

    def start(step, carry):
        copy(step).start()
        return carry

    def finish(step, carry):
        copy(step).wait()
        return carry

    lax.fori_loop(1, count, start, 0)
    lax.fori_loop(1, count, finish, 0)


def finish(row_blocks, wanted, more, head_grad, reduced, note, at, number):
    count = lax.axis_size("dp") * lax.axis_size("fsdp")
    dma = pltpu.SemaphoreType.DMA
    return pl.pallas_call(
        partial(finish_kernel, at),
        out_shape=(
            jax.ShapeDtypeStruct(more.shape[::-1], more.dtype),
            jax.ShapeDtypeStruct((count,) + note.shape, note.dtype),
        ),
        in_specs=[VMEM_SPEC] * 6,
        out_specs=(VMEM_SPEC,) * 2,
        scratch_shapes=[pltpu.VMEM(note.shape, note.dtype), dma((count,)), dma((count,))],
        compiler_params=pltpu.CompilerParams(
            collective_id=number, has_side_effects=True, vmem_limit_bytes=40 * 1024 * 1024
        ),
    )(row_blocks, wanted[None], more, head_grad, reduced, note)


def local(
    token_ids,
    valid_mask,
    seq_ids,
    mask_pos,
    mask_labels,
    teacher_in,
    teacher_flat,
    teacher_vec,
    teacher_head,
    emb_table,
    emb_first,
    emb_second,
    pos_table,
    pos_first,
    pos_second,
    layer_flat,
    layer_first,
    layer_second,
    proj_weight,
    proj_first,
    proj_second,
    layer_vec,
    vec_first,
    vec_second,
    misc_vec,
    misc_first,
    misc_second,
):
    micro, micro_rows, length = token_ids.shape
    rows = micro * micro_rows
    local_rows, width = emb_table.shape
    layers = layer_vec.shape[0]
    picks = mask_pos.shape[2]
    tokens = rows * length
    n_dp, groups = lax.axis_size("dp"), lax.axis_size("fsdp")
    place = lax.axis_index("fsdp")
    devices = n_dp * groups
    hidden_denom = float(rows * devices * length * DT)
    predict_denom = float(rows * devices * picks)
    flat_local = layer_flat.shape[1]
    by_rows = flat_local % DS == 0

    to_owner = [
        (d * groups + f, f * n_dp + d) for d in range(n_dp) for f in range(groups)
    ]
    from_owner = [(owner, holder) for holder, owner in to_owner]
    table_low = emb_table.astype(jnp.bfloat16)

    usable = valid_mask.reshape(rows, length) > 0
    docs = seq_ids.reshape(rows, length)
    same_doc = docs[:, :, None] == docs[:, None, :]
    pair_mask = same_doc & usable[:, :, None] & usable[:, None, :]
    allowed = pair_mask | jnp.eye(length, dtype=bool)
    ids = jnp.concatenate([token_ids.reshape(-1), mask_labels.reshape(-1)])
    plan = plan_requests(ids, local_rows)
    extra = jnp.stack([-1 - jnp.sum(pair_mask.astype(jnp.int32)), -1 - jnp.max(plan[3])])
    teacher_lines = teacher_flat.reshape(-1, DT)
    teacher_all = lax.all_gather(teacher_lines, BOTH, axis=0, tiled=True).reshape(-1, CHUNK, DT)
    own_parts = [
        layer_flat.astype(jnp.bfloat16),
        pos_table.astype(jnp.bfloat16),
        proj_weight.astype(jnp.bfloat16).T,
    ]
    if by_rows:
        chunk = flat_local // DS
        own_layers = [woven(part.reshape(-1, DS), False) for part in own_parts[0]]
        own_parts = [part.reshape(1, -1, DS) for part in own_layers + own_parts[1:]]
        line, lines = DS, sum(part.shape[1] for part in own_parts)
    else:
        own_parts = [part.reshape(1, -1) for part in own_parts]
        line, lines = 128, -(-sum(part.shape[1] for part in own_parts) // 128)
    block_rows = -(-lines // 16) * 16
    marks, asked = question(plan, 0, devices, extra)
    got, weights_all, token_blocks = entry(asked, pack(own_parts, line, block_rows)[0], table_low, 3)
    table_then = lax.optimization_barrier((table_low, got))[0]
    table_then = jnp.pad(table_then, ((0, 0), (0, d_all_width(width) - width)))
    slice_part = lax.ppermute(table_then, BOTH, from_owner)
    wanted = got[:, 0, :SLOTS].reshape(-1)
    notes = got[:, 0, SLOTS : SLOTS + 2]
    count = jnp.sum(-1 - notes[:, 0]).astype(jnp.float32)
    rounds = jnp.max(-1 - notes[:, 1]) // SLOTS + 1
    all_rows = outer_product(marks, token_blocks.reshape(devices * SLOTS, width))

    def more_rows(state):
        turn, so_far = state
        marks_now, wanted_now = ask(plan, turn, devices, extra)
        return (turn + 1, so_far + fetch(marks_now, wanted_now, table_low, devices))

    all_rows = lax.while_loop(lambda state: state[0] < rounds, more_rows, (1, all_rows))[1]
    token_rows, label_rows = (all_rows[:tokens], all_rows[tokens:])
    pos_local, proj_local = pos_table.shape[0], proj_weight.shape[1]
    if by_rows:
        where, matrices = block_plan(devices, chunk, layers, (pos_local, proj_local)), []
    else:
        where = ()
        flat_all = weights_all.reshape(devices, -1)
        split = []
        for index in range(layers):
            wide = flat_all[:, index * flat_local : (index + 1) * flat_local].reshape(WIDE, DS)
            qkv, out, up, down = split_rows(wide, DS, FS)
            split.append(
                (
                    qkv.reshape(DS, 3, DS).transpose(1, 0, 2),
                    out,
                    jnp.pad(up, ((0, 0), (0, WIDER - FS))),
                    jnp.pad(down, ((0, WIDER - FS), (0, 0))),
                )
            )
        matrices = sum(map(list, split), [])
        start = layers * flat_local
        places_all = flat_all[:, start : start + pos_local * DS].reshape(length, DS)
        start += pos_local * DS
        matrices += [places_all, flat_all[:, start : start + proj_local * DS].reshape(DT, DS)]

    proj_bias = misc_vec[2 * DS :]
    evec = misc_vec[: 2 * DS].reshape(2, DS)
    cut = 5 * DS
    vectors = jnp.concatenate([layer_vec[:, :cut], layer_vec[:, cut + FS :]], 1).reshape(
        layers, 8, DS
    )
    biases = jnp.pad(layer_vec[:, cut : cut + FS], ((0, 0), (0, WIDER - FS)))[:, None]

    mask = jnp.where(pair_mask, 2.0, jnp.where(allowed, 1.0, 0.0)).reshape(tokens, length)
    matrices, made = student_forward(
        token_rows, evec, vectors, biases, mask, where, weights_all, matrices
    )
    embedded, normed_zero, inverse_zero, hidden, *saved = made
    proj_all = matrices[-1]
    slice_part = lax.optimization_barrier((slice_part, teacher_all, hidden))[0]
    slice_table = lax.all_gather(slice_part, "dp", axis=0, tiled=True)

    flat_pick = (
        jnp.arange(rows, dtype=jnp.int32)[:, None] * length + mask_pos.reshape(rows, picks)
    ).reshape(-1)
    weight = valid_mask.reshape(tokens, 1).astype(jnp.float32)
    t_scores, back_zero, back_last, grad_proj, grad_bias, squares_of, picked_all, t_picked = (
        teacher_forward(
            teacher_in.reshape(tokens, DT),
            teacher_all,
            teacher_vec.astype(jnp.float32)[None],
            mask,
            embedded,
            hidden,
            proj_all,
            proj_bias[None],
            weight,
            flat_pick[:, None],
            hidden_denom,
        )
    )
    hidden_sum = jnp.sum(squares_of) / hidden_denom
    pick_marks = (flat_pick[:, None] == lax.broadcasted_iota(jnp.int32, (1, tokens), 1)).astype(
        jnp.bfloat16
    )
    picked = lax.dynamic_index_in_dim(picked_all, place, 0, False)
    d_picked, own_stats, head_grad = head(
        picked_all, t_picked, slice_table, teacher_head, predict_denom, 4
    )
    own_z = place // (groups // z_size_of(groups))
    own_stats = lax.dynamic_slice_in_dim(own_stats, own_z * rows * picks, rows * picks, 1)
    picked_wide = picked.astype(jnp.float32)
    target_logit = jnp.sum(picked_wide * label_rows, -1)
    predict_sum = (
        jnp.sum(2.0 * own_stats[0] - own_stats[3] - target_logit) / predict_denom
    )
    d_picked = d_picked[:, :width] - label_rows / predict_denom
    d_hidden = pick_exact(pick_marks, d_picked, True) + back_last

    if n_dp != 4:
        head_grad = lax.psum_scatter(head_grad, "dp", scatter_dimension=0, tiled=True)

    matrix_grads = [None] * layers
    vector_grads = [None] * layers
    attention_sum = jnp.float32(0.0)
    head_grad = lax.ppermute(head_grad, BOTH, to_owner)
    for layer_index in reversed(range(layers)):
        d_hidden, *others = student_backward(
            d_hidden,
            vectors[layer_index],
            biases[layer_index],
            mask,
            matrices[4 * layer_index : 4 * layer_index + 4],
            saved[7 * layer_index : 7 * layer_index + 7],
            [t_scores, count.reshape(1, 1)] if layer_index == layers - 1 else [],
            [] if layer_index else [back_zero, normed_zero, inverse_zero, evec],
        )
        matrix_grads[layer_index] = others[:6]
        d_vectors, d_bias_up, more = others[6], others[7], others[8:]
        d_vectors = d_vectors.reshape(-1)
        vector_grads[layer_index] = jnp.concatenate(
            [d_vectors[:cut], d_bias_up[0, :FS], d_vectors[cut:]]
        )
        if layer_index == layers - 1:
            attention_sum = jnp.sum(more.pop(0)) / count
    d_hidden, head_grad = lax.optimization_barrier((d_hidden, head_grad))
    d_token, (grad_places, d_edge) = d_hidden, more

    row_grads = jnp.concatenate([d_token, -picked_wide / predict_denom])
    def more_grads(state):
        turn, so_far = state
        marks_now, wanted_now = ask(plan, turn, devices, extra)
        return (
            turn + 1,
            so_far + give_back(marks_now, wanted_now, row_grads, local_rows, devices),
        )

    grad_small = jnp.concatenate(vector_grads + [d_edge[0], d_edge[1], grad_bias[0]])
    small_local = -(-grad_small.shape[0] // devices)
    small_local = -(-small_local // DS) * DS
    small_padded = jnp.pad(grad_small, (0, devices * small_local - grad_small.shape[0]))
    rest = [grad_places, grad_proj, small_padded.reshape(-1, DS)]
    sizes = [flat_local] * layers + [part.size // devices for part in rest]
    lines = -(-sum(sizes) // line)
    block = (-(-lines // 8) * 8, line)
    sent = pick_exact(marks, row_grads).reshape(devices, SLOTS, width)
    if by_rows:
        amounts = [size // DS for size in sizes[layers:]]
        grad_parts = sum(matrix_grads, []) + rest
        block_rows_of = block_plan(devices, chunk, layers, amounts)
    else:
        wides = []
        for grads in matrix_grads:
            first = jnp.stack(grads[:3], 1).reshape(-1, width)
            wides.append(jnp.concatenate([first, *grads[3:]]))
        grad_parts = [pack([part.reshape(devices, -1) for part in wides + rest], *block[::-1])]
        block_rows_of = ()
    reduced, row_blocks = reduce(grad_parts, block_rows_of, block, sent, 7)
    more = jnp.zeros((local_rows, width), jnp.float32)
    more = lax.while_loop(lambda state: state[0] < rounds, more_grads, (1, more))[1]
    if by_rows:
        pieces = []
        start = 0
        for size in sizes:
            pieces.append(reduced[start : start + size // DS])
            start += size // DS
    else:
        pieces = cut_pieces(reduced.reshape(-1), sizes)
    if by_rows:
        pieces[:layers] = [woven(piece, True) for piece in pieces[:layers]]
    layer_acc = jnp.stack([piece.reshape(-1) for piece in pieces[:layers]])
    g_places = pieces[layers].reshape(pos_local, DS)
    g_proj = pieces[layers + 1].reshape(proj_local, DS).T
    small_part = pieces[layers + 2].reshape(-1)
    note = jnp.concatenate(
        [small_part, (attention_sum + hidden_sum + predict_sum).reshape(1)]
    )
    note = jnp.pad(note, (0, -(-(small_local + 2) // 128) * 128 - note.shape[0])).reshape(1, -1)
    g_table, notes_all = finish(
        row_blocks.reshape(devices * SLOTS, width),
        wanted,
        more,
        head_grad,
        reduced,
        note,
        small_local + 1,
        8,
    )
    g_table, notes_all = g_table.T, notes_all[:, 0]
    small = notes_all[:, :small_local].reshape(-1)
    loss = jnp.sum(notes_all[:, small_local])
    norm = jnp.sqrt(jnp.sum(notes_all[:, small_local + 1]))
    g_vec = small[: layer_vec.size].reshape(layer_vec.shape)
    g_misc = small[layer_vec.size : layer_vec.size + misc_vec.shape[0]]
    factor = CLIP_NORM / jnp.maximum(norm, CLIP_NORM)
    return (
        loss,
        count,
        norm,
        *adam_update(emb_table, emb_first, emb_second, g_table * factor),
        *adam_update(pos_table, pos_first, pos_second, g_places * factor),
        *adam_update(layer_flat, layer_first, layer_second, layer_acc * factor),
        *adam_update(proj_weight, proj_first, proj_second, g_proj * factor),
        *adam_update(layer_vec, vec_first, vec_second, g_vec * factor),
        *adam_update(misc_vec, misc_first, misc_second, g_misc * factor),
    )


def solution(mesh):
    rows, lines, flat, tail, every = (
        P(None, BOTH),
        P(BOTH, None),
        P(BOTH),
        P(None, BOTH),
        P(),
    )
    placed = (
        *[rows] * 6,
        flat,
        every,
        P("fsdp", None),
        *[lines] * 6,
        *[tail] * 6,
        *[every] * 6,
    )
    return jax.shard_map(
        local,
        mesh=mesh,
        in_specs=placed,
        out_specs=(*[every] * 3, *[lines] * 6, *[tail] * 6, *[every] * 6),
        check_vma=False,
    )
```
